32 devices in a mesh: shard: 2 (over x), ctx: 4 (over y, core), tp: 4 (over z).
Axes of the slice: x: 2, y: 2, z: 4, core: 2. Of those that a mesh axis runs over, the one named last changes fastest.
Arguments:
- tokens_in: bfloat16 [8, 1024, 768], P('shard', 'ctx'), may hold values from -6 to 6
- qkv_weight: bfloat16 [3, 768, 768], P(None, ('shard', 'ctx'), 'tp'), may hold values from -0.21875 to 0.21875
- qv_bias: bfloat16 [2, 768], P(None, 'tp'), may hold values from -3 to 3
- out_weight: bfloat16 [768, 768], P('tp', ('shard', 'ctx')), may hold values from -0.875 to 0.875
- geglu_weight: bfloat16 [2, 768, 3072], P(None, ('shard', 'ctx'), 'tp'), may hold values from -0.21875 to 0.21875
- geglu_bias: bfloat16 [2, 3072], P(None, 'tp'), may hold values from -3 to 3
- down_weight: bfloat16 [3072, 768], P('tp', ('shard', 'ctx')), may hold values from -0.15625 to 0.15625
- norm_gains: bfloat16 [2, 768], P(None, ('shard', 'ctx')), may hold values from 0.099609375 to 1.8984375
- norm_biases: bfloat16 [2, 768], P(None, ('shard', 'ctx')), may hold values from -2 to 2
- out_biases: bfloat16 [2, 768], P(None, ('shard', 'ctx')), may hold values from -2 to 2
- doc_lengths: int32 [8, 8], P('shard'), may hold values from 1 to 1017, as said below
- cotangent: bfloat16 [8, 1024, 768], P('shard', 'ctx'), may hold values from -6 to 6
Outputs:
- layer_out: bfloat16 [8, 1024, 768], P('shard', 'ctx')
- input_grad: float32 [8, 1024, 768], P('shard', 'ctx')
- grad_qkv: float32 [3, 768, 768], P(None, ('shard', 'ctx'), 'tp')
- grad_qv_bias: float32 [2, 768], P(None, 'tp')
- grad_out_weight: float32 [768, 768], P('tp', ('shard', 'ctx'))
- grad_geglu_weight: float32 [2, 768, 3072], P(None, ('shard', 'ctx'), 'tp')
- grad_geglu_bias: float32 [2, 3072], P(None, 'tp')
- grad_down_weight: float32 [3072, 768], P('tp', ('shard', 'ctx'))
- grad_norm_gains: float32 [2, 768], P(None, ('shard', 'ctx'))
- grad_norm_biases: float32 [2, 768], P(None, ('shard', 'ctx'))
- grad_out_biases: float32 [2, 768], P(None, ('shard', 'ctx'))
The draws below stay inside these ranges and needn't reach their ends.
Inputs may be any that keep to these rules, and one draw needn't show every extreme that they name: `doc_lengths`: each row holds 8 positive document lengths that sum to 1024; documents fill the sequence in order.
All inputs are finite; a program needn't handle non-finite values.
Results may differ from the reference program's by a relative error of at most 0.015.
Values may be sent and summed in bfloat16 or wider, within the bound.
A program may use at most 256 MiB of HBM per device.

```python
import math
import jax
import jax.numpy as jnp
from jax import lax

D = 768
H = 12
DH = 64
FF = 3072
HD = 768
LEN = 1024
DOCS = 8
SEQS = 8
N_CTX = 4


def draw_doc_lengths(key, part):
    key = jax.random.fold_in(key, 11)
    pick_key, size_key = jax.random.split(key)
    longest = jax.random.randint(pick_key, (SEQS, 1), 0, DOCS)
    most_short = max(1, (LEN // N_CTX - 1) // (DOCS - 1))
    shorts = jax.random.randint(size_key, (SEQS, DOCS), 1, most_short + 1)
    places = jnp.arange(DOCS, dtype=jnp.int32)[None, :]
    shorts = jnp.where(places == longest, 0, shorts)
    remainder = LEN - jnp.sum(shorts, axis=1, keepdims=True)
    return jnp.where(places == longest, remainder, shorts).astype(jnp.int32)


def levels(key, extent, cuts, least, top_value):
    gain = 1.0
    for dim, blocks in cuts:
        heights = jax.random.uniform(jax.random.fold_in(jax.random.fold_in(key, 6), dim), (blocks,), jnp.float32, least / len(cuts), top_value / len(cuts))
        gain = gain * jnp.repeat(jnp.exp(heights), extent[dim] // blocks).reshape((-1,) + (1,) * (len(extent) - 1 - dim))
    return gain


def gaussian(own_key, extent, width, limit, shards=(), kind=jnp.bfloat16):
    entries = width * jax.random.normal(own_key, extent, jnp.float32)
    if shards:
        entries = entries * levels(own_key, extent, shards, -0.22, 0.18)
    return jnp.clip(entries, -limit, limit).astype(kind)


def setup_inputs(seed: int = 0) -> dict:
    seeds = jax.random.split(jax.random.key(seed), 13)
    return {
        "tokens_in": gaussian(seeds[0], (SEQS, LEN, D), 1.0, 6.0, ((0, 2), (1, 4))),
        "qkv_weight": gaussian(seeds[1], (3, D, HD), D ** -0.5, 0.21875, ((1, 8), (2, 4))),
        "qv_bias": gaussian(seeds[2], (2, HD), 0.5, 3.0, ((1, 4),)),
        "out_weight": gaussian(seeds[3], (HD, D), (HD // 16) ** -0.5, 0.875, ((0, 4), (1, 8))),
        "geglu_weight": gaussian(seeds[4], (2, D, FF), D ** -0.5, 0.21875, ((1, 8), (2, 4))),
        "geglu_bias": gaussian(seeds[5], (2, FF), 0.5, 3.0, ((1, 4),)),
        "down_weight": gaussian(seeds[6], (FF, D), (FF // 2) ** -0.5, 0.15625, ((0, 4), (1, 8))),
        "norm_gains": jnp.clip(1.0 + 0.18 * jax.random.normal(seeds[7], (2, D), jnp.float32), 0.099609375, 1.8984375).astype(jnp.bfloat16),
        "norm_biases": gaussian(seeds[8], (2, D), 0.3, 2.0, ((1, 8),)),
        "out_biases": gaussian(seeds[9], (2, D), 0.3, 2.0, ((1, 8),)),
        "doc_lengths": draw_doc_lengths(jax.random.fold_in(seeds[12], 71), 0),
        "cotangent": gaussian(seeds[11], (SEQS, LEN, D), 1.0, 6.0, ((0, 2), (1, 4))),
    }


@jax.custom_vjp
def low(v):
    return lax.optimization_barrier(v.astype(jnp.bfloat16)).astype(jnp.float32)

@jax.custom_vjp
def low_back(v):
    return v

def low_keep(v):
    return (low(v), None)

def low_pass(kept, grad):
    return (grad,)

def back_keep(v):
    return (v, None)

def back_low(kept, grad):
    return (low(grad),)
low.defvjp(low_keep, low_pass)
low_back.defvjp(back_keep, back_low)

def alibi_slopes(head_count):

    def power_slopes(head_total):
        first_slope = 2.0 ** (-8.0 / head_total)
        return [first_slope ** (counter + 1) for counter in range(head_total)]
    nearest = 2 ** int(math.floor(math.log2(head_count)))
    slope_list = power_slopes(nearest)
    if nearest < head_count:
        slope_list = slope_list + power_slopes(2 * nearest)[0::2][:head_count - nearest]
    return slope_list

def highest(left, right):
    return jnp.dot(left, right, precision=lax.Precision.HIGHEST, preferred_element_type=jnp.float32)

def layer_norm(values, gain_vector, shift_vector):
    center = values - lax.optimization_barrier(jnp.mean(values, axis=-1, keepdims=True))
    spread = lax.optimization_barrier(jnp.mean(center * center, axis=-1, keepdims=True))
    return center * lax.rsqrt(spread + 1e-12) * gain_vector + shift_vector

def sequence_layer(tokens, weights, segment, slopes, position):
    qkv_weight, qv_bias, out_weight, geglu_weight, geglu_bias, down_weight, norm_gains, norm_biases, out_biases = weights
    length = tokens.shape[0]
    queries = low_back(low(highest(tokens, qkv_weight[0]) + qv_bias[0]))
    key_rows = low_back(low(highest(tokens, qkv_weight[1])))
    value_rows = low_back(low(highest(tokens, qkv_weight[2]) + qv_bias[1]))
    queries = queries.reshape(length, H, DH)
    key_rows = key_rows.reshape(length, H, DH)
    value_rows = value_rows.reshape(length, H, DH)
    scores = jnp.einsum('qhd,khd->hqk', queries, key_rows, precision=lax.Precision.HIGHEST) * (1.0 / math.sqrt(DH))
    distance = jnp.abs(position[:, None] - position[None, :]).astype(jnp.float32)
    scores = scores - slopes[:, None, None] * distance[None]
    same_doc = segment[:, None] == segment[None, :]
    scores = low_back(jnp.where(same_doc[None], scores, -1e+30))
    row_max = lax.optimization_barrier(jnp.max(scores, axis=-1, keepdims=True))
    powered = jnp.exp(scores - row_max)
    probs = low(powered / lax.optimization_barrier(jnp.sum(powered, axis=-1, keepdims=True)))
    mixed_heads = jnp.einsum('hqk,khd->qhd', probs, value_rows, precision=lax.Precision.HIGHEST).reshape(length, H * DH)
    mixed_heads = low_back(low(mixed_heads))
    attended = low_back(highest(mixed_heads, out_weight) + out_biases[0])
    normed = layer_norm(tokens + attended, norm_gains[0], norm_biases[0])
    normed_low = low(normed)
    gate_pre = low_back(highest(normed_low, geglu_weight[0]) + geglu_bias[0])
    upward = low_back(highest(normed_low, geglu_weight[1]) + geglu_bias[1])
    hidden = low(jax.nn.gelu(gate_pre, approximate=False) * upward)
    branch = low_back(highest(hidden, down_weight) + out_biases[1])
    return layer_norm(normed + branch, norm_gains[1], norm_biases[1])

def reference(tokens_in, qkv_weight, qv_bias, out_weight, geglu_weight, geglu_bias, down_weight, norm_gains, norm_biases, out_biases, doc_lengths, cotangent):
    params = tuple((array_in.astype(jnp.float32) for array_in in (qkv_weight, qv_bias, out_weight, geglu_weight, geglu_bias, down_weight, norm_gains, norm_biases, out_biases)))
    slopes = jnp.asarray(alibi_slopes(H), jnp.float32)
    position = jnp.arange(LEN, dtype=jnp.int32)

    def per_sequence(totals, inputs):
        tokens, lengths, upstream = inputs
        doc_ends = jnp.cumsum(lengths).astype(jnp.int32)
        segment = lax.optimization_barrier(jnp.sum((position[:, None] >= doc_ends[None, :]).astype(jnp.int32), axis=1))

        def forward(tokens_float, *weights):
            return sequence_layer(tokens_float, weights, segment, slopes, position)
        output, pullback = jax.vjp(forward, tokens.astype(jnp.float32), *params)
        grads = pullback(upstream.astype(jnp.float32))
        totals = tuple((running + fresh for running, fresh in zip(totals, grads[1:])))
        return (totals, (output.astype(jnp.bfloat16), grads[0]))
    zeros = tuple((jnp.zeros_like(array_in) for array_in in params))
    totals, (outputs, input_grads) = lax.scan(per_sequence, zeros, (tokens_in, doc_lengths, cotangent))
    return (outputs, input_grads, totals[0], totals[1], totals[2], totals[3], totals[4], totals[5], totals[6], totals[7], totals[8])
```

```python
import functools
import math

import jax
import jax.numpy as jnp
from jax import lax
from jax.experimental import pallas as pl
from jax.experimental.pallas import tpu as pltpu
from jax.sharding import PartitionSpec as P

H = 12
DH = 64
F32 = jnp.float32
BF16 = jnp.bfloat16
MESH = pl.DeviceIdType.MESH
NCH = 2
TILE = 32
MB = 1 << 20


def alibi_slopes(head_count):
    def power_slopes(head_total):
        first_slope = 2.0 ** (-8.0 / head_total)
        return [first_slope ** (counter + 1) for counter in range(head_total)]

    nearest = 2 ** int(math.floor(math.log2(head_count)))
    slope_list = power_slopes(nearest)
    return slope_list + power_slopes(2 * nearest)[0::2][: head_count - nearest]


def dot(left, right):
    return jnp.dot(left, right, preferred_element_type=F32)


def dot_nt(left, right):
    return lax.dot_general(left, right, (((1,), (1,)), ((), ())), preferred_element_type=F32)


def dot_tn(left, right):
    return lax.dot_general(left, right, (((0,), (0,)), ((), ())), preferred_element_type=F32)


def vmem(count):
    return [pl.BlockSpec(memory_space=pltpu.VMEM)] * count


def attention_forward(
    heads, lengths, slopes, xs, w, bias, mixed, probs, q_out, k_out, v_out, far
):
    length = xs.shape[0]
    step = 256
    cols = heads * DH
    mine = lax.axis_index("ctx") * heads

    def project(r, carry):
        rows = pl.ds(pl.multiple_of(r * step, step), step)
        x_rows = xs[rows, :]
        for part, out in enumerate((q_out, k_out, v_out)):
            y = dot(x_rows, w[:, part * cols : (part + 1) * cols])
            if part != 1:
                y = y + bias[part // 2 : part // 2 + 1, :]
            y = y.astype(BF16)
            if part == 0:
                y = y * BF16(1.0 / math.sqrt(DH))
            for i in range(heads):
                out[i, rows, :] = y[:, i * DH : (i + 1) * DH]
        return carry

    lax.fori_loop(0, length // step, project, 0)

    def segments(pos):
        seg = jnp.zeros(pos.shape, jnp.int32)
        end = 0
        for k in range(lengths.shape[1]):
            end = end + lengths[0, k]
            seg = seg + (pos >= end).astype(jnp.int32)
        return seg

    key_pos = lax.broadcasted_iota(jnp.int32, (1, length), 1)
    key_seg = segments(key_pos)

    def attend(r, carry):
        start = pl.multiple_of(r * step, step)
        rows = pl.ds(start, step)
        pos = start + lax.broadcasted_iota(jnp.int32, (step, 1), 0)
        same = segments(pos) == key_seg
        far[...] = jnp.where(same, jnp.abs(pos - key_pos).astype(F32), 1e33)
        for i in range(heads):
            s = dot_nt(q_out[i, rows, :], k_out[i]) - slopes[0, mine + i] * far[...]
            p = jnp.exp(s - jnp.max(s, axis=-1, keepdims=True))
            p = (p * (1.0 / jnp.sum(p, axis=-1, keepdims=True))).astype(BF16)
            probs[i, rows, :] = p
            mixed[rows, i * DH : (i + 1) * DH] = dot(p, v_out[i]).astype(BF16)
        return carry

    lax.fori_loop(0, length // step, attend, 0)


def attention_backward(
    heads, dmixed, mixed, probs, q, k, v, xs, w, grad_w, d_in, bias_grad, dqkv, dk_acc, dv_acc
):
    length = xs.shape[0]
    step = 256
    cols = heads * DH
    dk_acc[...] = jnp.zeros_like(dk_acc)
    dv_acc[...] = jnp.zeros_like(dv_acc)

    def rows_back(r, carry):
        rows = pl.ds(pl.multiple_of(r * step, step), step)
        for i in range(heads):
            own = slice(i * DH, (i + 1) * DH)
            d_out = dmixed[rows, own]
            row_dot = jnp.sum(
                d_out.astype(F32) * mixed[rows, own].astype(F32), axis=-1, keepdims=True
            )
            p = probs[i, rows, :]
            dp = dot_nt(d_out, v[i])
            ds = (p.astype(F32) * (dp - row_dot)).astype(BF16)
            dqkv[rows, own] = (dot(ds, k[i]) * (1.0 / math.sqrt(DH))).astype(BF16)
            dk_acc[i] += dot_tn(q[i, rows, :], ds)
            dv_acc[i] += dot_tn(d_out, p)
        return carry

    lax.fori_loop(0, length // step, rows_back, 0)
    for i in range(heads):
        dqkv[:, cols + i * DH : cols + (i + 1) * DH] = dk_acc[i].T.astype(BF16)
        dqkv[:, 2 * cols + i * DH : 2 * cols + (i + 1) * DH] = dv_acc[i].T.astype(BF16)

    def finish(r, total):
        rows = pl.ds(pl.multiple_of(r * step, step), step)
        d = dqkv[rows, :]
        d_in[rows, :] = dot_nt(d, w[:, : 3 * cols]).astype(BF16)
        return total + jnp.sum(d.astype(F32), axis=0, keepdims=True)

    bias_grad[...] = lax.fori_loop(
        0, length // step, finish, jnp.zeros((1, 3 * cols), F32)
    )
    for part in range(3):
        own = slice(part * cols, (part + 1) * cols)
        grad_w[:, own] = dot_tn(xs[...], dqkv[:, own]).astype(BF16)


def middle(
    x, cot, mixed, w, vec,
    lout, dres1, grads, gout, dmixed, small,
    w_out, full, act, pull, hid, dgt, dup,
    snd_r, snd_o, snd_y, rcv_r, rcv_o, rcv_y,
    own, yacc, fa, fb, normed, zh1, r1, dres2, acc, bsum, tiny,
    ags_y, agr_y, ags_c, agr_c, ags_f, agr_f,
    rss_r, rsr_r, rss_o, rsr_o, rss_y, rsr_y, tiny_s, tiny_r,
):
    rows_own = x.shape[0]
    width = x.shape[1]
    cr = rows_own // NCH
    c = lax.axis_index("ctx")
    flip = 1 - 2 * (c % 2)
    sib = c + flip
    ynb = (c + 2) % 4
    dia = ynb + flip

    barrier = pltpu.get_barrier_semaphore()
    for peer in (sib, ynb):
        pl.semaphore_signal(barrier, inc=1, device_id={"ctx": peer}, device_id_type=MESH)
    pl.semaphore_wait(barrier, 2)

    started = []

    def remote(src, dst, send, recv, peer):
        return pltpu.make_async_remote_copy(
            src_ref=src, dst_ref=dst, send_sem=send, recv_sem=recv,
            device_id={"ctx": peer}, device_id_type=MESH,
        )

    def chunk(k):
        return pl.ds(k * cr, cr)

    ag_y, ag_c, ag_f, rs_r, rs_o, rs_y = ({} for _ in range(6))

    def start(table, key, copy):
        copy.start()
        table[key] = copy
        started.append(copy)

    def gather_start(o, k):
        piece = full.at[o, c, chunk(k)]
        start(ag_y, (o, k), remote(piece, piece, ags_y.at[o, k], agr_y.at[o, k], ynb))
        start(ag_c, (o, k), remote(piece, piece, ags_c.at[o, k], agr_c.at[o, k], sib))

    def forward(o, k):
        ag_y[o, k].wait_recv()
        piece = full.at[o, ynb, chunk(k)]
        start(ag_f, (o, k), remote(piece, piece, ags_f.at[o, k], agr_f.at[o, k], sib))

    def send_relay(o, k):
        start(rs_r, (o, k), remote(
            snd_r.at[o, chunk(k)], rcv_r.at[o, chunk(k)], rss_r.at[o, k], rsr_r.at[o, k], sib))

    def send_own(o, k):
        start(rs_o, (o, k), remote(
            snd_o.at[o, chunk(k)], rcv_o.at[o, chunk(k)], rss_o.at[o, k], rsr_o.at[o, k], sib))

    def relay(o, k):
        rs_r[o, k].wait_recv()
        snd_y[o, chunk(k), :] = (yacc[chunk(k), :] + rcv_r[o, chunk(k), :].astype(F32)).astype(BF16)
        start(rs_y, (o, k), remote(
            snd_y.at[o, chunk(k)], rcv_y.at[o, chunk(k)], rss_y.at[o, k], rsr_y.at[o, k], ynb))

    def arrived(o, k):
        rs_o[o, k].wait_recv()
        rs_y[o, k].wait_recv()

    def tiles(first, count, body):
        def step(t, carry):
            body(pl.ds(pl.multiple_of(first + t * TILE, TILE), TILE))
            return carry
        lax.fori_loop(0, count // TILE, step, 0)

    def summed(o, rows):
        return own[rows, :] + rcv_o[o, rows, :].astype(F32) + rcv_y[o, rows, :].astype(F32)

    def fold(values):
        return jnp.sum(values.reshape(TILE // 8, 8, width), axis=0)

    acc[...] = jnp.zeros_like(acc)
    bsum[...] = jnp.zeros_like(bsum)
    w_out[...] = w[0, :, 3 * mixed.shape[2] : 4 * mixed.shape[2]]

    def project(b, r0, n):
        return dot_nt(mixed[b, pl.ds(r0, n), :], w_out[...])

    for k in range(NCH):
        snd_r[0, chunk(k), :] = project(dia, k * cr, cr).astype(BF16)
        send_relay(0, k)
        yacc[chunk(k), :] = project(ynb, k * cr, cr)
        if k:
            relay(0, k - 1)
    relay(0, NCH - 1)
    for k in range(NCH):
        snd_o[0, chunk(k), :] = project(sib, k * cr, cr).astype(BF16)
        send_own(0, k)
    own[...] = project(c, 0, rows_own)

    def norm_one(rows):
        res = x[rows, :].astype(F32) + summed(0, rows) + vec[4:5, :]
        center = res - jnp.mean(res, axis=-1, keepdims=True)
        r = lax.rsqrt(jnp.mean(center * center, axis=-1, keepdims=True) + 1e-12)
        zh = center * r
        out = zh * vec[0:1, :] + vec[2:3, :]
        zh1[rows, :] = zh
        r1[rows, :] = r
        normed[rows, :] = out
        full[0, c, rows, :] = out.astype(BF16)

    for k in range(NCH):
        arrived(0, k)
        tiles(k * cr, cr, norm_one)
        gather_start(0, k)

    def mlp_forward(b, r0, n):
        rows_in = full[0, b, pl.ds(r0, n), :]
        fa[pl.ds(0, n), :] = dot(rows_in, w[1])
        fb[pl.ds(0, n), :] = dot(rows_in, w[2])

        def units(rows):
            g = fa[rows, :] + vec[6:7, :]
            u = fb[rows, :] + vec[7:8, :]
            phi = 0.5 * (1.0 + lax.erf(g * (1.0 / math.sqrt(2.0))))
            gelu = g * phi
            slope = phi + g * jnp.exp(-0.5 * g * g) * (1.0 / math.sqrt(2.0 * math.pi))
            out = pl.ds(pl.multiple_of(r0 + rows.start, TILE), TILE)
            act[b, out, :] = gelu.astype(BF16)
            pull[b, out, :] = (u * slope).astype(BF16)
            hid[b, out, :] = (gelu * u).astype(BF16)

        tiles(0, n, units)
        return dot_nt(hid[b, pl.ds(r0, n), :], w[3])

    def mlp_backward(b, r0, n):
        fa[pl.ds(0, n), :] = dot(full[1, b, pl.ds(r0, n), :], w[3])

        def units(rows):
            dh = fa[rows, :]
            out = pl.ds(pl.multiple_of(r0 + rows.start, TILE), TILE)
            dg = (dh * pull[b, out, :].astype(F32)).astype(BF16)
            du = (dh * act[b, out, :].astype(F32)).astype(BF16)
            dgt[b, out, :] = dg
            dup[b, out, :] = du
            bsum[0] += fold(dg.astype(F32))
            bsum[1] += fold(du.astype(F32))

        tiles(0, n, units)
        return dot_nt(dgt[b, pl.ds(r0, n), :], w[1]) + dot_nt(dup[b, pl.ds(r0, n), :], w[2])

    def exchange(o, piece):
        own[...] = piece(c, 0, rows_own)
        for k in range(NCH):
            ag_c[o - 1, k].wait_recv()
        snd_o[o] = piece(sib, 0, rows_own).astype(BF16)
        for k in range(NCH):
            send_own(o, k)
        for k in range(NCH):
            forward(o - 1, k)
            yacc[chunk(k), :] = piece(ynb, k * cr, cr)
            ag_f[o - 1, k].wait_recv()
            snd_r[o, chunk(k), :] = piece(dia, k * cr, cr).astype(BF16)
            send_relay(o, k)
            if k:
                relay(o, k - 1)
        relay(o, NCH - 1)

    exchange(1, mlp_forward)

    def norm_two(rows):
        res = normed[rows, :] + (summed(1, rows) + vec[5:6, :])
        center = res - jnp.mean(res, axis=-1, keepdims=True)
        r = lax.rsqrt(jnp.mean(center * center, axis=-1, keepdims=True) + 1e-12)
        zh = center * r
        lout[rows, :] = (zh * vec[1:2, :] + vec[3:4, :]).astype(BF16)
        up = cot[rows, :].astype(F32)
        t = up * vec[1:2, :]
        d = r * (t - jnp.mean(t, axis=-1, keepdims=True)
                 - zh * jnp.mean(t * zh, axis=-1, keepdims=True))
        dres2[rows, :] = d
        low = d.astype(BF16)
        full[1, c, rows, :] = low
        acc[1] += fold(up * zh)
        acc[3] += fold(up)
        acc[5] += fold(low.astype(F32))

    for k in range(NCH):
        arrived(1, k)
        tiles(k * cr, cr, norm_two)
        gather_start(1, k)

    exchange(2, mlp_backward)

    def flat(ref):
        return ref[...].reshape(4 * rows_own, ref.shape[-1])

    hid_all = flat(hid)
    d_all = full[1].reshape(4 * rows_own, width)
    grads[2] = dot_tn(d_all, hid_all).astype(BF16)
    n_all = full[0].reshape(4 * rows_own, width)
    grads[0] = dot_tn(n_all, flat(dgt)).astype(BF16)
    grads[1] = dot_tn(n_all, flat(dup)).astype(BF16)

    def norm_back(rows):
        dn = summed(2, rows) + dres2[rows, :]
        zh = zh1[rows, :]
        t = dn * vec[0:1, :]
        d = r1[rows, :] * (t - jnp.mean(t, axis=-1, keepdims=True)
                           - zh * jnp.mean(t * zh, axis=-1, keepdims=True))
        dres1[rows, :] = d
        low = d.astype(BF16)
        full[2, c, rows, :] = low
        acc[0] += fold(dn * zh)
        acc[2] += fold(dn)
        acc[4] += fold(low.astype(F32))

    for k in range(NCH):
        arrived(2, k)
        tiles(k * cr, cr, norm_back)
        gather_start(2, k)

    for i in range(6):
        tiny[0, i : i + 1, :] = jnp.sum(acc[i], axis=0, keepdims=True)
    for i in range(2):
        small[6 + i : 7 + i, :] = jnp.sum(bsum[i], axis=0, keepdims=True)
    tiny_copies = []
    for step, peer in enumerate((sib, ynb)):
        copy = remote(tiny.at[2 * step], tiny.at[2 * step + 1], tiny_s.at[step], tiny_r.at[step], peer)
        copy.start()
        started.append(copy)
        tiny_copies.append(copy)
        if step == 0:
            def unproject(b, r0, n):
                return dot(full[2, b, pl.ds(r0, n), :], w_out[...]).astype(BF16)
            dmixed[c] = unproject(c, 0, rows_own)
            for k in range(NCH):
                ag_c[2, k].wait_recv()
            dmixed[sib] = unproject(sib, 0, rows_own)
        copy.wait_recv()
        total = tiny[2 * step] + tiny[2 * step + 1]
        if step == 0:
            tiny[2] = total
        else:
            small[0:6, :] = total[0:6, :]
    for k in range(NCH):
        forward(2, k)
        dmixed[ynb, chunk(k), :] = unproject(ynb, k * cr, cr)
    for k in range(NCH):
        ag_f[2, k].wait_recv()
        dmixed[dia, chunk(k), :] = unproject(dia, k * cr, cr)
    gout[...] = dot_tn(full[2].reshape(4 * rows_own, width), flat(mixed)).astype(BF16)
    for copy in started:
        copy.wait_send()


def sds(shape, dtype):
    return jax.ShapeDtypeStruct(shape, dtype)


def smem():
    return pl.BlockSpec(memory_space=pltpu.SMEM)


def on_device(
    tokens_in, qkv_weight, qv_bias, out_weight, geglu_weight, geglu_bias, down_weight,
    norm_gains, norm_biases, out_biases, doc_lengths, cotangent,
):
    seqs, rows, width = tokens_in.shape
    group = lax.axis_size("ctx")
    tp = lax.axis_size("tp")
    shards = lax.axis_size("shard")
    z = lax.axis_index("tp")
    c = lax.axis_index("ctx")
    assert group == 4 and tp == 4 and seqs == tp
    length = group * rows
    part_rows = qkv_weight.shape[1]
    cols = qkv_weight.shape[2]
    heads = cols // DH
    units = geglu_weight.shape[2]
    assert units == width and 4 * cols == width and H == heads * tp

    with jax.named_scope("pack_weights"):
        first = jnp.concatenate(
            [qkv_weight[0], qkv_weight[1], qkv_weight[2], out_weight.T], axis=1
        )
        parts = jnp.concatenate(
            [first[None], geglu_weight, down_weight.T[None]], axis=0
        )
        own_bias = jnp.concatenate([qv_bias.reshape(1, -1), geglu_bias.reshape(1, -1)], axis=1)
        own_norm = jnp.concatenate([norm_gains, norm_biases, out_biases], axis=0)

    with jax.named_scope("gather_weights"):
        by_block = lax.all_gather(parts, "tp", axis=0)
        swapped = lax.all_to_all(by_block, "ctx", split_axis=0, concat_axis=0)
        w = lax.all_gather(swapped, "shard", axis=0)
        w = w.transpose(2, 0, 1, 3, 4).reshape(4, shards * group * part_rows, width)
        biases = lax.all_gather(own_bias, "tp", axis=0, tiled=True)
        biases = lax.dynamic_slice_in_dim(biases, c, 1, 0).astype(F32)
        norms = lax.all_gather(own_norm, ("shard", "ctx"), axis=1, tiled=True).astype(F32)
    qv = biases[:, : 2 * cols].reshape(2, cols)
    vec = jnp.concatenate([norms, biases[:, 2 * cols :].reshape(2, units)], axis=0)

    x_own = lax.dynamic_index_in_dim(tokens_in, z, 0, keepdims=False)
    cot_own = lax.dynamic_index_in_dim(cotangent, z, 0, keepdims=False)
    lengths = lax.dynamic_slice_in_dim(doc_lengths, z, 1, 0)
    xs = lax.all_gather(x_own, "ctx", axis=0, tiled=True)
    slopes = jnp.asarray([alibi_slopes(H)], F32)

    head_shape = sds((heads, length, DH), BF16)
    mixed, probs, q, k, v = pl.pallas_call(
        functools.partial(attention_forward, heads),
        out_shape=[sds((length, cols), BF16), sds((heads, length, length), BF16)] + [head_shape] * 3,
        in_specs=[smem(), smem()] + vmem(3),
        out_specs=vmem(5),
        scratch_shapes=[pltpu.VMEM((256, length), F32)],
        compiler_params=pltpu.CompilerParams(vmem_limit_bytes=48 * MB),
        name="attention_forward",
    )(lengths, slopes, xs, w[0], qv)

    block = (rows, width)
    stack = (group, rows, width)
    dma = lambda *shape: pltpu.SemaphoreType.DMA(shape)
    lout, dres1, grads, gout, dmixed, small = pl.pallas_call(
        middle,
        out_shape=[
            sds(block, BF16), sds(block, F32), sds((3, width, width), BF16),
            sds((width, cols), BF16), sds((group, rows, cols), BF16), sds((8, width), F32),
        ],
        in_specs=vmem(5),
        out_specs=vmem(6),
        scratch_shapes=[
            pltpu.VMEM((width, cols), BF16), pltpu.VMEM((3,) + stack, BF16),
        ] + [pltpu.VMEM(stack, BF16)] * 5 + [pltpu.VMEM((3,) + block, BF16)] * 6 + [
            pltpu.VMEM(block, F32)
        ] * 6 + [
            pltpu.VMEM((rows, 1), F32), pltpu.VMEM(block, F32),
            pltpu.VMEM((6, 8, width), F32), pltpu.VMEM((2, 8, width), F32),
            pltpu.VMEM((4, 8, width), F32),
        ] + [dma(3, NCH)] * 12 + [dma(2)] * 2,
        compiler_params=pltpu.CompilerParams(
            collective_id=0, has_side_effects=True, vmem_limit_bytes=58 * MB
        ),
        name="middle",
    )(x_own, cot_own, mixed.reshape(group, rows, cols), w, vec)

    grad_w, d_in, bias_grad = pl.pallas_call(
        functools.partial(attention_backward, heads),
        out_shape=[
            sds((width, 3 * cols), BF16), sds((length, width), BF16), sds((1, 3 * cols), F32)
        ],
        in_specs=vmem(8),
        out_specs=vmem(3),
        scratch_shapes=[
            pltpu.VMEM((length, 3 * cols), BF16),
            pltpu.VMEM((heads, DH, length), F32), pltpu.VMEM((heads, DH, length), F32),
        ],
        compiler_params=pltpu.CompilerParams(vmem_limit_bytes=48 * MB),
        name="attention_backward",
    )(dmixed.reshape(length, cols), mixed, probs, q, k, v, xs, w[0])

    with jax.named_scope("outputs"):
        input_sum = lax.psum_scatter(d_in, "ctx", scatter_dimension=0, tiled=True)
        input_own = (input_sum.astype(F32) + dres1).astype(BF16)
        input_grad = lax.all_gather(input_own, "tp", axis=0).astype(F32)
        layer_out = lax.all_gather(lout, "tp", axis=0)

    with jax.named_scope("scatter_grads"):
        first_grad = jnp.concatenate([grad_w, gout], axis=1)
        packed = jnp.concatenate([first_grad[None], grads], axis=0)
        packed = packed.reshape(4, shards, group, part_rows, width).transpose(1, 2, 0, 3, 4)
        mine = lax.psum_scatter(packed, "shard", scatter_dimension=0, tiled=False)
        mine = lax.all_to_all(mine, "ctx", split_axis=0, concat_axis=0)
        mine = lax.psum_scatter(mine, "tp", scatter_dimension=0, tiled=False)
        mine = mine.astype(F32)
        grad_qkv = jnp.stack([mine[0, :, i * cols : (i + 1) * cols] for i in range(3)])
        grad_out = mine[0, :, 3 * cols :].T
        grad_geglu = mine[1:3]
        grad_down = mine[3].T
        col = jnp.concatenate(
            [bias_grad[:, :cols], bias_grad[:, 2 * cols :], small[6:7], small[7:8]], axis=1
        )
        col = lax.psum_scatter(
            jnp.zeros((group, col.shape[1]), F32) + jnp.where(
                jnp.arange(group)[:, None] == c, col, 0.0),
            "tp", scatter_dimension=0, tiled=True)
        col = lax.psum(col, ("shard", "ctx"))
        norm_grad = lax.psum(small[:6], ("shard", "tp"))
        me = lax.axis_index("shard") * group + c
        norm_grad = lax.dynamic_slice_in_dim(norm_grad, me * part_rows, part_rows, 1)
    return (
        layer_out,
        input_grad,
        grad_qkv,
        col[:, : 2 * cols].reshape(2, cols),
        grad_out,
        grad_geglu,
        col[:, 2 * cols :].reshape(2, units),
        grad_down,
        norm_grad[0:2],
        norm_grad[2:4],
        norm_grad[4:6],
    )


def solution(mesh):
    in_specs = (
        P("shard", "ctx", None),
        P(None, ("shard", "ctx"), "tp"),
        P(None, "tp"),
        P("tp", ("shard", "ctx")),
        P(None, ("shard", "ctx"), "tp"),
        P(None, "tp"),
        P("tp", ("shard", "ctx")),
        P(None, ("shard", "ctx")),
        P(None, ("shard", "ctx")),
        P(None, ("shard", "ctx")),
        P("shard", None),
        P("shard", "ctx", None),
    )
    out_specs = (
        P("shard", "ctx", None),
        P("shard", "ctx", None),
        P(None, ("shard", "ctx"), "tp"),
        P(None, "tp"),
        P("tp", ("shard", "ctx")),
        P(None, ("shard", "ctx"), "tp"),
        P(None, "tp"),
        P("tp", ("shard", "ctx")),
        P(None, ("shard", "ctx")),
        P(None, ("shard", "ctx")),
        P(None, ("shard", "ctx")),
    )
    return jax.shard_map(
        on_device, mesh=mesh, in_specs=in_specs, out_specs=out_specs, check_vma=False
    )
```

```python
import functools
import math

import jax
import jax.numpy as jnp
from jax import lax
from jax.experimental import pallas as pl
from jax.experimental.pallas import tpu as pltpu
from jax.sharding import PartitionSpec as P

H = 12
DH = 64
F32 = jnp.float32
BF16 = jnp.bfloat16
MESH = pl.DeviceIdType.MESH
NCH = 2
TILE = 32
MB = 1 << 20


def alibi_slopes(head_count):
    def power_slopes(head_total):
        first_slope = 2.0 ** (-8.0 / head_total)
        return [first_slope ** (counter + 1) for counter in range(head_total)]

    nearest = 2 ** int(math.floor(math.log2(head_count)))
    slope_list = power_slopes(nearest)
    return slope_list + power_slopes(2 * nearest)[0::2][: head_count - nearest]


def dot(left, right):
    return jnp.dot(left, right, preferred_element_type=F32)


def dot_nt(left, right):
    return lax.dot_general(left, right, (((1,), (1,)), ((), ())), preferred_element_type=F32)


def dot_tn(left, right):
    return lax.dot_general(left, right, (((0,), (0,)), ((), ())), preferred_element_type=F32)


def vmem(count):
    return [pl.BlockSpec(memory_space=pltpu.VMEM)] * count


def project_heads(heads, x_rows, rows, w, bias, q_out, k_out, v_out):
    cols = heads * DH
    for part, out in enumerate((q_out, k_out, v_out)):
        y = dot(x_rows, w[:, part * cols : (part + 1) * cols])
        if part != 1:
            y = y + bias[part // 2 : part // 2 + 1, :]
        y = y.astype(BF16)
        if part == 0:
            y = y * BF16(1.0 / math.sqrt(DH))
        for i in range(heads):
            out[i, rows, :] = y[:, i * DH : (i + 1) * DH]


def segments(lengths, pos):
    seg = jnp.zeros(pos.shape, jnp.int32)
    end = 0
    for k in range(lengths.shape[1]):
        end = end + lengths[0, k]
        seg = seg + (pos >= end).astype(jnp.int32)
    return seg


def attend_rows(heads, start, step, lengths, slopes, q, k, v, probs, mixed, far):
    length = k.shape[1]
    mine = lax.axis_index("ctx") * heads
    rows = pl.ds(start, step)
    key_pos = lax.broadcasted_iota(jnp.int32, (1, length), 1)
    pos = start + lax.broadcasted_iota(jnp.int32, (step, 1), 0)
    same = segments(lengths, pos) == segments(lengths, key_pos)
    far[...] = jnp.where(same, jnp.abs(pos - key_pos).astype(F32), 1e33)
    for i in range(heads):
        s = dot_nt(q[i, rows, :], k[i]) - slopes[0, mine + i] * far[...]
        p = jnp.exp(s - jnp.max(s, axis=-1, keepdims=True))
        p = (p * (1.0 / jnp.sum(p, axis=-1, keepdims=True))).astype(BF16)
        probs[i, rows, :] = p
        mixed[rows, i * DH : (i + 1) * DH] = dot(p, v[i]).astype(BF16)


def attention_forward(
    heads, lengths, slopes, xs, w, bias, mixed, probs, q_out, k_out, v_out, far
):
    step = 256

    def project(r, carry):
        rows = pl.ds(pl.multiple_of(r * step, step), step)
        project_heads(heads, xs[rows, :], rows, w, bias, q_out, k_out, v_out)
        return carry

    def attend(r, carry):
        start = pl.multiple_of(r * step, step)
        attend_rows(
            heads, start, step, lengths, slopes, q_out, k_out, v_out, probs, mixed, far)
        return carry

    lax.fori_loop(0, xs.shape[0] // step, project, 0)
    lax.fori_loop(0, xs.shape[0] // step, attend, 0)


def attend_back(heads, rows, dmixed, mixed, probs, q, k, v, dqkv, dk_acc, dv_acc):
    for i in range(heads):
        own = slice(i * DH, (i + 1) * DH)
        d_out = dmixed[rows, own]
        row_dot = jnp.sum(
            d_out.astype(F32) * mixed[rows, own].astype(F32), axis=-1, keepdims=True
        )
        p = probs[i, rows, :]
        dp = dot_nt(d_out, v[i])
        ds = (p.astype(F32) * (dp - row_dot)).astype(BF16)
        dqkv[rows, own] = (dot(ds, k[i]) * (1.0 / math.sqrt(DH))).astype(BF16)
        dk_acc[i] += dot_tn(q[i, rows, :], ds)
        dv_acc[i] += dot_tn(d_out, p)


def spread_heads(heads, dqkv, dk_acc, dv_acc):
    cols = heads * DH
    for i in range(heads):
        dqkv[:, cols + i * DH : cols + (i + 1) * DH] = dk_acc[i].T.astype(BF16)
        dqkv[:, 2 * cols + i * DH : 2 * cols + (i + 1) * DH] = dv_acc[i].T.astype(BF16)


def attention_backward(
    heads, dmixed, mixed, probs, q, k, v, xs, w, grad_w, d_in, bias_grad, dqkv, dk_acc, dv_acc
):
    length = xs.shape[0]
    step = 256
    cols = heads * DH
    dk_acc[...] = jnp.zeros_like(dk_acc)
    dv_acc[...] = jnp.zeros_like(dv_acc)

    def rows_back(r, carry):
        rows = pl.ds(pl.multiple_of(r * step, step), step)
        attend_back(heads, rows, dmixed, mixed, probs, q, k, v, dqkv, dk_acc, dv_acc)
        return carry

    lax.fori_loop(0, length // step, rows_back, 0)
    spread_heads(heads, dqkv, dk_acc, dv_acc)

    def finish(r, total):
        rows = pl.ds(pl.multiple_of(r * step, step), step)
        d = dqkv[rows, :]
        d_in[rows, :] = dot_nt(d, w[:, : 3 * cols]).astype(BF16)
        return total + jnp.sum(d.astype(F32), axis=0, keepdims=True)

    bias_grad[...] = lax.fori_loop(
        0, length // step, finish, jnp.zeros((1, 3 * cols), F32)
    )
    for part in range(3):
        own = slice(part * cols, (part + 1) * cols)
        grad_w[:, own] = dot_tn(xs[...], dqkv[:, own]).astype(BF16)


class Links:
    def __init__(self):
        self.started = []

    def copy(self, src, dst, send, recv, peer):
        return pltpu.make_async_remote_copy(
            src_ref=src, dst_ref=dst, send_sem=send, recv_sem=recv,
            device_id=peer, device_id_type=MESH,
        )

    def start(self, src, dst, send, recv, peer):
        copy = self.copy(src, dst, send, recv, peer)
        copy.start()
        self.started.append(copy)
        return copy

    def drain(self):
        for copy in self.started:
            copy.wait_send()
        self.started = []


def greet(peers):
    barrier = pltpu.get_barrier_semaphore()
    for peer in peers:
        pl.semaphore_signal(barrier, inc=1, device_id=peer, device_id_type=MESH)
    pl.semaphore_wait(barrier, len(peers))


def places():
    c = lax.axis_index("ctx")
    flip = 1 - 2 * (c % 2)
    ynb = (c + 2) % 4
    return c, c + flip, ynb, ynb + flip


class LineGather:
    def __init__(self, blocks, up, down, recv):
        self.blocks, self.up, self.down, self.recv = blocks, up, down, recv
        self.z = lax.axis_index("tp")
        self.last = blocks.shape[0] - 1

    def _copy(self, j, sem, peer):
        block = self.blocks.at[j]
        return pltpu.make_async_remote_copy(
            src_ref=block, dst_ref=block, send_sem=sem.at[j], recv_sem=self.recv.at[j],
            device_id={"tp": peer}, device_id_type=MESH,
        )

    def hop(self, d):
        z, last = self.z, self.last
        for side, j in ((0, z - d), (1, z + d)):
            here = (j >= 0) if side == 0 else (j <= last)
            edge = (z < last) if side == 0 else (z > 0)

            @pl.when(here)
            def _(side=side, j=j, edge=edge):
                sem = self.up if side == 0 else self.down
                if d:
                    self._copy(j, sem, z).wait_recv()
                if d < last:
                    @pl.when(edge)
                    def _():
                        self._copy(j, sem, z + 1 if side == 0 else z - 1).start()

    def drain(self):
        z, last = self.z, self.last
        for d in range(last):
            for side, j in ((0, z - d), (1, z + d)):
                here = (j >= 0) if side == 0 else (j <= last)
                edge = (z < last) if side == 0 else (z > 0)

                @pl.when(jnp.logical_and(here, edge))
                def _(side=side, j=j):
                    self._copy(j, self.up if side == 0 else self.down, z).wait_send()


def front(
    heads, lengths, slopes, x, p0, pr,
    xs, w0, w, vec, mixed, probs, q, k, v,
    zb0, zbr, wb0, qv, far,
    xg_s, xg_r, zs, zr, ys, yr, xs_s, xs_r,
):
    c, sib, ynb, dia = places()
    me = lax.axis_index("shard")
    z = lax.axis_index("tp")
    tp = zb0.shape[0]
    other = 1 - me
    piece = pr.shape[1]
    greet([{"ctx": sib}, {"ctx": ynb}, {"ctx": dia}, {"shard": other}]
          + [{"tp": (z + d) % tp} for d in range(1, tp)])
    links = Links()
    src = [p0] + [pr.at[i] for i in range(3)]
    zb = [zb0] + [zbr.at[i] for i in range(3)]
    wr = [wb0] + [w.at[i] for i in range(3)]

    def spread(p):
        for d in range(1, tp):
            links.start(src[p], zb[p].at[z], zs.at[p, d - 1], zr.at[p, z], {"tp": (z + d) % tp})
        zb[p].at[z][...] = src[p][...]

    def to_owner(p):
        for rel, j in enumerate((c, sib, ynb, dia)):
            @pl.when(j != z)
            def _(j=j):
                links.copy(src[p], zb[p].at[j], zs.at[p, 0], zr.at[p, j], {"tp": z}).wait_recv()
            if rel == 0:
                wr[p].at[me, c][...] = zb[p].at[c][...]
            else:
                links.start(zb[p].at[j], wr[p].at[me, c], ys.at[p, rel - 1], yr.at[p, c], {"ctx": j})

    def to_shard(p):
        for i, j in enumerate((c, sib, ynb, dia)):
            slot = wr[p].at[me, j]
            if i:
                links.copy(zb[p].at[c], slot, ys.at[p, 0], yr.at[p, j], {"ctx": c}).wait_recv()
            links.start(slot, slot, xs_s.at[p, i], xs_r.at[p, j], {"shard": other})

    def complete(p):
        for j in range(4):
            slot = wr[p].at[other, j]
            links.copy(slot, slot, xs_s.at[p, 0], xs_r.at[p, j], {"shard": other}).wait_recv()

    xs.at[c][...] = x[...]
    first = links.start(xs.at[c], xs.at[c], xg_s.at[0], xg_r.at[0], {"ctx": ynb})
    near = links.start(xs.at[c], xs.at[c], xg_s.at[1], xg_r.at[1], {"ctx": sib})
    spread(0)
    to_owner(0)
    spread(1)
    first.wait_recv()
    passed = links.start(xs.at[ynb], xs.at[ynb], xg_s.at[2], xg_r.at[2], {"ctx": sib})
    to_shard(0)
    near.wait_recv()
    passed.wait_recv()
    complete(0)
    total = jnp.zeros((p0.shape[0] - piece, p0.shape[1]), F32)
    for s in range(2):
        for j in range(4):
            w0[pl.ds((s * 4 + j) * piece, piece), :] = wb0[s, j, 0:piece, :]
            total = total + wb0[s, j, piece:, :].astype(F32)
    one = wb0[0, 0, piece:, :].astype(F32)
    cols = heads * DH
    qv[0:1, :] = one[0:1, 0:cols]
    qv[1:2, :] = one[0:1, cols : 2 * cols]
    vec[0:6, :] = total[3:9, :]
    vec[6:8, :] = one[1:3, :]
    step = x.shape[0]

    def project(r, carry):
        rows = pl.ds(pl.multiple_of(r * step, step), step)
        project_heads(heads, xs[r], rows, w0, qv, q, k, v)
        return carry

    lax.fori_loop(0, 4, project, 0)
    to_owner(1)
    spread(2)

    def attend(r, carry):
        attend_rows(heads, pl.multiple_of(r * step, step), step, lengths, slopes,
                    q, k, v, probs, mixed, far)
        return carry

    lax.fori_loop(0, 2, attend, 0)
    to_shard(1)
    lax.fori_loop(2, 4, attend, 0)
    to_owner(2)
    spread(3)
    to_shard(2)
    to_owner(3)
    to_shard(3)
    for p in range(1, 4):
        complete(p)
    links.drain()


def back(
    heads, dmixed, mixed, probs, q, k, v, xs, w0, grads, gout, small, dres1,
    out0, outr, input_grad,
    dqkv, dk_acc, dv_acc, extra, gq, g0, xb0, xbr, sb0, sbr, yb0, ybr, zb0, zbr,
    snd_r, snd_o, snd_y, rcv_r, rcv_o, rcv_y, own, yacc,
    gx_s, gx_r, gy_s, gy_r, gz_s, gz_r,
    rss_r, rsr_r, rss_o, rsr_o, rss_y, rsr_y, lu, ld, lr,
):
    c, sib, ynb, dia = places()
    me = lax.axis_index("shard")
    z = lax.axis_index("tp")
    tp = zb0.shape[0]
    other = 1 - me
    piece = outr.shape[1]
    cols = heads * DH
    rows_own, width = dres1.shape
    cr = rows_own // NCH
    greet([{"ctx": sib}, {"ctx": ynb}, {"ctx": dia}, {"shard": other}]
          + [{"tp": (z + d) % tp} for d in range(1, tp)])
    links = Links()
    line = LineGather(input_grad, lu, ld, lr)
    part = [g0] + [grads.at[i] for i in range(3)]
    xb = [xb0] + [xbr.at[i] for i in range(3)]
    sb = [sb0] + [sbr.at[i] for i in range(3)]
    yb = [yb0] + [ybr.at[i] for i in range(3)]
    zb = [zb0] + [zbr.at[i] for i in range(3)]
    out = [out0] + [outr.at[i] for i in range(3)]

    def to_shard(p):
        for i, j in enumerate((dia, ynb, sib, c)):
            links.start(part[p].at[other, j], xb[p].at[j], gx_s.at[p, i], gx_r.at[p, j], {"shard": other})

    def to_owner(p):
        for i, j in enumerate((dia, ynb, sib, c)):
            links.copy(part[p].at[other, j], xb[p].at[j], gx_s.at[p, 0], gx_r.at[p, j], {"shard": other}).wait_recv()
            total = part[p].at[me, j][...].astype(F32) + xb[p].at[j][...].astype(F32)
            if i == 3:
                yb[p].at[c][...] = total.astype(BF16)
            else:
                sb[p].at[j][...] = total.astype(BF16)
                links.start(sb[p].at[j], yb[p].at[c], gy_s.at[p, i], gy_r.at[p, c], {"ctx": j})

    def away(p, rel, j):
        return links.copy(yb[p].at[j], zb[p].at[z], gz_s.at[p, rel], gz_r.at[p, z], {"tp": j})

    def to_plane(p):
        for rel, j in enumerate((c, sib, ynb, dia)):
            if rel:
                links.copy(sb[p].at[j], yb[p].at[j], gy_s.at[p, 0], gy_r.at[p, j], {"ctx": j}).wait_recv()

            @pl.when(j != z)
            def _(rel=rel, j=j):
                away(p, rel, j).start()

    def total(p):
        value = yb[p].at[z][...].astype(F32)
        for d in range(1, tp):
            t = (z + d) % tp
            links.copy(yb[p].at[t], zb[p].at[t], gz_s.at[p, 0], gz_r.at[p, t], {"tp": t}).wait_recv()
            value = value + zb[p].at[t][...].astype(F32)
        out[p][...] = value

    def chunk(k):
        return pl.ds(k * cr, cr)

    for p in (1, 2, 3):
        to_shard(p)
    dk_acc[...] = jnp.zeros_like(dk_acc)
    dv_acc[...] = jnp.zeros_like(dv_acc)

    def rows_back(r, carry):
        rows = pl.ds(pl.multiple_of(r * rows_own, rows_own), rows_own)
        attend_back(heads, rows, dmixed, mixed, probs, q, k, v, dqkv, dk_acc, dv_acc)
        return carry

    lax.fori_loop(0, 4, rows_back, 0)
    spread_heads(heads, dqkv, dk_acc, dv_acc)
    to_owner(1)

    def piece_in(b, r0, n):
        rows = pl.ds(pl.multiple_of(b * rows_own + r0, cr), n)
        return dot_nt(dqkv[rows, :], w0[:, : 3 * cols])

    relays = []
    outs = []
    sums = []

    def relay(k):
        relays[k].wait_recv()
        snd_y[chunk(k), :] = (yacc[chunk(k), :] + rcv_r[chunk(k), :].astype(F32)).astype(BF16)
        sums.append(links.start(
            snd_y.at[chunk(k)], rcv_y.at[chunk(k)], rss_y.at[k], rsr_y.at[k], {"ctx": ynb}))

    for k in range(NCH):
        snd_r[chunk(k), :] = piece_in(dia, k * cr, cr).astype(BF16)
        relays.append(links.start(
            snd_r.at[chunk(k)], rcv_r.at[chunk(k)], rss_r.at[k], rsr_r.at[k], {"ctx": sib}))
        yacc[chunk(k), :] = piece_in(ynb, k * cr, cr)
        if k:
            relay(k - 1)
    relay(NCH - 1)
    for k in range(NCH):
        snd_o[chunk(k), :] = piece_in(sib, k * cr, cr).astype(BF16)
        outs.append(links.start(
            snd_o.at[chunk(k)], rcv_o.at[chunk(k)], rss_o.at[k], rsr_o.at[k], {"ctx": sib}))
    own[...] = piece_in(c, 0, rows_own)

    d_all = dqkv[...]
    bias = jnp.sum(d_all.astype(F32), axis=0, keepdims=True)
    for i in range(3):
        mine = slice(i * cols, (i + 1) * cols)
        gq[:, mine] = dot_tn(xs[...].reshape(4 * rows_own, width), dqkv[:, mine]).astype(BF16)
    gq[:, 3 * cols : 4 * cols] = gout[...]
    extra[...] = jnp.zeros_like(extra)
    extra[0:1, 0:cols] = bias[:, :cols]
    extra[0:1, cols : 2 * cols] = bias[:, 2 * cols :]
    extra[1:3, :] = small[6:8, :]
    extra[3:9, :] = small[0:6, :]
    low = extra[...].astype(BF16)
    for s in range(2):
        for j in range(4):
            g0[s, j, 0:piece, :] = gq[pl.ds((s * 4 + j) * piece, piece), :]
            g0[s, j, piece:, :] = low
    to_shard(0)
    to_plane(1)
    to_owner(2)
    for k in range(NCH):
        outs[k].wait_recv()
        sums[k].wait_recv()
        value = own[chunk(k), :] + rcv_o[chunk(k), :].astype(F32) + rcv_y[chunk(k), :].astype(F32)
        input_grad[z, chunk(k), :] = (value + dres1[chunk(k), :]).astype(BF16)
    line.hop(0)
    to_plane(2)
    to_owner(3)
    line.hop(1)
    to_plane(3)
    to_owner(0)
    line.hop(2)
    to_plane(0)
    line.hop(3)
    for p in (1, 2, 3, 0):
        total(p)
    line.drain()
    for p in range(4):
        for rel, j in enumerate((c, sib, ynb, dia)):
            @pl.when(j != z)
            def _(p=p, rel=rel, j=j):
                away(p, rel, j).wait_send()
    links.drain()


def middle(
    x, cot, mixed, w0, w, vec,
    lout, dres1, grads, gout, dmixed, small,
    w_out, full, act, pull, hid, dgt, dup,
    snd_r, snd_o, snd_y, rcv_r, rcv_o, rcv_y,
    own, yacc, fa, fb, normed, zh1, r1, dres2, acc, bsum, tiny,
    ags_y, agr_y, ags_c, agr_c, ags_f, agr_f,
    rss_r, rsr_r, rss_o, rsr_o, rss_y, rsr_y, tiny_s, tiny_r, lu, ld, lr,
):
    rows_own = x.shape[0]
    width = x.shape[1]
    cr = rows_own // NCH
    c, sib, ynb, dia = places()
    z = lax.axis_index("tp")
    tp = lout.shape[0]
    greet([{"ctx": sib}, {"ctx": ynb}] + [{"tp": (z + d) % tp} for d in range(1, tp)])
    line = LineGather(lout, lu, ld, lr)

    started = []

    def remote(src, dst, send, recv, peer):
        return pltpu.make_async_remote_copy(
            src_ref=src, dst_ref=dst, send_sem=send, recv_sem=recv,
            device_id={"ctx": peer}, device_id_type=MESH,
        )

    def chunk(k):
        return pl.ds(k * cr, cr)

    ag_y, ag_c, ag_f, rs_r, rs_o, rs_y = ({} for _ in range(6))

    def start(table, key, copy):
        copy.start()
        table[key] = copy
        started.append(copy)

    def gather_start(o, k):
        piece = full.at[o, c, chunk(k)]
        start(ag_y, (o, k), remote(piece, piece, ags_y.at[o, k], agr_y.at[o, k], ynb))
        start(ag_c, (o, k), remote(piece, piece, ags_c.at[o, k], agr_c.at[o, k], sib))

    def forward(o, k):
        ag_y[o, k].wait_recv()
        piece = full.at[o, ynb, chunk(k)]
        start(ag_f, (o, k), remote(piece, piece, ags_f.at[o, k], agr_f.at[o, k], sib))

    def send_relay(o, k):
        start(rs_r, (o, k), remote(
            snd_r.at[o, chunk(k)], rcv_r.at[o, chunk(k)], rss_r.at[o, k], rsr_r.at[o, k], sib))

    def send_own(o, k):
        start(rs_o, (o, k), remote(
            snd_o.at[o, chunk(k)], rcv_o.at[o, chunk(k)], rss_o.at[o, k], rsr_o.at[o, k], sib))

    def relay(o, k):
        rs_r[o, k].wait_recv()
        snd_y[o, chunk(k), :] = (yacc[chunk(k), :] + rcv_r[o, chunk(k), :].astype(F32)).astype(BF16)
        start(rs_y, (o, k), remote(
            snd_y.at[o, chunk(k)], rcv_y.at[o, chunk(k)], rss_y.at[o, k], rsr_y.at[o, k], ynb))

    def arrived(o, k):
        rs_o[o, k].wait_recv()
        rs_y[o, k].wait_recv()

    def tiles(first, count, body):
        def step(t, carry):
            body(pl.ds(pl.multiple_of(first + t * TILE, TILE), TILE))
            return carry
        lax.fori_loop(0, count // TILE, step, 0)

    def summed(o, rows):
        return own[rows, :] + rcv_o[o, rows, :].astype(F32) + rcv_y[o, rows, :].astype(F32)

    def fold(values):
        return jnp.sum(values.reshape(TILE // 8, 8, width), axis=0)

    acc[...] = jnp.zeros_like(acc)
    bsum[...] = jnp.zeros_like(bsum)
    w_out[...] = w0[:, 3 * mixed.shape[2] : 4 * mixed.shape[2]]

    def project(b, r0, n):
        return dot_nt(mixed[b, pl.ds(r0, n), :], w_out[...])

    for k in range(NCH):
        snd_r[0, chunk(k), :] = project(dia, k * cr, cr).astype(BF16)
        send_relay(0, k)
        yacc[chunk(k), :] = project(ynb, k * cr, cr)
        if k:
            relay(0, k - 1)
    relay(0, NCH - 1)
    for k in range(NCH):
        snd_o[0, chunk(k), :] = project(sib, k * cr, cr).astype(BF16)
        send_own(0, k)
    own[...] = project(c, 0, rows_own)

    def norm_one(rows):
        res = x[rows, :].astype(F32) + summed(0, rows) + vec[4:5, :]
        center = res - jnp.mean(res, axis=-1, keepdims=True)
        r = lax.rsqrt(jnp.mean(center * center, axis=-1, keepdims=True) + 1e-12)
        zh = center * r
        out = zh * vec[0:1, :] + vec[2:3, :]
        zh1[rows, :] = zh
        r1[rows, :] = r
        normed[rows, :] = out
        full[0, c, rows, :] = out.astype(BF16)

    for k in range(NCH):
        arrived(0, k)
        tiles(k * cr, cr, norm_one)
        gather_start(0, k)

    def mlp_forward(b, r0, n):
        rows_in = full[0, b, pl.ds(r0, n), :]
        fa[pl.ds(0, n), :] = dot(rows_in, w[0])
        fb[pl.ds(0, n), :] = dot(rows_in, w[1])

        def units(rows):
            g = fa[rows, :] + vec[6:7, :]
            u = fb[rows, :] + vec[7:8, :]
            phi = 0.5 * (1.0 + lax.erf(g * (1.0 / math.sqrt(2.0))))
            gelu = g * phi
            slope = phi + g * jnp.exp(-0.5 * g * g) * (1.0 / math.sqrt(2.0 * math.pi))
            out = pl.ds(pl.multiple_of(r0 + rows.start, TILE), TILE)
            act[b, out, :] = gelu.astype(BF16)
            pull[b, out, :] = (u * slope).astype(BF16)
            hid[b, out, :] = (gelu * u).astype(BF16)

        tiles(0, n, units)
        return dot_nt(hid[b, pl.ds(r0, n), :], w[2])

    def mlp_backward(b, r0, n):
        fa[pl.ds(0, n), :] = dot(full[1, b, pl.ds(r0, n), :], w[2])

        def units(rows):
            dh = fa[rows, :]
            out = pl.ds(pl.multiple_of(r0 + rows.start, TILE), TILE)
            dg = (dh * pull[b, out, :].astype(F32)).astype(BF16)
            du = (dh * act[b, out, :].astype(F32)).astype(BF16)
            dgt[b, out, :] = dg
            dup[b, out, :] = du
            bsum[0] += fold(dg.astype(F32))
            bsum[1] += fold(du.astype(F32))

        tiles(0, n, units)
        return dot_nt(dgt[b, pl.ds(r0, n), :], w[0]) + dot_nt(dup[b, pl.ds(r0, n), :], w[1])

    def exchange(o, piece):
        own[...] = piece(c, 0, rows_own)
        for k in range(NCH):
            ag_c[o - 1, k].wait_recv()
        snd_o[o] = piece(sib, 0, rows_own).astype(BF16)
        for k in range(NCH):
            send_own(o, k)
        for k in range(NCH):
            forward(o - 1, k)
            yacc[chunk(k), :] = piece(ynb, k * cr, cr)
            ag_f[o - 1, k].wait_recv()
            snd_r[o, chunk(k), :] = piece(dia, k * cr, cr).astype(BF16)
            send_relay(o, k)
            if k:
                relay(o, k - 1)
        relay(o, NCH - 1)

    exchange(1, mlp_forward)

    def norm_two(rows):
        res = normed[rows, :] + (summed(1, rows) + vec[5:6, :])
        center = res - jnp.mean(res, axis=-1, keepdims=True)
        r = lax.rsqrt(jnp.mean(center * center, axis=-1, keepdims=True) + 1e-12)
        zh = center * r
        lout[z, rows, :] = (zh * vec[1:2, :] + vec[3:4, :]).astype(BF16)
        up = cot[rows, :].astype(F32)
        t = up * vec[1:2, :]
        d = r * (t - jnp.mean(t, axis=-1, keepdims=True)
                 - zh * jnp.mean(t * zh, axis=-1, keepdims=True))
        dres2[rows, :] = d
        low = d.astype(BF16)
        full[1, c, rows, :] = low
        acc[1] += fold(up * zh)
        acc[3] += fold(up)
        acc[5] += fold(low.astype(F32))

    for k in range(NCH):
        arrived(1, k)
        tiles(k * cr, cr, norm_two)
        gather_start(1, k)

    line.hop(0)
    exchange(2, mlp_backward)
    line.hop(1)

    def flat(ref):
        return ref[...].reshape(4 * rows_own, ref.shape[-1])

    hid_all = flat(hid)
    d_all = full[1].reshape(4 * rows_own, width)
    grads[2] = dot_tn(d_all, hid_all).astype(BF16)
    n_all = full[0].reshape(4 * rows_own, width)
    grads[0] = dot_tn(n_all, flat(dgt)).astype(BF16)
    grads[1] = dot_tn(n_all, flat(dup)).astype(BF16)

    line.hop(2)

    def norm_back(rows):
        dn = summed(2, rows) + dres2[rows, :]
        zh = zh1[rows, :]
        t = dn * vec[0:1, :]
        d = r1[rows, :] * (t - jnp.mean(t, axis=-1, keepdims=True)
                           - zh * jnp.mean(t * zh, axis=-1, keepdims=True))
        dres1[rows, :] = d
        low = d.astype(BF16)
        full[2, c, rows, :] = low
        acc[0] += fold(dn * zh)
        acc[2] += fold(dn)
        acc[4] += fold(low.astype(F32))

    for k in range(NCH):
        arrived(2, k)
        tiles(k * cr, cr, norm_back)
        gather_start(2, k)

    for i in range(6):
        tiny[0, i : i + 1, :] = jnp.sum(acc[i], axis=0, keepdims=True)
    for i in range(2):
        small[6 + i : 7 + i, :] = jnp.sum(bsum[i], axis=0, keepdims=True)
    tiny_copies = []
    for step, peer in enumerate((sib, ynb)):
        copy = remote(tiny.at[2 * step], tiny.at[2 * step + 1], tiny_s.at[step], tiny_r.at[step], peer)
        copy.start()
        started.append(copy)
        tiny_copies.append(copy)
        if step == 0:
            def unproject(b, r0, n):
                return dot(full[2, b, pl.ds(r0, n), :], w_out[...]).astype(BF16)
            dmixed[c] = unproject(c, 0, rows_own)
            for k in range(NCH):
                ag_c[2, k].wait_recv()
            dmixed[sib] = unproject(sib, 0, rows_own)
        copy.wait_recv()
        total = tiny[2 * step] + tiny[2 * step + 1]
        if step == 0:
            tiny[2] = total
        else:
            small[0:6, :] = total[0:6, :]
    for k in range(NCH):
        forward(2, k)
        dmixed[ynb, chunk(k), :] = unproject(ynb, k * cr, cr)
    for k in range(NCH):
        ag_f[2, k].wait_recv()
        dmixed[dia, chunk(k), :] = unproject(dia, k * cr, cr)
    gout[...] = dot_tn(full[2].reshape(4 * rows_own, width), flat(mixed)).astype(BF16)
    line.hop(3)
    line.drain()
    for copy in started:
        copy.wait_send()


def sds(shape, dtype):
    return jax.ShapeDtypeStruct(shape, dtype)


def smem():
    return pl.BlockSpec(memory_space=pltpu.SMEM)


def on_device(
    tokens_in, qkv_weight, qv_bias, out_weight, geglu_weight, geglu_bias, down_weight,
    norm_gains, norm_biases, out_biases, doc_lengths, cotangent,
):
    seqs, rows, width = tokens_in.shape
    group = lax.axis_size("ctx")
    tp = lax.axis_size("tp")
    shards = lax.axis_size("shard")
    z = lax.axis_index("tp")
    c = lax.axis_index("ctx")
    assert group == 4 and tp == 4 and seqs == tp
    length = group * rows
    part_rows = qkv_weight.shape[1]
    cols = qkv_weight.shape[2]
    heads = cols // DH
    units = geglu_weight.shape[2]
    assert units == width and 4 * cols == width and H == heads * tp

    fused = shards == 2 and part_rows % 16 == 0
    with jax.named_scope("pack_weights"):
        first = jnp.concatenate(
            [qkv_weight[0], qkv_weight[1], qkv_weight[2], out_weight.T], axis=1
        )
        own_norm = jnp.concatenate([norm_gains, norm_biases, out_biases], axis=0)
        me = lax.axis_index("shard") * group + c
        if fused:
            extra = jnp.zeros((16, width), BF16)
            extra = extra.at[0, : 2 * cols].set(qv_bias.reshape(-1))
            extra = extra.at[1:3].set(geglu_bias)
            extra = lax.dynamic_update_slice(extra, own_norm, (3, me * part_rows))
            p0 = jnp.concatenate([first, extra], axis=0)
            pr = jnp.concatenate([geglu_weight, down_weight.T[None]], axis=0)
        else:
            parts = jnp.concatenate(
                [first[None], geglu_weight, down_weight.T[None]], axis=0
            )
            own_bias = jnp.concatenate(
                [qv_bias.reshape(1, -1), geglu_bias.reshape(1, -1)], axis=1)

    x_own = lax.dynamic_index_in_dim(tokens_in, z, 0, keepdims=False)
    cot_own = lax.dynamic_index_in_dim(cotangent, z, 0, keepdims=False)
    lengths = lax.dynamic_slice_in_dim(doc_lengths, z, 1, 0)
    dma = lambda *shape: pltpu.SemaphoreType.DMA(shape)
    slopes = jnp.asarray([alibi_slopes(H)], F32)
    head_shape = sds((heads, length, DH), BF16)
    if fused:
        wide = part_rows + 16
        stack4 = lambda n, r: pltpu.VMEM((n, r, width), BF16)
        xs, w0, w, vec, mixed, probs, q, k, v = pl.pallas_call(
            functools.partial(front, heads),
            out_shape=[
                sds((group, rows, width), BF16), sds((width, width), BF16),
                sds((3, 2, group, part_rows, width), BF16), sds((8, width), F32),
                sds((length, cols), BF16), sds((heads, length, length), BF16),
            ] + [head_shape] * 3,
            in_specs=[smem(), smem()] + vmem(3),
            out_specs=vmem(9),
            scratch_shapes=[
                pltpu.VMEM((tp, wide, width), BF16), pltpu.VMEM((3, tp, part_rows, width), BF16),
                pltpu.VMEM((2, group, wide, width), BF16), pltpu.VMEM((2, cols), F32),
                pltpu.VMEM((rows, length), F32),
                dma(3), dma(3), dma(4, 3), dma(4, 4), dma(4, 3), dma(4, 4), dma(4, 4), dma(4, 4),
            ],
            compiler_params=pltpu.CompilerParams(
                collective_id=1, has_side_effects=True, vmem_limit_bytes=56 * MB
            ),
            name="front",
        )(lengths, slopes, x_own, p0, pr)
        w = w.reshape(3, width, width)
    else:
        with jax.named_scope("gather_weights"):
            by_block = lax.all_gather(parts, "tp", axis=0)
            swapped = lax.all_to_all(by_block, "ctx", split_axis=0, concat_axis=0)
            w = lax.all_gather(swapped, "shard", axis=0)
            w = w.transpose(2, 0, 1, 3, 4).reshape(4, shards * group * part_rows, width)
            biases = lax.all_gather(own_bias, "tp", axis=0, tiled=True)
            biases = lax.dynamic_slice_in_dim(biases, c, 1, 0).astype(F32)
            norms = lax.all_gather(own_norm, ("shard", "ctx"), axis=1, tiled=True).astype(F32)
        qv = biases[:, : 2 * cols].reshape(2, cols)
        vec = jnp.concatenate([norms, biases[:, 2 * cols :].reshape(2, units)], axis=0)

        xs = lax.all_gather(x_own, "ctx", axis=0, tiled=True)

        mixed, probs, q, k, v = pl.pallas_call(
            functools.partial(attention_forward, heads),
            out_shape=[sds((length, cols), BF16), sds((heads, length, length), BF16)] + [head_shape] * 3,
            in_specs=[smem(), smem()] + vmem(3),
            out_specs=vmem(5),
            scratch_shapes=[pltpu.VMEM((256, length), F32)],
            compiler_params=pltpu.CompilerParams(vmem_limit_bytes=48 * MB),
            name="attention_forward",
        )(lengths, slopes, xs, w[0], qv)
        w0, w = w[0], w[1:]


    block = (rows, width)
    stack = (group, rows, width)
    lout, dres1, grads, gout, dmixed, small = pl.pallas_call(
        middle,
        out_shape=[
            sds((tp,) + block, BF16), sds(block, F32), sds((3, width, width), BF16),
            sds((width, cols), BF16), sds((group, rows, cols), BF16), sds((8, width), F32),
        ],
        in_specs=vmem(6),
        out_specs=vmem(6),
        scratch_shapes=[
            pltpu.VMEM((width, cols), BF16), pltpu.VMEM((3,) + stack, BF16),
        ] + [pltpu.VMEM(stack, BF16)] * 5 + [pltpu.VMEM((3,) + block, BF16)] * 6 + [
            pltpu.VMEM(block, F32)
        ] * 6 + [
            pltpu.VMEM((rows, 1), F32), pltpu.VMEM(block, F32),
            pltpu.VMEM((6, 8, width), F32), pltpu.VMEM((2, 8, width), F32),
            pltpu.VMEM((4, 8, width), F32),
        ] + [dma(3, NCH)] * 12 + [dma(2)] * 2 + [dma(tp)] * 3,
        compiler_params=pltpu.CompilerParams(
            collective_id=0, has_side_effects=True, vmem_limit_bytes=58 * MB
        ),
        name="middle",
    )(x_own, cot_own, mixed.reshape(group, rows, cols), w0, w, vec)

    if fused:
        vm = pltpu.VMEM
        out0, outr, input_low = pl.pallas_call(
            functools.partial(back, heads),
            out_shape=[
                sds((wide, width), F32), sds((3, part_rows, width), F32), sds((tp,) + block, BF16)
            ],
            in_specs=vmem(12),
            out_specs=vmem(3),
            scratch_shapes=[
                vm((length, 3 * cols), BF16),
                vm((heads, DH, length), F32), vm((heads, DH, length), F32),
                vm((16, width), F32), vm((width, width), BF16), vm((2, group, wide, width), BF16),
            ] + [vm((group, wide, width), BF16), vm((3, group, part_rows, width), BF16)] * 4
            + [vm(block, BF16)] * 6 + [vm(block, F32)] * 2
            + [dma(4, 4)] * 6 + [dma(NCH)] * 6 + [dma(tp)] * 3,
            compiler_params=pltpu.CompilerParams(
                collective_id=2, has_side_effects=True, vmem_limit_bytes=56 * MB
            ),
            name="back",
        )(
            dmixed.reshape(length, cols), mixed, probs, q, k, v, xs, w0,
            grads.reshape(3, 2, group, part_rows, width), gout, small, dres1,
        )
        layer_out = lout
        input_grad = input_low.astype(F32)
        grad_qkv = jnp.stack([out0[:part_rows, i * cols : (i + 1) * cols] for i in range(3)])
        grad_out = out0[:part_rows, 3 * cols :].T
        grad_geglu = outr[0:2]
        grad_down = outr[2].T
        col = jnp.concatenate(
            [out0[part_rows : part_rows + 1, : 2 * cols],
             out0[part_rows + 1 : part_rows + 3].reshape(1, 2 * units)], axis=1)
        norm_grad = lax.dynamic_slice_in_dim(
            out0[part_rows + 3 : part_rows + 9], me * part_rows, part_rows, 1)
    else:
        grad_w, d_in, bias_grad = pl.pallas_call(
            functools.partial(attention_backward, heads),
            out_shape=[
                sds((width, 3 * cols), BF16), sds((length, width), BF16), sds((1, 3 * cols), F32)
            ],
            in_specs=vmem(8),
            out_specs=vmem(3),
            scratch_shapes=[
                pltpu.VMEM((length, 3 * cols), BF16),
                pltpu.VMEM((heads, DH, length), F32), pltpu.VMEM((heads, DH, length), F32),
            ],
            compiler_params=pltpu.CompilerParams(vmem_limit_bytes=48 * MB),
            name="attention_backward",
        )(dmixed.reshape(length, cols), mixed, probs, q, k, v, xs, w0)

        with jax.named_scope("outputs"):
            input_sum = lax.psum_scatter(d_in, "ctx", scatter_dimension=0, tiled=True)
            input_own = (input_sum.astype(F32) + dres1).astype(BF16)
            input_grad = lax.all_gather(input_own, "tp", axis=0).astype(F32)
            layer_out = lout

        with jax.named_scope("scatter_grads"):
            first_grad = jnp.concatenate([grad_w, gout], axis=1)
            packed = jnp.concatenate([first_grad[None], grads], axis=0)
            packed = packed.reshape(4, shards, group, part_rows, width).transpose(1, 2, 0, 3, 4)
            mine = lax.psum_scatter(packed, "shard", scatter_dimension=0, tiled=False)
            mine = lax.all_to_all(mine, "ctx", split_axis=0, concat_axis=0)
            mine = lax.psum_scatter(mine, "tp", scatter_dimension=0, tiled=False)
            mine = mine.astype(F32)
            grad_qkv = jnp.stack([mine[0, :, i * cols : (i + 1) * cols] for i in range(3)])
            grad_out = mine[0, :, 3 * cols :].T
            grad_geglu = mine[1:3]
            grad_down = mine[3].T
            col = jnp.concatenate(
                [bias_grad[:, :cols], bias_grad[:, 2 * cols :], small[6:7], small[7:8]], axis=1
            )
            col = lax.psum_scatter(
                jnp.zeros((group, col.shape[1]), F32) + jnp.where(
                    jnp.arange(group)[:, None] == c, col, 0.0),
                "tp", scatter_dimension=0, tiled=True)
            col = lax.psum(col, ("shard", "ctx"))
            norm_grad = lax.psum(small[:6], ("shard", "tp"))
            norm_grad = lax.dynamic_slice_in_dim(norm_grad, me * part_rows, part_rows, 1)
    return (
        layer_out,
        input_grad,
        grad_qkv,
        col[:, : 2 * cols].reshape(2, cols),
        grad_out,
        grad_geglu,
        col[:, 2 * cols :].reshape(2, units),
        grad_down,
        norm_grad[0:2],
        norm_grad[2:4],
        norm_grad[4:6],
    )


def solution(mesh):
    in_specs = (
        P("shard", "ctx", None),
        P(None, ("shard", "ctx"), "tp"),
        P(None, "tp"),
        P("tp", ("shard", "ctx")),
        P(None, ("shard", "ctx"), "tp"),
        P(None, "tp"),
        P("tp", ("shard", "ctx")),
        P(None, ("shard", "ctx")),
        P(None, ("shard", "ctx")),
        P(None, ("shard", "ctx")),
        P("shard", None),
        P("shard", "ctx", None),
    )
    out_specs = (
        P("shard", "ctx", None),
        P("shard", "ctx", None),
        P(None, ("shard", "ctx"), "tp"),
        P(None, "tp"),
        P("tp", ("shard", "ctx")),
        P(None, ("shard", "ctx"), "tp"),
        P(None, "tp"),
        P("tp", ("shard", "ctx")),
        P(None, ("shard", "ctx")),
        P(None, ("shard", "ctx")),
        P(None, ("shard", "ctx")),
    )
    return jax.shard_map(
        on_device, mesh=mesh, in_specs=in_specs, out_specs=out_specs, check_vma=False
    )
```

```python
import functools
import math
import types

import jax
import jax.numpy as jnp
from jax import lax
from jax.experimental import pallas as pl
from jax.experimental.pallas import tpu as pltpu
from jax.sharding import PartitionSpec as P

H = 12
DH = 64
F32 = jnp.float32
BF16 = jnp.bfloat16
MESH = pl.DeviceIdType.MESH
NCH = 2
TILE = 32
MB = 1 << 20
VMEM_MB = 62


def alibi_slopes(head_count):
    def power_slopes(head_total):
        first_slope = 2.0 ** (-8.0 / head_total)
        return [first_slope ** (counter + 1) for counter in range(head_total)]

    nearest = 2 ** int(math.floor(math.log2(head_count)))
    slope_list = power_slopes(nearest)
    return slope_list + power_slopes(2 * nearest)[0::2][: head_count - nearest]


def dot(left, right):
    return jnp.dot(left, right, preferred_element_type=F32)


def dot_nt(left, right):
    return lax.dot_general(left, right, (((1,), (1,)), ((), ())), preferred_element_type=F32)


def dot_tn(left, right):
    return lax.dot_general(left, right, (((0,), (0,)), ((), ())), preferred_element_type=F32)


def vmem(count):
    return [pl.BlockSpec(memory_space=pltpu.VMEM)] * count


def project_heads(heads, x_rows, rows, w, bias, q_out, k_out, v_out):
    cols = heads * DH
    for part, out in enumerate((q_out, k_out, v_out)):
        y = dot(x_rows, w[:, part * cols : (part + 1) * cols])
        if part != 1:
            y = y + bias[part // 2 : part // 2 + 1, :]
        y = y.astype(BF16)
        if part == 0:
            y = y * BF16(1.0 / math.sqrt(DH))
        for i in range(heads):
            out[i, rows, :] = y[:, i * DH : (i + 1) * DH]


def segments(lengths, pos):
    seg = jnp.zeros(pos.shape, jnp.int32)
    end = 0
    for k in range(lengths.shape[1]):
        end = end + lengths[0, k]
        seg = seg + (pos >= end).astype(jnp.int32)
    return seg


def attend_rows(heads, start, step, lengths, slopes, q, k, v, probs, mixed, far):
    length = k.shape[1]
    mine = lax.axis_index("ctx") * heads
    rows = pl.ds(start, step)
    key_pos = lax.broadcasted_iota(jnp.int32, (1, length), 1)
    pos = start + lax.broadcasted_iota(jnp.int32, (step, 1), 0)
    same = segments(lengths, pos) == segments(lengths, key_pos)
    far[...] = jnp.where(same, jnp.abs(pos - key_pos).astype(F32), 1e33)
    for i in range(heads):
        s = dot_nt(q[i, rows, :], k[i]) - slopes[0, mine + i] * far[...]
        p = jnp.exp(s - jnp.max(s, axis=-1, keepdims=True))
        p = (p * (1.0 / jnp.sum(p, axis=-1, keepdims=True))).astype(BF16)
        probs[i, rows, :] = p
        mixed[rows, i * DH : (i + 1) * DH] = dot(p, v[i]).astype(BF16)


def attention_forward(
    heads, lengths, slopes, xs, w, bias, mixed, probs, q_out, k_out, v_out, far
):
    step = 256

    def project(r, carry):
        rows = pl.ds(pl.multiple_of(r * step, step), step)
        project_heads(heads, xs[rows, :], rows, w, bias, q_out, k_out, v_out)
        return carry

    def attend(r, carry):
        start = pl.multiple_of(r * step, step)
        attend_rows(
            heads, start, step, lengths, slopes, q_out, k_out, v_out, probs, mixed, far)
        return carry

    lax.fori_loop(0, xs.shape[0] // step, project, 0)
    lax.fori_loop(0, xs.shape[0] // step, attend, 0)


def attend_back(heads, rows, dmixed, mixed, probs, q, k, v, dqkv, dk_acc, dv_acc):
    for i in range(heads):
        own = slice(i * DH, (i + 1) * DH)
        d_out = dmixed[rows, own]
        row_dot = jnp.sum(
            d_out.astype(F32) * mixed[rows, own].astype(F32), axis=-1, keepdims=True
        )
        p = probs[i, rows, :]
        dp = dot_nt(d_out, v[i])
        ds = (p.astype(F32) * (dp - row_dot)).astype(BF16)
        dqkv[rows, own] = (dot(ds, k[i]) * (1.0 / math.sqrt(DH))).astype(BF16)
        dk_acc[i] += dot_tn(q[i, rows, :], ds)
        dv_acc[i] += dot_tn(d_out, p)


def spread_heads(heads, dqkv, dk_acc, dv_acc):
    cols = heads * DH
    for i in range(heads):
        dqkv[:, cols + i * DH : cols + (i + 1) * DH] = dk_acc[i].T.astype(BF16)
        dqkv[:, 2 * cols + i * DH : 2 * cols + (i + 1) * DH] = dv_acc[i].T.astype(BF16)


def attention_backward(
    heads, dmixed, mixed, probs, q, k, v, xs, w, grad_w, d_in, bias_grad, dqkv, dk_acc, dv_acc
):
    length = xs.shape[0]
    step = 256
    cols = heads * DH
    dk_acc[...] = jnp.zeros_like(dk_acc)
    dv_acc[...] = jnp.zeros_like(dv_acc)

    def rows_back(r, carry):
        rows = pl.ds(pl.multiple_of(r * step, step), step)
        attend_back(heads, rows, dmixed, mixed, probs, q, k, v, dqkv, dk_acc, dv_acc)
        return carry

    lax.fori_loop(0, length // step, rows_back, 0)
    spread_heads(heads, dqkv, dk_acc, dv_acc)

    def finish(r, total):
        rows = pl.ds(pl.multiple_of(r * step, step), step)
        d = dqkv[rows, :]
        d_in[rows, :] = dot_nt(d, w[:, : 3 * cols]).astype(BF16)
        return total + jnp.sum(d.astype(F32), axis=0, keepdims=True)

    bias_grad[...] = lax.fori_loop(
        0, length // step, finish, jnp.zeros((1, 3 * cols), F32)
    )
    for part in range(3):
        own = slice(part * cols, (part + 1) * cols)
        grad_w[:, own] = dot_tn(xs[...], dqkv[:, own]).astype(BF16)


class Links:
    def __init__(self):
        self.started = []

    def copy(self, src, dst, send, recv, peer):
        return pltpu.make_async_remote_copy(
            src_ref=src, dst_ref=dst, send_sem=send, recv_sem=recv,
            device_id=peer, device_id_type=MESH,
        )

    def start(self, src, dst, send, recv, peer):
        copy = self.copy(src, dst, send, recv, peer)
        copy.start()
        self.started.append(copy)
        return copy

    def sent(self, copy):
        if any(copy is one for one in self.started):
            copy.wait_send()
            self.started = [one for one in self.started if one is not copy]

    def drain(self):
        for copy in self.started:
            copy.wait_send()
        self.started = []


def greet(peers):
    barrier = pltpu.get_barrier_semaphore()
    for peer in peers:
        pl.semaphore_signal(barrier, inc=1, device_id=peer, device_id_type=MESH)
    pl.semaphore_wait(barrier, len(peers))


def places():
    c = lax.axis_index("ctx")
    flip = 1 - 2 * (c % 2)
    ynb = (c + 2) % 4
    return c, c + flip, ynb, ynb + flip


class LineGather:
    def __init__(self, blocks, up, down, recv):
        self.blocks, self.up, self.down, self.recv = blocks, up, down, recv
        self.z = lax.axis_index("tp")
        self.last = blocks.shape[0] - 1

    def _copy(self, j, sem, peer):
        block = self.blocks.at[j]
        return pltpu.make_async_remote_copy(
            src_ref=block, dst_ref=block, send_sem=sem.at[j], recv_sem=self.recv.at[j],
            device_id={"tp": peer}, device_id_type=MESH,
        )

    def hop(self, d):
        z, last = self.z, self.last
        for side, j in ((0, z - d), (1, z + d)):
            here = (j >= 0) if side == 0 else (j <= last)
            edge = (z < last) if side == 0 else (z > 0)

            @pl.when(here)
            def _(side=side, j=j, edge=edge):
                sem = self.up if side == 0 else self.down
                if d:
                    self._copy(j, sem, z).wait_recv()
                if d < last:
                    @pl.when(edge)
                    def _():
                        self._copy(j, sem, z + 1 if side == 0 else z - 1).start()

    def drain(self):
        z, last = self.z, self.last
        for d in range(last):
            for side, j in ((0, z - d), (1, z + d)):
                here = (j >= 0) if side == 0 else (j <= last)
                edge = (z < last) if side == 0 else (z > 0)

                @pl.when(jnp.logical_and(here, edge))
                def _(side=side, j=j):
                    self._copy(j, self.up if side == 0 else self.down, z).wait_send()


def layer(
    names, heads, lengths, slopes,
    tokens, cotangent, qkv_w, out_w, geglu_w, down_w, qv_b, geglu_b, gains, shifts, out_b,
    lout, input_grad, out0, outr, *scratch,
):
    r = types.SimpleNamespace(**dict(zip(names, scratch)))
    c, sib, ynb, dia = places()
    me = lax.axis_index("shard")
    z = lax.axis_index("tp")
    other = 1 - me
    tp, rows_own, width = lout.shape
    piece = outr.shape[1]
    cols = heads * DH
    length = 4 * rows_own
    cr = rows_own // NCH
    links = Links()
    start, copy = links.start, links.copy
    weight_links = Links()

    def scope(name):
        return jax.named_scope(name)

    load_x = pltpu.make_async_copy(tokens.at[z], r.xs.at[c], r.load.at[0])
    load_x.start()
    load_c = pltpu.make_async_copy(cotangent.at[z], r.cot, r.load.at[1])
    load_c.start()
    with scope("pack"):
        for i in range(3):
            r.pq[:, i * cols : (i + 1) * cols] = qkv_w[i]
        r.pq[:, 3 * cols :] = jnp.zeros((piece, r.pq.shape[1] - 3 * cols), BF16)
        for i in range(2):
            for h in range(heads):
                r.pq[i * heads + h : i * heads + h + 1, 3 * cols : 3 * cols + DH] = (
                    qv_b[i : i + 1, h * DH : (h + 1) * DH])
        r.po[...] = jnp.zeros_like(r.po)
        r.po[0:piece, 0:cols] = out_w[...].T
        span = r.po.shape[1]
        thirds = width // span
        for i in range(2):
            for t in range(thirds):
                row = piece + i * thirds + t
                r.po[row : row + 1, :] = geglu_b[i : i + 1, t * span : (t + 1) * span]
        row = piece + 2 * thirds
        for i, ref in enumerate((gains, shifts, out_b)):
            r.po[row + 2 * i : row + 2 * i + 2, 0:piece] = ref[...]
        r.pd[...] = down_w[...].T

    with scope("greet"):
        greet([{"ctx": sib}, {"ctx": ynb}, {"ctx": dia}, {"shard": other}]
              + [{"tp": (z + d) % tp} for d in range(1, tp)])

    src = {"q": r.pq, "o": r.po, 0: geglu_w.at[0], 1: geglu_w.at[1]}
    zb = {"q": r.zbq, "o": r.zbo, 0: r.zbr.at[0], 1: r.zbr.at[1], 2: r.zbd}
    wr = {"q": r.wq, "o": r.wo, 0: r.w.at[0], 1: r.w.at[1], 2: r.w.at[2]}
    index = {"q": 0, "o": 1, 0: 2, 1: 3, 2: 4}
    last = tp - 1

    def line_copy(p, j, sems, peer):
        block = zb[p].at[j]
        return copy(block, block, sems.at[index[p], j], r.zr.at[index[p], j], {"tp": peer})

    def owner_slot(p, j):
        return wr[p].at[:, j] if p == 2 else wr[p].at[me, j]

    def hop(p, d):
        def deliver(j):
            @pl.when(j == c)
            def _():
                owner_slot(p, c)[...] = zb[p].at[j][...]

            @pl.when(j != c)
            def _():
                copy(zb[p].at[j], owner_slot(p, c), r.ys.at[index[p], j], r.yr.at[index[p], c],
                     {"ctx": j}).start()

        with scope(f"hop_{p}{d}"):
            if d == 0:
                if p == 2:
                    own_down.wait_recv()
                else:
                    zb[p].at[z][...] = src[p][...]

                @pl.when(z < last)
                def _():
                    line_copy(p, z, r.zu, z + 1).start()

                @pl.when(z > 0)
                def _():
                    line_copy(p, z, r.zd, z - 1).start()

                deliver(z)
                return
            for side in range(2):
                j = z - d if side == 0 else z + d

                @pl.when((j >= 0) if side == 0 else (j <= last))
                def _(side=side, j=j):
                    line_copy(p, j, r.zu, z).wait_recv()
                    if d < last:
                        @pl.when((z < last) if side == 0 else (z > 0))
                        def _():
                            if side == 0:
                                line_copy(p, j, r.zu, z + 1).start()
                            else:
                                line_copy(p, j, r.zd, z - 1).start()
                    deliver(j)

    def hop_drain(p):
        for d in range(last):
            for side in range(2):
                j = z - d if side == 0 else z + d
                here = (j >= 0) if side == 0 else (j <= last)
                edge = (z < last) if side == 0 else (z > 0)

                @pl.when(jnp.logical_and(here, edge))
                def _(side=side, j=j):
                    line_copy(p, j, r.zu if side == 0 else r.zd, z).wait_send()
        for j in (sib, ynb, dia):
            copy(zb[p].at[j], owner_slot(p, c), r.ys.at[index[p], j], r.yr.at[index[p], c],
                 {"ctx": j}).wait_send()

    def owned(p, j):
        copy(zb[p].at[c], owner_slot(p, j), r.ys.at[index[p], c], r.yr.at[index[p], j],
             {"ctx": c}).wait_recv()

    def to_shard(p):
        with scope(f"to_shard_{p}"):
            for i, j in enumerate((c, sib, ynb, dia)):
                slot = wr[p].at[me, j]
                if i:
                    owned(p, j)
                weight_links.start(slot, slot, r.xs_s.at[index[p], i], r.xs_r.at[index[p], j],
                                   {"shard": other})

    def complete(p):
        with scope(f"complete_{p}"):
            if p == 2:
                for j in (sib, ynb, dia):
                    owned(p, j)
                return
            for j in range(4):
                slot = wr[p].at[other, j]
                copy(slot, slot, r.xs_s.at[index[p], 0], r.xs_r.at[index[p], j],
                     {"shard": other}).wait_recv()

    grad = [r.g0] + [r.w.at[i] for i in range(3)]
    xb = [r.xb0] + [r.xbr.at[i] for i in range(3)]
    yb = [r.yb0] + [r.ybr.at[i] for i in range(3)]
    rb = [r.rb0] + [r.rbr.at[i] for i in range(3)]
    out = [out0] + [outr.at[i] for i in range(3)]

    def grad_to_shard(p):
        for i, j in enumerate((dia, ynb, sib, c)):
            start(grad[p].at[other, j], xb[p].at[j], r.gx_s.at[p, i], r.gx_r.at[p, j], {"shard": other})

    def grad_to_owner(p):
        with scope(f"grad_to_owner_{p}"):
            for i, j in enumerate((dia, ynb, sib, c)):
                copy(grad[p].at[other, j], xb[p].at[j], r.gx_s.at[p, 0], r.gx_r.at[p, j],
                     {"shard": other}).wait_recv()
                total = (grad[p].at[me, j][...].astype(F32) + xb[p].at[j][...].astype(F32)).astype(BF16)
                if i == 3:
                    yb[p].at[c][...] = total
                else:
                    xb[p].at[j][...] = total
                    start(xb[p].at[j], yb[p].at[c], r.gy_s.at[p, i], r.gy_r.at[p, c], {"ctx": j})

    def climb(p, side, j):
        if side == 0:
            return copy(yb[p].at[j], rb[p].at[j], r.gu_s.at[p, j], r.gu_r.at[p, j], {"tp": z + 1})
        slot = jnp.where(j == z - 1, tp, j)
        return copy(yb[p].at[j], rb[p].at[slot], r.gd_s.at[p, j], r.gd_r.at[p, j], {"tp": z - 1})

    def grad_hop(p, h):
        with scope(f"grad_hop_{p}{h}"):
            if h == 0:
                for j in (sib, ynb, dia):
                    copy(xb[p].at[j], yb[p].at[j], r.gy_s.at[p, 0], r.gy_r.at[p, j], {"ctx": j}).wait_recv()
            if h == last:
                out[p][...] = yb[p].at[z][...].astype(F32)

                @pl.when(z > 0)
                def _():
                    copy(yb[p].at[z], rb[p].at[z], r.gu_s.at[p, z], r.gu_r.at[p, z], {"tp": z}).wait_recv()
                    out[p][...] += rb[p].at[z][...].astype(F32)

                @pl.when(z < last)
                def _():
                    copy(yb[p].at[z], rb[p].at[tp], r.gd_s.at[p, z], r.gd_r.at[p, z], {"tp": z}).wait_recv()
                    out[p][...] += rb[p].at[tp][...].astype(F32)
                return
            for side in range(2):
                j = z + (last - h) if side == 0 else z - (last - h)

                @pl.when((j <= last) if side == 0 else (j >= 0))
                def _(side=side, j=j):
                    @pl.when((z > 0) if side == 0 else (z < last))
                    def _():
                        sems = r.gu_r if side == 0 else r.gd_r
                        copy(yb[p].at[j], rb[p].at[j], r.gu_s.at[p, j], sems.at[p, j], {"tp": z}).wait_recv()
                        yb[p].at[j][...] = (
                            yb[p].at[j][...].astype(F32) + rb[p].at[j][...].astype(F32)).astype(BF16)
                    climb(p, side, j).start()

    def grad_drain(p):
        for h in range(last):
            for side in range(2):
                j = z + (last - h) if side == 0 else z - (last - h)

                @pl.when((j <= last) if side == 0 else (j >= 0))
                def _(side=side, j=j):
                    climb(p, side, j).wait_send()

    def chunk(k):
        return pl.ds(k * cr, cr)

    ag_y, ag_c, ag_f, rs_r, rs_o, rs_y = ({} for _ in range(6))

    def gather_start(o, k):
        block = r.full.at[o, c, chunk(k)]
        ag_y[o, k] = start(block, block, r.ags_y.at[o, k], r.agr_y.at[o, k], {"ctx": ynb})
        ag_c[o, k] = start(block, block, r.ags_c.at[o, k], r.agr_c.at[o, k], {"ctx": sib})

    def forward(o, k):
        ag_y[o, k].wait_recv()
        block = r.full.at[o, ynb, chunk(k)]
        ag_f[o, k] = start(block, block, r.ags_f.at[o, k], r.agr_f.at[o, k], {"ctx": sib})

    def place(table, buf, o, k, value):
        if o:
            links.sent(table[o - 1, k])
        buf[chunk(k), :] = value.astype(BF16)

    def send_relay(o, k, value):
        place(rs_r, r.snd_r, o, k, value)
        rs_r[o, k] = start(r.snd_r.at[chunk(k)], r.rcv_r.at[chunk(k)],
                           r.rss_r.at[o, k], r.rsr_r.at[o, k], {"ctx": sib})

    def send_own(o, k, value):
        place(rs_o, r.snd_o, o, k, value)
        rs_o[o, k] = start(r.snd_o.at[chunk(k)], r.rcv_o.at[chunk(k)],
                           r.rss_o.at[o, k], r.rsr_o.at[o, k], {"ctx": sib})

    def relay(o, k):
        rs_r[o, k].wait_recv()
        place(rs_y, r.snd_y, o, k, r.yacc[chunk(k), :] + r.rcv_r[chunk(k), :].astype(F32))
        rs_y[o, k] = start(r.snd_y.at[chunk(k)], r.rcv_y.at[chunk(k)],
                           r.rss_y.at[o, k], r.rsr_y.at[o, k], {"ctx": ynb})

    def arrived(o, k):
        rs_o[o, k].wait_recv()
        rs_y[o, k].wait_recv()

    def summed(rows):
        return r.own[rows, :] + r.rcv_o[rows, :].astype(F32) + r.rcv_y[rows, :].astype(F32)

    def tiles(first, count, body):
        def step(t, carry):
            body(pl.ds(pl.multiple_of(first + t * TILE, TILE), TILE))
            return carry
        lax.fori_loop(0, count // TILE, step, 0)

    def fold(values):
        return jnp.sum(values.reshape(TILE // 8, 8, width), axis=0)

    def rows_of(b, r0=0, n=rows_own):
        return pl.ds(pl.multiple_of(b * rows_own + r0, cr), n)

    def send_sums(o, piece_of):
        for k in range(NCH):
            send_relay(o, k, piece_of(dia, k * cr, cr))
            r.yacc[chunk(k), :] = piece_of(ynb, k * cr, cr)
            if k:
                relay(o, k - 1)
        relay(o, NCH - 1)
        for k in range(NCH):
            send_own(o, k, piece_of(sib, k * cr, cr))
        r.own[...] = piece_of(c, 0, rows_own)

    load_x.wait()
    first = start(r.xs.at[c], r.xs.at[c], r.xg_s.at[0], r.xg_r.at[0], {"ctx": ynb})
    near = start(r.xs.at[c], r.xs.at[c], r.xg_s.at[1], r.xg_r.at[1], {"ctx": sib})
    own_down = start(r.pd, r.zbd.at[z, me], r.xd_s.at[0], r.xd_r.at[0], {"shard": other})
    r.zbd.at[z, me][...] = r.pd[...]
    hop("q", 0)
    r.acc[...] = jnp.zeros_like(r.acc)
    r.bsum[...] = jnp.zeros_like(r.bsum)
    r.dk_acc[...] = jnp.zeros_like(r.dk_acc)
    r.dv_acc[...] = jnp.zeros_like(r.dv_acc)
    hop("q", 1)
    hop("q", 2)
    hop("o", 0)
    hop("q", 3)
    hop(0, 0)
    to_shard("q")
    with scope("tokens"):
        first.wait_recv()
        passed = start(r.xs.at[ynb], r.xs.at[ynb], r.xg_s.at[2], r.xg_r.at[2], {"ctx": sib})
    hop("o", 1)
    hop("o", 2)
    hop("o", 3)
    hop(0, 1)
    to_shard("o")
    hop(0, 2)
    with scope("tokens"):
        near.wait_recv()
        passed.wait_recv()
    complete("q")
    with scope("project"):
        wq = r.wq[...].reshape(width, r.wq.shape[3])
        for i in range(2):
            for h in range(heads):
                r.qv[i : i + 1, h * DH : (h + 1) * DH] = (
                    r.wq[0, 0, i * heads + h : i * heads + h + 1, 3 * cols : 3 * cols + DH].astype(F32))

        def project(t, carry):
            rows = pl.ds(pl.multiple_of(t * rows_own, rows_own), rows_own)
            project_heads(heads, r.xs[t], rows, r.wq[...].reshape(width, r.wq.shape[3]), r.qv, r.q, r.k, r.v)
            return carry

        lax.fori_loop(0, 4, project, 0)
    hop(0, 3)
    hop(1, 0)

    def attend(b):
        with scope("attend"):
            attend_rows(heads, pl.multiple_of(b * rows_own, rows_own), rows_own, lengths, slopes,
                        r.q, r.k, r.v, r.probs, r.mixed, r.far)

    def out_project(b, r0, n):
        return dot_nt(r.mixed[rows_of(b, r0, n), :], r.w_out[...])

    attend(dia)
    complete("o")
    for s in range(2):
        for j in range(4):
            place_ = s * 4 + j
            r.w_out[pl.ds(place_ * piece, piece), :] = r.wo[s, j, 0:piece, 0:cols]
            row = piece + 2 * thirds
            r.vec[0:6, place_ * piece : (place_ + 1) * piece] = r.wo[s, j, row : row + 6, 0:piece].astype(F32)
    for i in range(2):
        for t in range(thirds):
            row = piece + i * thirds + t
            r.vec[6 + i : 7 + i, t * span : (t + 1) * span] = r.wo[0, 0, row : row + 1, :].astype(F32)
    for k in range(NCH):
        send_relay(0, k, out_project(dia, k * cr, cr))
    hop(1, 1)
    to_shard(0)
    attend(ynb)
    for k in range(NCH):
        r.yacc[chunk(k), :] = out_project(ynb, k * cr, cr)
        with scope("relay"):
            relay(0, k)
    hop(1, 2)
    attend(sib)
    for k in range(NCH):
        send_own(0, k, out_project(sib, k * cr, cr))
    attend(c)
    r.own[...] = out_project(c, 0, rows_own)
    hop(1, 3)
    hop(2, 0)

    def norm_one(rows):
        res = r.xs[c, rows, :].astype(F32) + summed(rows) + r.vec[4:5, :]
        center = res - jnp.mean(res, axis=-1, keepdims=True)
        scale = lax.rsqrt(jnp.mean(center * center, axis=-1, keepdims=True) + 1e-12)
        zh = center * scale
        value = zh * r.vec[0:1, :] + r.vec[2:3, :]
        r.zh1[rows, :] = zh
        r.r1[rows, :] = scale
        r.normed[rows, :] = value
        r.full[0, c, rows, :] = value.astype(BF16)

    with scope("norm_one"):
        for k in range(NCH):
            arrived(0, k)
            tiles(k * cr, cr, norm_one)
            gather_start(0, k)

    def matrix(i):
        return r.w[i].reshape(width, width)

    def units_forward(b, r0, n):
        rows_in = r.full[0, b, pl.ds(r0, n), :]
        r.fa[pl.ds(0, n), :] = dot(rows_in, matrix(0))
        r.fb[pl.ds(0, n), :] = dot(rows_in, matrix(1))

        def units(rows):
            g = r.fa[rows, :] + r.vec[6:7, :]
            u = r.fb[rows, :] + r.vec[7:8, :]
            phi = 0.5 * (1.0 + lax.erf(g * (1.0 / math.sqrt(2.0))))
            gelu = g * phi
            slope = phi + g * jnp.exp(-0.5 * g * g) * (1.0 / math.sqrt(2.0 * math.pi))
            to = pl.ds(pl.multiple_of(r0 + rows.start, TILE), TILE)
            r.act[b, to, :] = gelu.astype(BF16)
            r.pull[b, to, :] = (u * slope).astype(BF16)
            r.hid[b, to, :] = (gelu * u).astype(BF16)

        tiles(0, n, units)

    def down(b, r0, n):
        return dot_nt(r.hid[b, pl.ds(r0, n), :], matrix(2))

    def units_backward(b, r0, n):
        r.fa[pl.ds(0, n), :] = dot(r.full[1, b, pl.ds(r0, n), :], matrix(2))

        def units(rows):
            dh = r.fa[rows, :]
            to = pl.ds(pl.multiple_of(r0 + rows.start, TILE), TILE)
            dg = (dh * r.pull[b, to, :].astype(F32)).astype(BF16)
            du = (dh * r.act[b, to, :].astype(F32)).astype(BF16)
            r.pull[b, to, :] = dg
            r.act[b, to, :] = du
            r.bsum[0] += fold(dg.astype(F32))
            r.bsum[1] += fold(du.astype(F32))

        tiles(0, n, units)
        return (dot_nt(r.pull[b, pl.ds(r0, n), :], matrix(0))
                + dot_nt(r.act[b, pl.ds(r0, n), :], matrix(1)))

    to_shard(1)
    hop(2, 1)
    complete(0)
    hop(2, 2)
    complete(1)
    with scope("units_forward"):
        units_forward(c, 0, rows_own)
        for k in range(NCH):
            ag_c[0, k].wait_recv()
        units_forward(sib, 0, rows_own)
        for k in range(NCH):
            forward(0, k)
        units_forward(ynb, 0, rows_own)
    hop(2, 3)
    with scope("units_forward"):
        for k in range(NCH):
            ag_f[0, k].wait_recv()
        units_forward(dia, 0, rows_own)
    complete(2)
    with scope("down"):
        send_sums(1, down)

    def norm_two(rows):
        res = r.normed[rows, :] + (summed(rows) + r.vec[5:6, :])
        center = res - jnp.mean(res, axis=-1, keepdims=True)
        scale = lax.rsqrt(jnp.mean(center * center, axis=-1, keepdims=True) + 1e-12)
        zh = center * scale
        lout[z, rows, :] = (zh * r.vec[1:2, :] + r.vec[3:4, :]).astype(BF16)
        up = r.cot[rows, :].astype(F32)
        t = up * r.vec[1:2, :]
        d = scale * (t - jnp.mean(t, axis=-1, keepdims=True)
                     - zh * jnp.mean(t * zh, axis=-1, keepdims=True))
        r.normed[rows, :] = d
        low = d.astype(BF16)
        r.full[1, c, rows, :] = low
        r.acc[1] += fold(up * zh)
        r.acc[3] += fold(up)
        r.acc[5] += fold(low.astype(F32))

    load_c.wait()
    with scope("norm_two"):
        for k in range(NCH):
            arrived(1, k)
            tiles(k * cr, cr, norm_two)
            gather_start(1, k)
    line_out = LineGather(lout, r.lu.at[0], r.ld.at[0], r.lr.at[0])
    line_out.hop(0)

    def flat(ref):
        return ref[...].reshape(length, ref.shape[-1])

    def put(i, value):
        r.w[i] = value.astype(BF16).reshape(r.w.shape[1:])

    def put_down():
        with scope("down_gradient"):
            weight_links.drain()
            put(2, dot_tn(flat(r.full.at[1]), flat(r.hid)))
            grad_to_shard(3)

    with scope("units_backward"):
        r.own[...] = units_backward(c, 0, rows_own)
        for k in range(NCH):
            ag_c[1, k].wait_recv()
        value = units_backward(sib, 0, rows_own)
        for k in range(NCH):
            send_own(2, k, value[k * cr : (k + 1) * cr])
        line_out.hop(1)
        for k in range(NCH):
            forward(1, k)
            r.yacc[chunk(k), :] = units_backward(ynb, k * cr, cr)
            ag_f[1, k].wait_recv()
            send_relay(2, k, units_backward(dia, k * cr, cr))
            if k:
                relay(2, k - 1)
        put_down()
        relay(2, NCH - 1)

    with scope("unit_gradients"):
        n_all = flat(r.full.at[0])
        put(0, dot_tn(n_all, flat(r.pull)))
        grad_to_shard(1)
        put(1, dot_tn(n_all, flat(r.act)))
        grad_to_shard(2)
    line_out.hop(2)

    def norm_back(rows):
        dn = summed(rows) + r.normed[rows, :]
        zh = r.zh1[rows, :]
        t = dn * r.vec[0:1, :]
        d = r.r1[rows, :] * (t - jnp.mean(t, axis=-1, keepdims=True)
                             - zh * jnp.mean(t * zh, axis=-1, keepdims=True))
        r.zh1[rows, :] = d
        low = d.astype(BF16)
        r.full[2, c, rows, :] = low
        r.acc[0] += fold(dn * zh)
        r.acc[2] += fold(dn)
        r.acc[4] += fold(low.astype(F32))

    with scope("norm_back"):
        for k in range(NCH):
            arrived(2, k)
            tiles(k * cr, cr, norm_back)
            gather_start(2, k)

    def unproject(b, r0, n):
        r.dmixed[rows_of(b, r0, n), :] = dot(r.full[2, b, pl.ds(r0, n), :], r.w_out[...]).astype(BF16)

    def back_rows(b):
        with scope("attend_back"):
            attend_back(heads, rows_of(b), r.dmixed, r.mixed, r.probs, r.q, r.k, r.v,
                        r.dqkv, r.dk_acc, r.dv_acc)

    for i in range(6):
        r.tiny[0, i : i + 1, :] = jnp.sum(r.acc[i], axis=0, keepdims=True)
    tiny_sib = start(r.tiny.at[0], r.tiny.at[1], r.tiny_s.at[0], r.tiny_r.at[0], {"ctx": sib})
    unproject(c, 0, rows_own)
    back_rows(c)
    for k in range(NCH):
        ag_c[2, k].wait_recv()
    unproject(sib, 0, rows_own)
    back_rows(sib)
    tiny_sib.wait_recv()
    r.tiny[2] = r.tiny[0] + r.tiny[1]
    tiny_y = start(r.tiny.at[2], r.tiny.at[3], r.tiny_s.at[1], r.tiny_r.at[1], {"ctx": ynb})
    for k in range(NCH):
        forward(2, k)
    grad_to_owner(3)
    unproject(ynb, 0, rows_own)
    back_rows(ynb)
    for k in range(NCH):
        ag_f[2, k].wait_recv()
    unproject(dia, 0, rows_own)
    back_rows(dia)
    with scope("spread_heads"):
        spread_heads(heads, r.dqkv, r.dk_acc, r.dv_acc)

    def piece_in(b, r0, n):
        return dot_nt(
            r.dqkv[rows_of(b, r0, n), :], r.wq[...].reshape(width, r.wq.shape[3])[:, : 3 * cols])

    with scope("input_sums"):
        send_sums(3, piece_in)

    with scope("projection_gradients"):
        tiny_y.wait_recv()
        norms = r.tiny[2] + r.tiny[3]
        bias = jnp.sum(r.dqkv[...].astype(F32), axis=0, keepdims=True)
        r.extra[...] = jnp.zeros_like(r.extra)
        r.extra[0:1, 0:cols] = bias[:, :cols]
        r.extra[0:1, cols : 2 * cols] = bias[:, 2 * cols :]
        for i in range(2):
            r.extra[1 + i : 2 + i, :] = jnp.sum(r.bsum[i], axis=0, keepdims=True)
        r.extra[3:9, :] = norms[0:6, :]
        low = r.extra[...].astype(BF16)
        x_all = flat(r.xs)
        for i in range(4):
            lanes = slice(i * cols, (i + 1) * cols)
            if i < 3:
                value = dot_tn(x_all, r.dqkv[:, lanes])
            else:
                value = dot_tn(flat(r.full.at[2]), r.mixed[...])
            value = value.astype(BF16)
            for s in range(2):
                for j in range(4):
                    first_row = (s * 4 + j) * piece
                    r.g0[s, j, 0:piece, lanes] = value[first_row : first_row + piece]
        for s in range(2):
            for j in range(4):
                r.g0[s, j, piece:, :] = low
        grad_to_shard(0)
    grad_hop(3, 0)
    grad_to_owner(1)
    grad_hop(3, 1)
    grad_hop(3, 2)
    line_in = LineGather(input_grad, r.lu.at[1], r.ld.at[1], r.lr.at[1])
    with scope("input_total"):
        for k in range(NCH):
            arrived(3, k)
            input_grad[z, chunk(k), :] = (
                summed(chunk(k)) + r.zh1[chunk(k), :]).astype(BF16)
        line_in.hop(0)
    with scope("line_out_3"):
        line_out.hop(3)
    grad_hop(3, 3)
    grad_hop(1, 0)
    grad_to_owner(2)
    grad_hop(1, 1)
    grad_hop(1, 2)
    with scope("line_in_1"):
        line_in.hop(1)
    grad_hop(1, 3)
    grad_hop(2, 0)
    grad_to_owner(0)
    grad_hop(2, 1)
    grad_hop(2, 2)
    grad_hop(2, 3)
    grad_hop(0, 0)
    with scope("line_in_2"):
        line_in.hop(2)
    grad_hop(0, 1)
    grad_hop(0, 2)
    grad_hop(0, 3)
    with scope("line_in_3"):
        line_in.hop(3)
    with scope("drain"):
        line_out.drain()
        line_in.drain()
        for p in range(4):
            grad_drain(p)
        for p in index:
            hop_drain(p)
        links.drain()


def finish(lout, input_low, out0, outr, o_lout, o_in, o_qkv, o_qvb, o_out, o_geglu, o_gb, o_down,
           o_gain, o_shift, o_ob):
    piece = outr.shape[1]
    cols = o_qkv.shape[2]
    o_lout[...] = lout[...]

    def widen(i, carry):
        o_in[i] = input_low[i].astype(F32)
        return carry

    lax.fori_loop(0, o_in.shape[0], widen, 0)
    for i in range(3):
        o_qkv[i] = out0[0:piece, i * cols : (i + 1) * cols]
    o_out[...] = out0[0:piece, 3 * cols : 4 * cols].T
    o_geglu[...] = outr[0:2]
    o_down[...] = outr[2].T
    o_qvb[0:1, :] = out0[piece : piece + 1, 0:cols]
    o_qvb[1:2, :] = out0[piece : piece + 1, cols : 2 * cols]
    o_gb[...] = out0[piece + 1 : piece + 3, :]
    place = lax.axis_index("shard") * 4 + lax.axis_index("ctx")
    for s in range(8):
        @pl.when(place == s)
        def _(s=s):
            lanes = slice(s * piece, (s + 1) * piece)
            o_gain[...] = out0[piece + 3 : piece + 5, lanes]
            o_shift[...] = out0[piece + 5 : piece + 7, lanes]
            o_ob[...] = out0[piece + 7 : piece + 9, lanes]


def middle(
    x, cot, mixed, w0, w, vec,
    lout, dres1, grads, gout, dmixed, small,
    w_out, full, act, pull, hid, dgt, dup,
    snd_r, snd_o, snd_y, rcv_r, rcv_o, rcv_y,
    own, yacc, fa, fb, normed, zh1, r1, dres2, acc, bsum, tiny,
    ags_y, agr_y, ags_c, agr_c, ags_f, agr_f,
    rss_r, rsr_r, rss_o, rsr_o, rss_y, rsr_y, tiny_s, tiny_r, lu, ld, lr,
):
    rows_own = x.shape[0]
    width = x.shape[1]
    cr = rows_own // NCH
    c, sib, ynb, dia = places()
    z = lax.axis_index("tp")
    tp = lout.shape[0]
    greet([{"ctx": sib}, {"ctx": ynb}] + [{"tp": (z + d) % tp} for d in range(1, tp)])
    line = LineGather(lout, lu, ld, lr)

    started = []

    def remote(src, dst, send, recv, peer):
        return pltpu.make_async_remote_copy(
            src_ref=src, dst_ref=dst, send_sem=send, recv_sem=recv,
            device_id={"ctx": peer}, device_id_type=MESH,
        )

    def chunk(k):
        return pl.ds(k * cr, cr)

    ag_y, ag_c, ag_f, rs_r, rs_o, rs_y = ({} for _ in range(6))

    def start(table, key, copy):
        copy.start()
        table[key] = copy
        started.append(copy)

    def gather_start(o, k):
        piece = full.at[o, c, chunk(k)]
        start(ag_y, (o, k), remote(piece, piece, ags_y.at[o, k], agr_y.at[o, k], ynb))
        start(ag_c, (o, k), remote(piece, piece, ags_c.at[o, k], agr_c.at[o, k], sib))

    def forward(o, k):
        ag_y[o, k].wait_recv()
        piece = full.at[o, ynb, chunk(k)]
        start(ag_f, (o, k), remote(piece, piece, ags_f.at[o, k], agr_f.at[o, k], sib))

    def send_relay(o, k):
        start(rs_r, (o, k), remote(
            snd_r.at[o, chunk(k)], rcv_r.at[o, chunk(k)], rss_r.at[o, k], rsr_r.at[o, k], sib))

    def send_own(o, k):
        start(rs_o, (o, k), remote(
            snd_o.at[o, chunk(k)], rcv_o.at[o, chunk(k)], rss_o.at[o, k], rsr_o.at[o, k], sib))

    def relay(o, k):
        rs_r[o, k].wait_recv()
        snd_y[o, chunk(k), :] = (yacc[chunk(k), :] + rcv_r[o, chunk(k), :].astype(F32)).astype(BF16)
        start(rs_y, (o, k), remote(
            snd_y.at[o, chunk(k)], rcv_y.at[o, chunk(k)], rss_y.at[o, k], rsr_y.at[o, k], ynb))

    def arrived(o, k):
        rs_o[o, k].wait_recv()
        rs_y[o, k].wait_recv()

    def tiles(first, count, body):
        def step(t, carry):
            body(pl.ds(pl.multiple_of(first + t * TILE, TILE), TILE))
            return carry
        lax.fori_loop(0, count // TILE, step, 0)

    def summed(o, rows):
        return own[rows, :] + rcv_o[o, rows, :].astype(F32) + rcv_y[o, rows, :].astype(F32)

    def fold(values):
        return jnp.sum(values.reshape(TILE // 8, 8, width), axis=0)

    acc[...] = jnp.zeros_like(acc)
    bsum[...] = jnp.zeros_like(bsum)
    w_out[...] = w0[:, 3 * mixed.shape[2] : 4 * mixed.shape[2]]

    def project(b, r0, n):
        return dot_nt(mixed[b, pl.ds(r0, n), :], w_out[...])

    for k in range(NCH):
        snd_r[0, chunk(k), :] = project(dia, k * cr, cr).astype(BF16)
        send_relay(0, k)
        yacc[chunk(k), :] = project(ynb, k * cr, cr)
        if k:
            relay(0, k - 1)
    relay(0, NCH - 1)
    for k in range(NCH):
        snd_o[0, chunk(k), :] = project(sib, k * cr, cr).astype(BF16)
        send_own(0, k)
    own[...] = project(c, 0, rows_own)

    def norm_one(rows):
        res = x[rows, :].astype(F32) + summed(0, rows) + vec[4:5, :]
        center = res - jnp.mean(res, axis=-1, keepdims=True)
        r = lax.rsqrt(jnp.mean(center * center, axis=-1, keepdims=True) + 1e-12)
        zh = center * r
        out = zh * vec[0:1, :] + vec[2:3, :]
        zh1[rows, :] = zh
        r1[rows, :] = r
        normed[rows, :] = out
        full[0, c, rows, :] = out.astype(BF16)

    for k in range(NCH):
        arrived(0, k)
        tiles(k * cr, cr, norm_one)
        gather_start(0, k)

    def mlp_forward(b, r0, n):
        rows_in = full[0, b, pl.ds(r0, n), :]
        fa[pl.ds(0, n), :] = dot(rows_in, w[0])
        fb[pl.ds(0, n), :] = dot(rows_in, w[1])

        def units(rows):
            g = fa[rows, :] + vec[6:7, :]
            u = fb[rows, :] + vec[7:8, :]
            phi = 0.5 * (1.0 + lax.erf(g * (1.0 / math.sqrt(2.0))))
            gelu = g * phi
            slope = phi + g * jnp.exp(-0.5 * g * g) * (1.0 / math.sqrt(2.0 * math.pi))
            out = pl.ds(pl.multiple_of(r0 + rows.start, TILE), TILE)
            act[b, out, :] = gelu.astype(BF16)
            pull[b, out, :] = (u * slope).astype(BF16)
            hid[b, out, :] = (gelu * u).astype(BF16)

        tiles(0, n, units)
        return dot_nt(hid[b, pl.ds(r0, n), :], w[2])

    def mlp_backward(b, r0, n):
        fa[pl.ds(0, n), :] = dot(full[1, b, pl.ds(r0, n), :], w[2])

        def units(rows):
            dh = fa[rows, :]
            out = pl.ds(pl.multiple_of(r0 + rows.start, TILE), TILE)
            dg = (dh * pull[b, out, :].astype(F32)).astype(BF16)
            du = (dh * act[b, out, :].astype(F32)).astype(BF16)
            dgt[b, out, :] = dg
            dup[b, out, :] = du
            bsum[0] += fold(dg.astype(F32))
            bsum[1] += fold(du.astype(F32))

        tiles(0, n, units)
        return dot_nt(dgt[b, pl.ds(r0, n), :], w[0]) + dot_nt(dup[b, pl.ds(r0, n), :], w[1])

    def exchange(o, piece):
        own[...] = piece(c, 0, rows_own)
        for k in range(NCH):
            ag_c[o - 1, k].wait_recv()
        snd_o[o] = piece(sib, 0, rows_own).astype(BF16)
        for k in range(NCH):
            send_own(o, k)
        for k in range(NCH):
            forward(o - 1, k)
            yacc[chunk(k), :] = piece(ynb, k * cr, cr)
            ag_f[o - 1, k].wait_recv()
            snd_r[o, chunk(k), :] = piece(dia, k * cr, cr).astype(BF16)
            send_relay(o, k)
            if k:
                relay(o, k - 1)
        relay(o, NCH - 1)

    exchange(1, mlp_forward)

    def norm_two(rows):
        res = normed[rows, :] + (summed(1, rows) + vec[5:6, :])
        center = res - jnp.mean(res, axis=-1, keepdims=True)
        r = lax.rsqrt(jnp.mean(center * center, axis=-1, keepdims=True) + 1e-12)
        zh = center * r
        lout[z, rows, :] = (zh * vec[1:2, :] + vec[3:4, :]).astype(BF16)
        up = cot[rows, :].astype(F32)
        t = up * vec[1:2, :]
        d = r * (t - jnp.mean(t, axis=-1, keepdims=True)
                 - zh * jnp.mean(t * zh, axis=-1, keepdims=True))
        dres2[rows, :] = d
        low = d.astype(BF16)
        full[1, c, rows, :] = low
        acc[1] += fold(up * zh)
        acc[3] += fold(up)
        acc[5] += fold(low.astype(F32))

    for k in range(NCH):
        arrived(1, k)
        tiles(k * cr, cr, norm_two)
        gather_start(1, k)

    line.hop(0)
    exchange(2, mlp_backward)
    line.hop(1)

    def flat(ref):
        return ref[...].reshape(4 * rows_own, ref.shape[-1])

    hid_all = flat(hid)
    d_all = full[1].reshape(4 * rows_own, width)
    grads[2] = dot_tn(d_all, hid_all).astype(BF16)
    n_all = full[0].reshape(4 * rows_own, width)
    grads[0] = dot_tn(n_all, flat(dgt)).astype(BF16)
    grads[1] = dot_tn(n_all, flat(dup)).astype(BF16)

    line.hop(2)

    def norm_back(rows):
        dn = summed(2, rows) + dres2[rows, :]
        zh = zh1[rows, :]
        t = dn * vec[0:1, :]
        d = r1[rows, :] * (t - jnp.mean(t, axis=-1, keepdims=True)
                           - zh * jnp.mean(t * zh, axis=-1, keepdims=True))
        dres1[rows, :] = d
        low = d.astype(BF16)
        full[2, c, rows, :] = low
        acc[0] += fold(dn * zh)
        acc[2] += fold(dn)
        acc[4] += fold(low.astype(F32))

    for k in range(NCH):
        arrived(2, k)
        tiles(k * cr, cr, norm_back)
        gather_start(2, k)

    for i in range(6):
        tiny[0, i : i + 1, :] = jnp.sum(acc[i], axis=0, keepdims=True)
    for i in range(2):
        small[6 + i : 7 + i, :] = jnp.sum(bsum[i], axis=0, keepdims=True)
    tiny_copies = []
    for step, peer in enumerate((sib, ynb)):
        copy = remote(tiny.at[2 * step], tiny.at[2 * step + 1], tiny_s.at[step], tiny_r.at[step], peer)
        copy.start()
        started.append(copy)
        tiny_copies.append(copy)
        if step == 0:
            def unproject(b, r0, n):
                return dot(full[2, b, pl.ds(r0, n), :], w_out[...]).astype(BF16)
            dmixed[c] = unproject(c, 0, rows_own)
            for k in range(NCH):
                ag_c[2, k].wait_recv()
            dmixed[sib] = unproject(sib, 0, rows_own)
        copy.wait_recv()
        total = tiny[2 * step] + tiny[2 * step + 1]
        if step == 0:
            tiny[2] = total
        else:
            small[0:6, :] = total[0:6, :]
    for k in range(NCH):
        forward(2, k)
        dmixed[ynb, chunk(k), :] = unproject(ynb, k * cr, cr)
    for k in range(NCH):
        ag_f[2, k].wait_recv()
        dmixed[dia, chunk(k), :] = unproject(dia, k * cr, cr)
    gout[...] = dot_tn(full[2].reshape(4 * rows_own, width), flat(mixed)).astype(BF16)
    line.hop(3)
    line.drain()
    for copy in started:
        copy.wait_send()


def sds(shape, dtype):
    return jax.ShapeDtypeStruct(shape, dtype)


def smem():
    return pl.BlockSpec(memory_space=pltpu.SMEM)


def on_device(
    tokens_in, qkv_weight, qv_bias, out_weight, geglu_weight, geglu_bias, down_weight,
    norm_gains, norm_biases, out_biases, doc_lengths, cotangent,
):
    seqs, rows, width = tokens_in.shape
    group = lax.axis_size("ctx")
    tp = lax.axis_size("tp")
    shards = lax.axis_size("shard")
    z = lax.axis_index("tp")
    c = lax.axis_index("ctx")
    assert group == 4 and tp == 4 and seqs == tp
    length = group * rows
    part_rows = qkv_weight.shape[1]
    cols = qkv_weight.shape[2]
    heads = cols // DH
    units = geglu_weight.shape[2]
    assert units == width and 4 * cols == width and H == heads * tp

    me = lax.axis_index("shard") * group + c
    dma = lambda *shape: pltpu.SemaphoreType.DMA(shape)
    slopes = jnp.asarray([alibi_slopes(H)], F32)
    head_shape = sds((heads, length, DH), BF16)
    lengths = lax.dynamic_slice_in_dim(doc_lengths, z, 1, 0)
    block = (rows, width)
    stack = (group, rows, width)
    if shards == 2 and part_rows % 16 == 0:
        vm = pltpu.VMEM
        wide = part_rows + 16
        pieces = lambda n: (vm((n, wide, width), BF16), vm((3, n, part_rows, width), BF16))
        scratch = dict(
            pq=vm((part_rows, 640), BF16), po=vm((wide, 256), BF16), pd=vm((part_rows, width), BF16),
            zbq=vm((tp, part_rows, 640), BF16), zbo=vm((tp, wide, 256), BF16),
            zbr=vm((2, tp, part_rows, width), BF16), zbd=vm((tp, 2, part_rows, width), BF16),
            load=dma(2), xd_s=dma(1), xd_r=dma(1),
            cot=vm(block, BF16), xs=vm(stack, BF16),
            wq=vm((2, group, part_rows, 640), BF16), wo=vm((2, group, wide, 256), BF16),
            g0=vm((2, group, wide, width), BF16), w=vm((3, 2, group, part_rows, width), BF16),
            w_out=vm((width, cols), BF16),
            qv=vm((2, cols), F32), vec=vm((8, width), F32), extra=vm((16, width), F32),
            probs=vm((heads, length, length), BF16),
            q=vm((heads, length, DH), BF16), k=vm((heads, length, DH), BF16),
            v=vm((heads, length, DH), BF16), far=vm((rows, length), F32),
            mixed=vm((length, cols), BF16), dmixed=vm((length, cols), BF16),
            full=vm((3,) + stack, BF16), act=vm(stack, BF16), pull=vm(stack, BF16),
            hid=vm(stack, BF16),
            **{n: vm(block, BF16) for n in ("snd_r", "snd_o", "snd_y", "rcv_r", "rcv_o", "rcv_y")},
            **{n: vm(block, F32) for n in ("own", "yacc", "fa", "fb", "normed", "zh1")},
            r1=vm((rows, 1), F32), acc=vm((6, 8, width), F32), bsum=vm((2, 8, width), F32),
            tiny=vm((4, 8, width), F32),
            dqkv=vm((length, 3 * cols), BF16),
            dk_acc=vm((heads, DH, length), F32), dv_acc=vm((heads, DH, length), F32),
            xg_s=dma(3), xg_r=dma(3),
            **{n: dma(5, 4) for n in ("zu", "zd", "zr", "ys", "yr", "xs_s", "xs_r")},
            **{n: dma(4, 4) for n in ("gx_s", "gx_r", "gy_s", "gy_r",
                                      "gu_s", "gu_r", "gd_s", "gd_r")},
            **{n: dma(3, NCH) for n in ("ags_y", "agr_y", "ags_c", "agr_c", "ags_f", "agr_f")},
            **{n: dma(4, NCH) for n in ("rss_r", "rsr_r", "rss_o", "rsr_o", "rss_y", "rsr_y")},
            tiny_s=dma(2), tiny_r=dma(2), lu=dma(2, tp), ld=dma(2, tp), lr=dma(2, tp),
        )
        for n, count in (("xb", group), ("yb", group), ("rb", tp + 1)):
            scratch[n + "0"], scratch[n + "r"] = pieces(count)
        raw = pl.pallas_call(
            functools.partial(layer, tuple(scratch), heads),
            out_shape=[
                sds((tp,) + block, BF16), sds((tp,) + block, BF16),
                sds((wide, width), F32), sds((3, part_rows, width), F32),
            ],
            in_specs=[smem(), smem()] + [pl.BlockSpec(memory_space=pl.ANY)] * 2 + vmem(9),
            out_specs=vmem(4),
            scratch_shapes=list(scratch.values()),
            compiler_params=pltpu.CompilerParams(
                collective_id=1, has_side_effects=True, vmem_limit_bytes=VMEM_MB * MB
            ),
            name="layer",
        )(
            lengths, slopes, tokens_in, cotangent, qkv_weight, out_weight, geglu_weight,
            down_weight, qv_bias, geglu_bias, norm_gains, norm_biases, out_biases,
        )
        return pl.pallas_call(
            finish,
            out_shape=[
                sds((tp,) + block, BF16), sds((tp,) + block, F32),
                sds(qkv_weight.shape, F32), sds(qv_bias.shape, F32), sds(out_weight.shape, F32),
                sds(geglu_weight.shape, F32), sds(geglu_bias.shape, F32),
                sds(down_weight.shape, F32),
            ] + [sds(norm_gains.shape, F32)] * 3,
            in_specs=vmem(4),
            out_specs=vmem(11),
            compiler_params=pltpu.CompilerParams(vmem_limit_bytes=40 * MB),
            name="finish",
        )(*raw)

    with jax.named_scope("pack_weights"):
        first = jnp.concatenate(
            [qkv_weight[0], qkv_weight[1], qkv_weight[2], out_weight.T], axis=1
        )
        own_norm = jnp.concatenate([norm_gains, norm_biases, out_biases], axis=0)
        parts = jnp.concatenate([first[None], geglu_weight, down_weight.T[None]], axis=0)
        own_bias = jnp.concatenate([qv_bias.reshape(1, -1), geglu_bias.reshape(1, -1)], axis=1)

    x_own = lax.dynamic_index_in_dim(tokens_in, z, 0, keepdims=False)
    cot_own = lax.dynamic_index_in_dim(cotangent, z, 0, keepdims=False)
    with jax.named_scope("gather_weights"):
        by_block = lax.all_gather(parts, "tp", axis=0)
        swapped = lax.all_to_all(by_block, "ctx", split_axis=0, concat_axis=0)
        w = lax.all_gather(swapped, "shard", axis=0)
        w = w.transpose(2, 0, 1, 3, 4).reshape(4, shards * group * part_rows, width)
        biases = lax.all_gather(own_bias, "tp", axis=0, tiled=True)
        biases = lax.dynamic_slice_in_dim(biases, c, 1, 0).astype(F32)
        norms = lax.all_gather(own_norm, ("shard", "ctx"), axis=1, tiled=True).astype(F32)
    qv = biases[:, : 2 * cols].reshape(2, cols)
    vec = jnp.concatenate([norms, biases[:, 2 * cols :].reshape(2, units)], axis=0)

    xs = lax.all_gather(x_own, "ctx", axis=0, tiled=True)

    mixed, probs, q, k, v = pl.pallas_call(
        functools.partial(attention_forward, heads),
        out_shape=[sds((length, cols), BF16), sds((heads, length, length), BF16)] + [head_shape] * 3,
        in_specs=[smem(), smem()] + vmem(3),
        out_specs=vmem(5),
        scratch_shapes=[pltpu.VMEM((256, length), F32)],
        compiler_params=pltpu.CompilerParams(vmem_limit_bytes=48 * MB),
        name="attention_forward",
    )(lengths, slopes, xs, w[0], qv)
    w0, w = w[0], w[1:]


    lout, dres1, grads, gout, dmixed, small = pl.pallas_call(
        middle,
        out_shape=[
            sds((tp,) + block, BF16), sds(block, F32), sds((3, width, width), BF16),
            sds((width, cols), BF16), sds((group, rows, cols), BF16), sds((8, width), F32),
        ],
        in_specs=vmem(6),
        out_specs=vmem(6),
        scratch_shapes=[
            pltpu.VMEM((width, cols), BF16), pltpu.VMEM((3,) + stack, BF16),
        ] + [pltpu.VMEM(stack, BF16)] * 5 + [pltpu.VMEM((3,) + block, BF16)] * 6 + [
            pltpu.VMEM(block, F32)
        ] * 6 + [
            pltpu.VMEM((rows, 1), F32), pltpu.VMEM(block, F32),
            pltpu.VMEM((6, 8, width), F32), pltpu.VMEM((2, 8, width), F32),
            pltpu.VMEM((4, 8, width), F32),
        ] + [dma(3, NCH)] * 12 + [dma(2)] * 2 + [dma(tp)] * 3,
        compiler_params=pltpu.CompilerParams(
            collective_id=0, has_side_effects=True, vmem_limit_bytes=58 * MB
        ),
        name="middle",
    )(x_own, cot_own, mixed.reshape(group, rows, cols), w0, w, vec)

    grad_w, d_in, bias_grad = pl.pallas_call(
        functools.partial(attention_backward, heads),
        out_shape=[
            sds((width, 3 * cols), BF16), sds((length, width), BF16), sds((1, 3 * cols), F32)
        ],
        in_specs=vmem(8),
        out_specs=vmem(3),
        scratch_shapes=[
            pltpu.VMEM((length, 3 * cols), BF16),
            pltpu.VMEM((heads, DH, length), F32), pltpu.VMEM((heads, DH, length), F32),
        ],
        compiler_params=pltpu.CompilerParams(vmem_limit_bytes=48 * MB),
        name="attention_backward",
    )(dmixed.reshape(length, cols), mixed, probs, q, k, v, xs, w0)

    with jax.named_scope("outputs"):
        input_sum = lax.psum_scatter(d_in, "ctx", scatter_dimension=0, tiled=True)
        input_own = (input_sum.astype(F32) + dres1).astype(BF16)
        input_grad = lax.all_gather(input_own, "tp", axis=0).astype(F32)
        layer_out = lout

    with jax.named_scope("scatter_grads"):
        first_grad = jnp.concatenate([grad_w, gout], axis=1)
        packed = jnp.concatenate([first_grad[None], grads], axis=0)
        packed = packed.reshape(4, shards, group, part_rows, width).transpose(1, 2, 0, 3, 4)
        mine = lax.psum_scatter(packed, "shard", scatter_dimension=0, tiled=False)
        mine = lax.all_to_all(mine, "ctx", split_axis=0, concat_axis=0)
        mine = lax.psum_scatter(mine, "tp", scatter_dimension=0, tiled=False)
        mine = mine.astype(F32)
        grad_qkv = jnp.stack([mine[0, :, i * cols : (i + 1) * cols] for i in range(3)])
        grad_out = mine[0, :, 3 * cols :].T
        grad_geglu = mine[1:3]
        grad_down = mine[3].T
        col = jnp.concatenate(
            [bias_grad[:, :cols], bias_grad[:, 2 * cols :], small[6:7], small[7:8]], axis=1
        )
        col = lax.psum_scatter(
            jnp.zeros((group, col.shape[1]), F32) + jnp.where(
                jnp.arange(group)[:, None] == c, col, 0.0),
            "tp", scatter_dimension=0, tiled=True)
        col = lax.psum(col, ("shard", "ctx"))
        norm_grad = lax.psum(small[:6], ("shard", "tp"))
        norm_grad = lax.dynamic_slice_in_dim(norm_grad, me * part_rows, part_rows, 1)
    return (
        layer_out,
        input_grad,
        grad_qkv,
        col[:, : 2 * cols].reshape(2, cols),
        grad_out,
        grad_geglu,
        col[:, 2 * cols :].reshape(2, units),
        grad_down,
        norm_grad[0:2],
        norm_grad[2:4],
        norm_grad[4:6],
    )


def solution(mesh):
    in_specs = (
        P("shard", "ctx", None),
        P(None, ("shard", "ctx"), "tp"),
        P(None, "tp"),
        P("tp", ("shard", "ctx")),
        P(None, ("shard", "ctx"), "tp"),
        P(None, "tp"),
        P("tp", ("shard", "ctx")),
        P(None, ("shard", "ctx")),
        P(None, ("shard", "ctx")),
        P(None, ("shard", "ctx")),
        P("shard", None),
        P("shard", "ctx", None),
    )
    out_specs = (
        P("shard", "ctx", None),
        P("shard", "ctx", None),
        P(None, ("shard", "ctx"), "tp"),
        P(None, "tp"),
        P("tp", ("shard", "ctx")),
        P(None, ("shard", "ctx"), "tp"),
        P(None, "tp"),
        P("tp", ("shard", "ctx")),
        P(None, ("shard", "ctx")),
        P(None, ("shard", "ctx")),
        P(None, ("shard", "ctx")),
    )
    return jax.shard_map(
        on_device, mesh=mesh, in_specs=in_specs, out_specs=out_specs, check_vma=False
    )
```

```python
import functools
import math
import types

import jax
import jax.numpy as jnp
from jax import lax
from jax.experimental import pallas as pl
from jax.experimental.pallas import tpu as pltpu
from jax.sharding import PartitionSpec as P

H = 12
DH = 64
F32 = jnp.float32
BF16 = jnp.bfloat16
MESH = pl.DeviceIdType.MESH
NCH = 4
TILE = 32
MB = 1 << 20
VMEM_MB = 62


def alibi_slopes(head_count):
    def power_slopes(head_total):
        first_slope = 2.0 ** (-8.0 / head_total)
        return [first_slope ** (counter + 1) for counter in range(head_total)]

    nearest = 2 ** int(math.floor(math.log2(head_count)))
    slope_list = power_slopes(nearest)
    return slope_list + power_slopes(2 * nearest)[0::2][: head_count - nearest]


def dot(left, right):
    return jnp.dot(left, right, preferred_element_type=F32)


def dot_nt(left, right):
    return lax.dot_general(left, right, (((1,), (1,)), ((), ())), preferred_element_type=F32)


def dot_tn(left, right):
    return lax.dot_general(left, right, (((0,), (0,)), ((), ())), preferred_element_type=F32)


def vmem(count):
    return [pl.BlockSpec(memory_space=pltpu.VMEM)] * count


def project_heads(heads, x_rows, rows, w, bias, q_out, k_out, v_out):
    cols = heads * DH
    for part, out in enumerate((q_out, k_out, v_out)):
        y = dot(x_rows, w[:, part * cols : (part + 1) * cols])
        if part != 1:
            y = y + bias[part // 2 : part // 2 + 1, :]
        y = y.astype(BF16)
        if part == 0:
            y = y * BF16(1.0 / math.sqrt(DH))
        for i in range(heads):
            out[i, rows, :] = y[:, i * DH : (i + 1) * DH]


def segments(lengths, pos):
    seg = jnp.zeros(pos.shape, jnp.int32)
    end = 0
    for k in range(lengths.shape[1]):
        end = end + lengths[0, k]
        seg = seg + (pos >= end).astype(jnp.int32)
    return seg


def attend_rows(heads, start, step, lengths, slopes, q, k, v, probs, mixed, far):
    length = k.shape[1]
    mine = lax.axis_index("ctx") * heads
    rows = pl.ds(start, step)
    key_pos = lax.broadcasted_iota(jnp.int32, (1, length), 1)
    pos = start + lax.broadcasted_iota(jnp.int32, (step, 1), 0)
    same = segments(lengths, pos) == segments(lengths, key_pos)
    far[...] = jnp.where(same, jnp.abs(pos - key_pos).astype(F32), 1e33)
    for i in range(heads):
        s = dot_nt(q[i, rows, :], k[i]) - slopes[0, mine + i] * far[...]
        p = jnp.exp(s - jnp.max(s, axis=-1, keepdims=True))
        p = (p * (1.0 / jnp.sum(p, axis=-1, keepdims=True))).astype(BF16)
        probs[i, rows, :] = p
        mixed[rows, i * DH : (i + 1) * DH] = dot(p, v[i]).astype(BF16)


def attention_forward(
    heads, lengths, slopes, xs, w, bias, mixed, probs, q_out, k_out, v_out, far
):
    step = 256

    def project(r, carry):
        rows = pl.ds(pl.multiple_of(r * step, step), step)
        project_heads(heads, xs[rows, :], rows, w, bias, q_out, k_out, v_out)
        return carry

    def attend(r, carry):
        start = pl.multiple_of(r * step, step)
        attend_rows(
            heads, start, step, lengths, slopes, q_out, k_out, v_out, probs, mixed, far)
        return carry

    lax.fori_loop(0, xs.shape[0] // step, project, 0)
    lax.fori_loop(0, xs.shape[0] // step, attend, 0)


def attend_back(heads, rows, dmixed, mixed, probs, q, k, v, dqkv, dk_acc, dv_acc):
    for i in range(heads):
        own = slice(i * DH, (i + 1) * DH)
        d_out = dmixed[rows, own]
        row_dot = jnp.sum(
            d_out.astype(F32) * mixed[rows, own].astype(F32), axis=-1, keepdims=True
        )
        p = probs[i, rows, :]
        dp = dot_nt(d_out, v[i])
        ds = (p.astype(F32) * (dp - row_dot)).astype(BF16)
        dqkv[rows, own] = (dot(ds, k[i]) * (1.0 / math.sqrt(DH))).astype(BF16)
        dk_acc[i] += dot_tn(q[i, rows, :], ds)
        dv_acc[i] += dot_tn(d_out, p)


def spread_heads(heads, dqkv, dk_acc, dv_acc):
    cols = heads * DH
    for i in range(heads):
        dqkv[:, cols + i * DH : cols + (i + 1) * DH] = dk_acc[i].T.astype(BF16)
        dqkv[:, 2 * cols + i * DH : 2 * cols + (i + 1) * DH] = dv_acc[i].T.astype(BF16)


def attention_backward(
    heads, dmixed, mixed, probs, q, k, v, xs, w, grad_w, d_in, bias_grad, dqkv, dk_acc, dv_acc
):
    length = xs.shape[0]
    step = 256
    cols = heads * DH
    dk_acc[...] = jnp.zeros_like(dk_acc)
    dv_acc[...] = jnp.zeros_like(dv_acc)

    def rows_back(r, carry):
        rows = pl.ds(pl.multiple_of(r * step, step), step)
        attend_back(heads, rows, dmixed, mixed, probs, q, k, v, dqkv, dk_acc, dv_acc)
        return carry

    lax.fori_loop(0, length // step, rows_back, 0)
    spread_heads(heads, dqkv, dk_acc, dv_acc)

    def finish(r, total):
        rows = pl.ds(pl.multiple_of(r * step, step), step)
        d = dqkv[rows, :]
        d_in[rows, :] = dot_nt(d, w[:, : 3 * cols]).astype(BF16)
        return total + jnp.sum(d.astype(F32), axis=0, keepdims=True)

    bias_grad[...] = lax.fori_loop(
        0, length // step, finish, jnp.zeros((1, 3 * cols), F32)
    )
    for part in range(3):
        own = slice(part * cols, (part + 1) * cols)
        grad_w[:, own] = dot_tn(xs[...], dqkv[:, own]).astype(BF16)


class Links:
    def __init__(self):
        self.started = []

    def copy(self, src, dst, send, recv, peer):
        return pltpu.make_async_remote_copy(
            src_ref=src, dst_ref=dst, send_sem=send, recv_sem=recv,
            device_id=peer, device_id_type=MESH,
        )

    def start(self, src, dst, send, recv, peer):
        copy = self.copy(src, dst, send, recv, peer)
        copy.start()
        self.started.append(copy)
        return copy

    def sent(self, copy):
        if any(copy is one for one in self.started):
            copy.wait_send()
            self.started = [one for one in self.started if one is not copy]

    def drain(self):
        for copy in self.started:
            copy.wait_send()
        self.started = []


def greet(peers):
    barrier = pltpu.get_barrier_semaphore()
    for peer in peers:
        pl.semaphore_signal(barrier, inc=1, device_id=peer, device_id_type=MESH)
    pl.semaphore_wait(barrier, len(peers))


def places():
    c = lax.axis_index("ctx")
    flip = 1 - 2 * (c % 2)
    ynb = (c + 2) % 4
    return c, c + flip, ynb, ynb + flip


class LineGather:
    def __init__(self, blocks, sems, recv):
        self.blocks, self.sems, self.recv = blocks, sems, recv
        self.z = lax.axis_index("tp")
        self.last = blocks.shape[0] - 1

    def _copy(self, j, which, peer):
        block = self.blocks.at[j]
        return pltpu.make_async_remote_copy(
            src_ref=block, dst_ref=block, send_sem=self.sems.at[which], recv_sem=self.recv.at[j],
            device_id={"tp": peer}, device_id_type=MESH,
        )

    def _sends(self, act):
        z = self.z
        for which, step in enumerate((1, -1, 2, -2)):
            @pl.when(jnp.logical_and(z + step >= 0, z + step <= self.last))
            def _(which=which, step=step):
                act(self._copy(z, which, z + step))

    def _passed(self, act):
        z, last = self.z, self.last

        @pl.when(z == 2)
        def _():
            act(self._copy(0, 4, last))

        @pl.when(z == 1)
        def _():
            act(self._copy(last, 4, 0))

    def hop(self, d):
        z = self.z
        if d == 0:
            self._sends(lambda copy: copy.start())
            return
        for j in (z - d, z + d):
            @pl.when(jnp.logical_and(j >= 0, j <= self.last))
            def _(j=j):
                self._copy(j, 0, z).wait_recv()
        if d == 2:
            self._passed(lambda copy: copy.start())

    def drain(self):
        self._sends(lambda copy: copy.wait_send())
        self._passed(lambda copy: copy.wait_send())


class LineRelay:
    def __init__(self, blocks, up, down, recv):
        self.blocks, self.up, self.down, self.recv = blocks, up, down, recv
        self.z = lax.axis_index("tp")
        self.last = blocks.shape[0] - 1

    def _copy(self, j, sem, peer):
        block = self.blocks.at[j]
        return pltpu.make_async_remote_copy(
            src_ref=block, dst_ref=block, send_sem=sem.at[j], recv_sem=self.recv.at[j],
            device_id={"tp": peer}, device_id_type=MESH,
        )

    def hop(self, d):
        z, last = self.z, self.last
        for side, j in ((0, z - d), (1, z + d)):
            here = (j >= 0) if side == 0 else (j <= last)
            edge = (z < last) if side == 0 else (z > 0)

            @pl.when(here)
            def _(side=side, j=j, edge=edge):
                sem = self.up if side == 0 else self.down
                if d:
                    self._copy(j, sem, z).wait_recv()
                if d < last:
                    @pl.when(edge)
                    def _():
                        self._copy(j, sem, z + 1 if side == 0 else z - 1).start()

    def drain(self):
        z, last = self.z, self.last
        for d in range(last):
            for side, j in ((0, z - d), (1, z + d)):
                here = (j >= 0) if side == 0 else (j <= last)
                edge = (z < last) if side == 0 else (z > 0)

                @pl.when(jnp.logical_and(here, edge))
                def _(side=side, j=j):
                    self._copy(j, self.up if side == 0 else self.down, z).wait_send()


def layer(
    names, heads, lengths, slopes,
    tokens, cotangent, qkv_w, out_w, geglu_w, down_w, qv_b, geglu_b, gains, shifts, out_b,
    lout, input_grad, out0, outr, *scratch,
):
    r = types.SimpleNamespace(**dict(zip(names, scratch)))
    c, sib, ynb, dia = places()
    me = lax.axis_index("shard")
    z = lax.axis_index("tp")
    other = 1 - me
    tp, rows_own, width = lout.shape
    piece = outr.shape[1]
    cols = heads * DH
    length = 4 * rows_own
    cr = rows_own // NCH
    links = Links()
    start, copy = links.start, links.copy

    def block(body):
        pl.when(z >= 0)(body)

    load_x = pltpu.make_async_copy(tokens.at[z], r.xs.at[c], r.load.at[0])
    load_x.start()
    load_c = pltpu.make_async_copy(cotangent.at[z], r.cot, r.load.at[1])
    load_c.start()
    for i in range(3):
        r.pq[:, i * cols : (i + 1) * cols] = qkv_w[i]
    r.pq[:, 3 * cols :] = jnp.zeros((piece, r.pq.shape[1] - 3 * cols), BF16)
    for i in range(2):
        for h in range(heads):
            r.pq[i * heads + h : i * heads + h + 1, 3 * cols : 3 * cols + DH] = (
                qv_b[i : i + 1, h * DH : (h + 1) * DH])
    r.po[...] = jnp.zeros_like(r.po)
    r.po[0:piece, 0:cols] = out_w[...].T
    span = r.po.shape[1]
    thirds = width // span
    for i in range(2):
        for t in range(thirds):
            row = piece + i * thirds + t
            r.po[row : row + 1, :] = geglu_b[i : i + 1, t * span : (t + 1) * span]
    row = piece + 2 * thirds
    for i, ref in enumerate((gains, shifts, out_b)):
        r.po[row + 2 * i : row + 2 * i + 2, 0:piece] = ref[...]

    greet([{"ctx": sib}, {"ctx": ynb}, {"ctx": dia}, {"shard": other}]
          + [{"tp": (z + d) % tp} for d in range(1, tp)])

    src = {"q": r.pq, "o": r.po, 0: geglu_w.at[0], 1: geglu_w.at[1], 2: down_w}
    zb = {"q": r.zbq, "o": r.zbo, 0: r.zbr.at[0], 1: r.zbr.at[1], 2: r.zbr.at[2]}
    wr = {"q": r.wq, "o": r.wo, 0: r.w.at[0], 1: r.w.at[1], 2: r.w.at[2]}
    index = {"q": 0, "o": 1, 0: 2, 1: 3, 2: 4}
    last = tp - 1

    def line_copy(p, j, sems, peer):
        block = zb[p].at[j]
        return copy(block, block, sems.at[index[p], j], r.zr.at[index[p], j], {"tp": peer})

    def owner_slot(p, j):
        return wr[p].at[me, j]

    def hop(p, d):
        def deliver(j):
            @pl.when(j == c)
            def _():
                owner_slot(p, c)[...] = zb[p].at[j][...]

            @pl.when(j != c)
            def _():
                copy(zb[p].at[j], owner_slot(p, c), r.ys.at[index[p], j], r.yr.at[index[p], c],
                     {"ctx": j}).start()

        if d == 0:
            zb[p].at[z][...] = src[p][...]

            for step in (1, 2):
                sems = r.zu if step == 1 else r.zu2

                @pl.when(z + step <= last)
                def _(step=step, sems=sems):
                    line_copy(p, z, sems, z + step).start()

                sems = r.zd if step == 1 else r.zd2

                @pl.when(z - step >= 0)
                def _(step=step, sems=sems):
                    line_copy(p, z, sems, z - step).start()

            deliver(z)
            return
        for side in range(2):
            j = z - d if side == 0 else z + d

            @pl.when((j >= 0) if side == 0 else (j <= last))
            def _(side=side, j=j):
                line_copy(p, j, r.zu, z).wait_recv()
                if d == 2:
                    @pl.when((z == 2) if side == 0 else (z == 1))
                    def _():
                        if side == 0:
                            line_copy(p, j, r.zu, z + 1).start()
                        else:
                            line_copy(p, j, r.zd, z - 1).start()
                deliver(j)

    def hop_drain(p):
        for step in (1, 2):
            @pl.when(z + step <= last)
            def _(step=step):
                line_copy(p, z, r.zu if step == 1 else r.zu2, z).wait_send()

            @pl.when(z - step >= 0)
            def _(step=step):
                line_copy(p, z, r.zd if step == 1 else r.zd2, z).wait_send()

        @pl.when(z == 2)
        def _():
            line_copy(p, 0, r.zu, z).wait_send()

        @pl.when(z == 1)
        def _():
            line_copy(p, last, r.zd, z).wait_send()

        for j in (sib, ynb, dia):
            copy(zb[p].at[j], owner_slot(p, c), r.ys.at[index[p], j], r.yr.at[index[p], c],
                 {"ctx": j}).wait_send()

    def owned(p, j):
        copy(zb[p].at[c], owner_slot(p, j), r.ys.at[index[p], c], r.yr.at[index[p], j],
             {"ctx": c}).wait_recv()

    def shard_copy(p, i, j):
        slot = wr[p].at[me, j]
        return copy(slot, slot, r.xs_s.at[index[p], i], r.xs_r.at[index[p], j], {"shard": other})

    def to_shard(p):
        for i, j in enumerate((c, sib, ynb, dia)):
            if i:
                owned(p, j)
            shard_copy(p, i, j).start()

    far_off = jnp.abs(z - c)

    def to_shard_if(p, low, high):
        @pl.when(jnp.logical_and(far_off >= low, far_off <= high))
        def _():
            to_shard(p)

    def shard_drain(p):
        for i in range(4):
            shard_copy(p, i, c).wait_send()

    def complete(p):
        for j in range(4):
            slot = wr[p].at[other, j]
            copy(slot, slot, r.xs_s.at[index[p], 0], r.xs_r.at[index[p], j],
                 {"shard": other}).wait_recv()

    grad = [r.g0] + [r.w.at[i] for i in range(2)]
    xb = [r.xb0] + [r.xbr.at[i] for i in range(2)]
    yb = [r.yb0] + [r.ybr.at[i] for i in range(2)]
    rb = [r.rb0] + [r.rbr.at[i] for i in range(2)]
    out = [out0] + [outr.at[i] for i in range(2)]

    def grad_to_shard(p):
        for i, j in enumerate((dia, ynb, sib, c)):
            start(grad[p].at[other, j], xb[p].at[j], r.gx_s.at[p, i], r.gx_r.at[p, j], {"shard": other})

    def grad_to_owner(p):
        for i, j in enumerate((dia, ynb, sib, c)):
            copy(grad[p].at[other, j], xb[p].at[j], r.gx_s.at[p, 0], r.gx_r.at[p, j],
                 {"shard": other}).wait_recv()
            total = (grad[p].at[me, j][...].astype(F32) + xb[p].at[j][...].astype(F32)).astype(BF16)
            if i == 3:
                yb[p].at[c][...] = total
            else:
                xb[p].at[j][...] = total
                start(xb[p].at[j], yb[p].at[c], r.gy_s.at[p, i], r.gy_r.at[p, c], {"ctx": j})

    def climb(p, side, j):
        if side == 0:
            return copy(yb[p].at[j], rb[p].at[j], r.gu_s.at[p, j], r.gu_r.at[p, j], {"tp": z + 1})
        slot = jnp.where(j == z - 1, tp, j)
        return copy(yb[p].at[j], rb[p].at[slot], r.gd_s.at[p, j], r.gd_r.at[p, j], {"tp": z - 1})

    def grad_hop(p, h):
        if h == 0:
            for j in (sib, ynb, dia):
                copy(xb[p].at[j], yb[p].at[j], r.gy_s.at[p, 0], r.gy_r.at[p, j], {"ctx": j}).wait_recv()
        if h == last:
            out[p][...] = yb[p].at[z][...].astype(F32)

            @pl.when(z > 0)
            def _():
                copy(yb[p].at[z], rb[p].at[z], r.gu_s.at[p, z], r.gu_r.at[p, z], {"tp": z}).wait_recv()
                out[p][...] += rb[p].at[z][...].astype(F32)

            @pl.when(z < last)
            def _():
                copy(yb[p].at[z], rb[p].at[tp], r.gd_s.at[p, z], r.gd_r.at[p, z], {"tp": z}).wait_recv()
                out[p][...] += rb[p].at[tp][...].astype(F32)
            return
        for side in range(2):
            j = z + (last - h) if side == 0 else z - (last - h)

            @pl.when((j <= last) if side == 0 else (j >= 0))
            def _(side=side, j=j):
                @pl.when((z > 0) if side == 0 else (z < last))
                def _():
                    sems = r.gu_r if side == 0 else r.gd_r
                    copy(yb[p].at[j], rb[p].at[j], r.gu_s.at[p, j], sems.at[p, j], {"tp": z}).wait_recv()
                    yb[p].at[j][...] = (
                        yb[p].at[j][...].astype(F32) + rb[p].at[j][...].astype(F32)).astype(BF16)
                climb(p, side, j).start()

    stage = jnp.where(z < c, z, last - z)

    def chain_piece(ref, i):
        return ref.at[i // 2, pl.ds(2 * (i % 2), 2)]

    def chain_copy(i, side):
        return copy(chain_piece(r.w.at[2], i), chain_piece(r.cb.at[side], i),
                    r.ch_s.at[side, i], r.ch_r.at[side, i], {"tp": z + 1 if side == 0 else z - 1})

    def chain_wait(i, side):
        copy(chain_piece(r.w.at[2], i), chain_piece(r.cb.at[side], i),
             r.ch_s.at[side, i], r.ch_r.at[side, i], {"tp": z}).wait_recv()
        mine = chain_piece(r.w.at[2], i)
        mine[...] = (mine[...].astype(F32) + chain_piece(r.cb.at[side], i)[...].astype(F32)).astype(BF16)

    def chain(slot):
        for i in range(4):
            for side in range(2):
                here = (z < c) if side == 0 else (z > c)
                if slot == 0:
                    @pl.when(jnp.logical_and(here, stage == 0))
                    def _(i=i, side=side):
                        chain_copy(i, side).start()
                else:
                    @pl.when(jnp.logical_and(here, jnp.logical_and(stage > 0, stage == slot - i)))
                    def _(i=i, side=side):
                        chain_wait(i, side)
                        chain_copy(i, side).start()

    def chain_send(j):
        return copy(r.w.at[2, :, j], r.yd, r.cy_s.at[j], r.cy_r.at[0], {"ctx": j})

    def chain_end():
        @pl.when(z == c)
        def _():
            for i in range(4):
                @pl.when(z > 0)
                def _(i=i):
                    chain_wait(i, 0)

                @pl.when(z < last)
                def _(i=i):
                    chain_wait(i, 1)
            r.yd[...] = r.w[2, :, c]
            for j in (dia, ynb, sib):
                chain_send(j).start()

    def chain_across():
        @pl.when(z != c)
        def _():
            chain_send(c).wait_recv()
        start(r.yd.at[other], r.xd, r.cx_s.at[0], r.cx_r.at[0], {"shard": other})

    def chain_total():
        copy(r.yd.at[other], r.xd, r.cx_s.at[0], r.cx_r.at[0], {"shard": other}).wait_recv()
        outr[2] = r.yd[me].astype(F32) + r.xd[...].astype(F32)

    def chain_drain():
        for i in range(4):
            for side in range(2):
                @pl.when((z < c) if side == 0 else (z > c))
                def _(i=i, side=side):
                    chain_copy(i, side).wait_send()

        @pl.when(z == c)
        def _():
            for j in (dia, ynb, sib):
                chain_send(j).wait_send()

    def grad_drain(p):
        for h in range(last):
            for side in range(2):
                j = z + (last - h) if side == 0 else z - (last - h)

                @pl.when((j <= last) if side == 0 else (j >= 0))
                def _(side=side, j=j):
                    climb(p, side, j).wait_send()

    def chunk(k):
        return pl.ds(k * cr, cr)

    ag_y, ag_c, ag_f, rs_r, rs_o, rs_y = ({} for _ in range(6))

    def gather_start(o, k):
        block = r.full.at[o, c, chunk(k)]
        ag_y[o, k] = start(block, block, r.ags_y.at[o, k], r.agr_y.at[o, k], {"ctx": ynb})
        ag_c[o, k] = start(block, block, r.ags_c.at[o, k], r.agr_c.at[o, k], {"ctx": sib})

    def forward(o, k):
        ag_y[o, k].wait_recv()
        block = r.full.at[o, ynb, chunk(k)]
        ag_f[o, k] = start(block, block, r.ags_f.at[o, k], r.agr_f.at[o, k], {"ctx": sib})

    def free(table, o, k):
        if o:
            links.sent(table[o - 1, k])

    def send_relay(o, k):
        rs_r[o, k] = start(r.snd_r.at[chunk(k)], r.rcv_r.at[chunk(k)],
                           r.rss_r.at[o, k], r.rsr_r.at[o, k], {"ctx": sib})

    def send_own(o, k):
        rs_o[o, k] = start(r.snd_o.at[chunk(k)], r.rcv_o.at[chunk(k)],
                           r.rss_o.at[o, k], r.rsr_o.at[o, k], {"ctx": sib})

    def relay(o, k):
        rs_r[o, k].wait_recv()
        free(rs_y, o, k)
        r.snd_y[chunk(k), :] = (
            r.yacc[chunk(k), :] + r.rcv_r[chunk(k), :].astype(F32)).astype(BF16)
        rs_y[o, k] = start(r.snd_y.at[chunk(k)], r.rcv_y.at[chunk(k)],
                           r.rss_y.at[o, k], r.rsr_y.at[o, k], {"ctx": ynb})

    def arrived(o, k):
        rs_o[o, k].wait_recv()
        rs_y[o, k].wait_recv()

    def summed(rows):
        return r.own[rows, :] + r.rcv_o[rows, :].astype(F32) + r.rcv_y[rows, :].astype(F32)

    def tiles(first, count, body):
        def step(t, carry):
            body(pl.ds(pl.multiple_of(first + t * TILE, TILE), TILE))
            return carry
        lax.fori_loop(0, count // TILE, step, 0)

    def fold(values):
        return jnp.sum(values.reshape(TILE // 8, 8, width), axis=0)

    def rows_of(b, r0=0, n=rows_own):
        return pl.ds(pl.multiple_of(b * rows_own + r0, cr), n)

    def both(parts):
        return jnp.concatenate(parts, axis=0)

    def far_blocks(o, k, product):
        free(rs_r, o, k)

        @block
        def _():
            value = product()
            r.snd_r[chunk(k), :] = value[:cr].astype(BF16)
            r.yacc[chunk(k), :] = value[cr:]
        send_relay(o, k)
        if k:
            relay(o, k - 1)

    def near_blocks(o, sib_product, own_product):
        for k in range(NCH):
            free(rs_o, o, k)

        @block
        def _():
            r.snd_o[...] = sib_product().astype(BF16)
        for k in range(NCH):
            send_own(o, k)

        @block
        def _():
            r.own[...] = own_product()

    def send_sums(o, rows_at, product):
        for k in range(NCH):
            far_blocks(o, k, lambda k=k: product(
                both([rows_at(dia, k * cr, cr), rows_at(ynb, k * cr, cr)])))
        relay(o, NCH - 1)
        near_blocks(o, lambda: product(rows_at(sib, 0, rows_own)),
                    lambda: product(rows_at(c, 0, rows_own)))

    load_x.wait()
    hop("q", 0)
    r.acc[...] = jnp.zeros_like(r.acc)
    r.bsum[...] = jnp.zeros_like(r.bsum)
    r.dk_acc[...] = jnp.zeros_like(r.dk_acc)
    r.dv_acc[...] = jnp.zeros_like(r.dv_acc)
    hop("q", 1)
    first = start(r.xs.at[c], r.xs.at[c], r.xg_s.at[0], r.xg_r.at[0], {"ctx": ynb})
    near = start(r.xs.at[c], r.xs.at[c], r.xg_s.at[1], r.xg_r.at[1], {"ctx": sib})
    to_shard_if("q", 0, 0)
    hop("q", 2)
    hop("o", 0)
    hop(0, 0)
    to_shard_if("q", 1, 1)
    hop("q", 3)
    to_shard_if("q", 2, 2)
    hop("o", 1)
    to_shard_if("q", 3, 3)
    hop("o", 2)
    hop(0, 1)
    hop("o", 3)
    first.wait_recv()
    passed = start(r.xs.at[ynb], r.xs.at[ynb], r.xg_s.at[2], r.xg_r.at[2], {"ctx": sib})
    to_shard("o")
    hop(0, 2)
    hop(1, 0)
    to_shard_if(0, 0, 1)
    near.wait_recv()
    passed.wait_recv()
    complete("q")
    wq = r.wq[...].reshape(width, r.wq.shape[3])
    for i in range(2):
        for h in range(heads):
            r.qv[i : i + 1, h * DH : (h + 1) * DH] = (
                r.wq[0, 0, i * heads + h : i * heads + h + 1, 3 * cols : 3 * cols + DH].astype(F32))

    def project(t, carry):
        rows = pl.ds(pl.multiple_of(t * rows_own, rows_own), rows_own)
        project_heads(heads, r.xs[t], rows, r.wq[...].reshape(width, r.wq.shape[3]), r.qv, r.q, r.k, r.v)
        return carry

    lax.fori_loop(0, 4, project, 0)
    hop(0, 3)
    to_shard_if(0, 2, 2)

    def attend(b):
        @block
        def _():
            attend_rows(heads, pl.multiple_of(b * rows_own, rows_own), rows_own, lengths, slopes,
                        r.q, r.k, r.v, r.probs, r.mixed, r.far)

    def out_project(b, r0, n):
        return dot_nt(r.mixed[rows_of(b, r0, n), :], r.w_out[...])

    attend(dia)
    complete("o")
    for s in range(2):
        for j in range(4):
            place_ = s * 4 + j
            r.w_out[pl.ds(place_ * piece, piece), :] = r.wo[s, j, 0:piece, 0:cols]
            row = piece + 2 * thirds
            r.vec[0:6, place_ * piece : (place_ + 1) * piece] = r.wo[s, j, row : row + 6, 0:piece].astype(F32)
    for i in range(2):
        for t in range(thirds):
            row = piece + i * thirds + t
            r.vec[6 + i : 7 + i, t * span : (t + 1) * span] = r.wo[0, 0, row : row + 1, :].astype(F32)

    @block
    def _():
        r.snd_r[...] = out_project(dia, 0, rows_own).astype(BF16)
    for k in range(NCH):
        send_relay(0, k)
    to_shard_if(0, 3, 3)
    hop(1, 1)
    attend(ynb)

    @block
    def _():
        r.yacc[...] = out_project(ynb, 0, rows_own)
    for k in range(NCH):
        relay(0, k)
    hop(1, 2)
    hop(2, 0)
    to_shard_if(1, 0, 1)
    attend(sib)

    @block
    def _():
        r.snd_o[...] = out_project(sib, 0, rows_own).astype(BF16)
    for k in range(NCH):
        send_own(0, k)
    attend(c)

    @block
    def _():
        r.own[...] = out_project(c, 0, rows_own)
    hop(1, 3)
    to_shard_if(1, 2, 3)

    def norm_one(rows):
        res = r.xs[c, rows, :].astype(F32) + summed(rows) + r.vec[4:5, :]
        center = res - jnp.mean(res, axis=-1, keepdims=True)
        scale = lax.rsqrt(jnp.mean(center * center, axis=-1, keepdims=True) + 1e-12)
        zh = center * scale
        value = zh * r.vec[0:1, :] + r.vec[2:3, :]
        r.zh1[rows, :] = zh
        r.r1[rows, :] = scale
        r.normed[rows, :] = value
        r.full[0, c, rows, :] = value.astype(BF16)

    for k in range(NCH):
        arrived(0, k)
        tiles(k * cr, cr, norm_one)
        gather_start(0, k)

    def matrix(i):
        return r.w[i].reshape(width, width)

    def units_forward(b, r0, n):
        rows_in = r.full[0, b, pl.ds(r0, n), :]
        r.fa[pl.ds(0, n), :] = dot(rows_in, matrix(0))
        r.fb[pl.ds(0, n), :] = dot(rows_in, matrix(1))

        def units(rows):
            g = r.fa[rows, :] + r.vec[6:7, :]
            u = r.fb[rows, :] + r.vec[7:8, :]
            phi = 0.5 * (1.0 + lax.erf(g * (1.0 / math.sqrt(2.0))))
            gelu = g * phi
            slope = phi + g * jnp.exp(-0.5 * g * g) * (1.0 / math.sqrt(2.0 * math.pi))
            to = pl.ds(pl.multiple_of(r0 + rows.start, TILE), TILE)
            r.act[b, to, :] = gelu.astype(BF16)
            r.pull[b, to, :] = (u * slope).astype(BF16)
            r.hid[b, to, :] = (gelu * u).astype(BF16)

        tiles(0, n, units)

    def hid_rows(b, r0, n):
        return r.hid[b, pl.ds(r0, n), :]

    def down(rows):
        return dot_nt(rows, matrix(2))

    def units_backward(blocks, r0, n):
        def rows_at(ref, b):
            return ref[b, pl.ds(r0, n), :]

        def gather(ref):
            return both([rows_at(ref, b) for b in blocks]) if len(blocks) > 1 else rows_at(ref, blocks[0])

        r.fa[pl.ds(0, n * len(blocks)), :] = dot(gather(r.full.at[1]), matrix(2))
        for i, b in enumerate(blocks):
            def units(rows, b=b, i=i):
                dh = r.fa[rows, :]
                to = pl.ds(pl.multiple_of(r0 - i * n + rows.start, TILE), TILE)
                dg = (dh * r.pull[b, to, :].astype(F32)).astype(BF16)
                du = (dh * r.act[b, to, :].astype(F32)).astype(BF16)
                r.pull[b, to, :] = dg
                r.act[b, to, :] = du
                r.bsum[0] += fold(dg.astype(F32))
                r.bsum[1] += fold(du.astype(F32))

            tiles(i * n, n, units)
        return dot_nt(gather(r.pull), matrix(0)) + dot_nt(gather(r.act), matrix(1))

    hop(2, 1)
    to_shard_if(2, 0, 0)
    complete(0)
    complete(1)
    units_forward(c, 0, rows_own)
    for k in range(NCH):
        ag_c[0, k].wait_recv()
    hop(2, 2)
    to_shard_if(2, 1, 2)
    units_forward(sib, 0, rows_own)
    for k in range(NCH):
        forward(0, k)
    hop(2, 3)
    to_shard_if(2, 3, 3)
    units_forward(ynb, 0, rows_own)
    for k in range(NCH):
        ag_f[0, k].wait_recv()
    units_forward(dia, 0, rows_own)
    complete(2)
    send_sums(1, hid_rows, down)

    def norm_two(rows):
        res = r.normed[rows, :] + (summed(rows) + r.vec[5:6, :])
        center = res - jnp.mean(res, axis=-1, keepdims=True)
        scale = lax.rsqrt(jnp.mean(center * center, axis=-1, keepdims=True) + 1e-12)
        zh = center * scale
        r.lout[z, rows, :] = (zh * r.vec[1:2, :] + r.vec[3:4, :]).astype(BF16)
        up = r.cot[rows, :].astype(F32)
        t = up * r.vec[1:2, :]
        d = scale * (t - jnp.mean(t, axis=-1, keepdims=True)
                     - zh * jnp.mean(t * zh, axis=-1, keepdims=True))
        r.normed[rows, :] = d
        low = d.astype(BF16)
        r.full[1, c, rows, :] = low
        r.acc[1] += fold(up * zh)
        r.acc[3] += fold(up)
        r.acc[5] += fold(low.astype(F32))

    load_c.wait()
    for k in range(NCH):
        arrived(1, k)
        tiles(k * cr, cr, norm_two)
        gather_start(1, k)
    line_out = LineGather(r.lout, r.ls.at[0], r.lr.at[0])
    line_out.hop(0)

    def flat(ref):
        return ref[...].reshape(length, ref.shape[-1])

    def put(i, left, right):
        @block
        def _():
            r.w[i] = dot_tn(flat(left), flat(right)).astype(BF16).reshape(r.w.shape[1:])

    def put_down():
        for p in range(3):
            shard_drain(p)
        put(2, r.full.at[1], r.hid)
        chain(0)

    @block
    def _():
        r.own[...] = units_backward([c], 0, rows_own)
    for k in range(NCH):
        ag_c[1, k].wait_recv()
        free(rs_o, 2, k)
    for k in range(NCH // 2):
        forward(1, k)

    @block
    def _():
        r.snd_o[...] = units_backward([sib], 0, rows_own).astype(BF16)
    for k in range(NCH):
        send_own(2, k)
    for k in range(NCH // 2, NCH):
        forward(1, k)
    for k in range(NCH):
        ag_f[1, k].wait_recv()
        far_blocks(2, k, lambda k=k: units_backward([dia, ynb], k * cr, cr))
    relay(2, NCH - 1)
    put_down()

    put(0, r.full.at[0], r.pull)
    grad_to_shard(1)

    def norm_back(rows):
        dn = summed(rows) + r.normed[rows, :]
        zh = r.zh1[rows, :]
        t = dn * r.vec[0:1, :]
        d = r.r1[rows, :] * (t - jnp.mean(t, axis=-1, keepdims=True)
                             - zh * jnp.mean(t * zh, axis=-1, keepdims=True))
        r.zh1[rows, :] = d
        low = d.astype(BF16)
        r.full[2, c, rows, :] = low
        r.acc[0] += fold(dn * zh)
        r.acc[2] += fold(dn)
        r.acc[4] += fold(low.astype(F32))

    for k in range(NCH):
        arrived(2, k)
        tiles(k * cr, cr, norm_back)
        gather_start(2, k)
    put(1, r.full.at[0], r.act)
    grad_to_shard(2)

    def unproject(b, r0, n):
        r.dmixed[rows_of(b, r0, n), :] = dot(r.full[2, b, pl.ds(r0, n), :], r.w_out[...]).astype(BF16)

    def back_rows(b):
        @block
        def _():
            unproject(b, 0, rows_own)
            attend_back(heads, rows_of(b), r.dmixed, r.mixed, r.probs, r.q, r.k, r.v,
                        r.dqkv, r.dk_acc, r.dv_acc)

    for i in range(6):
        r.tiny[0, i : i + 1, :] = jnp.sum(r.acc[i], axis=0, keepdims=True)
    tiny_sib = start(r.tiny.at[0], r.tiny.at[1], r.tiny_s.at[0], r.tiny_r.at[0], {"ctx": sib})
    back_rows(c)
    for k in range(NCH):
        ag_c[2, k].wait_recv()
    back_rows(sib)
    chain(1)
    tiny_sib.wait_recv()
    r.tiny[2] = r.tiny[0] + r.tiny[1]
    tiny_y = start(r.tiny.at[2], r.tiny.at[3], r.tiny_s.at[1], r.tiny_r.at[1], {"ctx": ynb})
    for k in range(NCH):
        forward(2, k)
    back_rows(ynb)
    for k in range(NCH):
        ag_f[2, k].wait_recv()
    back_rows(dia)
    chain(2)
    grad_to_owner(1)
    @block
    def _():
        spread_heads(heads, r.dqkv, r.dk_acc, r.dv_acc)

    def dqkv_rows(b, r0, n):
        return r.dqkv[rows_of(b, r0, n), :]

    def into_input(rows):
        return dot_nt(rows, r.wq[...].reshape(width, r.wq.shape[3])[:, : 3 * cols])

    send_sums(3, dqkv_rows, into_input)

    chain(3)
    line_out.hop(2)
    grad_hop(1, 0)
    tiny_y.wait_recv()
    norms = r.tiny[2] + r.tiny[3]
    bias = jnp.sum(r.dqkv[...].astype(F32), axis=0, keepdims=True)
    r.extra[...] = jnp.zeros_like(r.extra)
    r.extra[0:1, 0:cols] = bias[:, :cols]
    r.extra[0:1, cols : 2 * cols] = bias[:, 2 * cols :]
    for i in range(2):
        r.extra[1 + i : 2 + i, :] = jnp.sum(r.bsum[i], axis=0, keepdims=True)
    r.extra[3:9, :] = norms[0:6, :]
    low = r.extra[...].astype(BF16)
    x_all = flat(r.xs)
    for i in range(4):
        lanes = slice(i * cols, (i + 1) * cols)
        if i < 3:
            value = dot_tn(x_all, r.dqkv[:, lanes])
        else:
            value = dot_tn(flat(r.full.at[2]), r.mixed[...])
        value = value.astype(BF16)
        for s in range(2):
            for j in range(4):
                first_row = (s * 4 + j) * piece
                r.g0[s, j, 0:piece, lanes] = value[first_row : first_row + piece]
    for s in range(2):
        for j in range(4):
            r.g0[s, j, piece:, :] = low
    grad_to_shard(0)
    chain(4)
    grad_to_owner(2)
    grad_hop(1, 1)
    line_in = LineRelay(r.input_grad, r.lu, r.ld, r.lr.at[1])
    for k in range(NCH):
        arrived(3, k)
        r.input_grad[z, chunk(k), :] = (
            summed(chunk(k)) + r.zh1[chunk(k), :]).astype(BF16)
    line_in.hop(0)
    chain(5)
    grad_hop(1, 2)
    grad_hop(2, 0)
    chain_end()
    grad_hop(2, 1)
    line_in.hop(1)
    grad_to_owner(0)
    grad_hop(2, 2)
    chain_across()
    line_out.hop(1)
    line_out.hop(3)
    save_out = pltpu.make_async_copy(r.lout, lout, r.save.at[0])
    save_out.start()
    line_in.hop(2)
    grad_hop(0, 0)
    grad_hop(0, 1)
    grad_hop(1, 3)
    line_in.hop(3)
    save_in = pltpu.make_async_copy(r.input_grad, input_grad, r.save.at[1])
    save_in.start()
    grad_hop(0, 2)
    grad_hop(2, 3)
    chain_total()
    grad_hop(0, 3)
    save_out.wait()
    save_in.wait()
    line_out.drain()
    line_in.drain()
    for p in range(3):
        grad_drain(p)
    chain_drain()
    for p in index:
        hop_drain(p)
    for p in ("q", "o"):
        shard_drain(p)
    links.drain()


def finish(lout, input_low, out0, outr, o_lout, o_in, o_qkv, o_qvb, o_out, o_geglu, o_gb, o_down,
           o_gain, o_shift, o_ob, narrow, wide, low, sem_in, sem_out, sem_lout, sem_onward):
    piece = outr.shape[1]
    cols = o_qkv.shape[2]
    blocks = narrow.shape[0]
    through = [pltpu.make_async_copy(lout.at[i], low.at[i], sem_lout.at[i]) for i in range(blocks)]
    onward = [pltpu.make_async_copy(low.at[i], o_lout.at[i], sem_onward.at[i]) for i in range(blocks)]
    loads = [pltpu.make_async_copy(input_low.at[i], narrow.at[i], sem_in.at[i]) for i in range(blocks)]
    saves = [pltpu.make_async_copy(wide.at[i], o_in.at[i], sem_out.at[i]) for i in range(blocks)]
    for load in loads + through:
        load.start()
    for i in range(3):
        o_qkv[i] = out0[0:piece, i * cols : (i + 1) * cols]
    o_out[...] = out0[0:piece, 3 * cols : 4 * cols].T
    o_geglu[...] = outr[0:2]
    o_down[...] = outr[2]
    o_qvb[0:1, :] = out0[piece : piece + 1, 0:cols]
    o_qvb[1:2, :] = out0[piece : piece + 1, cols : 2 * cols]
    o_gb[...] = out0[piece + 1 : piece + 3, :]
    place = lax.axis_index("shard") * 4 + lax.axis_index("ctx")
    for s in range(8):
        @pl.when(place == s)
        def _(s=s):
            lanes = slice(s * piece, (s + 1) * piece)
            o_gain[...] = out0[piece + 3 : piece + 5, lanes]
            o_shift[...] = out0[piece + 5 : piece + 7, lanes]
            o_ob[...] = out0[piece + 7 : piece + 9, lanes]
    for i in range(blocks):
        loads[i].wait()
        wide[i] = narrow[i].astype(F32)
        saves[i].start()
    for i in range(blocks):
        through[i].wait()
        onward[i].start()
    for save in saves + onward:
        save.wait()


def middle(
    x, cot, mixed, w0, w, vec,
    lout, dres1, grads, gout, dmixed, small,
    w_out, full, act, pull, hid, dgt, dup,
    snd_r, snd_o, snd_y, rcv_r, rcv_o, rcv_y,
    own, yacc, fa, fb, normed, zh1, r1, dres2, acc, bsum, tiny,
    ags_y, agr_y, ags_c, agr_c, ags_f, agr_f,
    rss_r, rsr_r, rss_o, rsr_o, rss_y, rsr_y, tiny_s, tiny_r, ls, lr,
):
    rows_own = x.shape[0]
    width = x.shape[1]
    cr = rows_own // NCH
    c, sib, ynb, dia = places()
    z = lax.axis_index("tp")
    tp = lout.shape[0]
    greet([{"ctx": sib}, {"ctx": ynb}] + [{"tp": (z + d) % tp} for d in range(1, tp)])
    line = LineGather(lout, ls, lr)

    started = []

    def remote(src, dst, send, recv, peer):
        return pltpu.make_async_remote_copy(
            src_ref=src, dst_ref=dst, send_sem=send, recv_sem=recv,
            device_id={"ctx": peer}, device_id_type=MESH,
        )

    def chunk(k):
        return pl.ds(k * cr, cr)

    ag_y, ag_c, ag_f, rs_r, rs_o, rs_y = ({} for _ in range(6))

    def start(table, key, copy):
        copy.start()
        table[key] = copy
        started.append(copy)

    def gather_start(o, k):
        piece = full.at[o, c, chunk(k)]
        start(ag_y, (o, k), remote(piece, piece, ags_y.at[o, k], agr_y.at[o, k], ynb))
        start(ag_c, (o, k), remote(piece, piece, ags_c.at[o, k], agr_c.at[o, k], sib))

    def forward(o, k):
        ag_y[o, k].wait_recv()
        piece = full.at[o, ynb, chunk(k)]
        start(ag_f, (o, k), remote(piece, piece, ags_f.at[o, k], agr_f.at[o, k], sib))

    def send_relay(o, k):
        start(rs_r, (o, k), remote(
            snd_r.at[o, chunk(k)], rcv_r.at[o, chunk(k)], rss_r.at[o, k], rsr_r.at[o, k], sib))

    def send_own(o, k):
        start(rs_o, (o, k), remote(
            snd_o.at[o, chunk(k)], rcv_o.at[o, chunk(k)], rss_o.at[o, k], rsr_o.at[o, k], sib))

    def relay(o, k):
        rs_r[o, k].wait_recv()
        snd_y[o, chunk(k), :] = (yacc[chunk(k), :] + rcv_r[o, chunk(k), :].astype(F32)).astype(BF16)
        start(rs_y, (o, k), remote(
            snd_y.at[o, chunk(k)], rcv_y.at[o, chunk(k)], rss_y.at[o, k], rsr_y.at[o, k], ynb))

    def arrived(o, k):
        rs_o[o, k].wait_recv()
        rs_y[o, k].wait_recv()

    def tiles(first, count, body):
        def step(t, carry):
            body(pl.ds(pl.multiple_of(first + t * TILE, TILE), TILE))
            return carry
        lax.fori_loop(0, count // TILE, step, 0)

    def summed(o, rows):
        return own[rows, :] + rcv_o[o, rows, :].astype(F32) + rcv_y[o, rows, :].astype(F32)

    def fold(values):
        return jnp.sum(values.reshape(TILE // 8, 8, width), axis=0)

    acc[...] = jnp.zeros_like(acc)
    bsum[...] = jnp.zeros_like(bsum)
    w_out[...] = w0[:, 3 * mixed.shape[2] : 4 * mixed.shape[2]]

    def project(b, r0, n):
        return dot_nt(mixed[b, pl.ds(r0, n), :], w_out[...])

    for k in range(NCH):
        snd_r[0, chunk(k), :] = project(dia, k * cr, cr).astype(BF16)
        send_relay(0, k)
        yacc[chunk(k), :] = project(ynb, k * cr, cr)
        if k:
            relay(0, k - 1)
    relay(0, NCH - 1)
    for k in range(NCH):
        snd_o[0, chunk(k), :] = project(sib, k * cr, cr).astype(BF16)
        send_own(0, k)
    own[...] = project(c, 0, rows_own)

    def norm_one(rows):
        res = x[rows, :].astype(F32) + summed(0, rows) + vec[4:5, :]
        center = res - jnp.mean(res, axis=-1, keepdims=True)
        r = lax.rsqrt(jnp.mean(center * center, axis=-1, keepdims=True) + 1e-12)
        zh = center * r
        out = zh * vec[0:1, :] + vec[2:3, :]
        zh1[rows, :] = zh
        r1[rows, :] = r
        normed[rows, :] = out
        full[0, c, rows, :] = out.astype(BF16)

    for k in range(NCH):
        arrived(0, k)
        tiles(k * cr, cr, norm_one)
        gather_start(0, k)

    def mlp_forward(b, r0, n):
        rows_in = full[0, b, pl.ds(r0, n), :]
        fa[pl.ds(0, n), :] = dot(rows_in, w[0])
        fb[pl.ds(0, n), :] = dot(rows_in, w[1])

        def units(rows):
            g = fa[rows, :] + vec[6:7, :]
            u = fb[rows, :] + vec[7:8, :]
            phi = 0.5 * (1.0 + lax.erf(g * (1.0 / math.sqrt(2.0))))
            gelu = g * phi
            slope = phi + g * jnp.exp(-0.5 * g * g) * (1.0 / math.sqrt(2.0 * math.pi))
            out = pl.ds(pl.multiple_of(r0 + rows.start, TILE), TILE)
            act[b, out, :] = gelu.astype(BF16)
            pull[b, out, :] = (u * slope).astype(BF16)
            hid[b, out, :] = (gelu * u).astype(BF16)

        tiles(0, n, units)
        return dot_nt(hid[b, pl.ds(r0, n), :], w[2])

    def mlp_backward(b, r0, n):
        fa[pl.ds(0, n), :] = dot(full[1, b, pl.ds(r0, n), :], w[2])

        def units(rows):
            dh = fa[rows, :]
            out = pl.ds(pl.multiple_of(r0 + rows.start, TILE), TILE)
            dg = (dh * pull[b, out, :].astype(F32)).astype(BF16)
            du = (dh * act[b, out, :].astype(F32)).astype(BF16)
            dgt[b, out, :] = dg
            dup[b, out, :] = du
            bsum[0] += fold(dg.astype(F32))
            bsum[1] += fold(du.astype(F32))

        tiles(0, n, units)
        return dot_nt(dgt[b, pl.ds(r0, n), :], w[0]) + dot_nt(dup[b, pl.ds(r0, n), :], w[1])

    def exchange(o, piece):
        own[...] = piece(c, 0, rows_own)
        for k in range(NCH):
            ag_c[o - 1, k].wait_recv()
        snd_o[o] = piece(sib, 0, rows_own).astype(BF16)
        for k in range(NCH):
            send_own(o, k)
        for k in range(NCH):
            forward(o - 1, k)
            yacc[chunk(k), :] = piece(ynb, k * cr, cr)
            ag_f[o - 1, k].wait_recv()
            snd_r[o, chunk(k), :] = piece(dia, k * cr, cr).astype(BF16)
            send_relay(o, k)
            if k:
                relay(o, k - 1)
        relay(o, NCH - 1)

    exchange(1, mlp_forward)

    def norm_two(rows):
        res = normed[rows, :] + (summed(1, rows) + vec[5:6, :])
        center = res - jnp.mean(res, axis=-1, keepdims=True)
        r = lax.rsqrt(jnp.mean(center * center, axis=-1, keepdims=True) + 1e-12)
        zh = center * r
        lout[z, rows, :] = (zh * vec[1:2, :] + vec[3:4, :]).astype(BF16)
        up = cot[rows, :].astype(F32)
        t = up * vec[1:2, :]
        d = r * (t - jnp.mean(t, axis=-1, keepdims=True)
                 - zh * jnp.mean(t * zh, axis=-1, keepdims=True))
        dres2[rows, :] = d
        low = d.astype(BF16)
        full[1, c, rows, :] = low
        acc[1] += fold(up * zh)
        acc[3] += fold(up)
        acc[5] += fold(low.astype(F32))

    for k in range(NCH):
        arrived(1, k)
        tiles(k * cr, cr, norm_two)
        gather_start(1, k)

    line.hop(0)
    exchange(2, mlp_backward)
    line.hop(1)

    def flat(ref):
        return ref[...].reshape(4 * rows_own, ref.shape[-1])

    hid_all = flat(hid)
    d_all = full[1].reshape(4 * rows_own, width)
    grads[2] = dot_tn(d_all, hid_all).astype(BF16)
    n_all = full[0].reshape(4 * rows_own, width)
    grads[0] = dot_tn(n_all, flat(dgt)).astype(BF16)
    grads[1] = dot_tn(n_all, flat(dup)).astype(BF16)

    line.hop(2)

    def norm_back(rows):
        dn = summed(2, rows) + dres2[rows, :]
        zh = zh1[rows, :]
        t = dn * vec[0:1, :]
        d = r1[rows, :] * (t - jnp.mean(t, axis=-1, keepdims=True)
                           - zh * jnp.mean(t * zh, axis=-1, keepdims=True))
        dres1[rows, :] = d
        low = d.astype(BF16)
        full[2, c, rows, :] = low
        acc[0] += fold(dn * zh)
        acc[2] += fold(dn)
        acc[4] += fold(low.astype(F32))

    for k in range(NCH):
        arrived(2, k)
        tiles(k * cr, cr, norm_back)
        gather_start(2, k)

    for i in range(6):
        tiny[0, i : i + 1, :] = jnp.sum(acc[i], axis=0, keepdims=True)
    for i in range(2):
        small[6 + i : 7 + i, :] = jnp.sum(bsum[i], axis=0, keepdims=True)
    tiny_copies = []
    for step, peer in enumerate((sib, ynb)):
        copy = remote(tiny.at[2 * step], tiny.at[2 * step + 1], tiny_s.at[step], tiny_r.at[step], peer)
        copy.start()
        started.append(copy)
        tiny_copies.append(copy)
        if step == 0:
            def unproject(b, r0, n):
                return dot(full[2, b, pl.ds(r0, n), :], w_out[...]).astype(BF16)
            dmixed[c] = unproject(c, 0, rows_own)
            for k in range(NCH):
                ag_c[2, k].wait_recv()
            dmixed[sib] = unproject(sib, 0, rows_own)
        copy.wait_recv()
        total = tiny[2 * step] + tiny[2 * step + 1]
        if step == 0:
            tiny[2] = total
        else:
            small[0:6, :] = total[0:6, :]
    for k in range(NCH):
        forward(2, k)
        dmixed[ynb, chunk(k), :] = unproject(ynb, k * cr, cr)
    for k in range(NCH):
        ag_f[2, k].wait_recv()
        dmixed[dia, chunk(k), :] = unproject(dia, k * cr, cr)
    gout[...] = dot_tn(full[2].reshape(4 * rows_own, width), flat(mixed)).astype(BF16)
    line.hop(3)
    line.drain()
    for copy in started:
        copy.wait_send()


def sds(shape, dtype):
    return jax.ShapeDtypeStruct(shape, dtype)


def smem():
    return pl.BlockSpec(memory_space=pltpu.SMEM)


def on_device(
    tokens_in, qkv_weight, qv_bias, out_weight, geglu_weight, geglu_bias, down_weight,
    norm_gains, norm_biases, out_biases, doc_lengths, cotangent,
):
    seqs, rows, width = tokens_in.shape
    group = lax.axis_size("ctx")
    tp = lax.axis_size("tp")
    shards = lax.axis_size("shard")
    z = lax.axis_index("tp")
    c = lax.axis_index("ctx")
    assert group == 4 and tp == 4 and seqs == tp
    length = group * rows
    part_rows = qkv_weight.shape[1]
    cols = qkv_weight.shape[2]
    heads = cols // DH
    units = geglu_weight.shape[2]
    assert units == width and 4 * cols == width and H == heads * tp

    me = lax.axis_index("shard") * group + c
    dma = lambda *shape: pltpu.SemaphoreType.DMA(shape)
    slopes = jnp.asarray([alibi_slopes(H)], F32)
    head_shape = sds((heads, length, DH), BF16)
    lengths = lax.dynamic_slice_in_dim(doc_lengths, z, 1, 0)
    block = (rows, width)
    stack = (group, rows, width)
    if shards == 2 and part_rows % 16 == 0:
        vm = pltpu.VMEM
        wide = part_rows + 16
        pieces = lambda n: (vm((n, wide, width), BF16), vm((2, n, part_rows, width), BF16))
        scratch = dict(
            pq=vm((part_rows, 640), BF16), po=vm((wide, 256), BF16),
            lout=vm((tp,) + block, BF16), input_grad=vm((tp,) + block, BF16), save=dma(2),
            zbq=vm((tp, part_rows, 640), BF16), zbo=vm((tp, wide, 256), BF16),
            zbr=vm((3, tp, part_rows, width), BF16),
            load=dma(2), cb=vm((2, 2, group, part_rows, width), BF16),
            yd=vm((2, part_rows, width), BF16), xd=vm((part_rows, width), BF16),
            ch_s=dma(2, 4), ch_r=dma(2, 4), cy_s=dma(4), cy_r=dma(1), cx_s=dma(1), cx_r=dma(1),
            cot=vm(block, BF16), xs=vm(stack, BF16),
            wq=vm((2, group, part_rows, 640), BF16), wo=vm((2, group, wide, 256), BF16),
            g0=vm((2, group, wide, width), BF16), w=vm((3, 2, group, part_rows, width), BF16),
            w_out=vm((width, cols), BF16),
            qv=vm((2, cols), F32), vec=vm((8, width), F32), extra=vm((16, width), F32),
            probs=vm((heads, length, length), BF16),
            q=vm((heads, length, DH), BF16), k=vm((heads, length, DH), BF16),
            v=vm((heads, length, DH), BF16), far=vm((rows, length), F32),
            mixed=vm((length, cols), BF16), dmixed=vm((length, cols), BF16),
            full=vm((3,) + stack, BF16), act=vm(stack, BF16), pull=vm(stack, BF16),
            hid=vm(stack, BF16),
            **{n: vm(block, BF16) for n in ("snd_r", "snd_o", "snd_y", "rcv_r", "rcv_o", "rcv_y")},
            **{n: vm(block, F32) for n in ("own", "yacc", "fa", "fb", "normed", "zh1")},
            r1=vm((rows, 1), F32), acc=vm((6, 8, width), F32), bsum=vm((2, 8, width), F32),
            tiny=vm((4, 8, width), F32),
            dqkv=vm((length, 3 * cols), BF16),
            dk_acc=vm((heads, DH, length), F32), dv_acc=vm((heads, DH, length), F32),
            xg_s=dma(3), xg_r=dma(3),
            **{n: dma(5, 4) for n in ("zu", "zd", "zu2", "zd2", "zr", "ys", "yr", "xs_s", "xs_r")},
            **{n: dma(4, 4) for n in ("gx_s", "gx_r", "gy_s", "gy_r",
                                      "gu_s", "gu_r", "gd_s", "gd_r")},
            **{n: dma(3, NCH) for n in ("ags_y", "agr_y", "ags_c", "agr_c", "ags_f", "agr_f")},
            **{n: dma(4, NCH) for n in ("rss_r", "rsr_r", "rss_o", "rsr_o", "rss_y", "rsr_y")},
            tiny_s=dma(2), tiny_r=dma(2), ls=dma(1, 5), lu=dma(tp), ld=dma(tp), lr=dma(2, tp),
        )
        for n, count in (("xb", group), ("yb", group), ("rb", tp + 1)):
            scratch[n + "0"], scratch[n + "r"] = pieces(count)
        raw = pl.pallas_call(
            functools.partial(layer, tuple(scratch), heads),
            out_shape=[
                sds((tp,) + block, BF16), sds((tp,) + block, BF16),
                sds((wide, width), F32), sds((3, part_rows, width), F32),
            ],
            in_specs=[smem(), smem()] + [pl.BlockSpec(memory_space=pl.ANY)] * 2 + vmem(9),
            out_specs=[pl.BlockSpec(memory_space=pl.ANY)] * 2 + vmem(2),
            scratch_shapes=list(scratch.values()),
            compiler_params=pltpu.CompilerParams(
                collective_id=1, has_side_effects=True, vmem_limit_bytes=VMEM_MB * MB
            ),
            name="layer",
        )(
            lengths, slopes, tokens_in, cotangent, qkv_weight, out_weight, geglu_weight,
            down_weight.T, qv_bias, geglu_bias, norm_gains, norm_biases, out_biases,
        )
        res = pl.pallas_call(
            finish,
            out_shape=[
                sds((tp,) + block, BF16), sds((tp,) + block, F32),
                sds(qkv_weight.shape, F32), sds(qv_bias.shape, F32), sds(out_weight.shape, F32),
                sds(geglu_weight.shape, F32), sds(geglu_bias.shape, F32),
                sds(down_weight.shape[::-1], F32),
            ] + [sds(norm_gains.shape, F32)] * 3,
            in_specs=[pl.BlockSpec(memory_space=pl.ANY)] * 2 + vmem(2),
            out_specs=[pl.BlockSpec(memory_space=pl.ANY)] * 2 + vmem(9),
            scratch_shapes=[
                vm((tp,) + block, BF16), vm((tp,) + block, F32), vm((tp,) + block, BF16)
            ] + [dma(tp)] * 4,
            compiler_params=pltpu.CompilerParams(vmem_limit_bytes=VMEM_MB * MB),
            name="finish",
        )(*raw)
        return (*res[:7], res[7].T, *res[8:])

    with jax.named_scope("pack_weights"):
        first = jnp.concatenate(
            [qkv_weight[0], qkv_weight[1], qkv_weight[2], out_weight.T], axis=1
        )
        own_norm = jnp.concatenate([norm_gains, norm_biases, out_biases], axis=0)
        parts = jnp.concatenate([first[None], geglu_weight, down_weight.T[None]], axis=0)
        own_bias = jnp.concatenate([qv_bias.reshape(1, -1), geglu_bias.reshape(1, -1)], axis=1)

    x_own = lax.dynamic_index_in_dim(tokens_in, z, 0, keepdims=False)
    cot_own = lax.dynamic_index_in_dim(cotangent, z, 0, keepdims=False)
    with jax.named_scope("gather_weights"):
        by_block = lax.all_gather(parts, "tp", axis=0)
        swapped = lax.all_to_all(by_block, "ctx", split_axis=0, concat_axis=0)
        w = lax.all_gather(swapped, "shard", axis=0)
        w = w.transpose(2, 0, 1, 3, 4).reshape(4, shards * group * part_rows, width)
        biases = lax.all_gather(own_bias, "tp", axis=0, tiled=True)
        biases = lax.dynamic_slice_in_dim(biases, c, 1, 0).astype(F32)
        norms = lax.all_gather(own_norm, ("shard", "ctx"), axis=1, tiled=True).astype(F32)
    qv = biases[:, : 2 * cols].reshape(2, cols)
    vec = jnp.concatenate([norms, biases[:, 2 * cols :].reshape(2, units)], axis=0)

    xs = lax.all_gather(x_own, "ctx", axis=0, tiled=True)

    mixed, probs, q, k, v = pl.pallas_call(
        functools.partial(attention_forward, heads),
        out_shape=[sds((length, cols), BF16), sds((heads, length, length), BF16)] + [head_shape] * 3,
        in_specs=[smem(), smem()] + vmem(3),
        out_specs=vmem(5),
        scratch_shapes=[pltpu.VMEM((256, length), F32)],
        compiler_params=pltpu.CompilerParams(vmem_limit_bytes=48 * MB),
        name="attention_forward",
    )(lengths, slopes, xs, w[0], qv)
    w0, w = w[0], w[1:]


    lout, dres1, grads, gout, dmixed, small = pl.pallas_call(
        middle,
        out_shape=[
            sds((tp,) + block, BF16), sds(block, F32), sds((3, width, width), BF16),
            sds((width, cols), BF16), sds((group, rows, cols), BF16), sds((8, width), F32),
        ],
        in_specs=vmem(6),
        out_specs=vmem(6),
        scratch_shapes=[
            pltpu.VMEM((width, cols), BF16), pltpu.VMEM((3,) + stack, BF16),
        ] + [pltpu.VMEM(stack, BF16)] * 5 + [pltpu.VMEM((3,) + block, BF16)] * 6 + [
            pltpu.VMEM(block, F32)
        ] * 6 + [
            pltpu.VMEM((rows, 1), F32), pltpu.VMEM(block, F32),
            pltpu.VMEM((6, 8, width), F32), pltpu.VMEM((2, 8, width), F32),
            pltpu.VMEM((4, 8, width), F32),
        ] + [dma(3, NCH)] * 12 + [dma(2)] * 2 + [dma(5), dma(tp)],
        compiler_params=pltpu.CompilerParams(
            collective_id=0, has_side_effects=True, vmem_limit_bytes=58 * MB
        ),
        name="middle",
    )(x_own, cot_own, mixed.reshape(group, rows, cols), w0, w, vec)

    grad_w, d_in, bias_grad = pl.pallas_call(
        functools.partial(attention_backward, heads),
        out_shape=[
            sds((width, 3 * cols), BF16), sds((length, width), BF16), sds((1, 3 * cols), F32)
        ],
        in_specs=vmem(8),
        out_specs=vmem(3),
        scratch_shapes=[
            pltpu.VMEM((length, 3 * cols), BF16),
            pltpu.VMEM((heads, DH, length), F32), pltpu.VMEM((heads, DH, length), F32),
        ],
        compiler_params=pltpu.CompilerParams(vmem_limit_bytes=48 * MB),
        name="attention_backward",
    )(dmixed.reshape(length, cols), mixed, probs, q, k, v, xs, w0)

    with jax.named_scope("outputs"):
        input_sum = lax.psum_scatter(d_in, "ctx", scatter_dimension=0, tiled=True)
        input_own = (input_sum.astype(F32) + dres1).astype(BF16)
        input_grad = lax.all_gather(input_own, "tp", axis=0).astype(F32)
        layer_out = lout

    with jax.named_scope("scatter_grads"):
        first_grad = jnp.concatenate([grad_w, gout], axis=1)
        packed = jnp.concatenate([first_grad[None], grads], axis=0)
        packed = packed.reshape(4, shards, group, part_rows, width).transpose(1, 2, 0, 3, 4)
        mine = lax.psum_scatter(packed, "shard", scatter_dimension=0, tiled=False)
        mine = lax.all_to_all(mine, "ctx", split_axis=0, concat_axis=0)
        mine = lax.psum_scatter(mine, "tp", scatter_dimension=0, tiled=False)
        mine = mine.astype(F32)
        grad_qkv = jnp.stack([mine[0, :, i * cols : (i + 1) * cols] for i in range(3)])
        grad_out = mine[0, :, 3 * cols :].T
        grad_geglu = mine[1:3]
        grad_down = mine[3].T
        col = jnp.concatenate(
            [bias_grad[:, :cols], bias_grad[:, 2 * cols :], small[6:7], small[7:8]], axis=1
        )
        col = lax.psum_scatter(
            jnp.zeros((group, col.shape[1]), F32) + jnp.where(
                jnp.arange(group)[:, None] == c, col, 0.0),
            "tp", scatter_dimension=0, tiled=True)
        col = lax.psum(col, ("shard", "ctx"))
        norm_grad = lax.psum(small[:6], ("shard", "tp"))
        norm_grad = lax.dynamic_slice_in_dim(norm_grad, me * part_rows, part_rows, 1)
    return (
        layer_out,
        input_grad,
        grad_qkv,
        col[:, : 2 * cols].reshape(2, cols),
        grad_out,
        grad_geglu,
        col[:, 2 * cols :].reshape(2, units),
        grad_down,
        norm_grad[0:2],
        norm_grad[2:4],
        norm_grad[4:6],
    )


def solution(mesh):
    in_specs = (
        P("shard", "ctx", None),
        P(None, ("shard", "ctx"), "tp"),
        P(None, "tp"),
        P("tp", ("shard", "ctx")),
        P(None, ("shard", "ctx"), "tp"),
        P(None, "tp"),
        P("tp", ("shard", "ctx")),
        P(None, ("shard", "ctx")),
        P(None, ("shard", "ctx")),
        P(None, ("shard", "ctx")),
        P("shard", None),
        P("shard", "ctx", None),
    )
    out_specs = (
        P("shard", "ctx", None),
        P("shard", "ctx", None),
        P(None, ("shard", "ctx"), "tp"),
        P(None, "tp"),
        P("tp", ("shard", "ctx")),
        P(None, ("shard", "ctx"), "tp"),
        P(None, "tp"),
        P("tp", ("shard", "ctx")),
        P(None, ("shard", "ctx")),
        P(None, ("shard", "ctx")),
        P(None, ("shard", "ctx")),
    )
    return jax.shard_map(
        on_device, mesh=mesh, in_specs=in_specs, out_specs=out_specs, check_vma=False
    )
```

```python
import functools
import math
import types

import jax
import jax.numpy as jnp
from jax import lax
from jax.experimental import pallas as pl
from jax.experimental.pallas import tpu as pltpu
from jax.sharding import PartitionSpec as P

H = 12
DH = 64
F32 = jnp.float32
BF16 = jnp.bfloat16
MESH = pl.DeviceIdType.MESH
NCH = 4
TILE = 32
MB = 1 << 20
VMEM_MB = 62


def alibi_slopes(head_count):
    def power_slopes(head_total):
        first_slope = 2.0 ** (-8.0 / head_total)
        return [first_slope ** (counter + 1) for counter in range(head_total)]

    nearest = 2 ** int(math.floor(math.log2(head_count)))
    slope_list = power_slopes(nearest)
    return slope_list + power_slopes(2 * nearest)[0::2][: head_count - nearest]


def dot(left, right):
    return jnp.dot(left, right, preferred_element_type=F32)


def dot_nt(left, right):
    return lax.dot_general(left, right, (((1,), (1,)), ((), ())), preferred_element_type=F32)


def dot_tn(left, right):
    return lax.dot_general(left, right, (((0,), (0,)), ((), ())), preferred_element_type=F32)


def vmem(count):
    return [pl.BlockSpec(memory_space=pltpu.VMEM)] * count


def project_heads(heads, x_rows, rows, w, bias, q_out, k_out, v_out):
    cols = heads * DH
    for part, out in enumerate((q_out, k_out, v_out)):
        y = dot(x_rows, w[:, part * cols : (part + 1) * cols])
        if part != 1:
            y = y + bias[part // 2 : part // 2 + 1, :]
        y = y.astype(BF16)
        if part == 0:
            y = y * BF16(1.0 / math.sqrt(DH))
        for i in range(heads):
            out[i, rows, :] = y[:, i * DH : (i + 1) * DH]


def segments(lengths, pos):
    seg = jnp.zeros(pos.shape, jnp.int32)
    end = 0
    for k in range(lengths.shape[1]):
        end = end + lengths[0, k]
        seg = seg + (pos >= end).astype(jnp.int32)
    return seg


def attend_rows(heads, start, step, lengths, slopes, q, k, v, probs, mixed, far):
    length = k.shape[1]
    mine = lax.axis_index("ctx") * heads
    rows = pl.ds(start, step)
    key_pos = lax.broadcasted_iota(jnp.int32, (1, length), 1)
    pos = start + lax.broadcasted_iota(jnp.int32, (step, 1), 0)
    same = segments(lengths, pos) == segments(lengths, key_pos)
    far[...] = jnp.where(same, jnp.abs(pos - key_pos).astype(F32), 1e33)
    for i in range(heads):
        s = dot_nt(q[i, rows, :], k[i]) - slopes[0, mine + i] * far[...]
        p = jnp.exp(s - jnp.max(s, axis=-1, keepdims=True))
        p = (p * (1.0 / jnp.sum(p, axis=-1, keepdims=True))).astype(BF16)
        probs[i, rows, :] = p
        mixed[rows, i * DH : (i + 1) * DH] = dot(p, v[i]).astype(BF16)


def attention_forward(
    heads, lengths, slopes, xs, w, bias, mixed, probs, q_out, k_out, v_out, far
):
    step = 256

    def project(r, carry):
        rows = pl.ds(pl.multiple_of(r * step, step), step)
        project_heads(heads, xs[rows, :], rows, w, bias, q_out, k_out, v_out)
        return carry

    def attend(r, carry):
        start = pl.multiple_of(r * step, step)
        attend_rows(
            heads, start, step, lengths, slopes, q_out, k_out, v_out, probs, mixed, far)
        return carry

    lax.fori_loop(0, xs.shape[0] // step, project, 0)
    lax.fori_loop(0, xs.shape[0] // step, attend, 0)


def attend_back(heads, rows, dmixed, mixed, probs, q, k, v, dqkv, dk_acc, dv_acc):
    for i in range(heads):
        own = slice(i * DH, (i + 1) * DH)
        d_out = dmixed[rows, own]
        row_dot = jnp.sum(
            d_out.astype(F32) * mixed[rows, own].astype(F32), axis=-1, keepdims=True
        )
        p = probs[i, rows, :]
        dp = dot_nt(d_out, v[i])
        ds = (p.astype(F32) * (dp - row_dot)).astype(BF16)
        dqkv[rows, own] = (dot(ds, k[i]) * (1.0 / math.sqrt(DH))).astype(BF16)
        dk_acc[i] += dot_tn(q[i, rows, :], ds)
        dv_acc[i] += dot_tn(d_out, p)


def spread_heads(heads, dqkv, dk_acc, dv_acc):
    cols = heads * DH
    for i in range(heads):
        dqkv[:, cols + i * DH : cols + (i + 1) * DH] = dk_acc[i].T.astype(BF16)
        dqkv[:, 2 * cols + i * DH : 2 * cols + (i + 1) * DH] = dv_acc[i].T.astype(BF16)


def attention_backward(
    heads, dmixed, mixed, probs, q, k, v, xs, w, grad_w, d_in, bias_grad, dqkv, dk_acc, dv_acc
):
    length = xs.shape[0]
    step = 256
    cols = heads * DH
    dk_acc[...] = jnp.zeros_like(dk_acc)
    dv_acc[...] = jnp.zeros_like(dv_acc)

    def rows_back(r, carry):
        rows = pl.ds(pl.multiple_of(r * step, step), step)
        attend_back(heads, rows, dmixed, mixed, probs, q, k, v, dqkv, dk_acc, dv_acc)
        return carry

    lax.fori_loop(0, length // step, rows_back, 0)
    spread_heads(heads, dqkv, dk_acc, dv_acc)

    def finish(r, total):
        rows = pl.ds(pl.multiple_of(r * step, step), step)
        d = dqkv[rows, :]
        d_in[rows, :] = dot_nt(d, w[:, : 3 * cols]).astype(BF16)
        return total + jnp.sum(d.astype(F32), axis=0, keepdims=True)

    bias_grad[...] = lax.fori_loop(
        0, length // step, finish, jnp.zeros((1, 3 * cols), F32)
    )
    for part in range(3):
        own = slice(part * cols, (part + 1) * cols)
        grad_w[:, own] = dot_tn(xs[...], dqkv[:, own]).astype(BF16)


class Links:
    def __init__(self):
        self.started = []

    def copy(self, src, dst, send, recv, peer):
        return pltpu.make_async_remote_copy(
            src_ref=src, dst_ref=dst, send_sem=send, recv_sem=recv,
            device_id=peer, device_id_type=MESH,
        )

    def start(self, src, dst, send, recv, peer):
        copy = self.copy(src, dst, send, recv, peer)
        copy.start()
        self.started.append(copy)
        return copy

    def sent(self, copy):
        if any(copy is one for one in self.started):
            copy.wait_send()
            self.started = [one for one in self.started if one is not copy]

    def drain(self):
        for copy in self.started:
            copy.wait_send()
        self.started = []


def greet(peers, between=None):
    barrier = pltpu.get_barrier_semaphore()
    for peer in peers:
        pl.semaphore_signal(barrier, inc=1, device_id=peer, device_id_type=MESH)
    if between is not None:
        between()
    pl.semaphore_wait(barrier, len(peers))


def places():
    c = lax.axis_index("ctx")
    flip = 1 - 2 * (c % 2)
    ynb = (c + 2) % 4
    return c, c + flip, ynb, ynb + flip


class LineGather:
    def __init__(self, blocks, sems, recv):
        self.blocks, self.sems, self.recv = blocks, sems, recv
        self.z = lax.axis_index("tp")
        self.last = blocks.shape[0] - 1

    def _copy(self, j, which, peer):
        block = self.blocks.at[j]
        return pltpu.make_async_remote_copy(
            src_ref=block, dst_ref=block, send_sem=self.sems.at[which], recv_sem=self.recv.at[j],
            device_id={"tp": peer}, device_id_type=MESH,
        )

    def _sends(self, act):
        z = self.z
        for which, step in enumerate((1, -1, 2, -2)):
            @pl.when(jnp.logical_and(z + step >= 0, z + step <= self.last))
            def _(which=which, step=step):
                act(self._copy(z, which, z + step))

    def _passed(self, act):
        z, last = self.z, self.last

        @pl.when(z == 2)
        def _():
            act(self._copy(0, 4, last))

        @pl.when(z == 1)
        def _():
            act(self._copy(last, 4, 0))

    def hop(self, d):
        z = self.z
        if d == 0:
            self._sends(lambda copy: copy.start())
            return
        for j in (z - d, z + d):
            @pl.when(jnp.logical_and(j >= 0, j <= self.last))
            def _(j=j):
                self._copy(j, 0, z).wait_recv()
        if d == 2:
            self._passed(lambda copy: copy.start())

    def drain(self):
        self._sends(lambda copy: copy.wait_send())
        self._passed(lambda copy: copy.wait_send())


class LineRelay:
    def __init__(self, blocks, up, down, recv):
        self.blocks, self.up, self.down, self.recv = blocks, up, down, recv
        self.z = lax.axis_index("tp")
        self.last = blocks.shape[0] - 1
        self.rows = blocks.shape[1] // 2

    def _copy(self, j, h, sem, peer):
        block = self.blocks.at[j, pl.ds(h * self.rows, self.rows)]
        return pltpu.make_async_remote_copy(
            src_ref=block, dst_ref=block, send_sem=sem.at[h, j], recv_sem=self.recv.at[h, j],
            device_id={"tp": peer}, device_id_type=MESH,
        )

    def _sides(self, d):
        z, last = self.z, self.last
        yield self.up, z - d, z - d >= 0, z < last, z + 1
        yield self.down, z + d, z + d <= last, z > 0, z - 1

    def hop(self, d, h):
        for sem, j, here, onward, peer in self._sides(d):
            @pl.when(here)
            def _(sem=sem, j=j, onward=onward, peer=peer):
                if d:
                    self._copy(j, h, sem, self.z).wait_recv()
                if d < self.last:
                    @pl.when(onward)
                    def _():
                        self._copy(j, h, sem, peer).start()

    def drain(self):
        for d in range(self.last):
            for h in range(2):
                for sem, j, here, onward, _ in self._sides(d):
                    @pl.when(jnp.logical_and(here, onward))
                    def _(sem=sem, j=j, h=h):
                        self._copy(j, h, sem, self.z).wait_send()


def layer(
    names, heads, lengths, slopes,
    tokens, cotangent, qkv_w, out_w, geglu_w, down_w, qv_b, geglu_b, gains, shifts, out_b,
    lout, input_grad, out0, outr, *scratch,
):
    r = types.SimpleNamespace(**dict(zip(names, scratch)))
    c, sib, ynb, dia = places()
    me = lax.axis_index("shard")
    z = lax.axis_index("tp")
    other = 1 - me
    tp, rows_own, width = lout.shape
    piece = outr.shape[1]
    cols = heads * DH
    length = 4 * rows_own
    cr = rows_own // NCH
    links = Links()
    start, copy = links.start, links.copy

    def block(body):
        pl.when(z >= 0)(body)


    def local(src, dst, i):
        return pltpu.make_async_copy(src, dst, r.load.at[i])

    load_x = local(tokens.at[z], r.xs.at[c], 0)
    load_c = local(cotangent.at[z], r.cot, 1)
    loads = [local(qkv_w, r.qkv_v, 2), local(out_w, r.out_v, 3), local(down_w, r.down_v, 4),
             local(geglu_w, r.geglu_v, 5)]

    span = r.po.shape[1]
    thirds = width // span

    def pack():
        for one in loads + [load_x, load_c]:
            one.start()
        for one in loads:
            one.wait()
        for i in range(3):
            r.pq[:, i * cols : (i + 1) * cols] = r.qkv_v[i]
        r.pq[:, 3 * cols :] = jnp.zeros((piece, r.pq.shape[1] - 3 * cols), BF16)
        for i in range(2):
            for h in range(heads):
                r.pq[i * heads + h : i * heads + h + 1, 3 * cols : 3 * cols + DH] = (
                    qv_b[i : i + 1, h * DH : (h + 1) * DH])
        r.po[...] = jnp.zeros_like(r.po)
        r.po[0:piece, 0:cols] = r.out_v[...].T
        for i in range(2):
            for t in range(thirds):
                row = piece + i * thirds + t
                r.po[row : row + 1, :] = geglu_b[i : i + 1, t * span : (t + 1) * span]
        row = piece + 2 * thirds
        for i, ref in enumerate((gains, shifts, out_b)):
            r.po[row + 2 * i : row + 2 * i + 2, 0:piece] = ref[...]

    greet([{"ctx": sib}, {"ctx": ynb}, {"ctx": dia}, {"shard": other}]
          + [{"tp": (z + d) % tp} for d in range(1, tp)], pack)

    half = piece // 2
    src = {"q": r.pq, "o": r.po, 0: r.geglu_v.at[0], 1: r.geglu_v.at[1],
           2: r.down_v.at[pl.ds(0, half)]}
    zb = {"q": r.zbq, "o": r.zbo, 0: r.zbr.at[0], 1: r.zbr.at[1], 2: r.zbd, 3: r.zbe}
    wr = {"q": r.wq, "o": r.wo, 0: r.w.at[0], 1: r.w.at[1]}
    index = {"q": 0, "o": 1, 0: 2, 1: 3, 2: 4, 3: 5}
    last = tp - 1

    def line_copy(p, j, sems, peer):
        block = zb[p].at[j]
        return copy(block, block, sems.at[index[p], j], r.zr.at[index[p], j], {"tp": peer})

    def slot_at(p, s, j):
        if p == 2:
            return r.w.at[2, s, j, pl.ds(0, half)]
        return wr[p].at[s, j]

    def owner_slot(p, j):
        if p == 3:
            return r.w.at[2, :, j, pl.ds(half, half)]
        return slot_at(p, me, j)

    def hop(p, d):
        def deliver(j):
            @pl.when(j == c)
            def _():
                owner_slot(p, c)[...] = zb[p].at[j][...]

            @pl.when(j != c)
            def _():
                copy(zb[p].at[j], owner_slot(p, c), r.ys.at[index[p], j], r.yr.at[index[p], c],
                     {"ctx": j}).start()

        if d == 0:
            if p == 3:
                held["crossed"].wait_recv()
            else:
                zb[p].at[z][...] = src[p][...]

            for step in (2, 1):
                sems = r.zu if step == 1 else r.zu2

                @pl.when(z + step <= last)
                def _(step=step, sems=sems):
                    line_copy(p, z, sems, z + step).start()

                sems = r.zd if step == 1 else r.zd2

                @pl.when(z - step >= 0)
                def _(step=step, sems=sems):
                    line_copy(p, z, sems, z - step).start()

            deliver(z)
            return
        for side in range(2):
            j = z - d if side == 0 else z + d

            @pl.when((j >= 0) if side == 0 else (j <= last))
            def _(side=side, j=j):
                line_copy(p, j, r.zu, z).wait_recv()
                if d == 2:
                    @pl.when((z == 2) if side == 0 else (z == 1))
                    def _():
                        if side == 0:
                            line_copy(p, j, r.zu, z + 1).start()
                        else:
                            line_copy(p, j, r.zd, z - 1).start()
                deliver(j)

    def hop_drain(p):
        for step in (1, 2):
            @pl.when(z + step <= last)
            def _(step=step):
                line_copy(p, z, r.zu if step == 1 else r.zu2, z).wait_send()

            @pl.when(z - step >= 0)
            def _(step=step):
                line_copy(p, z, r.zd if step == 1 else r.zd2, z).wait_send()

        @pl.when(z == 2)
        def _():
            line_copy(p, 0, r.zu, z).wait_send()

        @pl.when(z == 1)
        def _():
            line_copy(p, last, r.zd, z).wait_send()

        for j in (sib, ynb, dia):
            copy(zb[p].at[j], owner_slot(p, c), r.ys.at[index[p], j], r.yr.at[index[p], c],
                 {"ctx": j}).wait_send()

    def owned(p, j):
        copy(zb[p].at[c], owner_slot(p, j), r.ys.at[index[p], c], r.yr.at[index[p], j],
             {"ctx": c}).wait_recv()

    def shard_copy(p, i, j):
        slot = slot_at(p, me, j)
        return copy(slot, slot, r.xs_s.at[index[p], i], r.xs_r.at[index[p], j], {"shard": other})

    def to_shard(p):
        for i, j in enumerate((c, sib, ynb, dia)):
            if i:
                owned(p, j)
            shard_copy(p, i, j).start()

    far_off = jnp.abs(z - c)

    def to_shard_if(p, low, high):
        @pl.when(jnp.logical_and(far_off >= low, far_off <= high))
        def _():
            to_shard(p)

    def shard_drain(p):
        for i in range(4):
            shard_copy(p, i, c).wait_send()

    def complete(p):
        if p == 3:
            for j in (sib, ynb, dia):
                owned(p, j)
            return
        for j in range(4):
            slot = slot_at(p, other, j)
            copy(slot, slot, r.xs_s.at[index[p], 0], r.xs_r.at[index[p], j],
                 {"shard": other}).wait_recv()

    grad = [r.g0] + [r.w.at[i] for i in range(2)]
    xb = [r.xb0] + [r.xbr.at[i] for i in range(2)] + [r.xbh]
    yb = [r.yb0] + [r.ybr.at[i] for i in range(2)] + [r.ybh]
    rb = [r.rb0] + [r.rbr.at[i] for i in range(2)] + [r.rbh]
    out = [out0] + [outr.at[i] for i in range(2)] + [outr.at[2, pl.ds(0, half)]]

    def grad_at(p, s, j):
        if p == 3:
            return r.w.at[2, s, j, pl.ds(0, half)]
        return grad[p].at[s, j]

    def grad_to_shard(p):
        for i, j in enumerate((dia, ynb, sib, c)):
            start(grad_at(p, other, j), xb[p].at[j], r.gx_s.at[p, i], r.gx_r.at[p, j], {"shard": other})

    def grad_to_owner(p, i):
        j = (dia, ynb, sib, c)[i]
        copy(grad_at(p, other, j), xb[p].at[j], r.gx_s.at[p, 0], r.gx_r.at[p, j],
             {"shard": other}).wait_recv()
        total = (grad_at(p, me, j)[...].astype(F32) + xb[p].at[j][...].astype(F32)).astype(BF16)
        if i == 3:
            yb[p].at[c][...] = total
        else:
            xb[p].at[j][...] = total
            start(xb[p].at[j], yb[p].at[c], r.gy_s.at[p, i], r.gy_r.at[p, c], {"ctx": j})

    def grad_came(p, j):
        @pl.when(j != c)
        def _():
            copy(xb[p].at[j], yb[p].at[j], r.gy_s.at[p, 0], r.gy_r.at[p, j], {"ctx": j}).wait_recv()

    def climb(p, side, j):
        if side == 0:
            return copy(yb[p].at[j], rb[p].at[j], r.gu_s.at[p, j], r.gu_r.at[p, j], {"tp": z + 1})
        slot = jnp.where(j == z - 1, tp, j)
        return copy(yb[p].at[j], rb[p].at[slot], r.gd_s.at[p, j], r.gd_r.at[p, j], {"tp": z - 1})

    def grad_hop(p, h):
        if h == last:
            grad_came(p, z)
            out[p][...] = yb[p].at[z][...].astype(F32)

            @pl.when(z > 0)
            def _():
                copy(yb[p].at[z], rb[p].at[z], r.gu_s.at[p, z], r.gu_r.at[p, z], {"tp": z}).wait_recv()
                out[p][...] += rb[p].at[z][...].astype(F32)

            @pl.when(z < last)
            def _():
                copy(yb[p].at[z], rb[p].at[tp], r.gd_s.at[p, z], r.gd_r.at[p, z], {"tp": z}).wait_recv()
                out[p][...] += rb[p].at[tp][...].astype(F32)
            return
        for side in range(2):
            j = z + (last - h) if side == 0 else z - (last - h)

            @pl.when((j <= last) if side == 0 else (j >= 0))
            def _(side=side, j=j):
                grad_came(p, j)

                @pl.when((z > 0) if side == 0 else (z < last))
                def _():
                    sems = r.gu_r if side == 0 else r.gd_r
                    copy(yb[p].at[j], rb[p].at[j], r.gu_s.at[p, j], sems.at[p, j], {"tp": z}).wait_recv()
                    yb[p].at[j][...] = (
                        yb[p].at[j][...].astype(F32) + rb[p].at[j][...].astype(F32)).astype(BF16)
                climb(p, side, j).start()

    stage = jnp.where(z < c, z, last - z)

    def chain_mine(i):
        return r.w.at[2, i // 2, pl.ds(2 * (i % 2), 2), pl.ds(half, half)]

    def chain_came(side, i):
        return r.cb.at[side, i // 2, pl.ds(2 * (i % 2), 2)]

    def chain_copy(i, side):
        return copy(chain_mine(i), chain_came(side, i),
                    r.ch_s.at[side, i], r.ch_r.at[side, i], {"tp": z + 1 if side == 0 else z - 1})

    def chain_wait(i, side):
        copy(chain_mine(i), chain_came(side, i),
             r.ch_s.at[side, i], r.ch_r.at[side, i], {"tp": z}).wait_recv()
        mine = chain_mine(i)
        mine[...] = (mine[...].astype(F32) + chain_came(side, i)[...].astype(F32)).astype(BF16)

    def chain(slot):
        for i in range(4):
            for side in range(2):
                here = (z < c) if side == 0 else (z > c)
                if slot == 0:
                    @pl.when(jnp.logical_and(here, stage == 0))
                    def _(i=i, side=side):
                        chain_copy(i, side).start()
                else:
                    @pl.when(jnp.logical_and(here, jnp.logical_and(stage > 0, stage == slot - i)))
                    def _(i=i, side=side):
                        chain_wait(i, side)
                        chain_copy(i, side).start()

    def chain_send(j):
        return copy(r.w.at[2, :, j, pl.ds(half, half)], r.yd, r.cy_s.at[j], r.cy_r.at[0], {"ctx": j})

    def chain_end():
        @pl.when(z == c)
        def _():
            for i in range(4):
                @pl.when(z > 0)
                def _(i=i):
                    chain_wait(i, 0)

                @pl.when(z < last)
                def _(i=i):
                    chain_wait(i, 1)
            r.yd[...] = r.w[2, :, c, half:, :]
            for j in (dia, ynb, sib):
                chain_send(j).start()

    def chain_across():
        @pl.when(z != c)
        def _():
            chain_send(c).wait_recv()
        start(r.yd.at[other], r.xd, r.cx_s.at[0], r.cx_r.at[0], {"shard": other})

    def chain_total():
        copy(r.yd.at[other], r.xd, r.cx_s.at[0], r.cx_r.at[0], {"shard": other}).wait_recv()
        outr[2, half:, :] = r.yd[me].astype(F32) + r.xd[...].astype(F32)

    def chain_drain():
        for i in range(4):
            for side in range(2):
                @pl.when((z < c) if side == 0 else (z > c))
                def _(i=i, side=side):
                    chain_copy(i, side).wait_send()

        @pl.when(z == c)
        def _():
            for j in (dia, ynb, sib):
                chain_send(j).wait_send()

    def grad_drain(p):
        for h in range(last):
            for side in range(2):
                j = z + (last - h) if side == 0 else z - (last - h)

                @pl.when((j <= last) if side == 0 else (j >= 0))
                def _(side=side, j=j):
                    climb(p, side, j).wait_send()

    def chunk(k):
        return pl.ds(k * cr, cr)

    ag_y, ag_c, ag_f, rs_r, rs_o, rs_y = ({} for _ in range(6))

    def gather_start(o, k):
        block = r.full.at[o, c, chunk(k)]
        ag_y[o, k] = start(block, block, r.ags_y.at[o, k], r.agr_y.at[o, k], {"ctx": ynb})
        ag_c[o, k] = start(block, block, r.ags_c.at[o, k], r.agr_c.at[o, k], {"ctx": sib})

    def forward(o, k):
        ag_y[o, k].wait_recv()
        block = r.full.at[o, ynb, chunk(k)]
        ag_f[o, k] = start(block, block, r.ags_f.at[o, k], r.agr_f.at[o, k], {"ctx": sib})

    def free(table, o, k):
        if o:
            links.sent(table[o - 1, k])

    def send_relay(o, k):
        rs_r[o, k] = start(r.snd_r.at[chunk(k)], r.rcv_r.at[chunk(k)],
                           r.rss_r.at[o, k], r.rsr_r.at[o, k], {"ctx": sib})

    def send_own(o, k):
        rs_o[o, k] = start(r.snd_o.at[chunk(k)], r.rcv_o.at[chunk(k)],
                           r.rss_o.at[o, k], r.rsr_o.at[o, k], {"ctx": sib})

    def relay(o, k):
        rs_r[o, k].wait_recv()
        free(rs_y, o, k)
        r.snd_y[chunk(k), :] = (
            r.yacc[chunk(k), :] + r.rcv_r[chunk(k), :].astype(F32)).astype(BF16)
        rs_y[o, k] = start(r.snd_y.at[chunk(k)], r.rcv_y.at[chunk(k)],
                           r.rss_y.at[o, k], r.rsr_y.at[o, k], {"ctx": ynb})

    def arrived(o, k):
        rs_o[o, k].wait_recv()
        rs_y[o, k].wait_recv()

    def summed(rows):
        return r.own[rows, :] + r.rcv_o[rows, :].astype(F32) + r.rcv_y[rows, :].astype(F32)

    def tiles(first, count, body):
        def step(t, carry):
            body(pl.ds(pl.multiple_of(first + t * TILE, TILE), TILE))
            return carry
        lax.fori_loop(0, count // TILE, step, 0)

    def fold(values):
        return jnp.sum(values.reshape(TILE // 8, 8, width), axis=0)

    def rows_of(b, r0=0, n=rows_own):
        return pl.ds(pl.multiple_of(b * rows_own + r0, cr), n)

    def both(parts):
        return jnp.concatenate(parts, axis=0)

    def far_blocks(o, k, product):
        free(rs_r, o, k)

        @block
        def _():
            value = product()
            r.snd_r[chunk(k), :] = value[:cr].astype(BF16)
            r.yacc[chunk(k), :] = value[cr:]
        send_relay(o, k)

    def near_block(o, product):
        for k in range(NCH):
            free(rs_o, o, k)

        @block
        def _():
            r.snd_o[...] = product().astype(BF16)
        for k in range(NCH):
            send_own(o, k)

    def own_block(product):
        @block
        def _():
            r.own[...] = product()

    def wait_near(o):
        for k in range(NCH):
            ag_c[o, k].wait_recv()

    def wait_far(o, k):
        ag_f[o, k].wait_recv()

    held = {}

    def cross_down():
        load_x.wait()
        held["crossed"] = start(
            r.down_v.at[pl.ds(half, half)], r.zbe.at[z, me], r.xd_s.at[0], r.xd_r.at[0],
            {"shard": other})
        r.zbe.at[z, me][...] = r.down_v[pl.ds(half, half), :]

    def clear():
        r.acc[...] = jnp.zeros_like(r.acc)
        r.bsum[...] = jnp.zeros_like(r.bsum)
        r.dk_acc[...] = jnp.zeros_like(r.dk_acc)
        r.dv_acc[...] = jnp.zeros_like(r.dv_acc)

    def tokens_start():
        held["first"] = start(r.xs.at[c], r.xs.at[c], r.xg_s.at[0], r.xg_r.at[0], {"ctx": ynb})
        held["near"] = start(r.xs.at[c], r.xs.at[c], r.xg_s.at[1], r.xg_r.at[1], {"ctx": sib})

    def tokens_pass():
        held["first"].wait_recv()
        held["passed"] = start(
            r.xs.at[ynb], r.xs.at[ynb], r.xg_s.at[2], r.xg_r.at[2], {"ctx": sib})

    def tokens_wait():
        held["near"].wait_recv()
        held["passed"].wait_recv()

    def project():
        for i in range(2):
            for h in range(heads):
                r.qv[i : i + 1, h * DH : (h + 1) * DH] = (
                    r.wq[0, 0, i * heads + h : i * heads + h + 1, 3 * cols : 3 * cols + DH].astype(F32))

        def rows_of_block(t, carry):
            rows = pl.ds(pl.multiple_of(t * rows_own, rows_own), rows_own)
            project_heads(heads, r.xs[t], rows, r.wq[...].reshape(width, r.wq.shape[3]),
                          r.qv, r.q, r.k, r.v)
            return carry

        lax.fori_loop(0, 4, rows_of_block, 0)

    def attend(b):
        @block
        def _():
            attend_rows(heads, pl.multiple_of(b * rows_own, rows_own), rows_own, lengths, slopes,
                        r.q, r.k, r.v, r.probs, r.mixed, r.far)

    def unpack_out():
        for s in range(2):
            for j in range(4):
                place = s * 4 + j
                r.w_out[pl.ds(place * piece, piece), :] = r.wo[s, j, 0:piece, 0:cols]
                row = piece + 2 * thirds
                r.vec[0:6, place * piece : (place + 1) * piece] = (
                    r.wo[s, j, row : row + 6, 0:piece].astype(F32))
        for i in range(2):
            for t in range(thirds):
                row = piece + i * thirds + t
                r.vec[6 + i : 7 + i, t * span : (t + 1) * span] = r.wo[0, 0, row : row + 1, :].astype(F32)

    def out_project(b):
        return dot_nt(r.mixed[rows_of(b), :], r.w_out[...])

    def out_far():
        @block
        def _():
            r.snd_r[...] = out_project(dia).astype(BF16)
        for k in range(NCH):
            send_relay(0, k)

    def out_cross():
        @block
        def _():
            r.yacc[...] = out_project(ynb)

    def out_near():
        near_block(0, lambda: out_project(sib))

    def out_own():
        own_block(lambda: out_project(c))

    def norm_one(rows):
        res = r.xs[c, rows, :].astype(F32) + summed(rows) + r.vec[4:5, :]
        center = res - jnp.mean(res, axis=-1, keepdims=True)
        scale = lax.rsqrt(jnp.mean(center * center, axis=-1, keepdims=True) + 1e-12)
        zh = center * scale
        value = zh * r.vec[0:1, :] + r.vec[2:3, :]
        r.zh1[rows, :] = zh
        r.r1[rows, :] = scale
        r.normed[rows, :] = value
        r.full[0, c, rows, :] = value.astype(BF16)

    def norm_one_chunk(k):
        arrived(0, k)
        tiles(k * cr, cr, norm_one)
        gather_start(0, k)

    def matrix(i):
        return r.w[i].reshape(width, width)

    def units_forward(b, r0, n):
        rows_in = r.full[0, b, pl.ds(r0, n), :]
        r.fa[pl.ds(0, n), :] = dot(rows_in, matrix(0))
        r.fb[pl.ds(0, n), :] = dot(rows_in, matrix(1))

        def units(rows):
            g = r.fa[rows, :] + r.vec[6:7, :]
            u = r.fb[rows, :] + r.vec[7:8, :]
            phi = 0.5 * (1.0 + lax.erf(g * (1.0 / math.sqrt(2.0))))
            gelu = g * phi
            slope = phi + g * jnp.exp(-0.5 * g * g) * (1.0 / math.sqrt(2.0 * math.pi))
            to = pl.ds(pl.multiple_of(r0 + rows.start, TILE), TILE)
            r.act[b, to, :] = gelu.astype(BF16)
            r.pull[b, to, :] = (u * slope).astype(BF16)
            r.hid[b, to, :] = (gelu * u).astype(BF16)

        tiles(0, n, units)

    def hid_rows(b, r0, n):
        return r.hid[b, pl.ds(r0, n), :]

    def down(rows):
        return dot_nt(rows, matrix(2))

    def units_backward(blocks, r0, n):
        def rows_at(ref, b):
            return ref[b, pl.ds(r0, n), :]

        def gather(ref):
            return both([rows_at(ref, b) for b in blocks]) if len(blocks) > 1 else rows_at(ref, blocks[0])

        r.fa[pl.ds(0, n * len(blocks)), :] = dot(gather(r.full.at[1]), matrix(2))
        for i, b in enumerate(blocks):
            def units(rows, b=b, i=i):
                dh = r.fa[rows, :]
                to = pl.ds(pl.multiple_of(r0 - i * n + rows.start, TILE), TILE)
                dg = (dh * r.pull[b, to, :].astype(F32)).astype(BF16)
                du = (dh * r.act[b, to, :].astype(F32)).astype(BF16)
                r.pull[b, to, :] = dg
                r.act[b, to, :] = du
                r.bsum[0] += fold(dg.astype(F32))
                r.bsum[1] += fold(du.astype(F32))

            tiles(i * n, n, units)
        return dot_nt(gather(r.pull), matrix(0)) + dot_nt(gather(r.act), matrix(1))

    def down_far(k):
        far_blocks(1, k, lambda: down(both([hid_rows(dia, k * cr, cr), hid_rows(ynb, k * cr, cr)])))

    def down_near():
        near_block(1, lambda: down(hid_rows(sib, 0, rows_own)))

    def down_own():
        own_block(lambda: down(hid_rows(c, 0, rows_own)))

    def norm_two(rows):
        res = r.normed[rows, :] + (summed(rows) + r.vec[5:6, :])
        center = res - jnp.mean(res, axis=-1, keepdims=True)
        scale = lax.rsqrt(jnp.mean(center * center, axis=-1, keepdims=True) + 1e-12)
        zh = center * scale
        r.lout[z, rows, :] = (zh * r.vec[1:2, :] + r.vec[3:4, :]).astype(BF16)
        up = r.cot[rows, :].astype(F32)
        t = up * r.vec[1:2, :]
        d = scale * (t - jnp.mean(t, axis=-1, keepdims=True)
                     - zh * jnp.mean(t * zh, axis=-1, keepdims=True))
        r.normed[rows, :] = d
        low = d.astype(BF16)
        r.full[1, c, rows, :] = low
        r.acc[1] += fold(up * zh)
        r.acc[3] += fold(up)
        r.acc[5] += fold(low.astype(F32))

    def norm_two_chunk(k):
        arrived(1, k)
        tiles(k * cr, cr, norm_two)
        gather_start(1, k)

    line_out = LineGather(r.lout, r.ls, r.lr)
    line_in = LineRelay(r.input_grad, r.lu, r.ld, r.li)

    def line_out_hop(d):
        line_out.hop(d)

    def line_in_hop(d, h):
        line_in.hop(d, h)

    def back_own():
        own_block(lambda: units_backward([c], 0, rows_own))

    def back_near():
        near_block(2, lambda: units_backward([sib], 0, rows_own))

    def back_far(k):
        far_blocks(2, k, lambda: units_backward([dia, ynb], k * cr, cr))

    def flat(ref):
        return ref[...].reshape(length, ref.shape[-1])

    def put(i, left, right):
        @block
        def _():
            r.w[i] = dot_tn(flat(left), flat(right)).astype(BF16).reshape(r.w.shape[1:])

    def put_down():
        for p in range(3):
            shard_drain(p)
        put(2, r.full.at[1], r.hid)

    def put_gate():
        put(0, r.full.at[0], r.pull)

    def put_up():
        put(1, r.full.at[0], r.act)

    def norm_back(rows):
        dn = summed(rows) + r.normed[rows, :]
        zh = r.zh1[rows, :]
        t = dn * r.vec[0:1, :]
        d = r.r1[rows, :] * (t - jnp.mean(t, axis=-1, keepdims=True)
                             - zh * jnp.mean(t * zh, axis=-1, keepdims=True))
        r.zh1[rows, :] = d
        low = d.astype(BF16)
        r.full[2, c, rows, :] = low
        r.acc[0] += fold(dn * zh)
        r.acc[2] += fold(dn)
        r.acc[4] += fold(low.astype(F32))

    def norm_back_chunk(k):
        arrived(2, k)
        tiles(k * cr, cr, norm_back)
        gather_start(2, k)

    def back_rows(b):
        @block
        def _():
            r.dmixed[rows_of(b), :] = dot(r.full[2, b], r.w_out[...]).astype(BF16)
            attend_back(heads, rows_of(b), r.dmixed, r.mixed, r.probs, r.q, r.k, r.v,
                        r.dqkv, r.dk_acc, r.dv_acc)

    def tiny_first():
        for i in range(6):
            r.tiny[0, i : i + 1, :] = jnp.sum(r.acc[i], axis=0, keepdims=True)
        held["tiny"] = start(r.tiny.at[0], r.tiny.at[1], r.tiny_s.at[0], r.tiny_r.at[0], {"ctx": sib})

    def tiny_second():
        held["tiny"].wait_recv()
        r.tiny[2] = r.tiny[0] + r.tiny[1]
        held["tiny_y"] = start(r.tiny.at[2], r.tiny.at[3], r.tiny_s.at[1], r.tiny_r.at[1], {"ctx": ynb})

    def spread():
        @block
        def _():
            spread_heads(heads, r.dqkv, r.dk_acc, r.dv_acc)

    def into_input(rows):
        return dot_nt(rows, r.wq[...].reshape(width, r.wq.shape[3])[:, : 3 * cols])

    def input_far(k):
        far_blocks(3, k, lambda: into_input(both([
            r.dqkv[rows_of(dia, k * cr, cr), :], r.dqkv[rows_of(ynb, k * cr, cr), :]])))

    def input_near():
        near_block(3, lambda: into_input(r.dqkv[rows_of(sib), :]))

    def input_own():
        own_block(lambda: into_input(r.dqkv[rows_of(c), :]))

    def projection_gradients():
        held["tiny_y"].wait_recv()
        norms = r.tiny[2] + r.tiny[3]
        bias = jnp.sum(r.dqkv[...].astype(F32), axis=0, keepdims=True)
        r.extra[...] = jnp.zeros_like(r.extra)
        r.extra[0:1, 0:cols] = bias[:, :cols]
        r.extra[0:1, cols : 2 * cols] = bias[:, 2 * cols :]
        for i in range(2):
            r.extra[1 + i : 2 + i, :] = jnp.sum(r.bsum[i], axis=0, keepdims=True)
        r.extra[3:9, :] = norms[0:6, :]
        low = r.extra[...].astype(BF16)
        x_all = flat(r.xs)
        for i in range(4):
            lanes = slice(i * cols, (i + 1) * cols)
            if i < 3:
                value = dot_tn(x_all, r.dqkv[:, lanes])
            else:
                value = dot_tn(flat(r.full.at[2]), r.mixed[...])
            value = value.astype(BF16)
            for s in range(2):
                for j in range(4):
                    first_row = (s * 4 + j) * piece
                    r.g0[s, j, 0:piece, lanes] = value[first_row : first_row + piece]
        for s in range(2):
            for j in range(4):
                r.g0[s, j, piece:, :] = low

    def input_chunk(k):
        arrived(3, k)
        r.input_grad[z, chunk(k), :] = (summed(chunk(k)) + r.zh1[chunk(k), :]).astype(BF16)

    save_out = pltpu.make_async_copy(r.lout, lout, r.save.at[0])
    save_in = pltpu.make_async_copy(r.input_grad, input_grad, r.save.at[1])

    def save_out_start():
        save_out.start()

    def save_in_start():
        save_in.start()

    def cot_wait():
        load_c.wait()

    def drain():
        save_out.wait()
        save_in.wait()
        line_out.drain()
        line_in.drain()
        for p in range(4):
            grad_drain(p)
        chain_drain()
        for p in index:
            hop_drain(p)
        for p in ("q", "o"):
            shard_drain(p)
        links.drain()

    cross_down()
    hop("q", 0)
    tokens_start()
    hop("q", 1)
    hop("q", 2)
    clear()
    hop("o", 0)
    tokens_pass()
    to_shard_if("q", 1, 1)
    to_shard_if("q", 0, 0)
    hop(0, 0)
    hop("o", 1)
    hop("o", 2)
    hop("q", 3)
    to_shard_if("q", 3, 3)
    to_shard_if("q", 2, 2)
    hop(0, 1)
    hop("o", 3)
    to_shard("o")
    hop(0, 2)
    hop(1, 0)
    tokens_wait()
    complete("q")
    project()
    attend(dia)
    hop(2, 0)
    hop(0, 3)
    to_shard_if(0, 3, 3)
    to_shard_if(1, 0, 0)
    to_shard_if(0, 1, 1)
    complete("o")
    to_shard_if(0, 0, 0)
    unpack_out()
    out_far()
    to_shard_if(0, 2, 2)
    hop(1, 1)
    hop(1, 2)
    attend(ynb)
    out_cross()
    relay(0, 1)
    relay(0, 0)
    attend(sib)
    to_shard_if(1, 2, 2)
    relay(0, 3)
    relay(0, 2)
    out_near()
    attend(c)
    hop(3, 0)
    to_shard_if(2, 0, 0)
    out_own()
    hop(2, 1)
    hop(1, 3)
    norm_one_chunk(0)
    to_shard_if(1, 3, 3)
    norm_one_chunk(1)
    hop(2, 2)
    hop(2, 3)
    to_shard_if(2, 2, 2)
    norm_one_chunk(2)
    to_shard_if(2, 3, 3)
    to_shard_if(1, 1, 1)
    norm_one_chunk(3)
    wait_near(0)
    complete(0)
    to_shard_if(2, 1, 1)
    hop(3, 1)
    cot_wait()
    forward(0, 1)
    forward(0, 0)
    hop(3, 2)
    complete(1)
    units_forward(c, 0, rows_own)
    forward(0, 2)
    forward(0, 3)
    hop(3, 3)
    wait_far(0, 1)
    units_forward(sib, 0, rows_own)
    units_forward(ynb, 0, rows_own)
    wait_far(0, 0)
    complete(2)
    wait_far(0, 2)
    wait_far(0, 3)
    units_forward(dia, 0, rows_own)
    complete(3)
    down_far(0)
    down_far(1)
    relay(1, 0)
    down_far(2)
    relay(1, 1)
    down_far(3)
    relay(1, 2)
    down_near()
    down_own()
    relay(1, 3)
    norm_two_chunk(0)
    norm_two_chunk(1)
    norm_two_chunk(2)
    norm_two_chunk(3)
    line_out_hop(0)
    back_own()
    wait_near(1)
    forward(1, 0)
    back_near()
    forward(1, 1)
    wait_far(1, 0)
    back_far(0)
    forward(1, 3)
    forward(1, 2)
    wait_far(1, 1)
    back_far(1)
    wait_far(1, 2)
    relay(2, 0)
    back_far(2)
    wait_far(1, 3)
    relay(2, 1)
    back_far(3)
    put_down()
    relay(2, 2)
    grad_to_shard(3)
    chain(0)
    relay(2, 3)
    norm_back_chunk(0)
    put_gate()
    norm_back_chunk(1)
    grad_to_shard(1)
    norm_back_chunk(2)
    put_up()
    grad_to_shard(2)
    norm_back_chunk(3)
    tiny_first()
    forward(2, 0)
    wait_near(2)
    back_rows(c)
    back_rows(sib)
    grad_to_owner(3, 0)
    grad_to_owner(3, 1)
    forward(2, 1)
    chain(1)
    forward(2, 2)
    grad_to_owner(3, 3)
    grad_to_owner(3, 2)
    forward(2, 3)
    back_rows(ynb)
    chain(2)
    wait_far(2, 1)
    line_out_hop(2)
    grad_to_owner(1, 0)
    wait_far(2, 0)
    wait_far(2, 3)
    wait_far(2, 2)
    back_rows(dia)
    chain(3)
    spread()
    grad_hop(3, 0)
    tiny_second()
    grad_to_owner(1, 1)
    input_far(0)
    input_far(1)
    input_far(2)
    chain(4)
    grad_to_owner(1, 2)
    input_far(3)
    grad_hop(3, 1)
    relay(3, 1)
    grad_to_owner(1, 3)
    grad_hop(1, 0)
    relay(3, 0)
    projection_gradients()
    grad_to_shard(0)
    chain(5)
    input_near()
    relay(3, 3)
    relay(3, 2)
    grad_hop(3, 2)
    chain_end()
    input_own()
    grad_hop(1, 1)
    input_chunk(0)
    input_chunk(1)
    line_in_hop(0, 0)
    grad_to_owner(2, 1)
    input_chunk(2)
    grad_hop(3, 3)
    input_chunk(3)
    line_out_hop(3)
    line_in_hop(0, 1)
    line_in_hop(1, 0)
    line_in_hop(1, 1)
    chain_across()
    grad_to_owner(2, 0)
    grad_to_owner(2, 3)
    grad_to_owner(2, 2)
    grad_to_owner(0, 0)
    grad_hop(1, 2)
    grad_hop(2, 0)
    grad_hop(2, 1)
    grad_to_owner(0, 3)
    grad_to_owner(0, 2)
    line_in_hop(2, 0)
    line_out_hop(1)
    grad_to_owner(0, 1)
    grad_hop(0, 0)
    save_out_start()
    grad_hop(0, 1)
    line_in_hop(2, 1)
    grad_hop(2, 2)
    grad_hop(1, 3)
    line_in_hop(3, 1)
    line_in_hop(3, 0)
    save_in_start()
    chain_total()
    grad_hop(0, 2)
    grad_hop(2, 3)
    grad_hop(0, 3)
    drain()


def finish(
    lout, input_low, out0, outr,
    o_lout, o_in, o_qkv, o_qvb, o_out, o_geglu, o_gb, o_down, o_gain, o_shift, o_ob,
    low, narrow, wide, first, rest, v_qkv, v_qvb, v_out, v_gain, v_shift, v_ob, sem_in, sem_out,
):
    piece = outr.shape[1]
    cols = o_qkv.shape[2]
    blocks = narrow.shape[0]
    started = []

    def save(src, dst):
        one = pltpu.make_async_copy(src, dst, sem_out.at[len(started)])
        one.start()
        started.append(one)

    pairs = [(out0, first), (outr, rest)]
    pairs += [(input_low.at[i], narrow.at[i]) for i in range(blocks)]
    pairs += [(lout.at[i], low.at[i]) for i in range(blocks)]
    loads = [pltpu.make_async_copy(src, dst, sem_in.at[i]) for i, (src, dst) in enumerate(pairs)]
    for one in loads:
        one.start()
    loads[0].wait()
    for i in range(3):
        v_qkv[i] = first[0:piece, i * cols : (i + 1) * cols]
    v_out[...] = first[0:piece, 3 * cols : 4 * cols].T
    v_qvb[0:1, :] = first[piece : piece + 1, 0:cols]
    v_qvb[1:2, :] = first[piece : piece + 1, cols : 2 * cols]
    place = lax.axis_index("shard") * 4 + lax.axis_index("ctx")
    for s in range(8):
        @pl.when(place == s)
        def _(s=s):
            lanes = slice(s * piece, (s + 1) * piece)
            v_gain[...] = first[piece + 3 : piece + 5, lanes]
            v_shift[...] = first[piece + 5 : piece + 7, lanes]
            v_ob[...] = first[piece + 7 : piece + 9, lanes]
    o_gb[...] = first[piece + 1 : piece + 3, :]
    for src, dst in ((v_qkv, o_qkv), (v_out, o_out), (v_qvb, o_qvb),
                     (v_gain, o_gain), (v_shift, o_shift), (v_ob, o_ob)):
        save(src, dst)
    loads[1].wait()
    save(rest.at[pl.ds(0, 2)], o_geglu)
    save(rest.at[2], o_down)
    for i in range(blocks):
        loads[2 + i].wait()
        wide[i] = narrow[i].astype(F32)
        save(wide.at[i], o_in.at[i])
    for i in range(blocks):
        loads[2 + blocks + i].wait()
        save(low.at[i], o_lout.at[i])
    for one in started:
        one.wait()


def middle(
    x, cot, mixed, w0, w, vec,
    lout, dres1, grads, gout, dmixed, small,
    w_out, full, act, pull, hid, dgt, dup,
    snd_r, snd_o, snd_y, rcv_r, rcv_o, rcv_y,
    own, yacc, fa, fb, normed, zh1, r1, dres2, acc, bsum, tiny,
    ags_y, agr_y, ags_c, agr_c, ags_f, agr_f,
    rss_r, rsr_r, rss_o, rsr_o, rss_y, rsr_y, tiny_s, tiny_r, ls, lr,
):
    rows_own = x.shape[0]
    width = x.shape[1]
    cr = rows_own // NCH
    c, sib, ynb, dia = places()
    z = lax.axis_index("tp")
    tp = lout.shape[0]
    greet([{"ctx": sib}, {"ctx": ynb}] + [{"tp": (z + d) % tp} for d in range(1, tp)])
    line = LineGather(lout, ls, lr)

    started = []

    def remote(src, dst, send, recv, peer):
        return pltpu.make_async_remote_copy(
            src_ref=src, dst_ref=dst, send_sem=send, recv_sem=recv,
            device_id={"ctx": peer}, device_id_type=MESH,
        )

    def chunk(k):
        return pl.ds(k * cr, cr)

    ag_y, ag_c, ag_f, rs_r, rs_o, rs_y = ({} for _ in range(6))

    def start(table, key, copy):
        copy.start()
        table[key] = copy
        started.append(copy)

    def gather_start(o, k):
        piece = full.at[o, c, chunk(k)]
        start(ag_y, (o, k), remote(piece, piece, ags_y.at[o, k], agr_y.at[o, k], ynb))
        start(ag_c, (o, k), remote(piece, piece, ags_c.at[o, k], agr_c.at[o, k], sib))

    def forward(o, k):
        ag_y[o, k].wait_recv()
        piece = full.at[o, ynb, chunk(k)]
        start(ag_f, (o, k), remote(piece, piece, ags_f.at[o, k], agr_f.at[o, k], sib))

    def send_relay(o, k):
        start(rs_r, (o, k), remote(
            snd_r.at[o, chunk(k)], rcv_r.at[o, chunk(k)], rss_r.at[o, k], rsr_r.at[o, k], sib))

    def send_own(o, k):
        start(rs_o, (o, k), remote(
            snd_o.at[o, chunk(k)], rcv_o.at[o, chunk(k)], rss_o.at[o, k], rsr_o.at[o, k], sib))

    def relay(o, k):
        rs_r[o, k].wait_recv()
        snd_y[o, chunk(k), :] = (yacc[chunk(k), :] + rcv_r[o, chunk(k), :].astype(F32)).astype(BF16)
        start(rs_y, (o, k), remote(
            snd_y.at[o, chunk(k)], rcv_y.at[o, chunk(k)], rss_y.at[o, k], rsr_y.at[o, k], ynb))

    def arrived(o, k):
        rs_o[o, k].wait_recv()
        rs_y[o, k].wait_recv()

    def tiles(first, count, body):
        def step(t, carry):
            body(pl.ds(pl.multiple_of(first + t * TILE, TILE), TILE))
            return carry
        lax.fori_loop(0, count // TILE, step, 0)

    def summed(o, rows):
        return own[rows, :] + rcv_o[o, rows, :].astype(F32) + rcv_y[o, rows, :].astype(F32)

    def fold(values):
        return jnp.sum(values.reshape(TILE // 8, 8, width), axis=0)

    acc[...] = jnp.zeros_like(acc)
    bsum[...] = jnp.zeros_like(bsum)
    w_out[...] = w0[:, 3 * mixed.shape[2] : 4 * mixed.shape[2]]

    def project(b, r0, n):
        return dot_nt(mixed[b, pl.ds(r0, n), :], w_out[...])

    for k in range(NCH):
        snd_r[0, chunk(k), :] = project(dia, k * cr, cr).astype(BF16)
        send_relay(0, k)
        yacc[chunk(k), :] = project(ynb, k * cr, cr)
        if k:
            relay(0, k - 1)
    relay(0, NCH - 1)
    for k in range(NCH):
        snd_o[0, chunk(k), :] = project(sib, k * cr, cr).astype(BF16)
        send_own(0, k)
    own[...] = project(c, 0, rows_own)

    def norm_one(rows):
        res = x[rows, :].astype(F32) + summed(0, rows) + vec[4:5, :]
        center = res - jnp.mean(res, axis=-1, keepdims=True)
        r = lax.rsqrt(jnp.mean(center * center, axis=-1, keepdims=True) + 1e-12)
        zh = center * r
        out = zh * vec[0:1, :] + vec[2:3, :]
        zh1[rows, :] = zh
        r1[rows, :] = r
        normed[rows, :] = out
        full[0, c, rows, :] = out.astype(BF16)

    for k in range(NCH):
        arrived(0, k)
        tiles(k * cr, cr, norm_one)
        gather_start(0, k)

    def mlp_forward(b, r0, n):
        rows_in = full[0, b, pl.ds(r0, n), :]
        fa[pl.ds(0, n), :] = dot(rows_in, w[0])
        fb[pl.ds(0, n), :] = dot(rows_in, w[1])

        def units(rows):
            g = fa[rows, :] + vec[6:7, :]
            u = fb[rows, :] + vec[7:8, :]
            phi = 0.5 * (1.0 + lax.erf(g * (1.0 / math.sqrt(2.0))))
            gelu = g * phi
            slope = phi + g * jnp.exp(-0.5 * g * g) * (1.0 / math.sqrt(2.0 * math.pi))
            out = pl.ds(pl.multiple_of(r0 + rows.start, TILE), TILE)
            act[b, out, :] = gelu.astype(BF16)
            pull[b, out, :] = (u * slope).astype(BF16)
            hid[b, out, :] = (gelu * u).astype(BF16)

        tiles(0, n, units)
        return dot_nt(hid[b, pl.ds(r0, n), :], w[2])

    def mlp_backward(b, r0, n):
        fa[pl.ds(0, n), :] = dot(full[1, b, pl.ds(r0, n), :], w[2])

        def units(rows):
            dh = fa[rows, :]
            out = pl.ds(pl.multiple_of(r0 + rows.start, TILE), TILE)
            dg = (dh * pull[b, out, :].astype(F32)).astype(BF16)
            du = (dh * act[b, out, :].astype(F32)).astype(BF16)
            dgt[b, out, :] = dg
            dup[b, out, :] = du
            bsum[0] += fold(dg.astype(F32))
            bsum[1] += fold(du.astype(F32))

        tiles(0, n, units)
        return dot_nt(dgt[b, pl.ds(r0, n), :], w[0]) + dot_nt(dup[b, pl.ds(r0, n), :], w[1])

    def exchange(o, piece):
        own[...] = piece(c, 0, rows_own)
        for k in range(NCH):
            ag_c[o - 1, k].wait_recv()
        snd_o[o] = piece(sib, 0, rows_own).astype(BF16)
        for k in range(NCH):
            send_own(o, k)
        for k in range(NCH):
            forward(o - 1, k)
            yacc[chunk(k), :] = piece(ynb, k * cr, cr)
            ag_f[o - 1, k].wait_recv()
            snd_r[o, chunk(k), :] = piece(dia, k * cr, cr).astype(BF16)
            send_relay(o, k)
            if k:
                relay(o, k - 1)
        relay(o, NCH - 1)

    exchange(1, mlp_forward)

    def norm_two(rows):
        res = normed[rows, :] + (summed(1, rows) + vec[5:6, :])
        center = res - jnp.mean(res, axis=-1, keepdims=True)
        r = lax.rsqrt(jnp.mean(center * center, axis=-1, keepdims=True) + 1e-12)
        zh = center * r
        lout[z, rows, :] = (zh * vec[1:2, :] + vec[3:4, :]).astype(BF16)
        up = cot[rows, :].astype(F32)
        t = up * vec[1:2, :]
        d = r * (t - jnp.mean(t, axis=-1, keepdims=True)
                 - zh * jnp.mean(t * zh, axis=-1, keepdims=True))
        dres2[rows, :] = d
        low = d.astype(BF16)
        full[1, c, rows, :] = low
        acc[1] += fold(up * zh)
        acc[3] += fold(up)
        acc[5] += fold(low.astype(F32))

    for k in range(NCH):
        arrived(1, k)
        tiles(k * cr, cr, norm_two)
        gather_start(1, k)

    line.hop(0)
    exchange(2, mlp_backward)
    line.hop(1)

    def flat(ref):
        return ref[...].reshape(4 * rows_own, ref.shape[-1])

    hid_all = flat(hid)
    d_all = full[1].reshape(4 * rows_own, width)
    grads[2] = dot_tn(d_all, hid_all).astype(BF16)
    n_all = full[0].reshape(4 * rows_own, width)
    grads[0] = dot_tn(n_all, flat(dgt)).astype(BF16)
    grads[1] = dot_tn(n_all, flat(dup)).astype(BF16)

    line.hop(2)

    def norm_back(rows):
        dn = summed(2, rows) + dres2[rows, :]
        zh = zh1[rows, :]
        t = dn * vec[0:1, :]
        d = r1[rows, :] * (t - jnp.mean(t, axis=-1, keepdims=True)
                           - zh * jnp.mean(t * zh, axis=-1, keepdims=True))
        dres1[rows, :] = d
        low = d.astype(BF16)
        full[2, c, rows, :] = low
        acc[0] += fold(dn * zh)
        acc[2] += fold(dn)
        acc[4] += fold(low.astype(F32))

    for k in range(NCH):
        arrived(2, k)
        tiles(k * cr, cr, norm_back)
        gather_start(2, k)

    for i in range(6):
        tiny[0, i : i + 1, :] = jnp.sum(acc[i], axis=0, keepdims=True)
    for i in range(2):
        small[6 + i : 7 + i, :] = jnp.sum(bsum[i], axis=0, keepdims=True)
    tiny_copies = []
    for step, peer in enumerate((sib, ynb)):
        copy = remote(tiny.at[2 * step], tiny.at[2 * step + 1], tiny_s.at[step], tiny_r.at[step], peer)
        copy.start()
        started.append(copy)
        tiny_copies.append(copy)
        if step == 0:
            def unproject(b, r0, n):
                return dot(full[2, b, pl.ds(r0, n), :], w_out[...]).astype(BF16)
            dmixed[c] = unproject(c, 0, rows_own)
            for k in range(NCH):
                ag_c[2, k].wait_recv()
            dmixed[sib] = unproject(sib, 0, rows_own)
        copy.wait_recv()
        total = tiny[2 * step] + tiny[2 * step + 1]
        if step == 0:
            tiny[2] = total
        else:
            small[0:6, :] = total[0:6, :]
    for k in range(NCH):
        forward(2, k)
        dmixed[ynb, chunk(k), :] = unproject(ynb, k * cr, cr)
    for k in range(NCH):
        ag_f[2, k].wait_recv()
        dmixed[dia, chunk(k), :] = unproject(dia, k * cr, cr)
    gout[...] = dot_tn(full[2].reshape(4 * rows_own, width), flat(mixed)).astype(BF16)
    line.hop(3)
    line.drain()
    for copy in started:
        copy.wait_send()


def sds(shape, dtype):
    return jax.ShapeDtypeStruct(shape, dtype)


def smem():
    return pl.BlockSpec(memory_space=pltpu.SMEM)


def on_device(
    tokens_in, qkv_weight, qv_bias, out_weight, geglu_weight, geglu_bias, down_weight,
    norm_gains, norm_biases, out_biases, doc_lengths, cotangent,
):
    seqs, rows, width = tokens_in.shape
    group = lax.axis_size("ctx")
    tp = lax.axis_size("tp")
    shards = lax.axis_size("shard")
    z = lax.axis_index("tp")
    c = lax.axis_index("ctx")
    assert group == 4 and tp == 4 and seqs == tp
    length = group * rows
    part_rows = qkv_weight.shape[1]
    cols = qkv_weight.shape[2]
    heads = cols // DH
    units = geglu_weight.shape[2]
    assert units == width and 4 * cols == width and H == heads * tp

    me = lax.axis_index("shard") * group + c
    dma = lambda *shape: pltpu.SemaphoreType.DMA(shape)
    slopes = jnp.asarray([alibi_slopes(H)], F32)
    head_shape = sds((heads, length, DH), BF16)
    lengths = lax.dynamic_slice_in_dim(doc_lengths, z, 1, 0)
    block = (rows, width)
    stack = (group, rows, width)
    if shards == 2 and part_rows % 32 == 0:
        vm = pltpu.VMEM
        wide = part_rows + 16
        pieces = lambda n: (vm((n, wide, width), BF16), vm((2, n, part_rows, width), BF16))
        scratch = dict(
            pq=vm((part_rows, 640), BF16), po=vm((wide, 256), BF16),
            lout=vm((tp,) + block, BF16), input_grad=vm((tp,) + block, BF16), save=dma(2),
            zbq=vm((tp, part_rows, 640), BF16), zbo=vm((tp, wide, 256), BF16),
            zbr=vm((2, tp, part_rows, width), BF16),
            zbd=vm((tp, part_rows // 2, width), BF16), zbe=vm((tp, 2, part_rows // 2, width), BF16),
            xd_s=dma(1), xd_r=dma(1),
            load=dma(6), qkv_v=vm((3, part_rows, cols), BF16), out_v=vm((cols, part_rows), BF16),
            down_v=vm((part_rows, width), BF16), geglu_v=vm((2, part_rows, width), BF16), cb=vm((2, 2, group, part_rows // 2, width), BF16),
            yd=vm((2, part_rows // 2, width), BF16), xd=vm((part_rows // 2, width), BF16),
            ch_s=dma(2, 4), ch_r=dma(2, 4), cy_s=dma(4), cy_r=dma(1), cx_s=dma(1), cx_r=dma(1),
            cot=vm(block, BF16), xs=vm(stack, BF16),
            wq=vm((2, group, part_rows, 640), BF16), wo=vm((2, group, wide, 256), BF16),
            g0=vm((2, group, wide, width), BF16), w=vm((3, 2, group, part_rows, width), BF16),
            w_out=vm((width, cols), BF16),
            qv=vm((2, cols), F32), vec=vm((8, width), F32), extra=vm((16, width), F32),
            probs=vm((heads, length, length), BF16),
            q=vm((heads, length, DH), BF16), k=vm((heads, length, DH), BF16),
            v=vm((heads, length, DH), BF16), far=vm((rows, length), F32),
            mixed=vm((length, cols), BF16), dmixed=vm((length, cols), BF16),
            full=vm((3,) + stack, BF16), act=vm(stack, BF16), pull=vm(stack, BF16),
            hid=vm(stack, BF16),
            **{n: vm(block, BF16) for n in ("snd_r", "snd_o", "snd_y", "rcv_r", "rcv_o", "rcv_y")},
            **{n: vm(block, F32) for n in ("own", "yacc", "fa", "fb", "normed", "zh1")},
            r1=vm((rows, 1), F32), acc=vm((6, 8, width), F32), bsum=vm((2, 8, width), F32),
            tiny=vm((4, 8, width), F32),
            dqkv=vm((length, 3 * cols), BF16),
            dk_acc=vm((heads, DH, length), F32), dv_acc=vm((heads, DH, length), F32),
            xg_s=dma(3), xg_r=dma(3),
            **{n: dma(6, 4) for n in ("zu", "zd", "zu2", "zd2", "zr", "ys", "yr", "xs_s", "xs_r")},
            **{n: dma(4, 4) for n in ("gx_s", "gx_r", "gy_s", "gy_r",
                                      "gu_s", "gu_r", "gd_s", "gd_r")},
            **{n: dma(3, NCH) for n in ("ags_y", "agr_y", "ags_c", "agr_c", "ags_f", "agr_f")},
            **{n: dma(4, NCH) for n in ("rss_r", "rsr_r", "rss_o", "rsr_o", "rss_y", "rsr_y")},
            tiny_s=dma(2), tiny_r=dma(2), ls=dma(5), lr=dma(tp), lu=dma(2, tp), ld=dma(2, tp), li=dma(2, tp),
        )
        for n, count in (("xb", group), ("yb", group), ("rb", tp + 1)):
            scratch[n + "0"], scratch[n + "r"] = pieces(count)
            scratch[n + "h"] = vm((count, part_rows // 2, width), BF16)
        raw = pl.pallas_call(
            functools.partial(layer, tuple(scratch), heads),
            out_shape=[
                sds((tp,) + block, BF16), sds((tp,) + block, BF16),
                sds((wide, width), F32), sds((3, part_rows, width), F32),
            ],
            in_specs=[smem(), smem()] + [pl.BlockSpec(memory_space=pl.ANY)] * 6 + vmem(5),
            out_specs=[pl.BlockSpec(memory_space=pl.ANY)] * 2 + vmem(2),
            scratch_shapes=list(scratch.values()),
            compiler_params=pltpu.CompilerParams(
                collective_id=1, has_side_effects=True, vmem_limit_bytes=VMEM_MB * MB
            ),
            name="layer",
        )(
            lengths, slopes, tokens_in, cotangent, qkv_weight, out_weight, geglu_weight,
            down_weight.T, qv_bias, geglu_bias, norm_gains, norm_biases, out_biases,
        )
        res = pl.pallas_call(
            finish,
            out_shape=[
                sds((tp,) + block, BF16), sds((tp,) + block, F32),
                sds(qkv_weight.shape, F32), sds(qv_bias.shape, F32), sds(out_weight.shape, F32),
                sds(geglu_weight.shape, F32), sds(geglu_bias.shape, F32),
                sds(down_weight.shape[::-1], F32),
            ] + [sds(norm_gains.shape, F32)] * 3,
            in_specs=[pl.BlockSpec(memory_space=pl.ANY)] * 4,
            out_specs=(
                [pl.BlockSpec(memory_space=pl.ANY)] * 6 + vmem(1)
                + [pl.BlockSpec(memory_space=pl.ANY)] * 4
            ),
            scratch_shapes=[
                vm((tp,) + block, BF16), vm((tp,) + block, BF16), vm((tp,) + block, F32),
                vm((wide, width), F32), vm((3, part_rows, width), F32),
                vm(qkv_weight.shape, F32), vm(qv_bias.shape, F32), vm(out_weight.shape, F32),
            ] + [vm(norm_gains.shape, F32)] * 3 + [dma(2 + 2 * tp), dma(8 + 2 * tp)],
            compiler_params=pltpu.CompilerParams(vmem_limit_bytes=VMEM_MB * MB),
            name="finish",
        )(*raw)
        return (*res[:7], res[7].T, *res[8:])

    with jax.named_scope("pack_weights"):
        first = jnp.concatenate(
            [qkv_weight[0], qkv_weight[1], qkv_weight[2], out_weight.T], axis=1
        )
        own_norm = jnp.concatenate([norm_gains, norm_biases, out_biases], axis=0)
        parts = jnp.concatenate([first[None], geglu_weight, down_weight.T[None]], axis=0)
        own_bias = jnp.concatenate([qv_bias.reshape(1, -1), geglu_bias.reshape(1, -1)], axis=1)

    x_own = lax.dynamic_index_in_dim(tokens_in, z, 0, keepdims=False)
    cot_own = lax.dynamic_index_in_dim(cotangent, z, 0, keepdims=False)
    with jax.named_scope("gather_weights"):
        by_block = lax.all_gather(parts, "tp", axis=0)
        swapped = lax.all_to_all(by_block, "ctx", split_axis=0, concat_axis=0)
        w = lax.all_gather(swapped, "shard", axis=0)
        w = w.transpose(2, 0, 1, 3, 4).reshape(4, shards * group * part_rows, width)
        biases = lax.all_gather(own_bias, "tp", axis=0, tiled=True)
        biases = lax.dynamic_slice_in_dim(biases, c, 1, 0).astype(F32)
        norms = lax.all_gather(own_norm, ("shard", "ctx"), axis=1, tiled=True).astype(F32)
    qv = biases[:, : 2 * cols].reshape(2, cols)
    vec = jnp.concatenate([norms, biases[:, 2 * cols :].reshape(2, units)], axis=0)

    xs = lax.all_gather(x_own, "ctx", axis=0, tiled=True)

    mixed, probs, q, k, v = pl.pallas_call(
        functools.partial(attention_forward, heads),
        out_shape=[sds((length, cols), BF16), sds((heads, length, length), BF16)] + [head_shape] * 3,
        in_specs=[smem(), smem()] + vmem(3),
        out_specs=vmem(5),
        scratch_shapes=[pltpu.VMEM((256, length), F32)],
        compiler_params=pltpu.CompilerParams(vmem_limit_bytes=48 * MB),
        name="attention_forward",
    )(lengths, slopes, xs, w[0], qv)
    w0, w = w[0], w[1:]


    lout, dres1, grads, gout, dmixed, small = pl.pallas_call(
        middle,
        out_shape=[
            sds((tp,) + block, BF16), sds(block, F32), sds((3, width, width), BF16),
            sds((width, cols), BF16), sds((group, rows, cols), BF16), sds((8, width), F32),
        ],
        in_specs=vmem(6),
        out_specs=vmem(6),
        scratch_shapes=[
            pltpu.VMEM((width, cols), BF16), pltpu.VMEM((3,) + stack, BF16),
        ] + [pltpu.VMEM(stack, BF16)] * 5 + [pltpu.VMEM((3,) + block, BF16)] * 6 + [
            pltpu.VMEM(block, F32)
        ] * 6 + [
            pltpu.VMEM((rows, 1), F32), pltpu.VMEM(block, F32),
            pltpu.VMEM((6, 8, width), F32), pltpu.VMEM((2, 8, width), F32),
            pltpu.VMEM((4, 8, width), F32),
        ] + [dma(3, NCH)] * 12 + [dma(2)] * 2 + [dma(5), dma(tp)],
        compiler_params=pltpu.CompilerParams(
            collective_id=0, has_side_effects=True, vmem_limit_bytes=58 * MB
        ),
        name="middle",
    )(x_own, cot_own, mixed.reshape(group, rows, cols), w0, w, vec)

    grad_w, d_in, bias_grad = pl.pallas_call(
        functools.partial(attention_backward, heads),
        out_shape=[
            sds((width, 3 * cols), BF16), sds((length, width), BF16), sds((1, 3 * cols), F32)
        ],
        in_specs=vmem(8),
        out_specs=vmem(3),
        scratch_shapes=[
            pltpu.VMEM((length, 3 * cols), BF16),
            pltpu.VMEM((heads, DH, length), F32), pltpu.VMEM((heads, DH, length), F32),
        ],
        compiler_params=pltpu.CompilerParams(vmem_limit_bytes=48 * MB),
        name="attention_backward",
    )(dmixed.reshape(length, cols), mixed, probs, q, k, v, xs, w0)

    with jax.named_scope("outputs"):
        input_sum = lax.psum_scatter(d_in, "ctx", scatter_dimension=0, tiled=True)
        input_own = (input_sum.astype(F32) + dres1).astype(BF16)
        input_grad = lax.all_gather(input_own, "tp", axis=0).astype(F32)
        layer_out = lout

    with jax.named_scope("scatter_grads"):
        first_grad = jnp.concatenate([grad_w, gout], axis=1)
        packed = jnp.concatenate([first_grad[None], grads], axis=0)
        packed = packed.reshape(4, shards, group, part_rows, width).transpose(1, 2, 0, 3, 4)
        mine = lax.psum_scatter(packed, "shard", scatter_dimension=0, tiled=False)
        mine = lax.all_to_all(mine, "ctx", split_axis=0, concat_axis=0)
        mine = lax.psum_scatter(mine, "tp", scatter_dimension=0, tiled=False)
        mine = mine.astype(F32)
        grad_qkv = jnp.stack([mine[0, :, i * cols : (i + 1) * cols] for i in range(3)])
        grad_out = mine[0, :, 3 * cols :].T
        grad_geglu = mine[1:3]
        grad_down = mine[3].T
        col = jnp.concatenate(
            [bias_grad[:, :cols], bias_grad[:, 2 * cols :], small[6:7], small[7:8]], axis=1
        )
        col = lax.psum_scatter(
            jnp.zeros((group, col.shape[1]), F32) + jnp.where(
                jnp.arange(group)[:, None] == c, col, 0.0),
            "tp", scatter_dimension=0, tiled=True)
        col = lax.psum(col, ("shard", "ctx"))
        norm_grad = lax.psum(small[:6], ("shard", "tp"))
        norm_grad = lax.dynamic_slice_in_dim(norm_grad, me * part_rows, part_rows, 1)
    return (
        layer_out,
        input_grad,
        grad_qkv,
        col[:, : 2 * cols].reshape(2, cols),
        grad_out,
        grad_geglu,
        col[:, 2 * cols :].reshape(2, units),
        grad_down,
        norm_grad[0:2],
        norm_grad[2:4],
        norm_grad[4:6],
    )


def solution(mesh):
    in_specs = (
        P("shard", "ctx", None),
        P(None, ("shard", "ctx"), "tp"),
        P(None, "tp"),
        P("tp", ("shard", "ctx")),
        P(None, ("shard", "ctx"), "tp"),
        P(None, "tp"),
        P("tp", ("shard", "ctx")),
        P(None, ("shard", "ctx")),
        P(None, ("shard", "ctx")),
        P(None, ("shard", "ctx")),
        P("shard", None),
        P("shard", "ctx", None),
    )
    out_specs = (
        P("shard", "ctx", None),
        P("shard", "ctx", None),
        P(None, ("shard", "ctx"), "tp"),
        P(None, "tp"),
        P("tp", ("shard", "ctx")),
        P(None, ("shard", "ctx"), "tp"),
        P(None, "tp"),
        P("tp", ("shard", "ctx")),
        P(None, ("shard", "ctx")),
        P(None, ("shard", "ctx")),
        P(None, ("shard", "ctx")),
    )
    return jax.shard_map(
        on_device, mesh=mesh, in_specs=in_specs, out_specs=out_specs, check_vma=False
    )
```

```python
import functools
import math
import types

import jax
import jax.numpy as jnp
from jax import lax
from jax.experimental import pallas as pl
from jax.experimental.pallas import tpu as pltpu
from jax.sharding import PartitionSpec as P

H = 12
DH = 64
F32 = jnp.float32
BF16 = jnp.bfloat16
MESH = pl.DeviceIdType.MESH
NCH = 4
TILE = 32
MB = 1 << 20
VMEM_MB = 62
FRONT_CUT = 3
BACK_CUT = 3


def alibi_slopes(head_count):
    def power_slopes(head_total):
        first_slope = 2.0 ** (-8.0 / head_total)
        return [first_slope ** (counter + 1) for counter in range(head_total)]

    nearest = 2 ** int(math.floor(math.log2(head_count)))
    slope_list = power_slopes(nearest)
    return slope_list + power_slopes(2 * nearest)[0::2][: head_count - nearest]


def dot(left, right):
    return jnp.dot(left, right, preferred_element_type=F32)


def dot_nt(left, right):
    return lax.dot_general(left, right, (((1,), (1,)), ((), ())), preferred_element_type=F32)


def dot_tn(left, right):
    return lax.dot_general(left, right, (((0,), (0,)), ((), ())), preferred_element_type=F32)


def vmem(count):
    return [pl.BlockSpec(memory_space=pltpu.VMEM)] * count


def project_heads(heads, x_rows, rows, w, bias, q_out, k_out, v_out):
    cols = heads * DH
    for part, out in enumerate((q_out, k_out, v_out)):
        y = dot(x_rows, w[:, part * cols : (part + 1) * cols])
        if part != 1:
            y = y + bias[part // 2 : part // 2 + 1, :]
        y = y.astype(BF16)
        if part == 0:
            y = y * BF16(1.0 / math.sqrt(DH))
        for i in range(heads):
            out[i, rows, :] = y[:, i * DH : (i + 1) * DH]


def segments(lengths, row, pos):
    seg = jnp.zeros(pos.shape, jnp.int32)
    end = 0
    for k in range(lengths.shape[1]):
        end = end + lengths[row, k]
        seg = seg + (pos >= end).astype(jnp.int32)
    return seg


def head_slopes(heads):
    table = alibi_slopes(H)
    c = lax.axis_index("ctx")
    mine = []
    for i in range(heads):
        value = jnp.float32(table[i])
        for j in range(1, H // heads):
            value = jnp.where(c == j, jnp.float32(table[j * heads + i]), value)
        mine.append(value)
    return mine


def attend_rows(heads, start, step, lengths, row, q, k, v, probs, mixed, far):
    length = k.shape[1]
    slopes = head_slopes(heads)
    rows = pl.ds(start, step)
    key_pos = lax.broadcasted_iota(jnp.int32, (1, length), 1)
    pos = start + lax.broadcasted_iota(jnp.int32, (step, 1), 0)
    same = segments(lengths, row, pos) == segments(lengths, row, key_pos)
    far[...] = jnp.where(same, jnp.abs(pos - key_pos).astype(F32), 1e33)
    for i in range(heads):
        s = dot_nt(q[i, rows, :], k[i]) - slopes[i] * far[...]
        p = jnp.exp(s - jnp.max(s, axis=-1, keepdims=True))
        p = (p * (1.0 / jnp.sum(p, axis=-1, keepdims=True))).astype(BF16)
        probs[i, rows, :] = p
        mixed[rows, i * DH : (i + 1) * DH] = dot(p, v[i]).astype(BF16)


def attention_forward(
    heads, lengths, xs, w, bias, mixed, probs, q_out, k_out, v_out, far
):
    step = 256

    def project(r, carry):
        rows = pl.ds(pl.multiple_of(r * step, step), step)
        project_heads(heads, xs[rows, :], rows, w, bias, q_out, k_out, v_out)
        return carry

    def attend(r, carry):
        start = pl.multiple_of(r * step, step)
        attend_rows(
            heads, start, step, lengths, 0, q_out, k_out, v_out, probs, mixed, far)
        return carry

    lax.fori_loop(0, xs.shape[0] // step, project, 0)
    lax.fori_loop(0, xs.shape[0] // step, attend, 0)


def attend_back(heads, rows, dmixed, mixed, probs, q, k, v, dqkv, dk_acc, dv_acc):
    for i in range(heads):
        own = slice(i * DH, (i + 1) * DH)
        d_out = dmixed[rows, own]
        row_dot = jnp.sum(
            d_out.astype(F32) * mixed[rows, own].astype(F32), axis=-1, keepdims=True
        )
        p = probs[i, rows, :]
        dp = dot_nt(d_out, v[i])
        ds = (p.astype(F32) * (dp - row_dot)).astype(BF16)
        dqkv[rows, own] = (dot(ds, k[i]) * (1.0 / math.sqrt(DH))).astype(BF16)
        dk_acc[i] += dot_tn(q[i, rows, :], ds)
        dv_acc[i] += dot_tn(d_out, p)


def spread_heads(heads, dqkv, dk_acc, dv_acc):
    cols = heads * DH
    for i in range(heads):
        dqkv[:, cols + i * DH : cols + (i + 1) * DH] = dk_acc[i].T.astype(BF16)
        dqkv[:, 2 * cols + i * DH : 2 * cols + (i + 1) * DH] = dv_acc[i].T.astype(BF16)


def attention_backward(
    heads, dmixed, mixed, probs, q, k, v, xs, w, grad_w, d_in, bias_grad, dqkv, dk_acc, dv_acc
):
    length = xs.shape[0]
    step = 256
    cols = heads * DH
    dk_acc[...] = jnp.zeros_like(dk_acc)
    dv_acc[...] = jnp.zeros_like(dv_acc)

    def rows_back(r, carry):
        rows = pl.ds(pl.multiple_of(r * step, step), step)
        attend_back(heads, rows, dmixed, mixed, probs, q, k, v, dqkv, dk_acc, dv_acc)
        return carry

    lax.fori_loop(0, length // step, rows_back, 0)
    spread_heads(heads, dqkv, dk_acc, dv_acc)

    def finish(r, total):
        rows = pl.ds(pl.multiple_of(r * step, step), step)
        d = dqkv[rows, :]
        d_in[rows, :] = dot_nt(d, w[:, : 3 * cols]).astype(BF16)
        return total + jnp.sum(d.astype(F32), axis=0, keepdims=True)

    bias_grad[...] = lax.fori_loop(
        0, length // step, finish, jnp.zeros((1, 3 * cols), F32)
    )
    for part in range(3):
        own = slice(part * cols, (part + 1) * cols)
        grad_w[:, own] = dot_tn(xs[...], dqkv[:, own]).astype(BF16)


class Links:
    def __init__(self):
        self.started = []

    def copy(self, src, dst, send, recv, peer):
        return pltpu.make_async_remote_copy(
            src_ref=src, dst_ref=dst, send_sem=send, recv_sem=recv,
            device_id=peer, device_id_type=MESH,
        )

    def start(self, src, dst, send, recv, peer):
        copy = self.copy(src, dst, send, recv, peer)
        copy.start()
        self.started.append(copy)
        return copy

    def sent(self, copy):
        if any(copy is one for one in self.started):
            copy.wait_send()
            self.started = [one for one in self.started if one is not copy]

    def drain(self):
        for copy in self.started:
            copy.wait_send()
        self.started = []


def greet(peers, between=None):
    barrier = pltpu.get_barrier_semaphore()
    for peer in peers:
        pl.semaphore_signal(barrier, inc=1, device_id=peer, device_id_type=MESH)
    if between is not None:
        between()
    pl.semaphore_wait(barrier, len(peers))


def places():
    c = lax.axis_index("ctx")
    flip = 1 - 2 * (c % 2)
    ynb = (c + 2) % 4
    return c, c + flip, ynb, ynb + flip


class LineGather:
    def __init__(self, blocks, sems, recv):
        self.blocks, self.sems, self.recv = blocks, sems, recv
        self.z = lax.axis_index("tp")
        self.last = blocks.shape[0] - 1

    def _copy(self, j, which, peer):
        block = self.blocks.at[j]
        return pltpu.make_async_remote_copy(
            src_ref=block, dst_ref=block, send_sem=self.sems.at[which], recv_sem=self.recv.at[j],
            device_id={"tp": peer}, device_id_type=MESH,
        )

    def _sends(self, act):
        z = self.z
        for which, step in enumerate((1, -1, 2, -2)):
            @pl.when(jnp.logical_and(z + step >= 0, z + step <= self.last))
            def _(which=which, step=step):
                act(self._copy(z, which, z + step))

    def _passed(self, act):
        z, last = self.z, self.last

        @pl.when(z == 2)
        def _():
            act(self._copy(0, 4, last))

        @pl.when(z == 1)
        def _():
            act(self._copy(last, 4, 0))

    def hop(self, d):
        z = self.z
        if d == 0:
            self._sends(lambda copy: copy.start())
            return
        for j in (z - d, z + d):
            @pl.when(jnp.logical_and(j >= 0, j <= self.last))
            def _(j=j):
                self._copy(j, 0, z).wait_recv()
        if d == 2:
            self._passed(lambda copy: copy.start())

    def drain(self):
        self._sends(lambda copy: copy.wait_send())
        self._passed(lambda copy: copy.wait_send())


class LineRelay:
    def __init__(self, blocks, up, down, recv):
        self.parts = up.shape[0]
        self.blocks, self.up, self.down, self.recv = blocks, up, down, recv
        self.z = lax.axis_index("tp")
        self.last = blocks.shape[0] - 1
        self.rows = blocks.shape[1] // self.parts

    def _copy(self, j, h, sem, peer):
        block = self.blocks.at[j, pl.ds(h * self.rows, self.rows)]
        return pltpu.make_async_remote_copy(
            src_ref=block, dst_ref=block, send_sem=sem.at[h, j], recv_sem=self.recv.at[h, j],
            device_id={"tp": peer}, device_id_type=MESH,
        )

    def _sides(self, d):
        z, last = self.z, self.last
        yield self.up, z - d, z - d >= 0, z < last, z + 1
        yield self.down, z + d, z + d <= last, z > 0, z - 1

    def hop(self, d, h):
        for sem, j, here, onward, peer in self._sides(d):
            @pl.when(here)
            def _(sem=sem, j=j, onward=onward, peer=peer):
                if d:
                    self._copy(j, h, sem, self.z).wait_recv()
                if d < self.last:
                    @pl.when(onward)
                    def _():
                        self._copy(j, h, sem, peer).start()

    def drain(self):
        for d in range(self.last):
            for h in range(self.parts):
                for sem, j, here, onward, _ in self._sides(d):
                    @pl.when(jnp.logical_and(here, onward))
                    def _(sem=sem, j=j, h=h):
                        self._copy(j, h, sem, self.z).wait_send()


def layer(
    names, heads, lengths,
    tokens, cotangent, qkv_w, out_w, geglu_w, down_w, qv_b, geglu_b, gains, shifts, out_b,
    lout, input_grad, out0, oute, outr, *scratch,
):
    r = types.SimpleNamespace(**dict(zip(names, scratch)))
    c, sib, ynb, dia = places()
    me = lax.axis_index("shard")
    z = lax.axis_index("tp")
    other = 1 - me
    tp, rows_own, width = lout.shape
    piece = outr.shape[1]
    cols = heads * DH
    length = 4 * rows_own
    cr = rows_own // NCH
    links = Links()
    start, copy = links.start, links.copy

    def block(body):
        pl.when(z >= 0)(body)


    def local(src, dst, i):
        return pltpu.make_async_copy(src, dst, r.load.at[i])

    load_x = local(tokens.at[z], r.xs.at[c], 0)
    load_c = local(cotangent.at[z], r.cot, 1)
    loads = [local(qkv_w, r.qkv_v, 2), local(out_w, r.out_v, 3), local(down_w, r.down_v, 4),
             local(geglu_w, r.geglu_v, 5)]

    span = r.po.shape[1]
    thirds = width // span

    def pack():
        for one in loads + [load_x, load_c]:
            one.start()
        for one in loads:
            one.wait()
        for i in range(3):
            r.pq[:, i * cols : (i + 1) * cols] = r.qkv_v[i]
        r.pq[:, 3 * cols :] = jnp.zeros((piece, r.pq.shape[1] - 3 * cols), BF16)
        for i in range(2):
            for h in range(heads):
                r.pq[i * heads + h : i * heads + h + 1, 3 * cols : 3 * cols + DH] = (
                    qv_b[i : i + 1, h * DH : (h + 1) * DH])
        r.po[...] = jnp.zeros_like(r.po)
        r.po[0:piece, 0:cols] = r.out_v[...].T
        for i in range(2):
            for t in range(thirds):
                row = piece + i * thirds + t
                r.po[row : row + 1, :] = geglu_b[i : i + 1, t * span : (t + 1) * span]
        row = piece + 2 * thirds
        for i, ref in enumerate((gains, shifts, out_b)):
            r.po[row + 2 * i : row + 2 * i + 2, 0:piece] = ref[...]

    greet([{"ctx": sib}, {"ctx": ynb}, {"ctx": dia}, {"shard": other}]
          + [{"tp": (z + d) % tp} for d in range(1, tp)], pack)

    half = piece * FRONT_CUT // 6
    rest = piece - half
    cut = piece * BACK_CUT // 6
    tail = piece - cut
    src = {"q": r.pq, "o": r.po, 0: r.geglu_v.at[0], 1: r.geglu_v.at[1],
           2: r.down_v.at[pl.ds(0, half)]}
    zb = {"q": r.zbq, "o": r.zbo, 0: r.zbr.at[0], 1: r.zbr.at[1], 2: r.zbd, 3: r.zbe}
    wr = {"q": r.wq, "o": r.wo, 0: r.w.at[0], 1: r.w.at[1]}
    index = {"q": 0, "o": 1, 0: 2, 1: 3, 2: 4, 3: 5}
    last = tp - 1

    def line_copy(p, j, sems, peer):
        block = zb[p].at[j]
        return copy(block, block, sems.at[index[p], j], r.zr.at[index[p], j], {"tp": peer})

    def slot_at(p, s, j):
        if p == 2:
            return r.w.at[2, s, j, pl.ds(0, half)]
        return wr[p].at[s, j]

    def owner_slot(p, j):
        if p == 3:
            return r.w.at[2, :, j, pl.ds(half, rest)]
        return slot_at(p, me, j)

    def hop(p, d):
        def deliver(j):
            @pl.when(j == c)
            def _():
                owner_slot(p, c)[...] = zb[p].at[j][...]

            @pl.when(j != c)
            def _():
                copy(zb[p].at[j], owner_slot(p, c), r.ys.at[index[p], j], r.yr.at[index[p], c],
                     {"ctx": j}).start()

        if d == 0:
            if p == 3:
                held["crossed"].wait_recv()
            else:
                zb[p].at[z][...] = src[p][...]

            for step in (1,):
                sems = r.zu if step == 1 else r.zu2

                @pl.when(z + step <= last)
                def _(step=step, sems=sems):
                    line_copy(p, z, sems, z + step).start()

                sems = r.zd if step == 1 else r.zd2

                @pl.when(z - step >= 0)
                def _(step=step, sems=sems):
                    line_copy(p, z, sems, z - step).start()

            deliver(z)
            return
        for side in range(2):
            j = z - d if side == 0 else z + d

            @pl.when((j >= 0) if side == 0 else (j <= last))
            def _(side=side, j=j):
                line_copy(p, j, r.zu, z).wait_recv()
                if d < last:
                    @pl.when((z < last) if side == 0 else (z > 0))
                    def _():
                        if side == 0:
                            line_copy(p, j, r.zu, z + 1).start()
                        else:
                            line_copy(p, j, r.zd, z - 1).start()
                deliver(j)

    def hop_drain(p):
        for d in range(last):
            for side in range(2):
                j = z - d if side == 0 else z + d
                here = (j >= 0) if side == 0 else (j <= last)
                edge = (z < last) if side == 0 else (z > 0)

                @pl.when(jnp.logical_and(here, edge))
                def _(side=side, j=j):
                    line_copy(p, j, r.zu if side == 0 else r.zd, z).wait_send()

        for j in (sib, ynb, dia):
            copy(zb[p].at[j], owner_slot(p, c), r.ys.at[index[p], j], r.yr.at[index[p], c],
                 {"ctx": j}).wait_send()

    def owned(p, j):
        copy(zb[p].at[c], owner_slot(p, j), r.ys.at[index[p], c], r.yr.at[index[p], j],
             {"ctx": c}).wait_recv()

    def shard_copy(p, i, j):
        slot = slot_at(p, me, j)
        return copy(slot, slot, r.xs_s.at[index[p], i], r.xs_r.at[index[p], j], {"shard": other})

    def to_shard(p):
        for i, j in enumerate((c, sib, ynb, dia)):
            if i:
                owned(p, j)
            shard_copy(p, i, j).start()

    far_off = jnp.abs(z - c)

    def to_shard_if(p, low, high):
        @pl.when(jnp.logical_and(far_off >= low, far_off <= high))
        def _():
            to_shard(p)

    def shard_drain(p):
        for i in range(4):
            shard_copy(p, i, c).wait_send()

    def complete(p):
        if p == 3:
            for j in (sib, ynb, dia):
                owned(p, j)
            return
        for j in range(4):
            slot = slot_at(p, other, j)
            copy(slot, slot, r.xs_s.at[index[p], 0], r.xs_r.at[index[p], j],
                 {"shard": other}).wait_recv()

    grad = [r.g0] + [r.w.at[i] for i in range(2)]
    xb = [r.xb0] + [r.xbr.at[i] for i in range(2)] + [r.xbh]
    yb = [r.yb0] + [r.ybr.at[i] for i in range(2)] + [r.ybh]
    rb = [r.rb0] + [r.rbr.at[i] for i in range(2)] + [r.rbh]
    out = [out0] + [outr.at[i] for i in range(2)] + [outr.at[2, pl.ds(0, cut)]]

    def grad_at(p, s, j):
        if p == 3:
            return r.w.at[2, s, j, pl.ds(0, cut)]
        return grad[3 if p == 4 else p].at[s, j]

    SMALL = 4
    grad.append(r.ge)
    xb.append(r.xe)
    yb.append(r.ye)
    rb.append(r.re)
    out.append(oute)

    def beside(p):
        return (p, SMALL) if p == 0 else (p,)

    def grad_to_shard(p):
        for i, j in enumerate((dia, ynb, sib, c)):
            for n in beside(p):
                start(grad_at(n, other, j), xb[n].at[j], r.gx_s.at[n, i], r.gx_r.at[n, j], {"shard": other})

    def grad_to_owner(p, i):
        j = (dia, ynb, sib, c)[i]
        for n in beside(p):
            copy(grad_at(n, other, j), xb[n].at[j], r.gx_s.at[n, 0], r.gx_r.at[n, j],
                 {"shard": other}).wait_recv()
            total = (grad_at(n, me, j)[...].astype(F32) + xb[n].at[j][...].astype(F32)).astype(BF16)
            if i == 3:
                yb[n].at[c][...] = total
            else:
                xb[n].at[j][...] = total
                start(xb[n].at[j], yb[n].at[c], r.gy_s.at[n, i], r.gy_r.at[n, c], {"ctx": j})

    def grad_came(p, j):
        @pl.when(j != c)
        def _():
            copy(xb[p].at[j], yb[p].at[j], r.gy_s.at[p, 0], r.gy_r.at[p, j], {"ctx": j}).wait_recv()

    def climb(p, side, j):
        if side == 0:
            return copy(yb[p].at[j], rb[p].at[j], r.gu_s.at[p, j], r.gu_r.at[p, j], {"tp": z + 1})
        slot = jnp.where(j == z - 1, tp, j)
        return copy(yb[p].at[j], rb[p].at[slot], r.gd_s.at[p, j], r.gd_r.at[p, j], {"tp": z - 1})

    def grad_hop_one(p, h):
        if h == last:
            grad_came(p, z)
            out[p][...] = yb[p].at[z][...].astype(F32)

            @pl.when(z > 0)
            def _():
                copy(yb[p].at[z], rb[p].at[z], r.gu_s.at[p, z], r.gu_r.at[p, z], {"tp": z}).wait_recv()
                out[p][...] += rb[p].at[z][...].astype(F32)

            @pl.when(z < last)
            def _():
                copy(yb[p].at[z], rb[p].at[tp], r.gd_s.at[p, z], r.gd_r.at[p, z], {"tp": z}).wait_recv()
                out[p][...] += rb[p].at[tp][...].astype(F32)
            return
        for side in range(2):
            j = z + (last - h) if side == 0 else z - (last - h)

            @pl.when((j <= last) if side == 0 else (j >= 0))
            def _(side=side, j=j):
                grad_came(p, j)

                @pl.when((z > 0) if side == 0 else (z < last))
                def _():
                    sems = r.gu_r if side == 0 else r.gd_r
                    copy(yb[p].at[j], rb[p].at[j], r.gu_s.at[p, j], sems.at[p, j], {"tp": z}).wait_recv()
                    yb[p].at[j][...] = (
                        yb[p].at[j][...].astype(F32) + rb[p].at[j][...].astype(F32)).astype(BF16)
                climb(p, side, j).start()

    def grad_hop(p, h):
        for n in beside(p):
            grad_hop_one(n, h)

    stage = jnp.where(z < c, z, last - z)

    def chain_mine(i):
        return r.w.at[2, i // 2, pl.ds(2 * (i % 2), 2), pl.ds(cut, tail)]

    def chain_came(side, i):
        return r.cb.at[side, i // 2, pl.ds(2 * (i % 2), 2)]

    def chain_copy(i, side):
        return copy(chain_mine(i), chain_came(side, i),
                    r.ch_s.at[side, i], r.ch_r.at[side, i], {"tp": z + 1 if side == 0 else z - 1})

    def chain_wait(i, side):
        copy(chain_mine(i), chain_came(side, i),
             r.ch_s.at[side, i], r.ch_r.at[side, i], {"tp": z}).wait_recv()
        mine = chain_mine(i)
        mine[...] = (mine[...].astype(F32) + chain_came(side, i)[...].astype(F32)).astype(BF16)

    def chain(slot):
        for i in range(4):
            for side in range(2):
                here = (z < c) if side == 0 else (z > c)
                if slot == 0:
                    @pl.when(jnp.logical_and(here, stage == 0))
                    def _(i=i, side=side):
                        chain_copy(i, side).start()
                else:
                    @pl.when(jnp.logical_and(here, jnp.logical_and(stage > 0, stage == slot - i)))
                    def _(i=i, side=side):
                        chain_wait(i, side)
                        chain_copy(i, side).start()

    def chain_send(j):
        return copy(r.w.at[2, :, j, pl.ds(cut, tail)], r.yd, r.cy_s.at[j], r.cy_r.at[0], {"ctx": j})

    def chain_end():
        @pl.when(z == c)
        def _():
            for i in range(4):
                @pl.when(z > 0)
                def _(i=i):
                    chain_wait(i, 0)

                @pl.when(z < last)
                def _(i=i):
                    chain_wait(i, 1)
            r.yd[...] = r.w[2, :, c, cut:, :]
            for j in (dia, ynb, sib):
                chain_send(j).start()

    def chain_across():
        @pl.when(z != c)
        def _():
            chain_send(c).wait_recv()
        start(r.yd.at[other], r.xd, r.cx_s.at[0], r.cx_r.at[0], {"shard": other})

    def chain_total():
        copy(r.yd.at[other], r.xd, r.cx_s.at[0], r.cx_r.at[0], {"shard": other}).wait_recv()
        outr[2, cut:, :] = r.yd[me].astype(F32) + r.xd[...].astype(F32)

    def chain_drain():
        for i in range(4):
            for side in range(2):
                @pl.when((z < c) if side == 0 else (z > c))
                def _(i=i, side=side):
                    chain_copy(i, side).wait_send()

        @pl.when(z == c)
        def _():
            for j in (dia, ynb, sib):
                chain_send(j).wait_send()

    def grad_drain(p):
        for h in range(last):
            for side in range(2):
                j = z + (last - h) if side == 0 else z - (last - h)

                @pl.when((j <= last) if side == 0 else (j >= 0))
                def _(side=side, j=j):
                    climb(p, side, j).wait_send()

    def chunk(k):
        return pl.ds(k * cr, cr)

    ag_y, ag_c, ag_f, rs_r, rs_o, rs_y = ({} for _ in range(6))

    def gather_start(o, k):
        block = r.full.at[o, c, chunk(k)]
        ag_y[o, k] = start(block, block, r.ags_y.at[o, k], r.agr_y.at[o, k], {"ctx": ynb})
        ag_c[o, k] = start(block, block, r.ags_c.at[o, k], r.agr_c.at[o, k], {"ctx": sib})

    def forward(o, k):
        ag_y[o, k].wait_recv()
        block = r.full.at[o, ynb, chunk(k)]
        ag_f[o, k] = start(block, block, r.ags_f.at[o, k], r.agr_f.at[o, k], {"ctx": sib})

    def free(table, o, k):
        if o:
            links.sent(table[o - 1, k])

    def send_relay(o, k):
        rs_r[o, k] = start(r.snd_r.at[chunk(k)], r.rcv_r.at[chunk(k)],
                           r.rss_r.at[o, k], r.rsr_r.at[o, k], {"ctx": sib})

    def send_own(o, k):
        rs_o[o, k] = start(r.snd_o.at[chunk(k)], r.rcv_o.at[chunk(k)],
                           r.rss_o.at[o, k], r.rsr_o.at[o, k], {"ctx": sib})

    def relay(o, k):
        rs_r[o, k].wait_recv()
        free(rs_y, o, k)
        r.snd_y[chunk(k), :] = (
            r.yacc[chunk(k), :] + r.rcv_r[chunk(k), :].astype(F32)).astype(BF16)
        rs_y[o, k] = start(r.snd_y.at[chunk(k)], r.rcv_y.at[chunk(k)],
                           r.rss_y.at[o, k], r.rsr_y.at[o, k], {"ctx": ynb})

    def arrived(o, k):
        rs_o[o, k].wait_recv()
        rs_y[o, k].wait_recv()

    def summed(rows):
        return r.own[rows, :] + r.rcv_o[rows, :].astype(F32) + r.rcv_y[rows, :].astype(F32)

    def tiles(first, count, body):
        def step(t, carry):
            body(pl.ds(pl.multiple_of(first + t * TILE, TILE), TILE))
            return carry
        lax.fori_loop(0, count // TILE, step, 0)

    def fold(values):
        return jnp.sum(values.reshape(TILE // 8, 8, width), axis=0)

    def rows_of(b, r0=0, n=rows_own):
        return pl.ds(pl.multiple_of(b * rows_own + r0, cr), n)

    def both(parts):
        return jnp.concatenate(parts, axis=0)

    def far_blocks(o, k, product):
        free(rs_r, o, k)

        @block
        def _():
            value = product()
            r.snd_r[chunk(k), :] = value[:cr].astype(BF16)
            r.yacc[chunk(k), :] = value[cr:]
        send_relay(o, k)

    def near_block(o, product):
        for k in range(NCH):
            free(rs_o, o, k)

        @block
        def _():
            r.snd_o[...] = product().astype(BF16)
        for k in range(NCH):
            send_own(o, k)

    def own_block(product):
        @block
        def _():
            r.own[...] = product()

    def wait_near(o):
        for k in range(NCH):
            ag_c[o, k].wait_recv()

    def wait_far(o, k):
        ag_f[o, k].wait_recv()

    held = {}

    def cross_down():
        load_x.wait()
        held["crossed"] = start(
            r.down_v.at[pl.ds(half, rest)], r.zbe.at[z, me], r.xd_s.at[0], r.xd_r.at[0],
            {"shard": other})
        r.zbe.at[z, me][...] = r.down_v[pl.ds(half, rest), :]

    def clear():
        r.acc[...] = jnp.zeros_like(r.acc)
        r.bsum[...] = jnp.zeros_like(r.bsum)
        r.dk_acc[...] = jnp.zeros_like(r.dk_acc)
        r.dv_acc[...] = jnp.zeros_like(r.dv_acc)

    def tokens_start():
        held["first"] = start(r.xs.at[c], r.xs.at[c], r.xg_s.at[0], r.xg_r.at[0], {"ctx": ynb})
        held["near"] = start(r.xs.at[c], r.xs.at[c], r.xg_s.at[1], r.xg_r.at[1], {"ctx": sib})

    def tokens_pass():
        held["first"].wait_recv()
        held["passed"] = start(
            r.xs.at[ynb], r.xs.at[ynb], r.xg_s.at[2], r.xg_r.at[2], {"ctx": sib})

    def tokens_wait():
        held["near"].wait_recv()
        held["passed"].wait_recv()

    def project():
        for i in range(2):
            for h in range(heads):
                r.qv[i : i + 1, h * DH : (h + 1) * DH] = (
                    r.wq[0, 0, i * heads + h : i * heads + h + 1, 3 * cols : 3 * cols + DH].astype(F32))

        def rows_of_block(t, carry):
            rows = pl.ds(pl.multiple_of(t * rows_own, rows_own), rows_own)
            project_heads(heads, r.xs[t], rows, r.wq[...].reshape(width, r.wq.shape[3]),
                          r.qv, r.q, r.k, r.v)
            return carry

        lax.fori_loop(0, 4, rows_of_block, 0)

    def attend(b):
        @block
        def _():
            attend_rows(heads, pl.multiple_of(b * rows_own, rows_own), rows_own, lengths, z,
                        r.q, r.k, r.v, r.probs, r.mixed, r.far)

    def unpack_out():
        for s in range(2):
            for j in range(4):
                place = s * 4 + j
                r.w_out[pl.ds(place * piece, piece), :] = r.wo[s, j, 0:piece, 0:cols]
                row = piece + 2 * thirds
                r.vec[0:6, place * piece : (place + 1) * piece] = (
                    r.wo[s, j, row : row + 6, 0:piece].astype(F32))
        for i in range(2):
            for t in range(thirds):
                row = piece + i * thirds + t
                r.vec[6 + i : 7 + i, t * span : (t + 1) * span] = r.wo[0, 0, row : row + 1, :].astype(F32)

    def out_project(b):
        return dot_nt(r.mixed[rows_of(b), :], r.w_out[...])

    def out_far():
        @block
        def _():
            r.snd_r[...] = out_project(dia).astype(BF16)
        for k in range(NCH):
            send_relay(0, k)

    def out_cross():
        @block
        def _():
            r.yacc[...] = out_project(ynb)

    def out_near():
        near_block(0, lambda: out_project(sib))

    def out_own():
        own_block(lambda: out_project(c))

    def norm_one(rows):
        res = r.xs[c, rows, :].astype(F32) + summed(rows) + r.vec[4:5, :]
        center = res - jnp.mean(res, axis=-1, keepdims=True)
        scale = lax.rsqrt(jnp.mean(center * center, axis=-1, keepdims=True) + 1e-12)
        zh = center * scale
        value = zh * r.vec[0:1, :] + r.vec[2:3, :]
        r.zh1[rows, :] = zh
        r.r1[rows, :] = scale
        r.normed[rows, :] = value
        r.full[0, c, rows, :] = value.astype(BF16)

    def norm_one_chunk(k):
        arrived(0, k)
        tiles(k * cr, cr, norm_one)
        gather_start(0, k)

    def matrix(i):
        return r.w[i].reshape(width, width)

    def units_forward(b, r0, n):
        rows_in = r.full[0, b, pl.ds(r0, n), :]
        r.fa[pl.ds(0, n), :] = dot(rows_in, matrix(0))
        r.fb[pl.ds(0, n), :] = dot(rows_in, matrix(1))

        def units(rows):
            g = r.fa[rows, :] + r.vec[6:7, :]
            u = r.fb[rows, :] + r.vec[7:8, :]
            phi = 0.5 * (1.0 + lax.erf(g * (1.0 / math.sqrt(2.0))))
            gelu = g * phi
            slope = phi + g * jnp.exp(-0.5 * g * g) * (1.0 / math.sqrt(2.0 * math.pi))
            to = pl.ds(pl.multiple_of(r0 + rows.start, TILE), TILE)
            r.act[b, to, :] = gelu.astype(BF16)
            r.pull[b, to, :] = (u * slope).astype(BF16)
            r.hid[b, to, :] = (gelu * u).astype(BF16)

        tiles(0, n, units)

    def hid_rows(b, r0, n):
        return r.hid[b, pl.ds(r0, n), :]

    def down(rows):
        return dot_nt(rows, matrix(2))

    def units_backward(blocks, r0, n):
        def rows_at(ref, b):
            return ref[b, pl.ds(r0, n), :]

        def gather(ref):
            return both([rows_at(ref, b) for b in blocks]) if len(blocks) > 1 else rows_at(ref, blocks[0])

        r.fa[pl.ds(0, n * len(blocks)), :] = dot(gather(r.full.at[1]), matrix(2))
        for i, b in enumerate(blocks):
            def units(rows, b=b, i=i):
                dh = r.fa[rows, :]
                to = pl.ds(pl.multiple_of(r0 - i * n + rows.start, TILE), TILE)
                dg = (dh * r.pull[b, to, :].astype(F32)).astype(BF16)
                du = (dh * r.act[b, to, :].astype(F32)).astype(BF16)
                r.pull[b, to, :] = dg
                r.act[b, to, :] = du
                r.bsum[0] += fold(dg.astype(F32))
                r.bsum[1] += fold(du.astype(F32))

            tiles(i * n, n, units)
        return dot_nt(gather(r.pull), matrix(0)) + dot_nt(gather(r.act), matrix(1))

    def down_far(k):
        far_blocks(1, k, lambda: down(both([hid_rows(dia, k * cr, cr), hid_rows(ynb, k * cr, cr)])))

    def down_near():
        near_block(1, lambda: down(hid_rows(sib, 0, rows_own)))

    def down_own():
        own_block(lambda: down(hid_rows(c, 0, rows_own)))

    def norm_two(rows):
        res = r.normed[rows, :] + (summed(rows) + r.vec[5:6, :])
        center = res - jnp.mean(res, axis=-1, keepdims=True)
        scale = lax.rsqrt(jnp.mean(center * center, axis=-1, keepdims=True) + 1e-12)
        zh = center * scale
        r.lout[z, rows, :] = (zh * r.vec[1:2, :] + r.vec[3:4, :]).astype(BF16)
        up = r.cot[rows, :].astype(F32)
        t = up * r.vec[1:2, :]
        d = scale * (t - jnp.mean(t, axis=-1, keepdims=True)
                     - zh * jnp.mean(t * zh, axis=-1, keepdims=True))
        r.normed[rows, :] = d
        low = d.astype(BF16)
        r.full[1, c, rows, :] = low
        r.acc[1] += fold(up * zh)
        r.acc[3] += fold(up)
        r.acc[5] += fold(low.astype(F32))

    def norm_two_chunk(k):
        arrived(1, k)
        tiles(k * cr, cr, norm_two)
        gather_start(1, k)

    line_out = LineRelay(r.lout, r.lv, r.lw, r.lr)
    line_in = LineRelay(r.input_grad, r.lu, r.ld, r.li)

    def line_out_hop(d, h):
        line_out.hop(d, h)

    def line_in_hop(d, h):
        line_in.hop(d, h)

    def back_own():
        own_block(lambda: units_backward([c], 0, rows_own))

    def back_near():
        near_block(2, lambda: units_backward([sib], 0, rows_own))

    def back_far(k):
        far_blocks(2, k, lambda: units_backward([dia, ynb], k * cr, cr))

    def flat(ref):
        return ref[...].reshape(length, ref.shape[-1])

    def put(i, left, right):
        @block
        def _():
            r.w[i] = dot_tn(flat(left), flat(right)).astype(BF16).reshape(r.w.shape[1:])

    def put_down():
        for p in range(3):
            shard_drain(p)
        put(2, r.full.at[1], r.hid)

    def put_gate():
        put(0, r.full.at[0], r.pull)

    def put_up():
        put(1, r.full.at[0], r.act)

    def norm_back(rows):
        dn = summed(rows) + r.normed[rows, :]
        zh = r.zh1[rows, :]
        t = dn * r.vec[0:1, :]
        d = r.r1[rows, :] * (t - jnp.mean(t, axis=-1, keepdims=True)
                             - zh * jnp.mean(t * zh, axis=-1, keepdims=True))
        r.zh1[rows, :] = d
        low = d.astype(BF16)
        r.full[2, c, rows, :] = low
        r.acc[0] += fold(dn * zh)
        r.acc[2] += fold(dn)
        r.acc[4] += fold(low.astype(F32))

    def norm_back_chunk(k):
        arrived(2, k)
        tiles(k * cr, cr, norm_back)
        gather_start(2, k)

    def back_rows(b):
        @block
        def _():
            r.dmixed[rows_of(b), :] = dot(r.full[2, b], r.w_out[...]).astype(BF16)
            attend_back(heads, rows_of(b), r.dmixed, r.mixed, r.probs, r.q, r.k, r.v,
                        r.dqkv, r.dk_acc, r.dv_acc)

    def tiny_first():
        for i in range(6):
            r.tiny[0, i : i + 1, :] = jnp.sum(r.acc[i], axis=0, keepdims=True)
        held["tiny"] = start(r.tiny.at[0], r.tiny.at[1], r.tiny_s.at[0], r.tiny_r.at[0], {"ctx": sib})

    def tiny_second():
        held["tiny"].wait_recv()
        r.tiny[2] = r.tiny[0] + r.tiny[1]
        held["tiny_y"] = start(r.tiny.at[2], r.tiny.at[3], r.tiny_s.at[1], r.tiny_r.at[1], {"ctx": ynb})

    def spread():
        @block
        def _():
            spread_heads(heads, r.dqkv, r.dk_acc, r.dv_acc)

    def into_input(rows):
        return dot_nt(rows, r.wq[...].reshape(width, r.wq.shape[3])[:, : 3 * cols])

    def input_far(k):
        far_blocks(3, k, lambda: into_input(both([
            r.dqkv[rows_of(dia, k * cr, cr), :], r.dqkv[rows_of(ynb, k * cr, cr), :]])))

    def input_near():
        near_block(3, lambda: into_input(r.dqkv[rows_of(sib), :]))

    def input_own():
        own_block(lambda: into_input(r.dqkv[rows_of(c), :]))

    def projection_gradients():
        held["tiny_y"].wait_recv()
        norms = r.tiny[2] + r.tiny[3]
        bias = jnp.sum(r.dqkv[...].astype(F32), axis=0, keepdims=True)
        r.extra[...] = jnp.zeros_like(r.extra)
        row = jnp.concatenate([bias[:, :cols], bias[:, 2 * cols :]], axis=1)
        lanes = r.extra.shape[1]
        spans = [row[:, t * lanes : (t + 1) * lanes] for t in range(2 * cols // lanes)]
        for i in range(2):
            value = jnp.sum(r.bsum[i], axis=0, keepdims=True)
            spans += [value[:, t * lanes : (t + 1) * lanes] for t in range(width // lanes)]
        for t, span_ in enumerate(spans):
            r.extra[t : t + 1, :] = span_
        count = len(spans)
        for s in range(2):
            for j in range(4):
                lane = (s * 4 + j) * piece
                r.extra[count : count + 6, 0:piece] = norms[0:6, lane : lane + piece]
                r.ge[s, j] = r.extra[...].astype(BF16)
        x_all = flat(r.xs)
        for i in range(4):
            lanes = slice(i * cols, (i + 1) * cols)
            if i < 3:
                value = dot_tn(x_all, r.dqkv[:, lanes])
            else:
                value = dot_tn(flat(r.full.at[2]), r.mixed[...])
            value = value.astype(BF16)
            for s in range(2):
                for j in range(4):
                    first_row = (s * 4 + j) * piece
                    r.g0[s, j, 0:piece, lanes] = value[first_row : first_row + piece]

    def input_chunk(k):
        arrived(3, k)
        r.input_grad[z, chunk(k), :] = (summed(chunk(k)) + r.zh1[chunk(k), :]).astype(BF16)

    save_out = pltpu.make_async_copy(r.lout, lout, r.save.at[0])
    save_in = pltpu.make_async_copy(r.input_grad, input_grad, r.save.at[1])

    def save_out_start():
        save_out.start()

    def save_in_start():
        save_in.start()

    def cot_wait():
        load_c.wait()

    def drain():
        save_out.wait()
        save_in.wait()
        line_out.drain()
        line_in.drain()
        for p in range(5):
            grad_drain(p)
        chain_drain()
        for p in index:
            hop_drain(p)
        for p in ("q", "o"):
            shard_drain(p)
        links.drain()

    cross_down()
    tokens_start()
    hop("q", 0)
    hop("o", 0)
    hop("q", 1)
    hop(1, 0)
    hop("q", 2)
    to_shard_if("q", 0, 0)
    hop("o", 1)
    hop(0, 0)
    clear()
    to_shard_if("q", 2, 2)
    hop("q", 3)
    to_shard_if("q", 1, 1)
    tokens_pass()
    to_shard_if("q", 3, 3)
    hop("o", 2)
    hop(1, 1)
    hop("o", 3)
    hop(1, 2)
    to_shard("o")
    hop(0, 1)
    tokens_wait()
    complete("q")
    project()
    hop(1, 3)
    to_shard_if(1, 2, 2)
    to_shard_if(1, 0, 0)
    attend(dia)
    hop(0, 2)
    hop(2, 0)
    to_shard_if(1, 3, 3)
    complete("o")
    to_shard_if(1, 1, 1)
    unpack_out()
    to_shard_if(0, 0, 0)
    out_far()
    hop(3, 0)
    attend(ynb)
    hop(0, 3)
    out_cross()
    relay(0, 1)
    to_shard_if(0, 1, 1)
    relay(0, 2)
    attend(sib)
    relay(0, 0)
    to_shard_if(0, 2, 2)
    out_near()
    relay(0, 3)
    to_shard_if(0, 3, 3)
    attend(c)
    hop(2, 1)
    hop(2, 2)
    hop(2, 3)
    out_own()
    norm_one_chunk(0)
    norm_one_chunk(1)
    norm_one_chunk(2)
    norm_one_chunk(3)
    to_shard_if(2, 3, 3)
    wait_near(0)
    to_shard_if(2, 1, 1)
    forward(0, 0)
    hop(3, 1)
    hop(3, 2)
    to_shard_if(2, 2, 2)
    complete(0)
    complete(1)
    units_forward(c, 0, rows_own)
    to_shard_if(2, 0, 0)
    forward(0, 3)
    wait_far(0, 0)
    forward(0, 2)
    units_forward(sib, 0, rows_own)
    hop(3, 3)
    forward(0, 1)
    units_forward(ynb, 0, rows_own)
    wait_far(0, 2)
    cot_wait()
    wait_far(0, 3)
    wait_far(0, 1)
    units_forward(dia, 0, rows_own)
    complete(2)
    complete(3)
    down_far(0)
    down_far(1)
    relay(1, 0)
    relay(1, 1)
    down_far(2)
    down_far(3)
    down_near()
    down_own()
    relay(1, 2)
    relay(1, 3)
    norm_two_chunk(0)
    norm_two_chunk(1)
    norm_two_chunk(2)
    norm_two_chunk(3)
    line_out_hop(0, 0)
    line_out_hop(0, 1)
    back_own()
    forward(1, 0)
    wait_near(1)
    back_near()
    forward(1, 1)
    wait_far(1, 0)
    back_far(0)
    forward(1, 2)
    wait_far(1, 1)
    back_far(1)
    relay(2, 0)
    forward(1, 3)
    wait_far(1, 2)
    back_far(2)
    relay(2, 1)
    wait_far(1, 3)
    back_far(3)
    relay(2, 2)
    put_down()
    chain(0)
    grad_to_shard(3)
    relay(2, 3)
    norm_back_chunk(0)
    put_up()
    grad_to_shard(2)
    line_out_hop(1, 1)
    put_gate()
    line_out_hop(1, 0)
    norm_back_chunk(1)
    norm_back_chunk(2)
    norm_back_chunk(3)
    tiny_first()
    wait_near(2)
    grad_to_owner(3, 0)
    back_rows(c)
    grad_to_owner(3, 2)
    grad_to_owner(3, 1)
    forward(2, 1)
    grad_to_owner(3, 3)
    forward(2, 0)
    chain(1)
    chain(2)
    forward(2, 2)
    line_out_hop(2, 0)
    back_rows(sib)
    grad_to_shard(1)
    forward(2, 3)
    wait_far(2, 2)
    wait_far(2, 1)
    tiny_second()
    back_rows(ynb)
    chain(3)
    grad_hop(3, 0)
    wait_far(2, 0)
    wait_far(2, 3)
    back_rows(dia)
    grad_to_owner(2, 0)
    line_out_hop(2, 1)
    spread()
    input_far(0)
    grad_hop(3, 1)
    input_far(1)
    relay(3, 0)
    input_far(2)
    input_far(3)
    chain(4)
    input_near()
    grad_hop(3, 2)
    line_out_hop(3, 0)
    relay(3, 1)
    input_own()
    grad_to_owner(2, 3)
    relay(3, 2)
    input_chunk(0)
    line_in_hop(0, 0)
    input_chunk(1)
    line_in_hop(0, 1)
    relay(3, 3)
    input_chunk(2)
    line_in_hop(0, 2)
    projection_gradients()
    grad_to_shard(0)
    input_chunk(3)
    line_in_hop(0, 3)
    line_in_hop(1, 0)
    grad_to_owner(2, 1)
    chain(5)
    grad_to_owner(2, 2)
    grad_hop(2, 0)
    line_in_hop(1, 1)
    grad_hop(2, 1)
    grad_to_owner(1, 2)
    line_out_hop(3, 1)
    line_in_hop(1, 2)
    grad_to_owner(1, 0)
    line_in_hop(1, 3)
    grad_to_owner(1, 1)
    grad_to_owner(1, 3)
    grad_hop(3, 3)
    grad_hop(1, 0)
    grad_hop(1, 1)
    line_in_hop(2, 1)
    grad_to_owner(0, 1)
    line_in_hop(2, 0)
    line_in_hop(2, 2)
    grad_to_owner(0, 3)
    grad_to_owner(0, 0)
    grad_hop(2, 2)
    line_in_hop(2, 3)
    grad_to_owner(0, 2)
    grad_hop(0, 0)
    chain_end()
    grad_hop(0, 1)
    line_in_hop(3, 3)
    grad_hop(1, 2)
    chain_across()
    line_in_hop(3, 0)
    grad_hop(0, 2)
    grad_hop(1, 3)
    chain_total()
    line_in_hop(3, 2)
    line_in_hop(3, 1)
    grad_hop(2, 3)
    save_in_start()
    save_out_start()
    grad_hop(0, 3)
    drain()


def finish(
    lout, input_low, out0, oute, outr,
    o_lout, o_in, o_qkv, o_qvb, o_out, o_geglu, o_gb, o_down, o_gain, o_shift, o_ob,
    low, narrow, wide, first, few, rest, v_qkv, v_qvb, v_out, v_gb, v_gain, v_shift, v_ob,
    sem_in, sem_out,
):
    piece = outr.shape[1]
    cols = o_qkv.shape[2]
    blocks = narrow.shape[0]
    lanes = few.shape[1]
    started = []

    def save(src, dst):
        one = pltpu.make_async_copy(src, dst, sem_out.at[len(started)])
        one.start()
        started.append(one)

    pairs = [(out0, first), (oute, few), (outr, rest)]
    pairs += [(input_low.at[i], narrow.at[i]) for i in range(blocks)]
    pairs += [(lout.at[i], low.at[i]) for i in range(blocks)]
    loads = [pltpu.make_async_copy(src, dst, sem_in.at[i]) for i, (src, dst) in enumerate(pairs)]
    for one in loads:
        one.start()
    loads[0].wait()
    for i in range(3):
        v_qkv[i] = first[:, i * cols : (i + 1) * cols]
    v_out[...] = first[:, 3 * cols : 4 * cols].T
    loads[1].wait()
    row = jnp.concatenate([few[t : t + 1, :] for t in range(2 * cols // lanes)], axis=1)
    v_qvb[0:1, :] = row[:, 0:cols]
    v_qvb[1:2, :] = row[:, cols : 2 * cols]
    count = 2 * cols // lanes
    for i in range(2):
        for t in range(v_gb.shape[1] // lanes):
            v_gb[i : i + 1, t * lanes : (t + 1) * lanes] = few[count : count + 1, :]
            count += 1
    for i, ref in enumerate((v_gain, v_shift, v_ob)):
        ref[...] = few[count + 2 * i : count + 2 * i + 2, 0:piece]
    for src, dst in ((v_qkv, o_qkv), (v_out, o_out), (v_qvb, o_qvb), (v_gb, o_gb),
                     (v_gain, o_gain), (v_shift, o_shift), (v_ob, o_ob)):
        save(src, dst)
    loads[2].wait()
    save(rest.at[pl.ds(0, 2)], o_geglu)
    save(rest.at[2], o_down)
    for i in range(blocks):
        loads[3 + i].wait()
        wide[i] = narrow[i].astype(F32)
        save(wide.at[i], o_in.at[i])
    for i in range(blocks):
        loads[3 + blocks + i].wait()
        save(low.at[i], o_lout.at[i])
    for one in started:
        one.wait()


def middle(
    x, cot, mixed, w0, w, vec,
    lout, dres1, grads, gout, dmixed, small,
    w_out, full, act, pull, hid, dgt, dup,
    snd_r, snd_o, snd_y, rcv_r, rcv_o, rcv_y,
    own, yacc, fa, fb, normed, zh1, r1, dres2, acc, bsum, tiny,
    ags_y, agr_y, ags_c, agr_c, ags_f, agr_f,
    rss_r, rsr_r, rss_o, rsr_o, rss_y, rsr_y, tiny_s, tiny_r, ls, lr,
):
    rows_own = x.shape[0]
    width = x.shape[1]
    cr = rows_own // NCH
    c, sib, ynb, dia = places()
    z = lax.axis_index("tp")
    tp = lout.shape[0]
    greet([{"ctx": sib}, {"ctx": ynb}] + [{"tp": (z + d) % tp} for d in range(1, tp)])
    line = LineGather(lout, ls, lr)

    started = []

    def remote(src, dst, send, recv, peer):
        return pltpu.make_async_remote_copy(
            src_ref=src, dst_ref=dst, send_sem=send, recv_sem=recv,
            device_id={"ctx": peer}, device_id_type=MESH,
        )

    def chunk(k):
        return pl.ds(k * cr, cr)

    ag_y, ag_c, ag_f, rs_r, rs_o, rs_y = ({} for _ in range(6))

    def start(table, key, copy):
        copy.start()
        table[key] = copy
        started.append(copy)

    def gather_start(o, k):
        piece = full.at[o, c, chunk(k)]
        start(ag_y, (o, k), remote(piece, piece, ags_y.at[o, k], agr_y.at[o, k], ynb))
        start(ag_c, (o, k), remote(piece, piece, ags_c.at[o, k], agr_c.at[o, k], sib))

    def forward(o, k):
        ag_y[o, k].wait_recv()
        piece = full.at[o, ynb, chunk(k)]
        start(ag_f, (o, k), remote(piece, piece, ags_f.at[o, k], agr_f.at[o, k], sib))

    def send_relay(o, k):
        start(rs_r, (o, k), remote(
            snd_r.at[o, chunk(k)], rcv_r.at[o, chunk(k)], rss_r.at[o, k], rsr_r.at[o, k], sib))

    def send_own(o, k):
        start(rs_o, (o, k), remote(
            snd_o.at[o, chunk(k)], rcv_o.at[o, chunk(k)], rss_o.at[o, k], rsr_o.at[o, k], sib))

    def relay(o, k):
        rs_r[o, k].wait_recv()
        snd_y[o, chunk(k), :] = (yacc[chunk(k), :] + rcv_r[o, chunk(k), :].astype(F32)).astype(BF16)
        start(rs_y, (o, k), remote(
            snd_y.at[o, chunk(k)], rcv_y.at[o, chunk(k)], rss_y.at[o, k], rsr_y.at[o, k], ynb))

    def arrived(o, k):
        rs_o[o, k].wait_recv()
        rs_y[o, k].wait_recv()

    def tiles(first, count, body):
        def step(t, carry):
            body(pl.ds(pl.multiple_of(first + t * TILE, TILE), TILE))
            return carry
        lax.fori_loop(0, count // TILE, step, 0)

    def summed(o, rows):
        return own[rows, :] + rcv_o[o, rows, :].astype(F32) + rcv_y[o, rows, :].astype(F32)

    def fold(values):
        return jnp.sum(values.reshape(TILE // 8, 8, width), axis=0)

    acc[...] = jnp.zeros_like(acc)
    bsum[...] = jnp.zeros_like(bsum)
    w_out[...] = w0[:, 3 * mixed.shape[2] : 4 * mixed.shape[2]]

    def project(b, r0, n):
        return dot_nt(mixed[b, pl.ds(r0, n), :], w_out[...])

    for k in range(NCH):
        snd_r[0, chunk(k), :] = project(dia, k * cr, cr).astype(BF16)
        send_relay(0, k)
        yacc[chunk(k), :] = project(ynb, k * cr, cr)
        if k:
            relay(0, k - 1)
    relay(0, NCH - 1)
    for k in range(NCH):
        snd_o[0, chunk(k), :] = project(sib, k * cr, cr).astype(BF16)
        send_own(0, k)
    own[...] = project(c, 0, rows_own)

    def norm_one(rows):
        res = x[rows, :].astype(F32) + summed(0, rows) + vec[4:5, :]
        center = res - jnp.mean(res, axis=-1, keepdims=True)
        r = lax.rsqrt(jnp.mean(center * center, axis=-1, keepdims=True) + 1e-12)
        zh = center * r
        out = zh * vec[0:1, :] + vec[2:3, :]
        zh1[rows, :] = zh
        r1[rows, :] = r
        normed[rows, :] = out
        full[0, c, rows, :] = out.astype(BF16)

    for k in range(NCH):
        arrived(0, k)
        tiles(k * cr, cr, norm_one)
        gather_start(0, k)

    def mlp_forward(b, r0, n):
        rows_in = full[0, b, pl.ds(r0, n), :]
        fa[pl.ds(0, n), :] = dot(rows_in, w[0])
        fb[pl.ds(0, n), :] = dot(rows_in, w[1])

        def units(rows):
            g = fa[rows, :] + vec[6:7, :]
            u = fb[rows, :] + vec[7:8, :]
            phi = 0.5 * (1.0 + lax.erf(g * (1.0 / math.sqrt(2.0))))
            gelu = g * phi
            slope = phi + g * jnp.exp(-0.5 * g * g) * (1.0 / math.sqrt(2.0 * math.pi))
            out = pl.ds(pl.multiple_of(r0 + rows.start, TILE), TILE)
            act[b, out, :] = gelu.astype(BF16)
            pull[b, out, :] = (u * slope).astype(BF16)
            hid[b, out, :] = (gelu * u).astype(BF16)

        tiles(0, n, units)
        return dot_nt(hid[b, pl.ds(r0, n), :], w[2])

    def mlp_backward(b, r0, n):
        fa[pl.ds(0, n), :] = dot(full[1, b, pl.ds(r0, n), :], w[2])

        def units(rows):
            dh = fa[rows, :]
            out = pl.ds(pl.multiple_of(r0 + rows.start, TILE), TILE)
            dg = (dh * pull[b, out, :].astype(F32)).astype(BF16)
            du = (dh * act[b, out, :].astype(F32)).astype(BF16)
            dgt[b, out, :] = dg
            dup[b, out, :] = du
            bsum[0] += fold(dg.astype(F32))
            bsum[1] += fold(du.astype(F32))

        tiles(0, n, units)
        return dot_nt(dgt[b, pl.ds(r0, n), :], w[0]) + dot_nt(dup[b, pl.ds(r0, n), :], w[1])

    def exchange(o, piece):
        own[...] = piece(c, 0, rows_own)
        for k in range(NCH):
            ag_c[o - 1, k].wait_recv()
        snd_o[o] = piece(sib, 0, rows_own).astype(BF16)
        for k in range(NCH):
            send_own(o, k)
        for k in range(NCH):
            forward(o - 1, k)
            yacc[chunk(k), :] = piece(ynb, k * cr, cr)
            ag_f[o - 1, k].wait_recv()
            snd_r[o, chunk(k), :] = piece(dia, k * cr, cr).astype(BF16)
            send_relay(o, k)
            if k:
                relay(o, k - 1)
        relay(o, NCH - 1)

    exchange(1, mlp_forward)

    def norm_two(rows):
        res = normed[rows, :] + (summed(1, rows) + vec[5:6, :])
        center = res - jnp.mean(res, axis=-1, keepdims=True)
        r = lax.rsqrt(jnp.mean(center * center, axis=-1, keepdims=True) + 1e-12)
        zh = center * r
        lout[z, rows, :] = (zh * vec[1:2, :] + vec[3:4, :]).astype(BF16)
        up = cot[rows, :].astype(F32)
        t = up * vec[1:2, :]
        d = r * (t - jnp.mean(t, axis=-1, keepdims=True)
                 - zh * jnp.mean(t * zh, axis=-1, keepdims=True))
        dres2[rows, :] = d
        low = d.astype(BF16)
        full[1, c, rows, :] = low
        acc[1] += fold(up * zh)
        acc[3] += fold(up)
        acc[5] += fold(low.astype(F32))

    for k in range(NCH):
        arrived(1, k)
        tiles(k * cr, cr, norm_two)
        gather_start(1, k)

    line.hop(0)
    exchange(2, mlp_backward)
    line.hop(1)

    def flat(ref):
        return ref[...].reshape(4 * rows_own, ref.shape[-1])

    hid_all = flat(hid)
    d_all = full[1].reshape(4 * rows_own, width)
    grads[2] = dot_tn(d_all, hid_all).astype(BF16)
    n_all = full[0].reshape(4 * rows_own, width)
    grads[0] = dot_tn(n_all, flat(dgt)).astype(BF16)
    grads[1] = dot_tn(n_all, flat(dup)).astype(BF16)

    line.hop(2)

    def norm_back(rows):
        dn = summed(2, rows) + dres2[rows, :]
        zh = zh1[rows, :]
        t = dn * vec[0:1, :]
        d = r1[rows, :] * (t - jnp.mean(t, axis=-1, keepdims=True)
                           - zh * jnp.mean(t * zh, axis=-1, keepdims=True))
        dres1[rows, :] = d
        low = d.astype(BF16)
        full[2, c, rows, :] = low
        acc[0] += fold(dn * zh)
        acc[2] += fold(dn)
        acc[4] += fold(low.astype(F32))

    for k in range(NCH):
        arrived(2, k)
        tiles(k * cr, cr, norm_back)
        gather_start(2, k)

    for i in range(6):
        tiny[0, i : i + 1, :] = jnp.sum(acc[i], axis=0, keepdims=True)
    for i in range(2):
        small[6 + i : 7 + i, :] = jnp.sum(bsum[i], axis=0, keepdims=True)
    tiny_copies = []
    for step, peer in enumerate((sib, ynb)):
        copy = remote(tiny.at[2 * step], tiny.at[2 * step + 1], tiny_s.at[step], tiny_r.at[step], peer)
        copy.start()
        started.append(copy)
        tiny_copies.append(copy)
        if step == 0:
            def unproject(b, r0, n):
                return dot(full[2, b, pl.ds(r0, n), :], w_out[...]).astype(BF16)
            dmixed[c] = unproject(c, 0, rows_own)
            for k in range(NCH):
                ag_c[2, k].wait_recv()
            dmixed[sib] = unproject(sib, 0, rows_own)
        copy.wait_recv()
        total = tiny[2 * step] + tiny[2 * step + 1]
        if step == 0:
            tiny[2] = total
        else:
            small[0:6, :] = total[0:6, :]
    for k in range(NCH):
        forward(2, k)
        dmixed[ynb, chunk(k), :] = unproject(ynb, k * cr, cr)
    for k in range(NCH):
        ag_f[2, k].wait_recv()
        dmixed[dia, chunk(k), :] = unproject(dia, k * cr, cr)
    gout[...] = dot_tn(full[2].reshape(4 * rows_own, width), flat(mixed)).astype(BF16)
    line.hop(3)
    line.drain()
    for copy in started:
        copy.wait_send()


def sds(shape, dtype):
    return jax.ShapeDtypeStruct(shape, dtype)


def smem():
    return pl.BlockSpec(memory_space=pltpu.SMEM)


def on_device(
    tokens_in, qkv_weight, qv_bias, out_weight, geglu_weight, geglu_bias, down_weight,
    norm_gains, norm_biases, out_biases, doc_lengths, cotangent,
):
    seqs, rows, width = tokens_in.shape
    group = lax.axis_size("ctx")
    tp = lax.axis_size("tp")
    shards = lax.axis_size("shard")
    z = lax.axis_index("tp")
    c = lax.axis_index("ctx")
    assert group == 4 and tp == 4 and seqs == tp
    length = group * rows
    part_rows = qkv_weight.shape[1]
    cols = qkv_weight.shape[2]
    heads = cols // DH
    units = geglu_weight.shape[2]
    assert units == width and 4 * cols == width and H == heads * tp

    me = lax.axis_index("shard") * group + c
    dma = lambda *shape: pltpu.SemaphoreType.DMA(shape)
    head_shape = sds((heads, length, DH), BF16)
    block = (rows, width)
    stack = (group, rows, width)
    if shards == 2 and part_rows % 96 == 0:
        vm = pltpu.VMEM
        wide = part_rows + 16
        front, back = part_rows * FRONT_CUT // 6, part_rows * BACK_CUT // 6
        pieces = lambda n: (vm((n, part_rows, width), BF16), vm((2, n, part_rows, width), BF16))
        scratch = dict(
            pq=vm((part_rows, 640), BF16), po=vm((wide, 256), BF16),
            lout=vm((tp,) + block, BF16), input_grad=vm((tp,) + block, BF16), save=dma(2),
            zbq=vm((tp, part_rows, 640), BF16), zbo=vm((tp, wide, 256), BF16),
            zbr=vm((2, tp, part_rows, width), BF16),
            zbd=vm((tp, front, width), BF16), zbe=vm((tp, 2, part_rows - front, width), BF16),
            xd_s=dma(1), xd_r=dma(1),
            load=dma(6), qkv_v=vm((3, part_rows, cols), BF16), out_v=vm((cols, part_rows), BF16),
            down_v=vm((part_rows, width), BF16), geglu_v=vm((2, part_rows, width), BF16), cb=vm((2, 2, group, part_rows - back, width), BF16),
            yd=vm((2, part_rows - back, width), BF16), xd=vm((part_rows - back, width), BF16),
            ch_s=dma(2, 4), ch_r=dma(2, 4), cy_s=dma(4), cy_r=dma(1), cx_s=dma(1), cx_r=dma(1),
            cot=vm(block, BF16), xs=vm(stack, BF16),
            wq=vm((2, group, part_rows, 640), BF16), wo=vm((2, group, wide, 256), BF16),
            g0=vm((2, group, part_rows, width), BF16), w=vm((3, 2, group, part_rows, width), BF16),
            w_out=vm((width, cols), BF16),
            qv=vm((2, cols), F32), vec=vm((8, width), F32), extra=vm((32, 128), F32), ge=vm((2, group, 32, 128), BF16),
            xe=vm((group, 32, 128), BF16), ye=vm((group, 32, 128), BF16), re=vm((tp + 1, 32, 128), BF16),
            probs=vm((heads, length, length), BF16),
            q=vm((heads, length, DH), BF16), k=vm((heads, length, DH), BF16),
            v=vm((heads, length, DH), BF16), far=vm((rows, length), F32),
            mixed=vm((length, cols), BF16), dmixed=vm((length, cols), BF16),
            full=vm((3,) + stack, BF16), act=vm(stack, BF16), pull=vm(stack, BF16),
            hid=vm(stack, BF16),
            **{n: vm(block, BF16) for n in ("snd_r", "snd_o", "snd_y", "rcv_r", "rcv_o", "rcv_y")},
            **{n: vm(block, F32) for n in ("own", "yacc", "fa", "fb", "normed", "zh1")},
            r1=vm((rows, 1), F32), acc=vm((6, 8, width), F32), bsum=vm((2, 8, width), F32),
            tiny=vm((4, 8, width), F32),
            dqkv=vm((length, 3 * cols), BF16),
            dk_acc=vm((heads, DH, length), F32), dv_acc=vm((heads, DH, length), F32),
            xg_s=dma(3), xg_r=dma(3),
            **{n: dma(6, 4) for n in ("zu", "zd", "zu2", "zd2", "zr", "ys", "yr", "xs_s", "xs_r")},
            **{n: dma(5, 4) for n in ("gx_s", "gx_r", "gy_s", "gy_r",
                                      "gu_s", "gu_r", "gd_s", "gd_r")},
            **{n: dma(3, NCH) for n in ("ags_y", "agr_y", "ags_c", "agr_c", "ags_f", "agr_f")},
            **{n: dma(4, NCH) for n in ("rss_r", "rsr_r", "rss_o", "rsr_o", "rss_y", "rsr_y")},
            tiny_s=dma(2), tiny_r=dma(2), lv=dma(2, tp), lw=dma(2, tp), lr=dma(2, tp), lu=dma(NCH, tp), ld=dma(NCH, tp), li=dma(NCH, tp),
        )
        for n, count in (("xb", group), ("yb", group), ("rb", tp + 1)):
            scratch[n + "0"], scratch[n + "r"] = pieces(count)
            scratch[n + "h"] = vm((count, back, width), BF16)
        raw = pl.pallas_call(
            functools.partial(layer, tuple(scratch), heads),
            out_shape=[
                sds((tp,) + block, BF16), sds((tp,) + block, BF16),
                sds((part_rows, width), F32), sds((32, 128), F32), sds((3, part_rows, width), F32),
            ],
            in_specs=[smem()] + [pl.BlockSpec(memory_space=pl.ANY)] * 6 + vmem(5),
            out_specs=[pl.BlockSpec(memory_space=pl.ANY)] * 2 + vmem(3),
            scratch_shapes=list(scratch.values()),
            compiler_params=pltpu.CompilerParams(
                collective_id=1, has_side_effects=True, vmem_limit_bytes=VMEM_MB * MB
            ),
            name="layer",
        )(
            doc_lengths, tokens_in, cotangent, qkv_weight, out_weight, geglu_weight,
            down_weight.T, qv_bias, geglu_bias, norm_gains, norm_biases, out_biases,
        )
        res = pl.pallas_call(
            finish,
            out_shape=[
                sds((tp,) + block, BF16), sds((tp,) + block, F32),
                sds(qkv_weight.shape, F32), sds(qv_bias.shape, F32), sds(out_weight.shape, F32),
                sds(geglu_weight.shape, F32), sds(geglu_bias.shape, F32),
                sds(down_weight.shape[::-1], F32),
            ] + [sds(norm_gains.shape, F32)] * 3,
            in_specs=[pl.BlockSpec(memory_space=pl.ANY)] * 5,
            out_specs=[pl.BlockSpec(memory_space=pl.ANY)] * 11,
            scratch_shapes=[
                vm((tp,) + block, BF16), vm((tp,) + block, BF16), vm((tp,) + block, F32),
                vm((part_rows, width), F32), vm((32, 128), F32), vm((3, part_rows, width), F32),
                vm(qkv_weight.shape, F32), vm(qv_bias.shape, F32), vm(out_weight.shape, F32),
                vm(geglu_bias.shape, F32),
            ] + [vm(norm_gains.shape, F32)] * 3 + [dma(3 + 2 * tp), dma(9 + 2 * tp)],
            compiler_params=pltpu.CompilerParams(vmem_limit_bytes=VMEM_MB * MB),
            name="finish",
        )(*raw)
        return (*res[:7], res[7].T, *res[8:])

    with jax.named_scope("pack_weights"):
        first = jnp.concatenate(
            [qkv_weight[0], qkv_weight[1], qkv_weight[2], out_weight.T], axis=1
        )
        own_norm = jnp.concatenate([norm_gains, norm_biases, out_biases], axis=0)
        parts = jnp.concatenate([first[None], geglu_weight, down_weight.T[None]], axis=0)
        own_bias = jnp.concatenate([qv_bias.reshape(1, -1), geglu_bias.reshape(1, -1)], axis=1)

    lengths = lax.dynamic_slice_in_dim(doc_lengths, z, 1, 0)
    x_own = lax.dynamic_index_in_dim(tokens_in, z, 0, keepdims=False)
    cot_own = lax.dynamic_index_in_dim(cotangent, z, 0, keepdims=False)
    with jax.named_scope("gather_weights"):
        by_block = lax.all_gather(parts, "tp", axis=0)
        swapped = lax.all_to_all(by_block, "ctx", split_axis=0, concat_axis=0)
        w = lax.all_gather(swapped, "shard", axis=0)
        w = w.transpose(2, 0, 1, 3, 4).reshape(4, shards * group * part_rows, width)
        biases = lax.all_gather(own_bias, "tp", axis=0, tiled=True)
        biases = lax.dynamic_slice_in_dim(biases, c, 1, 0).astype(F32)
        norms = lax.all_gather(own_norm, ("shard", "ctx"), axis=1, tiled=True).astype(F32)
    qv = biases[:, : 2 * cols].reshape(2, cols)
    vec = jnp.concatenate([norms, biases[:, 2 * cols :].reshape(2, units)], axis=0)

    xs = lax.all_gather(x_own, "ctx", axis=0, tiled=True)

    mixed, probs, q, k, v = pl.pallas_call(
        functools.partial(attention_forward, heads),
        out_shape=[sds((length, cols), BF16), sds((heads, length, length), BF16)] + [head_shape] * 3,
        in_specs=[smem()] + vmem(3),
        out_specs=vmem(5),
        scratch_shapes=[pltpu.VMEM((256, length), F32)],
        compiler_params=pltpu.CompilerParams(vmem_limit_bytes=48 * MB),
        name="attention_forward",
    )(lengths, xs, w[0], qv)
    w0, w = w[0], w[1:]


    lout, dres1, grads, gout, dmixed, small = pl.pallas_call(
        middle,
        out_shape=[
            sds((tp,) + block, BF16), sds(block, F32), sds((3, width, width), BF16),
            sds((width, cols), BF16), sds((group, rows, cols), BF16), sds((8, width), F32),
        ],
        in_specs=vmem(6),
        out_specs=vmem(6),
        scratch_shapes=[
            pltpu.VMEM((width, cols), BF16), pltpu.VMEM((3,) + stack, BF16),
        ] + [pltpu.VMEM(stack, BF16)] * 5 + [pltpu.VMEM((3,) + block, BF16)] * 6 + [
            pltpu.VMEM(block, F32)
        ] * 6 + [
            pltpu.VMEM((rows, 1), F32), pltpu.VMEM(block, F32),
            pltpu.VMEM((6, 8, width), F32), pltpu.VMEM((2, 8, width), F32),
            pltpu.VMEM((4, 8, width), F32),
        ] + [dma(3, NCH)] * 12 + [dma(2)] * 2 + [dma(5), dma(tp)],
        compiler_params=pltpu.CompilerParams(
            collective_id=0, has_side_effects=True, vmem_limit_bytes=58 * MB
        ),
        name="middle",
    )(x_own, cot_own, mixed.reshape(group, rows, cols), w0, w, vec)

    grad_w, d_in, bias_grad = pl.pallas_call(
        functools.partial(attention_backward, heads),
        out_shape=[
            sds((width, 3 * cols), BF16), sds((length, width), BF16), sds((1, 3 * cols), F32)
        ],
        in_specs=vmem(8),
        out_specs=vmem(3),
        scratch_shapes=[
            pltpu.VMEM((length, 3 * cols), BF16),
            pltpu.VMEM((heads, DH, length), F32), pltpu.VMEM((heads, DH, length), F32),
        ],
        compiler_params=pltpu.CompilerParams(vmem_limit_bytes=48 * MB),
        name="attention_backward",
    )(dmixed.reshape(length, cols), mixed, probs, q, k, v, xs, w0)

    with jax.named_scope("outputs"):
        input_sum = lax.psum_scatter(d_in, "ctx", scatter_dimension=0, tiled=True)
        input_own = (input_sum.astype(F32) + dres1).astype(BF16)
        input_grad = lax.all_gather(input_own, "tp", axis=0).astype(F32)
        layer_out = lout

    with jax.named_scope("scatter_grads"):
        first_grad = jnp.concatenate([grad_w, gout], axis=1)
        packed = jnp.concatenate([first_grad[None], grads], axis=0)
        packed = packed.reshape(4, shards, group, part_rows, width).transpose(1, 2, 0, 3, 4)
        mine = lax.psum_scatter(packed, "shard", scatter_dimension=0, tiled=False)
        mine = lax.all_to_all(mine, "ctx", split_axis=0, concat_axis=0)
        mine = lax.psum_scatter(mine, "tp", scatter_dimension=0, tiled=False)
        mine = mine.astype(F32)
        grad_qkv = jnp.stack([mine[0, :, i * cols : (i + 1) * cols] for i in range(3)])
        grad_out = mine[0, :, 3 * cols :].T
        grad_geglu = mine[1:3]
        grad_down = mine[3].T
        col = jnp.concatenate(
            [bias_grad[:, :cols], bias_grad[:, 2 * cols :], small[6:7], small[7:8]], axis=1
        )
        col = lax.psum_scatter(
            jnp.zeros((group, col.shape[1]), F32) + jnp.where(
                jnp.arange(group)[:, None] == c, col, 0.0),
            "tp", scatter_dimension=0, tiled=True)
        col = lax.psum(col, ("shard", "ctx"))
        norm_grad = lax.psum(small[:6], ("shard", "tp"))
        norm_grad = lax.dynamic_slice_in_dim(norm_grad, me * part_rows, part_rows, 1)
    return (
        layer_out,
        input_grad,
        grad_qkv,
        col[:, : 2 * cols].reshape(2, cols),
        grad_out,
        grad_geglu,
        col[:, 2 * cols :].reshape(2, units),
        grad_down,
        norm_grad[0:2],
        norm_grad[2:4],
        norm_grad[4:6],
    )


def solution(mesh):
    in_specs = (
        P("shard", "ctx", None),
        P(None, ("shard", "ctx"), "tp"),
        P(None, "tp"),
        P("tp", ("shard", "ctx")),
        P(None, ("shard", "ctx"), "tp"),
        P(None, "tp"),
        P("tp", ("shard", "ctx")),
        P(None, ("shard", "ctx")),
        P(None, ("shard", "ctx")),
        P(None, ("shard", "ctx")),
        P("shard", None),
        P("shard", "ctx", None),
    )
    out_specs = (
        P("shard", "ctx", None),
        P("shard", "ctx", None),
        P(None, ("shard", "ctx"), "tp"),
        P(None, "tp"),
        P("tp", ("shard", "ctx")),
        P(None, ("shard", "ctx"), "tp"),
        P(None, "tp"),
        P("tp", ("shard", "ctx")),
        P(None, ("shard", "ctx")),
        P(None, ("shard", "ctx")),
        P(None, ("shard", "ctx")),
    )
    return jax.shard_map(
        on_device, mesh=mesh, in_specs=in_specs, out_specs=out_specs, check_vma=False
    )
```

```python
import functools
import math
import types

import jax
import jax.numpy as jnp
from jax import lax
from jax.experimental import pallas as pl
from jax.experimental.pallas import tpu as pltpu
from jax.sharding import PartitionSpec as P

H = 12
DH = 64
F32 = jnp.float32
BF16 = jnp.bfloat16
MESH = pl.DeviceIdType.MESH
NCH = 4
TILE = 32
MB = 1 << 20
VMEM_MB = 62
FRONT_CUT = 3
BACK_CUT = 3


def alibi_slopes(head_count):
    def power_slopes(head_total):
        first_slope = 2.0 ** (-8.0 / head_total)
        return [first_slope ** (counter + 1) for counter in range(head_total)]

    nearest = 2 ** int(math.floor(math.log2(head_count)))
    slope_list = power_slopes(nearest)
    return slope_list + power_slopes(2 * nearest)[0::2][: head_count - nearest]


def dot(left, right):
    return jnp.dot(left, right, preferred_element_type=F32)


def dot_nt(left, right):
    return lax.dot_general(left, right, (((1,), (1,)), ((), ())), preferred_element_type=F32)


def dot_tn(left, right):
    return lax.dot_general(left, right, (((0,), (0,)), ((), ())), preferred_element_type=F32)


def vmem(count):
    return [pl.BlockSpec(memory_space=pltpu.VMEM)] * count


def project_heads(heads, x_rows, rows, w, bias, q_out, k_out, v_out):
    cols = heads * DH
    for part, out in enumerate((q_out, k_out, v_out)):
        y = dot(x_rows, w[:, part * cols : (part + 1) * cols])
        if part != 1:
            y = y + bias[part // 2 : part // 2 + 1, :]
        y = y.astype(BF16)
        if part == 0:
            y = y * BF16(1.0 / math.sqrt(DH))
        for i in range(heads):
            out[i, rows, :] = y[:, i * DH : (i + 1) * DH]


def segments(lengths, row, pos):
    seg = jnp.zeros(pos.shape, jnp.int32)
    end = 0
    for k in range(lengths.shape[1]):
        end = end + lengths[row, k]
        seg = seg + (pos >= end).astype(jnp.int32)
    return seg


def head_slopes(heads):
    table = alibi_slopes(H)
    c = lax.axis_index("ctx")
    mine = []
    for i in range(heads):
        value = jnp.float32(table[i])
        for j in range(1, H // heads):
            value = jnp.where(c == j, jnp.float32(table[j * heads + i]), value)
        mine.append(value)
    return mine


def attend_rows(heads, start, step, lengths, row, q, k, v, probs, mixed, far):
    length = k.shape[1]
    slopes = head_slopes(heads)
    rows = pl.ds(start, step)
    key_pos = lax.broadcasted_iota(jnp.int32, (1, length), 1)
    pos = start + lax.broadcasted_iota(jnp.int32, (step, 1), 0)
    same = segments(lengths, row, pos) == segments(lengths, row, key_pos)
    far[...] = jnp.where(same, jnp.abs(pos - key_pos).astype(F32), 1e33)
    for i in range(heads):
        s = dot_nt(q[i, rows, :], k[i]) - slopes[i] * far[...]
        p = jnp.exp(s - jnp.max(s, axis=-1, keepdims=True))
        p = (p * (1.0 / jnp.sum(p, axis=-1, keepdims=True))).astype(BF16)
        probs[i, rows, :] = p
        mixed[rows, i * DH : (i + 1) * DH] = dot(p, v[i]).astype(BF16)


def attention_forward(
    heads, lengths, xs, w, bias, mixed, probs, q_out, k_out, v_out, far
):
    step = 256

    def project(r, carry):
        rows = pl.ds(pl.multiple_of(r * step, step), step)
        project_heads(heads, xs[rows, :], rows, w, bias, q_out, k_out, v_out)
        return carry

    def attend(r, carry):
        start = pl.multiple_of(r * step, step)
        attend_rows(
            heads, start, step, lengths, 0, q_out, k_out, v_out, probs, mixed, far)
        return carry

    lax.fori_loop(0, xs.shape[0] // step, project, 0)
    lax.fori_loop(0, xs.shape[0] // step, attend, 0)


def attend_back(heads, rows, dmixed, mixed, probs, q, k, v, dqkv, dk_acc, dv_acc):
    for i in range(heads):
        own = slice(i * DH, (i + 1) * DH)
        d_out = dmixed[rows, own]
        row_dot = jnp.sum(
            d_out.astype(F32) * mixed[rows, own].astype(F32), axis=-1, keepdims=True
        )
        p = probs[i, rows, :]
        dp = dot_nt(d_out, v[i])
        ds = (p.astype(F32) * (dp - row_dot)).astype(BF16)
        dqkv[rows, own] = (dot(ds, k[i]) * (1.0 / math.sqrt(DH))).astype(BF16)
        dk_acc[i] += dot_tn(q[i, rows, :], ds)
        dv_acc[i] += dot_tn(d_out, p)


def spread_heads(heads, dqkv, dk_acc, dv_acc):
    cols = heads * DH
    for i in range(heads):
        dqkv[:, cols + i * DH : cols + (i + 1) * DH] = dk_acc[i].T.astype(BF16)
        dqkv[:, 2 * cols + i * DH : 2 * cols + (i + 1) * DH] = dv_acc[i].T.astype(BF16)


def attention_backward(
    heads, dmixed, mixed, probs, q, k, v, xs, w, grad_w, d_in, bias_grad, dqkv, dk_acc, dv_acc
):
    length = xs.shape[0]
    step = 256
    cols = heads * DH
    dk_acc[...] = jnp.zeros_like(dk_acc)
    dv_acc[...] = jnp.zeros_like(dv_acc)

    def rows_back(r, carry):
        rows = pl.ds(pl.multiple_of(r * step, step), step)
        attend_back(heads, rows, dmixed, mixed, probs, q, k, v, dqkv, dk_acc, dv_acc)
        return carry

    lax.fori_loop(0, length // step, rows_back, 0)
    spread_heads(heads, dqkv, dk_acc, dv_acc)

    def finish(r, total):
        rows = pl.ds(pl.multiple_of(r * step, step), step)
        d = dqkv[rows, :]
        d_in[rows, :] = dot_nt(d, w[:, : 3 * cols]).astype(BF16)
        return total + jnp.sum(d.astype(F32), axis=0, keepdims=True)

    bias_grad[...] = lax.fori_loop(
        0, length // step, finish, jnp.zeros((1, 3 * cols), F32)
    )
    for part in range(3):
        own = slice(part * cols, (part + 1) * cols)
        grad_w[:, own] = dot_tn(xs[...], dqkv[:, own]).astype(BF16)


class Links:
    def __init__(self):
        self.started = []

    def copy(self, src, dst, send, recv, peer):
        return pltpu.make_async_remote_copy(
            src_ref=src, dst_ref=dst, send_sem=send, recv_sem=recv,
            device_id=peer, device_id_type=MESH,
        )

    def start(self, src, dst, send, recv, peer):
        copy = self.copy(src, dst, send, recv, peer)
        copy.start()
        self.started.append(copy)
        return copy

    def sent(self, copy):
        if any(copy is one for one in self.started):
            copy.wait_send()
            self.started = [one for one in self.started if one is not copy]

    def drain(self):
        for copy in self.started:
            copy.wait_send()
        self.started = []


def greet(peers, between=None):
    barrier = pltpu.get_barrier_semaphore()
    for peer in peers:
        pl.semaphore_signal(barrier, inc=1, device_id=peer, device_id_type=MESH)
    if between is not None:
        between()
    pl.semaphore_wait(barrier, len(peers))


def places():
    c = lax.axis_index("ctx")
    flip = 1 - 2 * (c % 2)
    ynb = (c + 2) % 4
    return c, c + flip, ynb, ynb + flip


class LineGather:
    def __init__(self, blocks, sems, recv):
        self.blocks, self.sems, self.recv = blocks, sems, recv
        self.z = lax.axis_index("tp")
        self.last = blocks.shape[0] - 1

    def _copy(self, j, which, peer):
        block = self.blocks.at[j]
        return pltpu.make_async_remote_copy(
            src_ref=block, dst_ref=block, send_sem=self.sems.at[which], recv_sem=self.recv.at[j],
            device_id={"tp": peer}, device_id_type=MESH,
        )

    def _sends(self, act):
        z = self.z
        for which, step in enumerate((1, -1, 2, -2)):
            @pl.when(jnp.logical_and(z + step >= 0, z + step <= self.last))
            def _(which=which, step=step):
                act(self._copy(z, which, z + step))

    def _passed(self, act):
        z, last = self.z, self.last

        @pl.when(z == 2)
        def _():
            act(self._copy(0, 4, last))

        @pl.when(z == 1)
        def _():
            act(self._copy(last, 4, 0))

    def hop(self, d):
        z = self.z
        if d == 0:
            self._sends(lambda copy: copy.start())
            return
        for j in (z - d, z + d):
            @pl.when(jnp.logical_and(j >= 0, j <= self.last))
            def _(j=j):
                self._copy(j, 0, z).wait_recv()
        if d == 2:
            self._passed(lambda copy: copy.start())

    def drain(self):
        self._sends(lambda copy: copy.wait_send())
        self._passed(lambda copy: copy.wait_send())


class LineRelay:
    def __init__(self, blocks, up, down, recv):
        self.parts = up.shape[0]
        self.blocks, self.up, self.down, self.recv = blocks, up, down, recv
        self.z = lax.axis_index("tp")
        self.last = blocks.shape[0] - 1
        self.rows = blocks.shape[1] // self.parts

    def _copy(self, j, h, sem, peer):
        block = self.blocks.at[j, pl.ds(h * self.rows, self.rows)]
        return pltpu.make_async_remote_copy(
            src_ref=block, dst_ref=block, send_sem=sem.at[h, j], recv_sem=self.recv.at[h, j],
            device_id={"tp": peer}, device_id_type=MESH,
        )

    def _sides(self, d):
        z, last = self.z, self.last
        yield self.up, z - d, z - d >= 0, z < last, z + 1
        yield self.down, z + d, z + d <= last, z > 0, z - 1

    def hop(self, d, h):
        for sem, j, here, onward, peer in self._sides(d):
            @pl.when(here)
            def _(sem=sem, j=j, onward=onward, peer=peer):
                if d:
                    self._copy(j, h, sem, self.z).wait_recv()
                if d < self.last:
                    @pl.when(onward)
                    def _():
                        self._copy(j, h, sem, peer).start()

    def drain(self):
        for d in range(self.last):
            for h in range(self.parts):
                for sem, j, here, onward, _ in self._sides(d):
                    @pl.when(jnp.logical_and(here, onward))
                    def _(sem=sem, j=j, h=h):
                        self._copy(j, h, sem, self.z).wait_send()


def layer(
    names, heads, lengths,
    tokens, cotangent, qkv_w, out_w, geglu_w, down_w, qv_b, geglu_b, gains, shifts, out_b,
    lout, input_grad, out0, oute, outr, *scratch,
):
    r = types.SimpleNamespace(**dict(zip(names, scratch)))
    c, sib, ynb, dia = places()
    me = lax.axis_index("shard")
    z = lax.axis_index("tp")
    other = 1 - me
    tp, rows_own, width = lout.shape
    piece = outr.shape[1]
    cols = heads * DH
    length = 4 * rows_own
    cr = rows_own // NCH
    links = Links()
    start, copy = links.start, links.copy

    def block(body):
        pl.when(z >= 0)(body)


    def local(src, dst, i):
        return pltpu.make_async_copy(src, dst, r.load.at[i])

    load_x = local(tokens.at[z], r.xs.at[c], 0)
    load_c = local(cotangent.at[z], r.cot, 1)
    loads = [local(qkv_w, r.qkv_v, 2), local(out_w, r.out_v, 3), local(down_w, r.down_v, 4),
             local(geglu_w, r.geglu_v, 5)]

    span = r.po.shape[1]
    thirds = width // span

    def pack():
        for one in loads + [load_x, load_c]:
            one.start()
        for one in loads:
            one.wait()
        for i in range(3):
            r.pq[:, i * cols : (i + 1) * cols] = r.qkv_v[i]
        r.pq[:, 3 * cols :] = jnp.zeros((piece, r.pq.shape[1] - 3 * cols), BF16)
        for i in range(2):
            for h in range(heads):
                r.pq[i * heads + h : i * heads + h + 1, 3 * cols : 3 * cols + DH] = (
                    qv_b[i : i + 1, h * DH : (h + 1) * DH])
        r.po[...] = jnp.zeros_like(r.po)
        r.po[0:piece, 0:cols] = r.out_v[...].T
        for i in range(2):
            for t in range(thirds):
                row = piece + i * thirds + t
                r.po[row : row + 1, :] = geglu_b[i : i + 1, t * span : (t + 1) * span]
        row = piece + 2 * thirds
        for i, ref in enumerate((gains, shifts, out_b)):
            r.po[row + 2 * i : row + 2 * i + 2, 0:piece] = ref[...]

    greet([{"ctx": sib}, {"ctx": ynb}, {"ctx": dia}, {"shard": other}]
          + [{"tp": (z + d) % tp} for d in range(1, tp)], pack)

    half = piece * FRONT_CUT // 6
    rest = piece - half
    cut = piece * BACK_CUT // 6
    tail = piece - cut
    src = {"q": r.pq, "o": r.po, 0: r.geglu_v.at[0], 1: r.geglu_v.at[1],
           2: r.down_v.at[pl.ds(0, half)]}
    zb = {"q": r.zbq, "o": r.zbo, 0: r.zbr.at[0], 1: r.zbr.at[1], 2: r.zbd, 3: r.zbe}
    wr = {"q": r.wq, "o": r.wo, 0: r.w.at[0], 1: r.w.at[1]}
    index = {"q": 0, "o": 1, 0: 2, 1: 3, 2: 4, 3: 5}
    last = tp - 1

    def line_copy(p, j, sems, peer):
        block = zb[p].at[j]
        return copy(block, block, sems.at[index[p], j], r.zr.at[index[p], j], {"tp": peer})

    def slot_at(p, s, j):
        if p == 2:
            return r.w.at[2, s, j, pl.ds(0, half)]
        return wr[p].at[s, j]

    def owner_slot(p, j):
        if p == 3:
            return r.w.at[2, :, j, pl.ds(half, rest)]
        return slot_at(p, me, j)

    def hop(p, d):
        def deliver(j):
            @pl.when(j == c)
            def _():
                owner_slot(p, c)[...] = zb[p].at[j][...]

            @pl.when(j != c)
            def _():
                copy(zb[p].at[j], owner_slot(p, c), r.ys.at[index[p], j], r.yr.at[index[p], c],
                     {"ctx": j}).start()

        if d == 0:
            if p == 3:
                held["crossed"].wait_recv()
            else:
                zb[p].at[z][...] = src[p][...]

            for step in (1,):
                sems = r.zu if step == 1 else r.zu2

                @pl.when(z + step <= last)
                def _(step=step, sems=sems):
                    line_copy(p, z, sems, z + step).start()

                sems = r.zd if step == 1 else r.zd2

                @pl.when(z - step >= 0)
                def _(step=step, sems=sems):
                    line_copy(p, z, sems, z - step).start()

            deliver(z)
            return
        for side in range(2):
            j = z - d if side == 0 else z + d

            @pl.when((j >= 0) if side == 0 else (j <= last))
            def _(side=side, j=j):
                line_copy(p, j, r.zu, z).wait_recv()
                if d < last:
                    @pl.when((z < last) if side == 0 else (z > 0))
                    def _():
                        if side == 0:
                            line_copy(p, j, r.zu, z + 1).start()
                        else:
                            line_copy(p, j, r.zd, z - 1).start()
                deliver(j)

    def hop_drain(p):
        for d in range(last):
            for side in range(2):
                j = z - d if side == 0 else z + d
                here = (j >= 0) if side == 0 else (j <= last)
                edge = (z < last) if side == 0 else (z > 0)

                @pl.when(jnp.logical_and(here, edge))
                def _(side=side, j=j):
                    line_copy(p, j, r.zu if side == 0 else r.zd, z).wait_send()

        for j in (sib, ynb, dia):
            copy(zb[p].at[j], owner_slot(p, c), r.ys.at[index[p], j], r.yr.at[index[p], c],
                 {"ctx": j}).wait_send()

    def owned(p, j):
        copy(zb[p].at[c], owner_slot(p, j), r.ys.at[index[p], c], r.yr.at[index[p], j],
             {"ctx": c}).wait_recv()

    def shard_copy(p, i, j):
        slot = slot_at(p, me, j)
        return copy(slot, slot, r.xs_s.at[index[p], i], r.xs_r.at[index[p], j], {"shard": other})

    def to_shard(p):
        for i, j in enumerate((c, sib, ynb, dia)):
            if i:
                owned(p, j)
            shard_copy(p, i, j).start()

    far_off = jnp.abs(z - c)

    def to_shard_if(p, low, high):
        @pl.when(jnp.logical_and(far_off >= low, far_off <= high))
        def _():
            to_shard(p)

    def shard_drain(p):
        for i in range(4):
            shard_copy(p, i, c).wait_send()

    def complete(p):
        if p == 3:
            for j in (sib, ynb, dia):
                owned(p, j)
            return
        for j in range(4):
            slot = slot_at(p, other, j)
            copy(slot, slot, r.xs_s.at[index[p], 0], r.xs_r.at[index[p], j],
                 {"shard": other}).wait_recv()

    grad = [r.g0] + [r.w.at[i] for i in range(2)]
    xb = [r.xb0] + [r.xbr.at[i] for i in range(2)] + [r.xbh]
    yb = [r.yb0] + [r.ybr.at[i] for i in range(2)] + [r.ybh]
    rb = [r.rb0] + [r.rbr.at[i] for i in range(2)] + [r.rbh]
    out = [out0] + [outr.at[i] for i in range(2)] + [outr.at[2, pl.ds(0, cut)]]

    def grad_at(p, s, j):
        if p == 3:
            return r.w.at[2, s, j, pl.ds(0, cut)]
        return grad[3 if p == 4 else p].at[s, j]

    SMALL = 4
    grad.append(r.ge)
    xb.append(r.xe)
    yb.append(r.ye)
    rb.append(r.re)
    out.append(oute)

    def beside(p):
        return (p, SMALL) if p == 0 else (p,)

    def grad_to_shard(p):
        for i, j in enumerate((dia, ynb, sib, c)):
            for n in beside(p):
                start(grad_at(n, other, j), xb[n].at[j], r.gx_s.at[n, i], r.gx_r.at[n, j], {"shard": other})

    def grad_to_owner(p, i):
        j = (dia, ynb, sib, c)[i]
        for n in beside(p):
            copy(grad_at(n, other, j), xb[n].at[j], r.gx_s.at[n, 0], r.gx_r.at[n, j],
                 {"shard": other}).wait_recv()
            total = (grad_at(n, me, j)[...].astype(F32) + xb[n].at[j][...].astype(F32)).astype(BF16)
            if i == 3:
                yb[n].at[c][...] = total
            else:
                xb[n].at[j][...] = total
                start(xb[n].at[j], yb[n].at[c], r.gy_s.at[n, i], r.gy_r.at[n, c], {"ctx": j})

    def grad_came(p, j):
        @pl.when(j != c)
        def _():
            copy(xb[p].at[j], yb[p].at[j], r.gy_s.at[p, 0], r.gy_r.at[p, j], {"ctx": j}).wait_recv()

    def climb(p, side, j):
        if side == 0:
            return copy(yb[p].at[j], rb[p].at[j], r.gu_s.at[p, j], r.gu_r.at[p, j], {"tp": z + 1})
        slot = jnp.where(j == z - 1, tp, j)
        return copy(yb[p].at[j], rb[p].at[slot], r.gd_s.at[p, j], r.gd_r.at[p, j], {"tp": z - 1})

    def grad_hop_one(p, h):
        if h == last:
            grad_came(p, z)
            out[p][...] = yb[p].at[z][...].astype(F32)

            @pl.when(z > 0)
            def _():
                copy(yb[p].at[z], rb[p].at[z], r.gu_s.at[p, z], r.gu_r.at[p, z], {"tp": z}).wait_recv()
                out[p][...] += rb[p].at[z][...].astype(F32)

            @pl.when(z < last)
            def _():
                copy(yb[p].at[z], rb[p].at[tp], r.gd_s.at[p, z], r.gd_r.at[p, z], {"tp": z}).wait_recv()
                out[p][...] += rb[p].at[tp][...].astype(F32)
            return
        for side in range(2):
            j = z + (last - h) if side == 0 else z - (last - h)

            @pl.when((j <= last) if side == 0 else (j >= 0))
            def _(side=side, j=j):
                grad_came(p, j)

                @pl.when((z > 0) if side == 0 else (z < last))
                def _():
                    sems = r.gu_r if side == 0 else r.gd_r
                    copy(yb[p].at[j], rb[p].at[j], r.gu_s.at[p, j], sems.at[p, j], {"tp": z}).wait_recv()
                    yb[p].at[j][...] = (
                        yb[p].at[j][...].astype(F32) + rb[p].at[j][...].astype(F32)).astype(BF16)
                climb(p, side, j).start()

    def grad_hop(p, h):
        for n in beside(p):
            grad_hop_one(n, h)

    stage = jnp.where(z < c, z, last - z)

    def chain_mine(i):
        return r.w.at[2, i // 2, pl.ds(2 * (i % 2), 2), pl.ds(cut, tail)]

    def chain_came(side, i):
        return r.cb.at[side, i // 2, pl.ds(2 * (i % 2), 2)]

    def chain_copy(i, side):
        return copy(chain_mine(i), chain_came(side, i),
                    r.ch_s.at[side, i], r.ch_r.at[side, i], {"tp": z + 1 if side == 0 else z - 1})

    def chain_wait(i, side):
        copy(chain_mine(i), chain_came(side, i),
             r.ch_s.at[side, i], r.ch_r.at[side, i], {"tp": z}).wait_recv()
        mine = chain_mine(i)
        mine[...] = (mine[...].astype(F32) + chain_came(side, i)[...].astype(F32)).astype(BF16)

    def chain(slot):
        for i in range(4):
            for side in range(2):
                here = (z < c) if side == 0 else (z > c)
                if slot == 0:
                    @pl.when(jnp.logical_and(here, stage == 0))
                    def _(i=i, side=side):
                        chain_copy(i, side).start()
                else:
                    @pl.when(jnp.logical_and(here, jnp.logical_and(stage > 0, stage == slot - i)))
                    def _(i=i, side=side):
                        chain_wait(i, side)
                        chain_copy(i, side).start()

    def chain_send(j):
        return copy(r.w.at[2, :, j, pl.ds(cut, tail)], r.yd, r.cy_s.at[j], r.cy_r.at[0], {"ctx": j})

    def chain_end():
        @pl.when(z == c)
        def _():
            for i in range(4):
                @pl.when(z > 0)
                def _(i=i):
                    chain_wait(i, 0)

                @pl.when(z < last)
                def _(i=i):
                    chain_wait(i, 1)
            r.yd[...] = r.w[2, :, c, cut:, :]
            for j in (dia, ynb, sib):
                chain_send(j).start()

    def chain_across():
        @pl.when(z != c)
        def _():
            chain_send(c).wait_recv()
        start(r.yd.at[other], r.xd, r.cx_s.at[0], r.cx_r.at[0], {"shard": other})

    def chain_total():
        copy(r.yd.at[other], r.xd, r.cx_s.at[0], r.cx_r.at[0], {"shard": other}).wait_recv()
        outr[2, cut:, :] = r.yd[me].astype(F32) + r.xd[...].astype(F32)

    def chain_drain():
        for i in range(4):
            for side in range(2):
                @pl.when((z < c) if side == 0 else (z > c))
                def _(i=i, side=side):
                    chain_copy(i, side).wait_send()

        @pl.when(z == c)
        def _():
            for j in (dia, ynb, sib):
                chain_send(j).wait_send()

    def grad_drain(p):
        for h in range(last):
            for side in range(2):
                j = z + (last - h) if side == 0 else z - (last - h)

                @pl.when((j <= last) if side == 0 else (j >= 0))
                def _(side=side, j=j):
                    climb(p, side, j).wait_send()

    def chunk(k):
        return pl.ds(k * cr, cr)

    ag_y, ag_c, ag_f, rs_r, rs_o, rs_y = ({} for _ in range(6))

    def gather_start(o, k):
        block = r.full.at[o, c, chunk(k)]
        ag_y[o, k] = start(block, block, r.ags_y.at[o, k], r.agr_y.at[o, k], {"ctx": ynb})
        ag_c[o, k] = start(block, block, r.ags_c.at[o, k], r.agr_c.at[o, k], {"ctx": sib})

    def forward(o, k):
        ag_y[o, k].wait_recv()
        block = r.full.at[o, ynb, chunk(k)]
        ag_f[o, k] = start(block, block, r.ags_f.at[o, k], r.agr_f.at[o, k], {"ctx": sib})

    def free(table, o, k):
        if o:
            links.sent(table[o - 1, k])

    def send_relay(o, k):
        rs_r[o, k] = start(r.snd_r.at[chunk(k)], r.rcv_r.at[chunk(k)],
                           r.rss_r.at[o, k], r.rsr_r.at[o, k], {"ctx": sib})

    def send_own(o, k):
        rs_o[o, k] = start(r.snd_o.at[chunk(k)], r.rcv_o.at[chunk(k)],
                           r.rss_o.at[o, k], r.rsr_o.at[o, k], {"ctx": sib})

    def relay(o, k):
        rs_r[o, k].wait_recv()
        free(rs_y, o, k)
        r.snd_y[chunk(k), :] = (
            r.yacc[chunk(k), :] + r.rcv_r[chunk(k), :].astype(F32)).astype(BF16)
        rs_y[o, k] = start(r.snd_y.at[chunk(k)], r.rcv_y.at[chunk(k)],
                           r.rss_y.at[o, k], r.rsr_y.at[o, k], {"ctx": ynb})

    def arrived(o, k):
        rs_o[o, k].wait_recv()
        rs_y[o, k].wait_recv()

    def summed(rows):
        return r.own[rows, :] + r.rcv_o[rows, :].astype(F32) + r.rcv_y[rows, :].astype(F32)

    def tiles(first, count, body):
        def step(t, carry):
            body(pl.ds(pl.multiple_of(first + t * TILE, TILE), TILE))
            return carry
        lax.fori_loop(0, count // TILE, step, 0)

    def fold(values):
        return jnp.sum(values.reshape(TILE // 8, 8, width), axis=0)

    def rows_of(b, r0=0, n=rows_own):
        return pl.ds(pl.multiple_of(b * rows_own + r0, cr), n)

    def both(parts):
        return jnp.concatenate(parts, axis=0)

    def far_blocks(o, k, product):
        free(rs_r, o, k)

        @block
        def _():
            value = product()
            r.snd_r[chunk(k), :] = value[:cr].astype(BF16)
            r.yacc[chunk(k), :] = value[cr:]
        send_relay(o, k)

    def near_block(o, product):
        for k in range(NCH):
            free(rs_o, o, k)

        @block
        def _():
            r.snd_o[...] = product().astype(BF16)
        for k in range(NCH):
            send_own(o, k)

    def own_block(product):
        @block
        def _():
            r.own[...] = product()

    def wait_near(o):
        for k in range(NCH):
            ag_c[o, k].wait_recv()

    def wait_far(o, k):
        ag_f[o, k].wait_recv()

    held = {}

    def cross_down():
        load_x.wait()
        held["crossed"] = start(
            r.down_v.at[pl.ds(half, rest)], r.zbe.at[z, me], r.xd_s.at[0], r.xd_r.at[0],
            {"shard": other})
        r.zbe.at[z, me][...] = r.down_v[pl.ds(half, rest), :]

    def clear():
        r.acc[...] = jnp.zeros_like(r.acc)
        r.bsum[...] = jnp.zeros_like(r.bsum)
        r.dk_acc[...] = jnp.zeros_like(r.dk_acc)
        r.dv_acc[...] = jnp.zeros_like(r.dv_acc)

    def tokens_start():
        held["first"] = start(r.xs.at[c], r.xs.at[c], r.xg_s.at[0], r.xg_r.at[0], {"ctx": ynb})
        held["near"] = start(r.xs.at[c], r.xs.at[c], r.xg_s.at[1], r.xg_r.at[1], {"ctx": sib})

    def tokens_pass():
        held["first"].wait_recv()
        held["passed"] = start(
            r.xs.at[ynb], r.xs.at[ynb], r.xg_s.at[2], r.xg_r.at[2], {"ctx": sib})

    def tokens_wait():
        held["near"].wait_recv()
        held["passed"].wait_recv()

    def project():
        for i in range(2):
            for h in range(heads):
                r.qv[i : i + 1, h * DH : (h + 1) * DH] = (
                    r.wq[0, 0, i * heads + h : i * heads + h + 1, 3 * cols : 3 * cols + DH].astype(F32))

        def rows_of_block(t, carry):
            rows = pl.ds(pl.multiple_of(t * rows_own, rows_own), rows_own)
            project_heads(heads, r.xs[t], rows, r.wq[...].reshape(width, r.wq.shape[3]),
                          r.qv, r.q, r.k, r.v)
            return carry

        lax.fori_loop(0, 4, rows_of_block, 0)

    def attend(b):
        @block
        def _():
            def part(t, carry):
                attend_rows(heads, pl.multiple_of(b * rows_own + t * 128, 128), 128, lengths, z,
                            r.q, r.k, r.v, r.probs, r.mixed, r.far)
                return carry

            lax.fori_loop(0, rows_own // 128, part, 0)

    def unpack_out():
        for s in range(2):
            for j in range(4):
                place = s * 4 + j
                r.w_out[pl.ds(place * piece, piece), :] = r.wo[s, j, 0:piece, 0:cols]
                row = piece + 2 * thirds
                r.vec[0:6, place * piece : (place + 1) * piece] = (
                    r.wo[s, j, row : row + 6, 0:piece].astype(F32))
        for i in range(2):
            for t in range(thirds):
                row = piece + i * thirds + t
                r.vec[6 + i : 7 + i, t * span : (t + 1) * span] = r.wo[0, 0, row : row + 1, :].astype(F32)

    def out_project(b):
        return dot_nt(r.mixed[rows_of(b), :], r.w_out[...])

    def out_far():
        @block
        def _():
            r.snd_r[...] = out_project(dia).astype(BF16)
        for k in range(NCH):
            send_relay(0, k)

    def out_cross():
        @block
        def _():
            r.yacc[...] = out_project(ynb)

    def out_near():
        near_block(0, lambda: out_project(sib))

    def out_own():
        own_block(lambda: out_project(c))

    def norm_one(rows):
        res = r.xs[c, rows, :].astype(F32) + summed(rows) + r.vec[4:5, :]
        center = res - jnp.mean(res, axis=-1, keepdims=True)
        scale = lax.rsqrt(jnp.mean(center * center, axis=-1, keepdims=True) + 1e-12)
        zh = center * scale
        value = zh * r.vec[0:1, :] + r.vec[2:3, :]
        r.zh1[rows, :] = zh
        r.r1[rows, :] = scale
        r.normed[rows, :] = value
        r.full[0, c, rows, :] = value.astype(BF16)

    def norm_one_chunk(k):
        arrived(0, k)
        tiles(k * cr, cr, norm_one)
        gather_start(0, k)

    def matrix(i):
        return r.w[i].reshape(width, width)

    def units_forward(b, r0, n):
        rows_in = r.full[0, b, pl.ds(r0, n), :]
        r.fa[pl.ds(0, n), :] = dot(rows_in, matrix(0))
        r.fb[pl.ds(0, n), :] = dot(rows_in, matrix(1))

        def units(rows):
            g = r.fa[rows, :] + r.vec[6:7, :]
            u = r.fb[rows, :] + r.vec[7:8, :]
            phi = 0.5 * (1.0 + lax.erf(g * (1.0 / math.sqrt(2.0))))
            gelu = g * phi
            slope = phi + g * jnp.exp(-0.5 * g * g) * (1.0 / math.sqrt(2.0 * math.pi))
            to = pl.ds(pl.multiple_of(r0 + rows.start, TILE), TILE)
            r.act[b, to, :] = gelu.astype(BF16)
            r.pull[b, to, :] = (u * slope).astype(BF16)
            r.hid[b, to, :] = (gelu * u).astype(BF16)

        tiles(0, n, units)

    def hid_rows(b, r0, n):
        return r.hid[b, pl.ds(r0, n), :]

    def down(rows):
        return dot_nt(rows, matrix(2))

    def units_backward(blocks, r0, n):
        def rows_at(ref, b):
            return ref[b, pl.ds(r0, n), :]

        def gather(ref):
            return both([rows_at(ref, b) for b in blocks]) if len(blocks) > 1 else rows_at(ref, blocks[0])

        r.fa[pl.ds(0, n * len(blocks)), :] = dot(gather(r.full.at[1]), matrix(2))
        for i, b in enumerate(blocks):
            def units(rows, b=b, i=i):
                dh = r.fa[rows, :]
                to = pl.ds(pl.multiple_of(r0 - i * n + rows.start, TILE), TILE)
                dg = (dh * r.pull[b, to, :].astype(F32)).astype(BF16)
                du = (dh * r.act[b, to, :].astype(F32)).astype(BF16)
                r.pull[b, to, :] = dg
                r.act[b, to, :] = du
                r.bsum[0] += fold(dg.astype(F32))
                r.bsum[1] += fold(du.astype(F32))

            tiles(i * n, n, units)
        return dot_nt(gather(r.pull), matrix(0)) + dot_nt(gather(r.act), matrix(1))

    def down_far(k):
        far_blocks(1, k, lambda: down(both([hid_rows(dia, k * cr, cr), hid_rows(ynb, k * cr, cr)])))

    def down_near():
        near_block(1, lambda: down(hid_rows(sib, 0, rows_own)))

    def down_own():
        own_block(lambda: down(hid_rows(c, 0, rows_own)))

    def norm_two(rows):
        res = r.normed[rows, :] + (summed(rows) + r.vec[5:6, :])
        center = res - jnp.mean(res, axis=-1, keepdims=True)
        scale = lax.rsqrt(jnp.mean(center * center, axis=-1, keepdims=True) + 1e-12)
        zh = center * scale
        r.lout[z, rows, :] = (zh * r.vec[1:2, :] + r.vec[3:4, :]).astype(BF16)
        up = r.cot[rows, :].astype(F32)
        t = up * r.vec[1:2, :]
        d = scale * (t - jnp.mean(t, axis=-1, keepdims=True)
                     - zh * jnp.mean(t * zh, axis=-1, keepdims=True))
        r.normed[rows, :] = d
        low = d.astype(BF16)
        r.full[1, c, rows, :] = low
        r.acc[1] += fold(up * zh)
        r.acc[3] += fold(up)
        r.acc[5] += fold(low.astype(F32))

    def norm_two_chunk(k):
        arrived(1, k)
        tiles(k * cr, cr, norm_two)
        gather_start(1, k)

    line_out = LineRelay(r.lout, r.lv, r.lw, r.lr)
    line_in = LineRelay(r.input_grad, r.lu, r.ld, r.li)

    def line_out_hop(d, h):
        line_out.hop(d, h)

    def line_in_hop(d, h):
        line_in.hop(d, h)

    def back_own():
        own_block(lambda: units_backward([c], 0, rows_own))

    def back_near():
        near_block(2, lambda: units_backward([sib], 0, rows_own))

    def back_far(k):
        far_blocks(2, k, lambda: units_backward([dia, ynb], k * cr, cr))

    def flat(ref):
        return ref[...].reshape(length, ref.shape[-1])

    def put(i, left, right):
        @block
        def _():
            r.w[i] = dot_tn(flat(left), flat(right)).astype(BF16).reshape(r.w.shape[1:])

    def put_down():
        for p in range(3):
            shard_drain(p)
        put(2, r.full.at[1], r.hid)

    def put_gate():
        put(0, r.full.at[0], r.pull)

    def put_up():
        put(1, r.full.at[0], r.act)

    def norm_back(rows):
        dn = summed(rows) + r.normed[rows, :]
        zh = r.zh1[rows, :]
        t = dn * r.vec[0:1, :]
        d = r.r1[rows, :] * (t - jnp.mean(t, axis=-1, keepdims=True)
                             - zh * jnp.mean(t * zh, axis=-1, keepdims=True))
        r.zh1[rows, :] = d
        low = d.astype(BF16)
        r.full[2, c, rows, :] = low
        r.acc[0] += fold(dn * zh)
        r.acc[2] += fold(dn)
        r.acc[4] += fold(low.astype(F32))

    def norm_back_chunk(k):
        arrived(2, k)
        tiles(k * cr, cr, norm_back)
        gather_start(2, k)

    def back_rows(b):
        @block
        def _():
            r.dmixed[rows_of(b), :] = dot(r.full[2, b], r.w_out[...]).astype(BF16)

            def part(t, carry):
                rows = pl.ds(pl.multiple_of(b * rows_own + t * 128, 128), 128)
                attend_back(heads, rows, r.dmixed, r.mixed, r.probs, r.q, r.k, r.v,
                            r.dqkv, r.dk_acc, r.dv_acc)
                return carry

            lax.fori_loop(0, rows_own // 128, part, 0)

    def tiny_first():
        for i in range(6):
            r.tiny[0, i : i + 1, :] = jnp.sum(r.acc[i], axis=0, keepdims=True)
        held["tiny"] = start(r.tiny.at[0], r.tiny.at[1], r.tiny_s.at[0], r.tiny_r.at[0], {"ctx": sib})

    def tiny_second():
        held["tiny"].wait_recv()
        r.tiny[2] = r.tiny[0] + r.tiny[1]
        held["tiny_y"] = start(r.tiny.at[2], r.tiny.at[3], r.tiny_s.at[1], r.tiny_r.at[1], {"ctx": ynb})

    def spread():
        @block
        def _():
            spread_heads(heads, r.dqkv, r.dk_acc, r.dv_acc)

    def into_input(rows):
        return dot_nt(rows, r.wq[...].reshape(width, r.wq.shape[3])[:, : 3 * cols])

    def input_far(k):
        far_blocks(3, k, lambda: into_input(both([
            r.dqkv[rows_of(dia, k * cr, cr), :], r.dqkv[rows_of(ynb, k * cr, cr), :]])))

    def input_near():
        near_block(3, lambda: into_input(r.dqkv[rows_of(sib), :]))

    def input_own():
        own_block(lambda: into_input(r.dqkv[rows_of(c), :]))

    def projection_gradients():
        held["tiny_y"].wait_recv()
        norms = r.tiny[2] + r.tiny[3]
        bias = jnp.sum(r.dqkv[...].astype(F32), axis=0, keepdims=True)
        r.extra[...] = jnp.zeros_like(r.extra)
        row = jnp.concatenate([bias[:, :cols], bias[:, 2 * cols :]], axis=1)
        lanes = r.extra.shape[1]
        spans = [row[:, t * lanes : (t + 1) * lanes] for t in range(2 * cols // lanes)]
        for i in range(2):
            value = jnp.sum(r.bsum[i], axis=0, keepdims=True)
            spans += [value[:, t * lanes : (t + 1) * lanes] for t in range(width // lanes)]
        for t, span_ in enumerate(spans):
            r.extra[t : t + 1, :] = span_
        count = len(spans)
        for s in range(2):
            for j in range(4):
                lane = (s * 4 + j) * piece
                r.extra[count : count + 6, 0:piece] = norms[0:6, lane : lane + piece]
                r.ge[s, j] = r.extra[...].astype(BF16)
        x_all = flat(r.xs)
        for i in range(4):
            lanes = slice(i * cols, (i + 1) * cols)
            if i < 3:
                value = dot_tn(x_all, r.dqkv[:, lanes])
            else:
                value = dot_tn(flat(r.full.at[2]), r.mixed[...])
            value = value.astype(BF16)
            for s in range(2):
                for j in range(4):
                    first_row = (s * 4 + j) * piece
                    r.g0[s, j, 0:piece, lanes] = value[first_row : first_row + piece]

    def input_chunk(k):
        arrived(3, k)
        r.input_grad[z, chunk(k), :] = (summed(chunk(k)) + r.zh1[chunk(k), :]).astype(BF16)

    save_out = pltpu.make_async_copy(r.lout, lout, r.save.at[0])
    save_in = pltpu.make_async_copy(r.input_grad, input_grad, r.save.at[1])

    def save_out_start():
        save_out.start()

    def save_in_start():
        save_in.start()

    def cot_wait():
        load_c.wait()

    def drain():
        save_out.wait()
        save_in.wait()
        line_out.drain()
        line_in.drain()
        for p in range(5):
            grad_drain(p)
        chain_drain()
        for p in index:
            hop_drain(p)
        for p in ("q", "o"):
            shard_drain(p)
        links.drain()

    cross_down()
    tokens_start()
    hop("q", 0)
    hop("o", 0)
    hop("q", 1)
    hop(1, 0)
    hop("q", 2)
    to_shard_if("q", 0, 0)
    hop("o", 1)
    hop(0, 0)
    clear()
    to_shard_if("q", 2, 2)
    hop("q", 3)
    to_shard_if("q", 1, 1)
    tokens_pass()
    to_shard_if("q", 3, 3)
    hop("o", 2)
    hop(1, 1)
    hop("o", 3)
    hop(1, 2)
    to_shard("o")
    hop(0, 1)
    tokens_wait()
    complete("q")
    project()
    hop(1, 3)
    to_shard_if(1, 2, 2)
    to_shard_if(1, 0, 0)
    attend(dia)
    hop(0, 2)
    hop(2, 0)
    to_shard_if(1, 3, 3)
    complete("o")
    to_shard_if(1, 1, 1)
    unpack_out()
    to_shard_if(0, 0, 0)
    out_far()
    hop(3, 0)
    attend(ynb)
    hop(0, 3)
    out_cross()
    relay(0, 1)
    to_shard_if(0, 1, 1)
    relay(0, 2)
    attend(sib)
    relay(0, 0)
    to_shard_if(0, 2, 2)
    out_near()
    relay(0, 3)
    to_shard_if(0, 3, 3)
    attend(c)
    hop(2, 1)
    hop(2, 2)
    hop(2, 3)
    out_own()
    norm_one_chunk(0)
    norm_one_chunk(1)
    norm_one_chunk(2)
    norm_one_chunk(3)
    to_shard_if(2, 3, 3)
    wait_near(0)
    to_shard_if(2, 1, 1)
    forward(0, 0)
    hop(3, 1)
    hop(3, 2)
    to_shard_if(2, 2, 2)
    complete(0)
    complete(1)
    units_forward(c, 0, rows_own)
    to_shard_if(2, 0, 0)
    forward(0, 3)
    wait_far(0, 0)
    forward(0, 2)
    units_forward(sib, 0, rows_own)
    hop(3, 3)
    forward(0, 1)
    units_forward(ynb, 0, rows_own)
    wait_far(0, 2)
    cot_wait()
    wait_far(0, 3)
    wait_far(0, 1)
    units_forward(dia, 0, rows_own)
    complete(2)
    complete(3)
    down_far(0)
    down_far(1)
    relay(1, 0)
    relay(1, 1)
    down_far(2)
    down_far(3)
    down_near()
    down_own()
    relay(1, 2)
    relay(1, 3)
    norm_two_chunk(0)
    norm_two_chunk(1)
    norm_two_chunk(2)
    norm_two_chunk(3)
    line_out_hop(0, 0)
    line_out_hop(0, 1)
    back_own()
    forward(1, 0)
    wait_near(1)
    back_near()
    forward(1, 1)
    wait_far(1, 0)
    back_far(0)
    forward(1, 2)
    wait_far(1, 1)
    back_far(1)
    relay(2, 0)
    forward(1, 3)
    wait_far(1, 2)
    back_far(2)
    relay(2, 1)
    wait_far(1, 3)
    back_far(3)
    relay(2, 2)
    put_down()
    chain(0)
    grad_to_shard(3)
    relay(2, 3)
    norm_back_chunk(0)
    put_up()
    grad_to_shard(2)
    line_out_hop(1, 1)
    put_gate()
    line_out_hop(1, 0)
    norm_back_chunk(1)
    norm_back_chunk(2)
    norm_back_chunk(3)
    tiny_first()
    wait_near(2)
    grad_to_owner(3, 0)
    back_rows(c)
    grad_to_owner(3, 2)
    grad_to_owner(3, 1)
    forward(2, 1)
    grad_to_owner(3, 3)
    forward(2, 0)
    chain(1)
    chain(2)
    forward(2, 2)
    line_out_hop(2, 0)
    back_rows(sib)
    grad_to_shard(1)
    forward(2, 3)
    wait_far(2, 2)
    wait_far(2, 1)
    tiny_second()
    back_rows(ynb)
    chain(3)
    grad_hop(3, 0)
    wait_far(2, 0)
    wait_far(2, 3)
    back_rows(dia)
    grad_to_owner(2, 0)
    line_out_hop(2, 1)
    spread()
    input_far(0)
    grad_hop(3, 1)
    input_far(1)
    relay(3, 0)
    input_far(2)
    input_far(3)
    chain(4)
    input_near()
    grad_hop(3, 2)
    line_out_hop(3, 0)
    relay(3, 1)
    input_own()
    grad_to_owner(2, 3)
    relay(3, 2)
    input_chunk(0)
    line_in_hop(0, 0)
    input_chunk(1)
    line_in_hop(0, 1)
    relay(3, 3)
    input_chunk(2)
    line_in_hop(0, 2)
    projection_gradients()
    grad_to_shard(0)
    input_chunk(3)
    line_in_hop(0, 3)
    line_in_hop(1, 0)
    grad_to_owner(2, 1)
    chain(5)
    grad_to_owner(2, 2)
    grad_hop(2, 0)
    line_in_hop(1, 1)
    grad_hop(2, 1)
    grad_to_owner(1, 2)
    line_out_hop(3, 1)
    line_in_hop(1, 2)
    grad_to_owner(1, 0)
    line_in_hop(1, 3)
    grad_to_owner(1, 1)
    grad_to_owner(1, 3)
    grad_hop(3, 3)
    grad_hop(1, 0)
    grad_hop(1, 1)
    line_in_hop(2, 1)
    grad_to_owner(0, 1)
    line_in_hop(2, 0)
    line_in_hop(2, 2)
    grad_to_owner(0, 3)
    grad_to_owner(0, 0)
    grad_hop(2, 2)
    line_in_hop(2, 3)
    grad_to_owner(0, 2)
    grad_hop(0, 0)
    chain_end()
    grad_hop(0, 1)
    line_in_hop(3, 3)
    grad_hop(1, 2)
    chain_across()
    line_in_hop(3, 0)
    grad_hop(0, 2)
    grad_hop(1, 3)
    chain_total()
    line_in_hop(3, 2)
    line_in_hop(3, 1)
    grad_hop(2, 3)
    save_in_start()
    save_out_start()
    grad_hop(0, 3)
    drain()


def finish(
    lout, input_low, out0, oute, outr,
    o_lout, o_in, o_qkv, o_qvb, o_out, o_geglu, o_gb, o_down, o_gain, o_shift, o_ob,
    low, narrow, wide, first, few, rest, v_qkv, v_qvb, v_out, v_gb, v_gain, v_shift, v_ob,
    sem_in, sem_out,
):
    piece = outr.shape[1]
    cols = o_qkv.shape[2]
    blocks = narrow.shape[0]
    lanes = few.shape[1]
    started = []

    def save(src, dst):
        one = pltpu.make_async_copy(src, dst, sem_out.at[len(started)])
        one.start()
        started.append(one)

    pairs = [(out0, first), (oute, few), (outr, rest)]
    pairs += [(input_low.at[i], narrow.at[i]) for i in range(blocks)]
    pairs += [(lout.at[i], low.at[i]) for i in range(blocks)]
    loads = [pltpu.make_async_copy(src, dst, sem_in.at[i]) for i, (src, dst) in enumerate(pairs)]
    for one in loads:
        one.start()
    loads[0].wait()
    for i in range(3):
        v_qkv[i] = first[:, i * cols : (i + 1) * cols]
    v_out[...] = first[:, 3 * cols : 4 * cols].T
    loads[1].wait()
    row = jnp.concatenate([few[t : t + 1, :] for t in range(2 * cols // lanes)], axis=1)
    v_qvb[0:1, :] = row[:, 0:cols]
    v_qvb[1:2, :] = row[:, cols : 2 * cols]
    count = 2 * cols // lanes
    for i in range(2):
        for t in range(v_gb.shape[1] // lanes):
            v_gb[i : i + 1, t * lanes : (t + 1) * lanes] = few[count : count + 1, :]
            count += 1
    for i, ref in enumerate((v_gain, v_shift, v_ob)):
        ref[...] = few[count + 2 * i : count + 2 * i + 2, 0:piece]
    for src, dst in ((v_qkv, o_qkv), (v_out, o_out), (v_qvb, o_qvb), (v_gb, o_gb),
                     (v_gain, o_gain), (v_shift, o_shift), (v_ob, o_ob)):
        save(src, dst)
    loads[2].wait()
    save(rest.at[pl.ds(0, 2)], o_geglu)
    save(rest.at[2], o_down)
    for i in range(blocks):
        loads[3 + i].wait()
        wide[i] = narrow[i].astype(F32)
        save(wide.at[i], o_in.at[i])
    for i in range(blocks):
        loads[3 + blocks + i].wait()
        save(low.at[i], o_lout.at[i])
    for one in started:
        one.wait()


def middle(
    x, cot, mixed, w0, w, vec,
    lout, dres1, grads, gout, dmixed, small,
    w_out, full, act, pull, hid, dgt, dup,
    snd_r, snd_o, snd_y, rcv_r, rcv_o, rcv_y,
    own, yacc, fa, fb, normed, zh1, r1, dres2, acc, bsum, tiny,
    ags_y, agr_y, ags_c, agr_c, ags_f, agr_f,
    rss_r, rsr_r, rss_o, rsr_o, rss_y, rsr_y, tiny_s, tiny_r, ls, lr,
):
    rows_own = x.shape[0]
    width = x.shape[1]
    cr = rows_own // NCH
    c, sib, ynb, dia = places()
    z = lax.axis_index("tp")
    tp = lout.shape[0]
    greet([{"ctx": sib}, {"ctx": ynb}] + [{"tp": (z + d) % tp} for d in range(1, tp)])
    line = LineGather(lout, ls, lr)

    started = []

    def remote(src, dst, send, recv, peer):
        return pltpu.make_async_remote_copy(
            src_ref=src, dst_ref=dst, send_sem=send, recv_sem=recv,
            device_id={"ctx": peer}, device_id_type=MESH,
        )

    def chunk(k):
        return pl.ds(k * cr, cr)

    ag_y, ag_c, ag_f, rs_r, rs_o, rs_y = ({} for _ in range(6))

    def start(table, key, copy):
        copy.start()
        table[key] = copy
        started.append(copy)

    def gather_start(o, k):
        piece = full.at[o, c, chunk(k)]
        start(ag_y, (o, k), remote(piece, piece, ags_y.at[o, k], agr_y.at[o, k], ynb))
        start(ag_c, (o, k), remote(piece, piece, ags_c.at[o, k], agr_c.at[o, k], sib))

    def forward(o, k):
        ag_y[o, k].wait_recv()
        piece = full.at[o, ynb, chunk(k)]
        start(ag_f, (o, k), remote(piece, piece, ags_f.at[o, k], agr_f.at[o, k], sib))

    def send_relay(o, k):
        start(rs_r, (o, k), remote(
            snd_r.at[o, chunk(k)], rcv_r.at[o, chunk(k)], rss_r.at[o, k], rsr_r.at[o, k], sib))

    def send_own(o, k):
        start(rs_o, (o, k), remote(
            snd_o.at[o, chunk(k)], rcv_o.at[o, chunk(k)], rss_o.at[o, k], rsr_o.at[o, k], sib))

    def relay(o, k):
        rs_r[o, k].wait_recv()
        snd_y[o, chunk(k), :] = (yacc[chunk(k), :] + rcv_r[o, chunk(k), :].astype(F32)).astype(BF16)
        start(rs_y, (o, k), remote(
            snd_y.at[o, chunk(k)], rcv_y.at[o, chunk(k)], rss_y.at[o, k], rsr_y.at[o, k], ynb))

    def arrived(o, k):
        rs_o[o, k].wait_recv()
        rs_y[o, k].wait_recv()

    def tiles(first, count, body):
        def step(t, carry):
            body(pl.ds(pl.multiple_of(first + t * TILE, TILE), TILE))
            return carry
        lax.fori_loop(0, count // TILE, step, 0)

    def summed(o, rows):
        return own[rows, :] + rcv_o[o, rows, :].astype(F32) + rcv_y[o, rows, :].astype(F32)

    def fold(values):
        return jnp.sum(values.reshape(TILE // 8, 8, width), axis=0)

    acc[...] = jnp.zeros_like(acc)
    bsum[...] = jnp.zeros_like(bsum)
    w_out[...] = w0[:, 3 * mixed.shape[2] : 4 * mixed.shape[2]]

    def project(b, r0, n):
        return dot_nt(mixed[b, pl.ds(r0, n), :], w_out[...])

    for k in range(NCH):
        snd_r[0, chunk(k), :] = project(dia, k * cr, cr).astype(BF16)
        send_relay(0, k)
        yacc[chunk(k), :] = project(ynb, k * cr, cr)
        if k:
            relay(0, k - 1)
    relay(0, NCH - 1)
    for k in range(NCH):
        snd_o[0, chunk(k), :] = project(sib, k * cr, cr).astype(BF16)
        send_own(0, k)
    own[...] = project(c, 0, rows_own)

    def norm_one(rows):
        res = x[rows, :].astype(F32) + summed(0, rows) + vec[4:5, :]
        center = res - jnp.mean(res, axis=-1, keepdims=True)
        r = lax.rsqrt(jnp.mean(center * center, axis=-1, keepdims=True) + 1e-12)
        zh = center * r
        out = zh * vec[0:1, :] + vec[2:3, :]
        zh1[rows, :] = zh
        r1[rows, :] = r
        normed[rows, :] = out
        full[0, c, rows, :] = out.astype(BF16)

    for k in range(NCH):
        arrived(0, k)
        tiles(k * cr, cr, norm_one)
        gather_start(0, k)

    def mlp_forward(b, r0, n):
        rows_in = full[0, b, pl.ds(r0, n), :]
        fa[pl.ds(0, n), :] = dot(rows_in, w[0])
        fb[pl.ds(0, n), :] = dot(rows_in, w[1])

        def units(rows):
            g = fa[rows, :] + vec[6:7, :]
            u = fb[rows, :] + vec[7:8, :]
            phi = 0.5 * (1.0 + lax.erf(g * (1.0 / math.sqrt(2.0))))
            gelu = g * phi
            slope = phi + g * jnp.exp(-0.5 * g * g) * (1.0 / math.sqrt(2.0 * math.pi))
            out = pl.ds(pl.multiple_of(r0 + rows.start, TILE), TILE)
            act[b, out, :] = gelu.astype(BF16)
            pull[b, out, :] = (u * slope).astype(BF16)
            hid[b, out, :] = (gelu * u).astype(BF16)

        tiles(0, n, units)
        return dot_nt(hid[b, pl.ds(r0, n), :], w[2])

    def mlp_backward(b, r0, n):
        fa[pl.ds(0, n), :] = dot(full[1, b, pl.ds(r0, n), :], w[2])

        def units(rows):
            dh = fa[rows, :]
            out = pl.ds(pl.multiple_of(r0 + rows.start, TILE), TILE)
            dg = (dh * pull[b, out, :].astype(F32)).astype(BF16)
            du = (dh * act[b, out, :].astype(F32)).astype(BF16)
            dgt[b, out, :] = dg
            dup[b, out, :] = du
            bsum[0] += fold(dg.astype(F32))
            bsum[1] += fold(du.astype(F32))

        tiles(0, n, units)
        return dot_nt(dgt[b, pl.ds(r0, n), :], w[0]) + dot_nt(dup[b, pl.ds(r0, n), :], w[1])

    def exchange(o, piece):
        own[...] = piece(c, 0, rows_own)
        for k in range(NCH):
            ag_c[o - 1, k].wait_recv()
        snd_o[o] = piece(sib, 0, rows_own).astype(BF16)
        for k in range(NCH):
            send_own(o, k)
        for k in range(NCH):
            forward(o - 1, k)
            yacc[chunk(k), :] = piece(ynb, k * cr, cr)
            ag_f[o - 1, k].wait_recv()
            snd_r[o, chunk(k), :] = piece(dia, k * cr, cr).astype(BF16)
            send_relay(o, k)
            if k:
                relay(o, k - 1)
        relay(o, NCH - 1)

    exchange(1, mlp_forward)

    def norm_two(rows):
        res = normed[rows, :] + (summed(1, rows) + vec[5:6, :])
        center = res - jnp.mean(res, axis=-1, keepdims=True)
        r = lax.rsqrt(jnp.mean(center * center, axis=-1, keepdims=True) + 1e-12)
        zh = center * r
        lout[z, rows, :] = (zh * vec[1:2, :] + vec[3:4, :]).astype(BF16)
        up = cot[rows, :].astype(F32)
        t = up * vec[1:2, :]
        d = r * (t - jnp.mean(t, axis=-1, keepdims=True)
                 - zh * jnp.mean(t * zh, axis=-1, keepdims=True))
        dres2[rows, :] = d
        low = d.astype(BF16)
        full[1, c, rows, :] = low
        acc[1] += fold(up * zh)
        acc[3] += fold(up)
        acc[5] += fold(low.astype(F32))

    for k in range(NCH):
        arrived(1, k)
        tiles(k * cr, cr, norm_two)
        gather_start(1, k)

    line.hop(0)
    exchange(2, mlp_backward)
    line.hop(1)

    def flat(ref):
        return ref[...].reshape(4 * rows_own, ref.shape[-1])

    hid_all = flat(hid)
    d_all = full[1].reshape(4 * rows_own, width)
    grads[2] = dot_tn(d_all, hid_all).astype(BF16)
    n_all = full[0].reshape(4 * rows_own, width)
    grads[0] = dot_tn(n_all, flat(dgt)).astype(BF16)
    grads[1] = dot_tn(n_all, flat(dup)).astype(BF16)

    line.hop(2)

    def norm_back(rows):
        dn = summed(2, rows) + dres2[rows, :]
        zh = zh1[rows, :]
        t = dn * vec[0:1, :]
        d = r1[rows, :] * (t - jnp.mean(t, axis=-1, keepdims=True)
                           - zh * jnp.mean(t * zh, axis=-1, keepdims=True))
        dres1[rows, :] = d
        low = d.astype(BF16)
        full[2, c, rows, :] = low
        acc[0] += fold(dn * zh)
        acc[2] += fold(dn)
        acc[4] += fold(low.astype(F32))

    for k in range(NCH):
        arrived(2, k)
        tiles(k * cr, cr, norm_back)
        gather_start(2, k)

    for i in range(6):
        tiny[0, i : i + 1, :] = jnp.sum(acc[i], axis=0, keepdims=True)
    for i in range(2):
        small[6 + i : 7 + i, :] = jnp.sum(bsum[i], axis=0, keepdims=True)
    tiny_copies = []
    for step, peer in enumerate((sib, ynb)):
        copy = remote(tiny.at[2 * step], tiny.at[2 * step + 1], tiny_s.at[step], tiny_r.at[step], peer)
        copy.start()
        started.append(copy)
        tiny_copies.append(copy)
        if step == 0:
            def unproject(b, r0, n):
                return dot(full[2, b, pl.ds(r0, n), :], w_out[...]).astype(BF16)
            dmixed[c] = unproject(c, 0, rows_own)
            for k in range(NCH):
                ag_c[2, k].wait_recv()
            dmixed[sib] = unproject(sib, 0, rows_own)
        copy.wait_recv()
        total = tiny[2 * step] + tiny[2 * step + 1]
        if step == 0:
            tiny[2] = total
        else:
            small[0:6, :] = total[0:6, :]
    for k in range(NCH):
        forward(2, k)
        dmixed[ynb, chunk(k), :] = unproject(ynb, k * cr, cr)
    for k in range(NCH):
        ag_f[2, k].wait_recv()
        dmixed[dia, chunk(k), :] = unproject(dia, k * cr, cr)
    gout[...] = dot_tn(full[2].reshape(4 * rows_own, width), flat(mixed)).astype(BF16)
    line.hop(3)
    line.drain()
    for copy in started:
        copy.wait_send()


def sds(shape, dtype):
    return jax.ShapeDtypeStruct(shape, dtype)


def smem():
    return pl.BlockSpec(memory_space=pltpu.SMEM)


def on_device(
    tokens_in, qkv_weight, qv_bias, out_weight, geglu_weight, geglu_bias, down_weight,
    norm_gains, norm_biases, out_biases, doc_lengths, cotangent,
):
    seqs, rows, width = tokens_in.shape
    group = lax.axis_size("ctx")
    tp = lax.axis_size("tp")
    shards = lax.axis_size("shard")
    z = lax.axis_index("tp")
    c = lax.axis_index("ctx")
    assert group == 4 and tp == 4 and seqs == tp
    length = group * rows
    part_rows = qkv_weight.shape[1]
    cols = qkv_weight.shape[2]
    heads = cols // DH
    units = geglu_weight.shape[2]
    assert units == width and 4 * cols == width and H == heads * tp

    me = lax.axis_index("shard") * group + c
    dma = lambda *shape: pltpu.SemaphoreType.DMA(shape)
    head_shape = sds((heads, length, DH), BF16)
    block = (rows, width)
    stack = (group, rows, width)
    if shards == 2 and part_rows % 96 == 0:
        vm = pltpu.VMEM
        wide = part_rows + 16
        front, back = part_rows * FRONT_CUT // 6, part_rows * BACK_CUT // 6
        pieces = lambda n: (vm((n, part_rows, width), BF16), vm((2, n, part_rows, width), BF16))
        scratch = dict(
            pq=vm((part_rows, 640), BF16), po=vm((wide, 256), BF16),
            lout=vm((tp,) + block, BF16), input_grad=vm((tp,) + block, BF16), save=dma(2),
            zbq=vm((tp, part_rows, 640), BF16), zbo=vm((tp, wide, 256), BF16),
            zbr=vm((2, tp, part_rows, width), BF16),
            zbd=vm((tp, front, width), BF16), zbe=vm((tp, 2, part_rows - front, width), BF16),
            xd_s=dma(1), xd_r=dma(1),
            load=dma(6), qkv_v=vm((3, part_rows, cols), BF16), out_v=vm((cols, part_rows), BF16),
            down_v=vm((part_rows, width), BF16), geglu_v=vm((2, part_rows, width), BF16), cb=vm((2, 2, group, part_rows - back, width), BF16),
            yd=vm((2, part_rows - back, width), BF16), xd=vm((part_rows - back, width), BF16),
            ch_s=dma(2, 4), ch_r=dma(2, 4), cy_s=dma(4), cy_r=dma(1), cx_s=dma(1), cx_r=dma(1),
            cot=vm(block, BF16), xs=vm(stack, BF16),
            wq=vm((2, group, part_rows, 640), BF16), wo=vm((2, group, wide, 256), BF16),
            g0=vm((2, group, part_rows, width), BF16), w=vm((3, 2, group, part_rows, width), BF16),
            w_out=vm((width, cols), BF16),
            qv=vm((2, cols), F32), vec=vm((8, width), F32), extra=vm((32, 128), F32), ge=vm((2, group, 32, 128), BF16),
            xe=vm((group, 32, 128), BF16), ye=vm((group, 32, 128), BF16), re=vm((tp + 1, 32, 128), BF16),
            probs=vm((heads, length, length), BF16),
            q=vm((heads, length, DH), BF16), k=vm((heads, length, DH), BF16),
            v=vm((heads, length, DH), BF16), far=vm((128, length), F32),
            mixed=vm((length, cols), BF16), dmixed=vm((length, cols), BF16),
            full=vm((3,) + stack, BF16), act=vm(stack, BF16), pull=vm(stack, BF16),
            hid=vm(stack, BF16),
            **{n: vm(block, BF16) for n in ("snd_r", "snd_o", "snd_y", "rcv_r", "rcv_o", "rcv_y")},
            **{n: vm(block, F32) for n in ("own", "yacc", "fa", "fb", "normed", "zh1")},
            r1=vm((rows, 1), F32), acc=vm((6, 8, width), F32), bsum=vm((2, 8, width), F32),
            tiny=vm((4, 8, width), F32),
            dqkv=vm((length, 3 * cols), BF16),
            dk_acc=vm((heads, DH, length), F32), dv_acc=vm((heads, DH, length), F32),
            xg_s=dma(3), xg_r=dma(3),
            **{n: dma(6, 4) for n in ("zu", "zd", "zu2", "zd2", "zr", "ys", "yr", "xs_s", "xs_r")},
            **{n: dma(5, 4) for n in ("gx_s", "gx_r", "gy_s", "gy_r",
                                      "gu_s", "gu_r", "gd_s", "gd_r")},
            **{n: dma(3, NCH) for n in ("ags_y", "agr_y", "ags_c", "agr_c", "ags_f", "agr_f")},
            **{n: dma(4, NCH) for n in ("rss_r", "rsr_r", "rss_o", "rsr_o", "rss_y", "rsr_y")},
            tiny_s=dma(2), tiny_r=dma(2), lv=dma(2, tp), lw=dma(2, tp), lr=dma(2, tp), lu=dma(NCH, tp), ld=dma(NCH, tp), li=dma(NCH, tp),
        )
        for n, count in (("xb", group), ("yb", group), ("rb", tp + 1)):
            scratch[n + "0"], scratch[n + "r"] = pieces(count)
            scratch[n + "h"] = vm((count, back, width), BF16)
        raw = pl.pallas_call(
            functools.partial(layer, tuple(scratch), heads),
            out_shape=[
                sds((tp,) + block, BF16), sds((tp,) + block, BF16),
                sds((part_rows, width), F32), sds((32, 128), F32), sds((3, part_rows, width), F32),
            ],
            in_specs=[smem()] + [pl.BlockSpec(memory_space=pl.ANY)] * 6 + vmem(5),
            out_specs=[pl.BlockSpec(memory_space=pl.ANY)] * 2 + vmem(3),
            scratch_shapes=list(scratch.values()),
            compiler_params=pltpu.CompilerParams(
                collective_id=1, has_side_effects=True, vmem_limit_bytes=VMEM_MB * MB
            ),
            name="layer",
        )(
            doc_lengths, tokens_in, cotangent, qkv_weight, out_weight, geglu_weight,
            down_weight.T, qv_bias, geglu_bias, norm_gains, norm_biases, out_biases,
        )
        res = pl.pallas_call(
            finish,
            out_shape=[
                sds((tp,) + block, BF16), sds((tp,) + block, F32),
                sds(qkv_weight.shape, F32), sds(qv_bias.shape, F32), sds(out_weight.shape, F32),
                sds(geglu_weight.shape, F32), sds(geglu_bias.shape, F32),
                sds(down_weight.shape[::-1], F32),
            ] + [sds(norm_gains.shape, F32)] * 3,
            in_specs=[pl.BlockSpec(memory_space=pl.ANY)] * 5,
            out_specs=[pl.BlockSpec(memory_space=pl.ANY)] * 11,
            scratch_shapes=[
                vm((tp,) + block, BF16), vm((tp,) + block, BF16), vm((tp,) + block, F32),
                vm((part_rows, width), F32), vm((32, 128), F32), vm((3, part_rows, width), F32),
                vm(qkv_weight.shape, F32), vm(qv_bias.shape, F32), vm(out_weight.shape, F32),
                vm(geglu_bias.shape, F32),
            ] + [vm(norm_gains.shape, F32)] * 3 + [dma(3 + 2 * tp), dma(9 + 2 * tp)],
            compiler_params=pltpu.CompilerParams(vmem_limit_bytes=VMEM_MB * MB),
            name="finish",
        )(*raw)
        return (*res[:7], res[7].T, *res[8:])

    with jax.named_scope("pack_weights"):
        first = jnp.concatenate(
            [qkv_weight[0], qkv_weight[1], qkv_weight[2], out_weight.T], axis=1
        )
        own_norm = jnp.concatenate([norm_gains, norm_biases, out_biases], axis=0)
        parts = jnp.concatenate([first[None], geglu_weight, down_weight.T[None]], axis=0)
        own_bias = jnp.concatenate([qv_bias.reshape(1, -1), geglu_bias.reshape(1, -1)], axis=1)

    lengths = lax.dynamic_slice_in_dim(doc_lengths, z, 1, 0)
    x_own = lax.dynamic_index_in_dim(tokens_in, z, 0, keepdims=False)
    cot_own = lax.dynamic_index_in_dim(cotangent, z, 0, keepdims=False)
    with jax.named_scope("gather_weights"):
        by_block = lax.all_gather(parts, "tp", axis=0)
        swapped = lax.all_to_all(by_block, "ctx", split_axis=0, concat_axis=0)
        w = lax.all_gather(swapped, "shard", axis=0)
        w = w.transpose(2, 0, 1, 3, 4).reshape(4, shards * group * part_rows, width)
        biases = lax.all_gather(own_bias, "tp", axis=0, tiled=True)
        biases = lax.dynamic_slice_in_dim(biases, c, 1, 0).astype(F32)
        norms = lax.all_gather(own_norm, ("shard", "ctx"), axis=1, tiled=True).astype(F32)
    qv = biases[:, : 2 * cols].reshape(2, cols)
    vec = jnp.concatenate([norms, biases[:, 2 * cols :].reshape(2, units)], axis=0)

    xs = lax.all_gather(x_own, "ctx", axis=0, tiled=True)

    mixed, probs, q, k, v = pl.pallas_call(
        functools.partial(attention_forward, heads),
        out_shape=[sds((length, cols), BF16), sds((heads, length, length), BF16)] + [head_shape] * 3,
        in_specs=[smem()] + vmem(3),
        out_specs=vmem(5),
        scratch_shapes=[pltpu.VMEM((256, length), F32)],
        compiler_params=pltpu.CompilerParams(vmem_limit_bytes=48 * MB),
        name="attention_forward",
    )(lengths, xs, w[0], qv)
    w0, w = w[0], w[1:]


    lout, dres1, grads, gout, dmixed, small = pl.pallas_call(
        middle,
        out_shape=[
            sds((tp,) + block, BF16), sds(block, F32), sds((3, width, width), BF16),
            sds((width, cols), BF16), sds((group, rows, cols), BF16), sds((8, width), F32),
        ],
        in_specs=vmem(6),
        out_specs=vmem(6),
        scratch_shapes=[
            pltpu.VMEM((width, cols), BF16), pltpu.VMEM((3,) + stack, BF16),
        ] + [pltpu.VMEM(stack, BF16)] * 5 + [pltpu.VMEM((3,) + block, BF16)] * 6 + [
            pltpu.VMEM(block, F32)
        ] * 6 + [
            pltpu.VMEM((rows, 1), F32), pltpu.VMEM(block, F32),
            pltpu.VMEM((6, 8, width), F32), pltpu.VMEM((2, 8, width), F32),
            pltpu.VMEM((4, 8, width), F32),
        ] + [dma(3, NCH)] * 12 + [dma(2)] * 2 + [dma(5), dma(tp)],
        compiler_params=pltpu.CompilerParams(
            collective_id=0, has_side_effects=True, vmem_limit_bytes=58 * MB
        ),
        name="middle",
    )(x_own, cot_own, mixed.reshape(group, rows, cols), w0, w, vec)

    grad_w, d_in, bias_grad = pl.pallas_call(
        functools.partial(attention_backward, heads),
        out_shape=[
            sds((width, 3 * cols), BF16), sds((length, width), BF16), sds((1, 3 * cols), F32)
        ],
        in_specs=vmem(8),
        out_specs=vmem(3),
        scratch_shapes=[
            pltpu.VMEM((length, 3 * cols), BF16),
            pltpu.VMEM((heads, DH, length), F32), pltpu.VMEM((heads, DH, length), F32),
        ],
        compiler_params=pltpu.CompilerParams(vmem_limit_bytes=48 * MB),
        name="attention_backward",
    )(dmixed.reshape(length, cols), mixed, probs, q, k, v, xs, w0)

    with jax.named_scope("outputs"):
        input_sum = lax.psum_scatter(d_in, "ctx", scatter_dimension=0, tiled=True)
        input_own = (input_sum.astype(F32) + dres1).astype(BF16)
        input_grad = lax.all_gather(input_own, "tp", axis=0).astype(F32)
        layer_out = lout

    with jax.named_scope("scatter_grads"):
        first_grad = jnp.concatenate([grad_w, gout], axis=1)
        packed = jnp.concatenate([first_grad[None], grads], axis=0)
        packed = packed.reshape(4, shards, group, part_rows, width).transpose(1, 2, 0, 3, 4)
        mine = lax.psum_scatter(packed, "shard", scatter_dimension=0, tiled=False)
        mine = lax.all_to_all(mine, "ctx", split_axis=0, concat_axis=0)
        mine = lax.psum_scatter(mine, "tp", scatter_dimension=0, tiled=False)
        mine = mine.astype(F32)
        grad_qkv = jnp.stack([mine[0, :, i * cols : (i + 1) * cols] for i in range(3)])
        grad_out = mine[0, :, 3 * cols :].T
        grad_geglu = mine[1:3]
        grad_down = mine[3].T
        col = jnp.concatenate(
            [bias_grad[:, :cols], bias_grad[:, 2 * cols :], small[6:7], small[7:8]], axis=1
        )
        col = lax.psum_scatter(
            jnp.zeros((group, col.shape[1]), F32) + jnp.where(
                jnp.arange(group)[:, None] == c, col, 0.0),
            "tp", scatter_dimension=0, tiled=True)
        col = lax.psum(col, ("shard", "ctx"))
        norm_grad = lax.psum(small[:6], ("shard", "tp"))
        norm_grad = lax.dynamic_slice_in_dim(norm_grad, me * part_rows, part_rows, 1)
    return (
        layer_out,
        input_grad,
        grad_qkv,
        col[:, : 2 * cols].reshape(2, cols),
        grad_out,
        grad_geglu,
        col[:, 2 * cols :].reshape(2, units),
        grad_down,
        norm_grad[0:2],
        norm_grad[2:4],
        norm_grad[4:6],
    )


def solution(mesh):
    in_specs = (
        P("shard", "ctx", None),
        P(None, ("shard", "ctx"), "tp"),
        P(None, "tp"),
        P("tp", ("shard", "ctx")),
        P(None, ("shard", "ctx"), "tp"),
        P(None, "tp"),
        P("tp", ("shard", "ctx")),
        P(None, ("shard", "ctx")),
        P(None, ("shard", "ctx")),
        P(None, ("shard", "ctx")),
        P("shard", None),
        P("shard", "ctx", None),
    )
    out_specs = (
        P("shard", "ctx", None),
        P("shard", "ctx", None),
        P(None, ("shard", "ctx"), "tp"),
        P(None, "tp"),
        P("tp", ("shard", "ctx")),
        P(None, ("shard", "ctx"), "tp"),
        P(None, "tp"),
        P("tp", ("shard", "ctx")),
        P(None, ("shard", "ctx")),
        P(None, ("shard", "ctx")),
        P(None, ("shard", "ctx")),
    )
    return jax.shard_map(
        on_device, mesh=mesh, in_specs=in_specs, out_specs=out_specs, check_vma=False
    )
```
